32 devices in a mesh: grp: 2 (over y), cp: 4 (over z), dec: 4 (over x, core).
Axes of the slice: x: 2, y: 2, z: 4, core: 2. Of those that a mesh axis runs over, the one named last changes fastest.
Arguments:
- queries: bfloat16 [1024, 12288], P(('grp', 'cp'), 'dec'), parts along dimension 0, may hold values from -120 to 120
- latent_rows: bfloat16 [1024, 576], P(('grp', 'cp')), parts along dimension 0, may hold values from -16 to 16
- key_absorb: bfloat16 [64, 128, 512], P('dec'), may hold values from -0.5 to 0.5
- value_expand: bfloat16 [64, 512, 128], P('dec'), may hold values from -0.25 to 0.25
- prompt_pages: int32 [4], P('grp'), parts along dimension 0, may hold values from 1 to 24, 32 in all
- decode_owner: int32 [4, 2], P('grp'), parts along dimension 0, may hold values from 0 to 3, as said below
- slot_offset: int32 [4], P('grp'), parts along dimension 0, may hold values from 0 to 23
Outputs:
- attended: bfloat16 [1024, 8192], P(('grp', 'cp'), 'dec'), parts along dimension 0
- page_cache: bfloat16 [8, 4, 3, 16, 576], P(('grp', 'cp'), 'dec'), parts along dimension 0
- page_scales: bfloat16 [8, 4, 3, 16, 4], P(('grp', 'cp'), 'dec'), parts along dimension 0
The draws below stay inside these ranges and needn't reach their ends.
There are 2 independent parts, one for each index of `grp`. The reference program is written for one: setup_inputs(seed, part) draws one part's arguments, and reference() takes and returns one part's arrays. A program takes and returns all parts, laid end to end along the dimension named above; an argument that names none is the same for every part. Nothing has to cross between parts.
Inputs may be any that keep to these rules, and one draw needn't show every extreme that they name: `prompt_pages`: the lengths sum to 32; every owner device receives at most 3 pages and some receive exactly that many. `decode_owner`: every owner appears exactly once in the whole list.
All inputs are finite; a program needn't handle non-finite values. Where the reference program divides by a largest or mean magnitude, that divisor is 1e-20 or more.
Results may differ from the reference program's by a relative error of at most 0.008.
Values may be sent and summed in bfloat16 or wider, within the bound.
No kernel may reach another device: no remote copies, remote signals or barrier semaphores. Data moves between devices by JAX's collectives and lax.ppermute only.
A program may use at most 64 MiB of HBM per device.

```python
import math
import jax
import jax.numpy as jnp
import numpy as np
from jax import lax

LAT = 512
ROPE = 64
NOPE = 128
VDIM = 128
HEADS = 64
PAGE = 16
BLOCK = 128
PROMPTS = 2
TOK_DEV = 128
TOKENS = 512
PAGES = 32
OWNERS = 4
GROUPW = 2
DECS = 4
CAP_DEC = 3
MOSTP = 24
NBLK = 4
N_CP = 4


def draw_latent_rows(key, part):
    key = jax.random.fold_in(key, 11)
    scale_key, value_key, rotary_key = jax.random.split(key, 3)
    block_scale = jnp.exp(jax.random.uniform(scale_key, (TOKENS, LAT // BLOCK, 1), minval=math.log(0.4), maxval=math.log(4.0)))
    latent = block_scale * jnp.clip(jax.random.normal(value_key, (TOKENS, LAT // BLOCK, BLOCK)), -4.0, 4.0)
    rotary = jnp.clip(jax.random.normal(rotary_key, (TOKENS, ROPE)), -4.0, 4.0)
    return jnp.concatenate([latent.reshape(TOKENS, LAT), rotary], axis=1).astype(jnp.bfloat16)


def draw_queries(key, part):
    key = jax.random.fold_in(key, 23)
    result = jnp.clip(jax.random.normal(key, (TOKENS, HEADS, NOPE + ROPE)), -4.0, 4.0)
    return result.reshape(TOKENS, HEADS * (NOPE + ROPE)).astype(jnp.bfloat16)


def draw_decode_owner(key, part):
    key = jax.random.fold_in(key, 31)
    return jax.random.permutation(key, OWNERS).astype(jnp.int32).reshape(PROMPTS, GROUPW)


def shard_levels(own_key, dims, cuts, smallest, largest):
    def one(dim, parts):
        steps = jax.random.uniform(jax.random.fold_in(jax.random.fold_in(own_key, 6), dim), (parts,), jnp.float32, smallest / len(cuts), largest / len(cuts))
        return jnp.repeat(jnp.exp(steps), dims[dim] // parts).reshape((-1,) + (1,) * (len(dims) - dim - 1))

    loudness = one(*cuts[0])
    for cut in cuts[1:]:
        loudness = loudness * one(*cut)
    return loudness


def profile(amount, total, limit, skew):
    portions = [(1 << 20) // math.isqrt(grade ** skew) + 1 for grade in range(2, amount + 1)]
    surplus, holding = total - limit - (amount - 1), [1] * (amount - 1)
    while surplus > 0:
        free = [i for i in range(amount - 1) if holding[i] < limit]
        whole, remaining = sum([portions[i] for i in free]), surplus
        for i in free:
            addition = min(limit - holding[i], max(1, remaining * portions[i] // whole), surplus)
            holding[i] = holding[i] + addition
            surplus = surplus - addition
    return np.array([limit] + holding)


def uneven(own_key, number_of, total, most, slope):
    if number_of == 2:
        one = jax.random.randint(own_key, (), max(1, total - most), min(most, total - 1) + 1)
        return jnp.stack([one, total - one])
    sizes = jnp.asarray(profile(number_of, total, most, slope), jnp.int32)
    pairs = (number_of - 1) // 2
    giver, receiver = sizes[1:1 + 2 * pairs:2], sizes[2:2 + 2 * pairs:2]
    margin = jnp.minimum(giver - 1, most - receiver)
    shifted = jax.random.randint(jax.random.fold_in(own_key, 1), (pairs,), 0, 1 << 20) % (margin + 1)
    sizes = sizes.at[1:1 + 2 * pairs:2].set(giver - shifted).at[2:2 + 2 * pairs:2].set(receiver + shifted)
    return sizes[jax.random.permutation(jax.random.fold_in(own_key, 2), number_of)]


def normal_values(stream_key, dims, spread, limit, cuts=(), kind=jnp.bfloat16):
    entries = spread * jax.random.normal(stream_key, dims, jnp.float32)
    if cuts:
        entries = entries * shard_levels(stream_key, dims, cuts, -0.22, 0.18)
    return jnp.clip(entries, -limit, limit).astype(kind)


def setup_inputs(seed: int = 0, part: int = 0) -> dict:
    keys = jax.random.split(jax.random.key(seed), 8)
    part_splits = jax.random.split(jax.random.fold_in(keys[7], part), 8)
    queries = draw_queries(jax.random.fold_in(jax.random.fold_in(keys[7], part), 71), part)
    latent_rows = draw_latent_rows(jax.random.fold_in(jax.random.fold_in(keys[7], part), 71), part)
    key_absorb = normal_values(keys[2], (HEADS, NOPE, LAT), NOPE ** -0.5, 0.5, ((0, 4),))
    value_expand = normal_values(keys[3], (HEADS, LAT, VDIM), LAT ** -0.5, 0.25, ((0, 4),))
    prompt_pages = uneven(part_splits[4], PROMPTS, PAGES, MOSTP, 2).astype(jnp.int32)
    decode_owner = draw_decode_owner(jax.random.fold_in(jax.random.fold_in(keys[7], part), 71), part)
    slot_offset = jax.random.randint(part_splits[6], (PROMPTS,), 0, MOSTP).astype(jnp.int32)
    return dict(queries=queries, latent_rows=latent_rows, key_absorb=key_absorb, value_expand=value_expand, prompt_pages=prompt_pages, decode_owner=decode_owner, slot_offset=slot_offset)


masked_fill = -1.0e30
amax_epsilon = 1.0e-6


def page_targets(page_index, prompt_pages, decode_owner, slot_offset, dec_count, slot_count):
    group_width = decode_owner.shape[1]
    page_ends = jnp.cumsum(prompt_pages).astype(jnp.int32)
    page_starts = (page_ends - prompt_pages).astype(jnp.int32)
    prompt_of = jnp.sum((page_ends[None, :] <= page_index[:, None]).astype(jnp.int32), axis=1).astype(jnp.int32)
    choose = (prompt_of[:, None] == jnp.arange(prompt_pages.shape[0], dtype=jnp.int32)[None, :]).astype(jnp.int32)
    first_page = jnp.sum(choose * page_starts[None, :], axis=1).astype(jnp.int32)
    rotation = jnp.sum(choose * slot_offset[None, :], axis=1).astype(jnp.int32)
    owner_rows = jnp.sum(choose[:, :, None] * decode_owner[None, :, :], axis=1).astype(jnp.int32)
    cycle_index = (rotation + page_index - first_page).astype(jnp.int32)
    position = (cycle_index % group_width).astype(jnp.int32)
    pick = (position[:, None] == jnp.arange(group_width, dtype=jnp.int32)[None, :]).astype(jnp.int32)
    target = jnp.sum(pick * owner_rows, axis=1).astype(jnp.int32)
    cycle_slot = ((cycle_index // group_width) % (dec_count * slot_count)).astype(jnp.int32)
    return target, cycle_slot // slot_count, cycle_slot % slot_count


def prompt_start(positions, prompt_pages):
    token_starts = ((jnp.cumsum(prompt_pages) - prompt_pages) * PAGE).astype(jnp.int32)
    chosen = jnp.where(token_starts[None, :] <= positions[:, None], token_starts[None, :], 0)
    return jnp.max(chosen, axis=1).astype(jnp.int32)


def encode_rows(latent_rows):
    row_count = latent_rows.shape[0]
    blocks = latent_rows[:, :LAT].astype(jnp.float32).reshape(row_count, LAT // BLOCK, BLOCK)
    scales = (jnp.max(jnp.abs(blocks), axis=2) + amax_epsilon).astype(jnp.bfloat16)
    encoded = (blocks / scales.astype(jnp.float32)[:, :, None]).astype(jnp.bfloat16).reshape(row_count, LAT)
    return jnp.concatenate([encoded, latent_rows[:, LAT:]], axis=1), scales


def reference(queries, latent_rows, key_absorb, value_expand, prompt_pages, decode_owner, slot_offset):
    score_scale = 1.0 / (NOPE + ROPE) ** 0.5
    reach = MOSTP * PAGE
    key_width = reach + TOK_DEV
    heads_split = queries.reshape(TOKENS, HEADS, NOPE + ROPE)
    absorbed = jnp.einsum("thn,hnl->thl", heads_split[:, :, :NOPE].astype(jnp.float32), key_absorb.astype(jnp.float32)).astype(jnp.bfloat16)
    combined = jnp.concatenate([absorbed, heads_split[:, :, NOPE:]], axis=2)
    padded = jnp.concatenate([jnp.zeros((reach, LAT + ROPE), latent_rows.dtype), latent_rows], axis=0)

    def one_block(block_index):
        first_row = (block_index * TOK_DEV).astype(jnp.int32)
        query_part = lax.dynamic_slice_in_dim(combined, first_row, TOK_DEV, 0)
        key_part = lax.dynamic_slice_in_dim(padded, first_row, key_width, 0)
        query_pos = first_row + jnp.arange(TOK_DEV, dtype=jnp.int32)
        key_pos = first_row - reach + jnp.arange(key_width, dtype=jnp.int32)
        start_pos = prompt_start(query_pos, prompt_pages)
        visible = (key_pos[None, :] >= start_pos[:, None]) & (key_pos[None, :] <= query_pos[:, None])
        scores = jnp.einsum("thl,kl->thk", query_part.astype(jnp.float32), key_part.astype(jnp.float32)) * score_scale
        scores = jnp.where(visible[:, None, :], scores, masked_fill)
        row_max = jnp.max(scores, axis=2, keepdims=True)
        weights = jnp.where(visible[:, None, :], jnp.exp(scores - row_max), 0.0)
        total = jnp.sum(weights, axis=2)
        rounded = weights.astype(jnp.bfloat16)
        summed = jnp.einsum("thk,kl->thl", rounded.astype(jnp.float32), key_part[:, :LAT].astype(jnp.float32))
        mixed_latent = (summed / total[:, :, None]).astype(jnp.bfloat16)
        output_rows = jnp.einsum("thl,hlv->thv", mixed_latent.astype(jnp.float32), value_expand.astype(jnp.float32))
        return output_rows.astype(jnp.bfloat16).reshape(TOK_DEV, HEADS * VDIM)

    attended = lax.map(one_block, jnp.arange(N_CP, dtype=jnp.int32)).reshape(TOKENS, HEADS * VDIM)
    encoded, scales = encode_rows(latent_rows)
    page_index = jnp.arange(PAGES, dtype=jnp.int32)
    target, holder, cycle_slot = page_targets(page_index, prompt_pages, decode_owner, slot_offset, DECS, CAP_DEC)
    page_cache = jnp.zeros((OWNERS, DECS, CAP_DEC, PAGE, LAT + ROPE), encoded.dtype)
    page_cache = page_cache.at[target, holder, cycle_slot].set(encoded.reshape(PAGES, PAGE, LAT + ROPE))
    page_scales = jnp.zeros((OWNERS, DECS, CAP_DEC, PAGE, NBLK), scales.dtype)
    page_scales = page_scales.at[target, holder, cycle_slot].set(scales.reshape(PAGES, PAGE, NBLK))
    return attended, page_cache, page_scales
```

```python
import functools
import math

import jax
import jax.numpy as jnp
from jax import lax
from jax.experimental import pallas as pl
from jax.experimental.pallas import tpu as pltpu
from jax.sharding import PartitionSpec as P

LAT = 512
ROPE = 64
NOPE = 128
VDIM = 128
PAGE = 16
BLOCK = 128
NBLK = LAT // BLOCK
ROW = LAT + ROPE
HEAD = NOPE + ROPE

masked_fill = -1e30
amax_epsilon = 1e-06
exp2_scale = math.log2(math.e) / math.sqrt(HEAD)

NT = (((1,), (1,)), ((), ()))


def absorb_kernel(group, queries, key_absorb, combined):
    rows = queries.shape[0]
    for h in range(group):
        at = h * HEAD
        absorbed = jnp.dot(queries[:, at:at + NOPE], key_absorb[h], preferred_element_type=jnp.float32)
        combined[h * rows:(h + 1) * rows, :LAT] = absorbed.astype(jnp.bfloat16)
        combined[h * rows:(h + 1) * rows, LAT:] = queries[:, at + NOPE:at + HEAD]


def prompt_starts(prompt_pages):
    starts = [jnp.int32(0)]
    for k in range(prompt_pages.shape[0] - 1):
        starts.append(starts[-1] + prompt_pages[k])
    return starts


def write_cache(n_cp, slot_count, prompt_pages, decode_owner, slot_offset, pieces, page_cache, page_scales):
    prompts, width = decode_owner.shape
    cp_index = lax.axis_index("cp")
    dec_index = lax.axis_index("dec")
    rows_here = pieces[0].shape[1]
    cycle = width * lax.axis_size("dec") * slot_count
    starts = prompt_starts(prompt_pages)
    pages, start, offset, place = jnp.int32(0), jnp.int32(0), jnp.int32(0), jnp.int32(0)
    for k in range(prompts):
        for p in range(width):
            mine = decode_owner[k, p] == cp_index
            pages = jnp.where(mine, prompt_pages[k], pages)
            start = jnp.where(mine, starts[k], start)
            offset = jnp.where(mine, slot_offset[k], offset)
            place = jnp.where(mine, p, place)
    kept = slot_count * PAGE
    row = lax.broadcasted_iota(jnp.int32, (kept, 1), 0)
    lane = lax.broadcasted_iota(jnp.int32, (1, kept), 1)
    row_target = jnp.full((kept, 1), -1, jnp.int32)
    lane_valid = jnp.zeros((1, kept), jnp.float32)
    for c in range(slot_count):
        turn = width * (dec_index * slot_count + c) + place
        page = lax.rem(turn - offset + 2 * cycle, cycle)
        valid = page < pages
        token = (start + page) * PAGE
        source = token // rows_here
        steps_back = lax.rem(cp_index - source + n_cp, n_cp)
        column = steps_back * rows_here + lax.rem(token, rows_here)
        column = jnp.where(valid, column, -kept)
        row_target = jnp.where(row // PAGE == c, column + row % PAGE, row_target)
        lane_valid = jnp.where(lane // PAGE == c, valid.astype(jnp.float32), lane_valid)
    rows = jnp.zeros((kept, ROW), jnp.float32)
    turned = jnp.zeros((LAT, kept), jnp.float32)
    for b, piece in enumerate(pieces):
        column = b * rows_here + lax.broadcasted_iota(jnp.int32, (1, rows_here), 1)
        chosen = jnp.where(column == row_target, 1.0, 0.0).astype(jnp.bfloat16)
        block = piece[...]
        rows = rows + lax.dot_general(chosen, block, NT, preferred_element_type=jnp.float32)
        turned = turned + lax.dot_general(block[:LAT], chosen, NT, preferred_element_type=jnp.float32)
    encoded = []
    scales = []
    for b in range(NBLK):
        values = rows[:, b * BLOCK:(b + 1) * BLOCK]
        scale = jnp.max(jnp.abs(values), axis=1, keepdims=True) + amax_epsilon
        scale = scale.astype(jnp.bfloat16).astype(jnp.float32)
        encoded.append((values / scale).astype(jnp.bfloat16))
        scales.append(jnp.max(jnp.abs(turned[b * BLOCK:(b + 1) * BLOCK]), axis=0, keepdims=True))
    encoded.append(rows[:, LAT:].astype(jnp.bfloat16))
    scales = jnp.concatenate(scales, axis=0) + amax_epsilon
    scales = (scales * lane_valid).astype(jnp.bfloat16)
    for c in range(slot_count):
        for b, values in enumerate(encoded):
            page_cache[c, :, b * BLOCK:b * BLOCK + values.shape[1]] = values[c * PAGE:(c + 1) * PAGE]
        page_scales[c] = scales[:, c * PAGE:(c + 1) * PAGE]


def attend_kernel(n_cp, key_blocks, group, slot_count, prompt_pages, decode_owner, slot_offset, combined, value_expand, *rest):
    pieces = rest[:n_cp]
    attended, page_cache, page_scales, keys, values, bias = rest[n_cp:]
    rows = attended.shape[0]

    @pl.when(pl.program_id(0) == 0)
    def _():
        first = lax.axis_index("cp") * rows
        token = first + lax.broadcasted_iota(jnp.int32, (rows, 1), 0)
        begin = jnp.zeros((rows, 1), jnp.int32)
        for start in prompt_starts(prompt_pages):
            begin = jnp.maximum(begin, jnp.where(start * PAGE <= token, start * PAGE, 0))
        for b in range(key_blocks):
            block = pieces[b][...]
            keys[:, b * rows:(b + 1) * rows] = block
            values[b * rows:(b + 1) * rows, :] = block[:LAT].T
            spot = first - b * rows + lax.broadcasted_iota(jnp.int32, (1, rows), 1)
            visible = (spot >= begin) & (spot <= token)
            bias[:, b * rows:(b + 1) * rows] = jnp.where(visible, 0.0, masked_fill)
        write_cache(n_cp, slot_count, prompt_pages, decode_owner, slot_offset, pieces, page_cache, page_scales)

    scores = jnp.dot(combined[...], keys[...], preferred_element_type=jnp.float32)
    scores = scores.reshape(group, rows, key_blocks * rows) + bias[...][None]
    peak = jnp.max(scores, axis=2, keepdims=True)
    weights = jnp.exp2((scores - peak) * exp2_scale)
    total = jnp.sum(weights, axis=2, keepdims=True).reshape(group * rows, 1)
    weights = weights.astype(jnp.bfloat16).reshape(group * rows, key_blocks * rows)
    summed = jnp.dot(weights, values[...], preferred_element_type=jnp.float32)
    mixed = (summed * (1.0 / total)).astype(jnp.bfloat16)
    for h in range(group):
        result = jnp.dot(mixed[h * rows:(h + 1) * rows], value_expand[h], preferred_element_type=jnp.float32)
        attended[:, h * VDIM:(h + 1) * VDIM] = result.astype(jnp.bfloat16)


def on_device(queries, latent_rows, key_absorb, value_expand, prompt_pages, decode_owner, slot_offset):
    n_cp = lax.axis_size("cp")
    dec_count = lax.axis_size("dec")
    heads = key_absorb.shape[0]
    rows = latent_rows.shape[0]
    prompts, width = decode_owner.shape
    slot_count = 3 * (rows // PAGE) // (2 * dec_count)
    reach = width * dec_count * slot_count * PAGE
    key_blocks = min(n_cp, -(-reach // rows) + (0 if prompts == 2 else 1))
    own = latent_rows.T
    pieces = [own]
    for step in range(1, n_cp):
        pieces.append(lax.ppermute(own, "cp", [(i, (i + step) % n_cp) for i in range(n_cp)]))

    group = 4
    combined = pl.pallas_call(
        functools.partial(absorb_kernel, group),
        grid=(heads // group,),
        in_specs=[
            pl.BlockSpec((rows, group * HEAD), lambda g: (0, g)),
            pl.BlockSpec((group, NOPE, LAT), lambda g: (g, 0, 0)),
        ],
        out_specs=pl.BlockSpec((group * rows, ROW), lambda g: (g, 0)),
        out_shape=jax.ShapeDtypeStruct((heads * rows, ROW), jnp.bfloat16),
        cost_estimate=pl.CostEstimate(
            flops=2 * rows * heads * NOPE * LAT,
            bytes_accessed=2 * (queries.size + key_absorb.size + heads * rows * ROW),
            transcendentals=0,
        ),
        compiler_params=pltpu.CompilerParams(vmem_limit_bytes=48 * 2**20),
        name="absorb",
    )(queries, key_absorb)

    group = 4 if key_blocks <= 4 else 1
    width_keys = key_blocks * rows
    smem = pl.BlockSpec(memory_space=pltpu.SMEM)
    attended, page_cache, page_scales = pl.pallas_call(
        functools.partial(attend_kernel, n_cp, key_blocks, group, slot_count),
        grid=(heads // group,),
        in_specs=[
            smem,
            smem,
            smem,
            pl.BlockSpec((group * rows, ROW), lambda g: (g, 0)),
            pl.BlockSpec((group, LAT, VDIM), lambda g: (g, 0, 0)),
        ] + [pl.BlockSpec((ROW, rows), lambda g: (0, 0))] * n_cp,
        out_specs=[
            pl.BlockSpec((rows, group * VDIM), lambda g: (0, g)),
            pl.BlockSpec((slot_count, PAGE, ROW), lambda g: (0, 0, 0)),
            pl.BlockSpec((slot_count, NBLK, PAGE), lambda g: (0, 0, 0)),
        ],
        out_shape=[
            jax.ShapeDtypeStruct((rows, heads * VDIM), jnp.bfloat16),
            jax.ShapeDtypeStruct((slot_count, PAGE, ROW), jnp.bfloat16),
            jax.ShapeDtypeStruct((slot_count, NBLK, PAGE), jnp.bfloat16),
        ],
        scratch_shapes=[
            pltpu.VMEM((ROW, width_keys), jnp.bfloat16),
            pltpu.VMEM((width_keys, LAT), jnp.bfloat16),
            pltpu.VMEM((rows, width_keys), jnp.float32),
        ],
        cost_estimate=pl.CostEstimate(
            flops=2 * rows * heads * (width_keys * (ROW + LAT) + LAT * VDIM),
            bytes_accessed=2 * (heads * rows * (ROW + VDIM) + value_expand.size),
            transcendentals=rows * heads * width_keys,
        ),
        compiler_params=pltpu.CompilerParams(vmem_limit_bytes=48 * 2**20),
        name="attend",
    )(prompt_pages, decode_owner, slot_offset, combined, value_expand, *pieces)
    page_cache = page_cache.reshape(1, 1, slot_count, PAGE, ROW)
    page_scales = page_scales.transpose(0, 2, 1).reshape(1, 1, slot_count, PAGE, NBLK)
    return attended, page_cache, page_scales


def solution(mesh):
    return jax.shard_map(
        on_device,
        mesh=mesh,
        in_specs=(
            P(("grp", "cp"), "dec"),
            P(("grp", "cp"), None),
            P("dec", None, None),
            P("dec", None, None),
            P("grp"),
            P("grp", None),
            P("grp"),
        ),
        out_specs=(
            P(("grp", "cp"), "dec"),
            P(("grp", "cp"), "dec", None, None, None),
            P(("grp", "cp"), "dec", None, None, None),
        ),
        check_vma=False,
    )
```

```python
import functools
import math

import jax
import jax.numpy as jnp
from jax import lax
from jax.experimental import pallas as pl
from jax.experimental.pallas import tpu as pltpu
from jax.sharding import PartitionSpec as P

LAT = 512
ROPE = 64
NOPE = 128
VDIM = 128
PAGE = 16
BLOCK = 128
NBLK = LAT // BLOCK
ROW = LAT + ROPE
HEAD = NOPE + ROPE

masked_fill = -1e30
amax_epsilon = 1e-06
exp2_scale = math.log2(math.e) / math.sqrt(HEAD)

NT = (((1,), (1,)), ((), ()))


def own_kernel(group, prompt_pages, queries, key_absorb, own, combined, summed, stats, q_buf, w_buf, sems, values):
    rows = own.shape[1]
    heads = key_absorb.shape[0]
    copies = []
    for g in range(heads // group):
        wide = group * HEAD
        copies.append((
            pltpu.make_async_copy(queries.at[:, pl.ds(g * wide, wide)], q_buf.at[:, pl.ds(g * wide, wide)], sems.at[0, g]),
            pltpu.make_async_copy(key_absorb.at[pl.ds(g * group, group)], w_buf.at[pl.ds(g * group, group)], sems.at[1, g]),
        ))
    for pair in copies:
        for copy in pair:
            copy.start()
    block = own[...]
    values[...] = block[:LAT].T
    bias = visible_bias(prompt_pages, rows, 0)
    for g in range(heads // group):
        for copy in copies[g]:
            copy.wait()
        for h in range(g * group, (g + 1) * group):
            at = h * HEAD
            absorbed = jnp.dot(q_buf[:, at:at + NOPE], w_buf[h], preferred_element_type=jnp.float32)
            combined[h * rows:(h + 1) * rows, :LAT] = absorbed.astype(jnp.bfloat16)
            combined[h * rows:(h + 1) * rows, LAT:] = q_buf[:, at + NOPE:at + HEAD]
        span = pl.ds(g * group * rows, group * rows)
        scores = jnp.dot(combined[span, :], block, preferred_element_type=jnp.float32)
        scores = (scores.reshape(group, rows, rows) + bias[None]).reshape(group * rows, rows)
        peak = jnp.max(scores, axis=1, keepdims=True)
        weights = jnp.exp2((scores - peak) * exp2_scale)
        total = jnp.sum(weights, axis=1, keepdims=True)
        summed[span, :] = jnp.dot(weights.astype(jnp.bfloat16), values[...], preferred_element_type=jnp.float32)
        stats[span, 0:1] = peak
        stats[span, 1:2] = total


def visible_bias(prompt_pages, rows, steps_back):
    first = lax.axis_index("cp") * rows
    token = first + lax.broadcasted_iota(jnp.int32, (rows, 1), 0)
    begin = jnp.zeros((rows, 1), jnp.int32)
    for start in prompt_starts(prompt_pages):
        begin = jnp.maximum(begin, jnp.where(start * PAGE <= token, start * PAGE, 0))
    spot = first - steps_back * rows + lax.broadcasted_iota(jnp.int32, (1, rows), 1)
    return jnp.where((spot >= begin) & (spot <= token), 0.0, masked_fill)


def swap_pair(position, n_cp):
    odd = lax.rem(lax.axis_index("dec"), 2)
    within = lax.rem(position + 1, 2)
    swapped = position - within + lax.rem(within + odd, 2)
    paired = (position >= 1) & (position <= (n_cp - 1) // 2 * 2)
    return jnp.where(paired, swapped, position)


def prompt_starts(prompt_pages):
    starts = [jnp.int32(0)]
    for k in range(prompt_pages.shape[0] - 1):
        starts.append(starts[-1] + prompt_pages[k])
    return starts


def cache_kernel(n_cp, slot_count, prompt_pages, decode_owner, slot_offset, *rest):
    pieces = rest[:n_cp]
    page_cache, page_scales = rest[n_cp:]
    prompts, width = decode_owner.shape
    cp_index = lax.axis_index("cp")
    dec_index = lax.axis_index("dec")
    rows_here = pieces[0].shape[1]
    cycle = width * lax.axis_size("dec") * slot_count
    starts = prompt_starts(prompt_pages)
    pages, start, offset, place = jnp.int32(0), jnp.int32(0), jnp.int32(0), jnp.int32(0)
    for k in range(prompts):
        for p in range(width):
            mine = decode_owner[k, p] == cp_index
            pages = jnp.where(mine, prompt_pages[k], pages)
            start = jnp.where(mine, starts[k], start)
            offset = jnp.where(mine, slot_offset[k], offset)
            place = jnp.where(mine, p, place)
    kept = slot_count * PAGE
    row = lax.broadcasted_iota(jnp.int32, (kept, 1), 0)
    lane = lax.broadcasted_iota(jnp.int32, (1, kept), 1)
    row_target = jnp.full((kept, 1), -1, jnp.int32)
    lane_valid = jnp.zeros((1, kept), jnp.float32)
    for c in range(slot_count):
        turn = width * (dec_index * slot_count + c) + place
        page = lax.rem(turn - offset + 2 * cycle, cycle)
        valid = page < pages
        token = (start + page) * PAGE
        source = token // rows_here
        steps_back = lax.rem(cp_index - source + n_cp, n_cp)
        column = swap_pair(steps_back, n_cp) * rows_here + lax.rem(token, rows_here)
        column = jnp.where(valid, column, -kept)
        row_target = jnp.where(row // PAGE == c, column + row % PAGE, row_target)
        lane_valid = jnp.where(lane // PAGE == c, valid.astype(jnp.float32), lane_valid)
    rows = jnp.zeros((kept, ROW), jnp.float32)
    turned = jnp.zeros((LAT, kept), jnp.float32)
    for b, piece in enumerate(pieces):
        column = b * rows_here + lax.broadcasted_iota(jnp.int32, (1, rows_here), 1)
        chosen = jnp.where(column == row_target, 1.0, 0.0).astype(jnp.bfloat16)
        block = piece[...]
        rows = rows + lax.dot_general(chosen, block, NT, preferred_element_type=jnp.float32)
        turned = turned + lax.dot_general(block[:LAT], chosen, NT, preferred_element_type=jnp.float32)
    encoded = []
    scales = []
    for b in range(NBLK):
        values = rows[:, b * BLOCK:(b + 1) * BLOCK]
        scale = jnp.max(jnp.abs(values), axis=1, keepdims=True) + amax_epsilon
        scale = scale.astype(jnp.bfloat16).astype(jnp.float32)
        encoded.append((values / scale).astype(jnp.bfloat16))
        scales.append(jnp.max(jnp.abs(turned[b * BLOCK:(b + 1) * BLOCK]), axis=0, keepdims=True))
    encoded.append(rows[:, LAT:].astype(jnp.bfloat16))
    scales = jnp.concatenate(scales, axis=0) + amax_epsilon
    scales = (scales * lane_valid).astype(jnp.bfloat16)
    for c in range(slot_count):
        for b, values in enumerate(encoded):
            page_cache[c, :, b * BLOCK:b * BLOCK + values.shape[1]] = values[c * PAGE:(c + 1) * PAGE]
        page_scales[c] = scales[:, c * PAGE:(c + 1) * PAGE]


def earlier_kernel(n_cp, count, group, prompt_pages, combined, summed, stats, value_expand, *rest):
    pieces = rest[:count]
    attended, keys, values, bias = rest[count:]
    rows = attended.shape[0]

    @pl.when(pl.program_id(0) == 0)
    def _():
        for b in range(count):
            block = pieces[b][...]
            keys[:, b * rows:(b + 1) * rows] = block
            values[b * rows:(b + 1) * rows, :] = block[:LAT].T
            bias[:, b * rows:(b + 1) * rows] = visible_bias(prompt_pages, rows, swap_pair(jnp.int32(b + 1), n_cp))

    scores = jnp.dot(combined[...], keys[...], preferred_element_type=jnp.float32)
    scores = (scores.reshape(group, rows, count * rows) + bias[...][None]).reshape(group * rows, count * rows)
    old_peak = stats[:, 0:1]
    peak = jnp.maximum(old_peak, jnp.max(scores, axis=1, keepdims=True))
    weights = jnp.exp2((scores - peak) * exp2_scale)
    factor = jnp.exp2((old_peak - peak) * exp2_scale)
    total = stats[:, 1:2] * factor + jnp.sum(weights, axis=1, keepdims=True)
    added = jnp.dot(weights.astype(jnp.bfloat16), values[...], preferred_element_type=jnp.float32)
    mixed = ((summed[...] * factor + added) * (1.0 / total)).astype(jnp.bfloat16)
    for h in range(group):
        result = jnp.dot(mixed[h * rows:(h + 1) * rows], value_expand[h], preferred_element_type=jnp.float32)
        attended[:, h * VDIM:(h + 1) * VDIM] = result.astype(jnp.bfloat16)


def fetch(own, n_cp, n_dec):
    blocks = []
    for step in range(1, n_cp - 1, 2):
        pairs = [(c * n_dec + e, (c + step + e % 2) % n_cp * n_dec + e) for c in range(n_cp) for e in range(n_dec)]
        blocks.append(lax.ppermute(own, ("cp", "dec"), pairs))
    last = []
    if n_cp % 2 == 0:
        last.append(lax.ppermute(own, "cp", [(c, (c + n_cp - 1) % n_cp) for c in range(n_cp)]))
    return blocks, last


def swap(blocks, n_dec):
    pieces = []
    for block in blocks:
        pieces += [block, lax.ppermute(block, "dec", [(e, e ^ 1) for e in range(n_dec)])]
    return pieces


def on_device(queries, latent_rows, key_absorb, value_expand, prompt_pages, decode_owner, slot_offset):
    n_cp = lax.axis_size("cp")
    dec_count = lax.axis_size("dec")
    heads = key_absorb.shape[0]
    rows = latent_rows.shape[0]
    prompts, width = decode_owner.shape
    slot_count = 3 * (rows // PAGE) // (2 * dec_count)
    reach = width * dec_count * slot_count * PAGE
    count = -(-reach // rows) - (1 if prompts == 2 else 0)
    count = min(n_cp - 1, count + count % 2)
    own = latent_rows.T
    blocks, last = fetch(own, n_cp, dec_count)

    smem = pl.BlockSpec(memory_space=pltpu.SMEM)
    vmem = pl.BlockSpec(memory_space=pltpu.VMEM)
    hbm = pl.BlockSpec(memory_space=pltpu.HBM)
    params = pltpu.CompilerParams(vmem_limit_bytes=32 * 2**20)
    group = 4
    combined, summed, stats = pl.pallas_call(
        functools.partial(own_kernel, group),
        in_specs=[smem, hbm, hbm, vmem],
        out_specs=[vmem, vmem, vmem],
        out_shape=[
            jax.ShapeDtypeStruct((heads * rows, ROW), jnp.bfloat16),
            jax.ShapeDtypeStruct((heads * rows, LAT), jnp.float32),
            jax.ShapeDtypeStruct((heads * rows, 2), jnp.float32),
        ],
        scratch_shapes=[
            pltpu.VMEM((rows, heads * HEAD), jnp.bfloat16),
            pltpu.VMEM((heads, NOPE, LAT), jnp.bfloat16),
            pltpu.SemaphoreType.DMA((2, heads // group)),
            pltpu.VMEM((rows, LAT), jnp.bfloat16),
        ],
        cost_estimate=pl.CostEstimate(
            flops=2 * rows * heads * (NOPE * LAT + rows * (ROW + LAT)),
            bytes_accessed=2 * (queries.size + key_absorb.size + heads * rows * ROW),
            transcendentals=rows * heads * rows,
        ),
        compiler_params=params,
        name="own",
    )(prompt_pages, *[pltpu.with_memory_space_constraint(x, pltpu.HBM) for x in (queries, key_absorb)], own)
    blocks, combined = lax.optimization_barrier((blocks, combined))
    pieces = swap(blocks, dec_count)

    group = 4 if count <= 4 else 1
    attended = pl.pallas_call(
        functools.partial(earlier_kernel, n_cp, count, group),
        grid=(heads // group,),
        in_specs=[
            smem,
            pl.BlockSpec((group * rows, ROW), lambda g: (g, 0)),
            pl.BlockSpec((group * rows, LAT), lambda g: (g, 0)),
            pl.BlockSpec((group * rows, 2), lambda g: (g, 0)),
            pl.BlockSpec((group, LAT, VDIM), lambda g: (g, 0, 0)),
        ] + [pl.BlockSpec((ROW, rows), lambda g: (0, 0))] * count,
        out_specs=pl.BlockSpec((rows, group * VDIM), lambda g: (0, g)),
        out_shape=jax.ShapeDtypeStruct((rows, heads * VDIM), jnp.bfloat16),
        scratch_shapes=[
            pltpu.VMEM((ROW, count * rows), jnp.bfloat16),
            pltpu.VMEM((count * rows, LAT), jnp.bfloat16),
            pltpu.VMEM((rows, count * rows), jnp.float32),
        ],
        cost_estimate=pl.CostEstimate(
            flops=2 * rows * heads * (count * rows * (ROW + LAT) + LAT * VDIM),
            bytes_accessed=2 * (heads * rows * (ROW + VDIM) + value_expand.size),
            transcendentals=rows * heads * count * rows,
        ),
        compiler_params=params,
        name="earlier",
    )(prompt_pages, combined, summed, stats, value_expand, *pieces[:count])

    last, attended = lax.optimization_barrier((last, attended))
    pieces += last
    page_cache, page_scales = pl.pallas_call(
        functools.partial(cache_kernel, n_cp, slot_count),
        in_specs=[smem, smem, smem] + [vmem] * n_cp,
        out_specs=[vmem, vmem],
        out_shape=[
            jax.ShapeDtypeStruct((slot_count, PAGE, ROW), jnp.bfloat16),
            jax.ShapeDtypeStruct((slot_count, NBLK, PAGE), jnp.bfloat16),
        ],
        cost_estimate=pl.CostEstimate(
            flops=4 * n_cp * rows * slot_count * PAGE * ROW,
            bytes_accessed=2 * n_cp * rows * ROW,
            transcendentals=0,
        ),
        compiler_params=params,
        name="cache",
    )(prompt_pages, decode_owner, slot_offset, own, *pieces)
    page_cache = page_cache.reshape(1, 1, slot_count, PAGE, ROW)
    page_scales = page_scales.transpose(0, 2, 1).reshape(1, 1, slot_count, PAGE, NBLK)
    return attended, page_cache, page_scales


def solution(mesh):
    return jax.shard_map(
        on_device,
        mesh=mesh,
        in_specs=(
            P(("grp", "cp"), "dec"),
            P(("grp", "cp"), None),
            P("dec", None, None),
            P("dec", None, None),
            P("grp"),
            P("grp", None),
            P("grp"),
        ),
        out_specs=(
            P(("grp", "cp"), "dec"),
            P(("grp", "cp"), "dec", None, None, None),
            P(("grp", "cp"), "dec", None, None, None),
        ),
        check_vma=False,
    )
```

```python
import functools
import math

import jax
import jax.numpy as jnp
from jax import lax
from jax.experimental import pallas as pl
from jax.experimental.pallas import tpu as pltpu
from jax.sharding import PartitionSpec as P

LAT = 512
ROPE = 64
NOPE = 128
VDIM = 128
PAGE = 16
BLOCK = 128
NBLK = LAT // BLOCK
ROW = LAT + ROPE
HEAD = NOPE + ROPE
LANES = 128

masked_fill = -1e30
amax_epsilon = 1e-06
exp2_scale = math.log2(math.e) / math.sqrt(HEAD)

NT = (((1,), (1,)), ((), ()))


def prompt_starts(prompt_pages):
    starts = [jnp.int32(0)]
    for k in range(prompt_pages.shape[0] - 1):
        starts.append(starts[-1] + prompt_pages[k])
    return starts


def visible_bias(prompt_pages, rows, steps_back):
    first = lax.axis_index("cp") * rows
    token = first + lax.broadcasted_iota(jnp.int32, (rows, 1), 0)
    begin = jnp.zeros((rows, 1), jnp.int32)
    for start in prompt_starts(prompt_pages):
        begin = jnp.maximum(begin, jnp.where(start * PAGE <= token, start * PAGE, 0))
    spot = first - steps_back * rows + lax.broadcasted_iota(jnp.int32, (1, rows), 1)
    return jnp.where((spot >= begin) & (spot <= token), 0.0, masked_fill)


def swap_pair(position, n_cp):
    odd = lax.rem(lax.axis_index("dec"), 2)
    within = lax.rem(position + 1, 2)
    swapped = position - within + lax.rem(within + odd, 2)
    paired = (position >= 1) & (position <= (n_cp - 1) // 2 * 2)
    return jnp.where(paired, swapped, position)


def slot_pages(owner, slot_count, prompt_pages, decode_owner, slot_offset):
    prompts, width = decode_owner.shape
    cycle = width * lax.axis_size("dec") * slot_count
    starts = prompt_starts(prompt_pages)
    pages, start, offset, place = jnp.int32(0), jnp.int32(0), jnp.int32(0), jnp.int32(0)
    for k in range(prompts):
        for p in range(width):
            mine = decode_owner[k, p] == owner
            pages = jnp.where(mine, prompt_pages[k], pages)
            start = jnp.where(mine, starts[k], start)
            offset = jnp.where(mine, slot_offset[k], offset)
            place = jnp.where(mine, p, place)
    result = []
    for c in range(slot_count):
        turn = width * (lax.axis_index("dec") * slot_count + c) + place
        page = lax.rem(turn - offset + 2 * cycle, cycle)
        result.append((page < pages, start + page))
    return result


def row_picker(targets, columns):
    kept = len(targets) * PAGE
    row = lax.broadcasted_iota(jnp.int32, (kept, 1), 0)
    target = jnp.full((kept, 1), -1, jnp.int32)
    for c, column in enumerate(targets):
        target = jnp.where(row // PAGE == c, column + row % PAGE, target)
    column = lax.broadcasted_iota(jnp.int32, (1, columns), 1)
    return jnp.where(column == target, 1.0, 0.0).astype(jnp.bfloat16)


def own_kernel(n_cp, count, group, slot_count, *refs):
    inputs, refs = refs[:6], refs[6:]
    combined, summed, peaks, totals, bias, picked, kept_rows, sent_rows, filled = refs[:9]
    buffers, sems, values = refs[9:15], refs[15], refs[16]
    pages_hbm, owner_hbm, offset_hbm, own_hbm, queries_hbm, absorb_hbm = inputs
    prompt_pages, decode_owner, slot_offset, own, queries, key_absorb = buffers
    rows = own.shape[1]
    heads = key_absorb.shape[0]
    wide = group * HEAD
    small = [pltpu.make_async_copy(inputs[i], buffers[i], sems.at[i]) for i in range(4)]
    large = []
    for g in range(heads // group):
        at = 4 + 2 * g
        large.append((
            pltpu.make_async_copy(queries_hbm.at[:, pl.ds(g * wide, wide)], queries.at[:, pl.ds(g * wide, wide)], sems.at[at]),
            pltpu.make_async_copy(absorb_hbm.at[pl.ds(g * group, group)], key_absorb.at[pl.ds(g * group, group)], sems.at[at + 1]),
        ))
    for copy in small:
        copy.start()
    for pair in large:
        for copy in pair:
            copy.start()
    for copy in small:
        copy.wait()
    block = own[...]
    values[...] = block[:LAT].T
    own_bias = visible_bias(prompt_pages, rows, 0)
    for b in range(count):
        bias[:, b * rows:(b + 1) * rows] = visible_bias(prompt_pages, rows, swap_pair(jnp.int32(b + 1), n_cp))

    me = lax.axis_index("cp")
    targets = []
    lane = lax.broadcasted_iota(jnp.int32, filled.shape, 1)
    lane_filled = jnp.zeros(filled.shape, jnp.float32)
    for c, (valid, page) in enumerate(slot_pages(me, slot_count, prompt_pages, decode_owner, slot_offset)):
        source = page * PAGE // rows
        column = swap_pair(lax.rem(me - source + n_cp, n_cp), n_cp) * rows + lax.rem(page * PAGE, rows)
        targets.append(jnp.where(valid, column, -PAGE))
        lane_filled = jnp.where(lane // PAGE == c, valid.astype(jnp.float32), lane_filled)
    filled[...] = lane_filled
    choice = row_picker(targets, (n_cp - 1) * rows)
    picked[...] = choice
    kept_rows[...] = lax.dot_general(choice[:, :rows], block, NT, preferred_element_type=jnp.float32).astype(jnp.bfloat16)
    targets = []
    behind = lax.rem(me + n_cp - 1, n_cp)
    for valid, page in slot_pages(behind, slot_count, prompt_pages, decode_owner, slot_offset):
        here = valid & (page * PAGE // rows == me)
        targets.append(jnp.where(here, lax.rem(page * PAGE, rows), -PAGE))
    choice = row_picker(targets, rows)
    sent_rows[...] = lax.dot_general(choice, block, NT, preferred_element_type=jnp.float32).astype(jnp.bfloat16)

    for g in range(heads // group):
        for copy in large[g]:
            copy.wait()
        for h in range(g * group, (g + 1) * group):
            at = h * HEAD
            absorbed = jnp.dot(queries[:, at:at + NOPE], key_absorb[h], preferred_element_type=jnp.float32)
            combined[h * rows:(h + 1) * rows, :LAT] = absorbed.astype(jnp.bfloat16)
            combined[h * rows:(h + 1) * rows, LAT:] = queries[:, at + NOPE:at + HEAD]
        span = pl.ds(g * group * rows, group * rows)
        scores = jnp.dot(combined[span, :], block, preferred_element_type=jnp.float32)
        scores = (scores.reshape(group, rows, rows) + own_bias[None]).reshape(group * rows, rows)
        peak = jnp.max(scores, axis=1, keepdims=True)
        weights = jnp.exp2((scores - peak) * exp2_scale)
        total = jnp.sum(weights, axis=1, keepdims=True)
        summed[span, :] = jnp.dot(weights.astype(jnp.bfloat16), values[...], preferred_element_type=jnp.float32)
        peaks[span, :] = jnp.broadcast_to(peak, (group * rows, LANES))
        totals[span, :] = jnp.broadcast_to(total, (group * rows, LANES))


def write_cache(rows, filled, page_cache, page_scales):
    slot_count = page_cache.shape[0]
    scales = []
    for b in range(NBLK):
        values = rows[:, b * BLOCK:(b + 1) * BLOCK]
        scale = jnp.max(jnp.abs(values), axis=1, keepdims=True) + amax_epsilon
        scale = scale.astype(jnp.bfloat16).astype(jnp.float32)
        encoded = (values / scale).astype(jnp.bfloat16)
        for c in range(slot_count):
            page_cache[c, :, b * BLOCK:(b + 1) * BLOCK] = encoded[c * PAGE:(c + 1) * PAGE]
        scales.append(scale)
    kept = rows.shape[0]
    which = lax.broadcasted_iota(jnp.int32, (kept, LANES), 1)
    table = jnp.zeros((kept, LANES), jnp.float32)
    for b, scale in enumerate(scales):
        table = jnp.where(which == b, scale, table)
    table = (table.T[:NBLK] * filled[:1, :kept]).astype(jnp.bfloat16)
    for c in range(slot_count):
        page_cache[c, :, LAT:] = rows[c * PAGE:(c + 1) * PAGE, LAT:].astype(jnp.bfloat16)
        page_scales[c] = table[:, c * PAGE:(c + 1) * PAGE]


def earlier_kernel(n_cp, count, group, *refs):
    combined, summed, peaks, totals, value_expand, bias, picked, kept_rows, sent_rows, filled = refs[:10]
    pieces = refs[10:8 + n_cp]
    attended, page_cache, page_scales, keys, values, result, sems = refs[8 + n_cp:]
    rows = attended.shape[0]
    heads = value_expand.shape[0]
    width = count * rows
    for b in range(count):
        block = pieces[b][...]
        keys[:, b * rows:(b + 1) * rows] = block
        values[b * rows:(b + 1) * rows, :] = block[:LAT].T

    def one_group(g, _):
        span = pl.ds(pl.multiple_of(g * group * rows, group * rows), group * rows)
        scores = jnp.dot(combined[span, :], keys[...], preferred_element_type=jnp.float32)
        scores = (scores.reshape(group, rows, width) + bias[...][None]).reshape(group * rows, width)
        old_peak = peaks[span, :]
        peak = jnp.maximum(old_peak, jnp.max(scores, axis=1, keepdims=True))
        total = jnp.zeros((group * rows, 1), jnp.float32)
        weights = []
        for b in range(count):
            part = jnp.exp2((scores[:, b * rows:(b + 1) * rows] - peak) * exp2_scale)
            total = total + jnp.sum(part, axis=1, keepdims=True)
            weights.append(part.astype(jnp.bfloat16))
        factor = jnp.exp2((old_peak - peak) * exp2_scale)
        inverse = 1.0 / (totals[span, :] * factor + total)
        factor = factor * inverse
        added = jnp.dot(jnp.concatenate(weights, axis=1), values[...], preferred_element_type=jnp.float32)
        mixed = []
        for b in range(NBLK):
            part = slice(b * BLOCK, (b + 1) * BLOCK)
            mixed.append((summed[span, part] * factor + added[:, part] * inverse).astype(jnp.bfloat16))
        mixed = jnp.concatenate(mixed, axis=1)
        for h in range(group):
            out = jnp.dot(mixed[h * rows:(h + 1) * rows], value_expand[g * group + h], preferred_element_type=jnp.float32)
            at = pl.ds(pl.multiple_of((g * group + h) * VDIM, VDIM), VDIM)
            result[:, at] = out.astype(jnp.bfloat16)
        send(g).start()
        return 0

    def send(g):
        at = pl.ds(pl.multiple_of(g * group * VDIM, group * VDIM), group * VDIM)
        return pltpu.make_async_copy(result.at[:, at], attended.at[:, at], sems.at[g])

    if count <= 4:
        for g in range(heads // group):
            one_group(g, 0)
    else:
        lax.fori_loop(0, heads // group, one_group, 0)
    found = kept_rows[...].astype(jnp.float32) + sent_rows[...].astype(jnp.float32)
    for b, piece in enumerate(pieces):
        choice = picked[:, (b + 1) * rows:(b + 2) * rows]
        found = found + lax.dot_general(choice, piece[...], NT, preferred_element_type=jnp.float32)
    write_cache(found, filled, page_cache, page_scales)
    for g in range(heads // group):
        send(g).wait()


def fetch(own, n_cp, n_dec):
    blocks = []
    for step in range(1, n_cp - 1, 2):
        pairs = [(c * n_dec + e, (c + step + e % 2) % n_cp * n_dec + e) for c in range(n_cp) for e in range(n_dec)]
        blocks.append(lax.ppermute(own, ("cp", "dec"), pairs))
    return blocks


def swap(blocks, n_dec):
    pieces = []
    for block in blocks:
        pieces += [block, lax.ppermute(block, "dec", [(e, e ^ 1) for e in range(n_dec)])]
    return pieces


def on_device(queries, latent_rows, key_absorb, value_expand, prompt_pages, decode_owner, slot_offset):
    n_cp = lax.axis_size("cp")
    dec_count = lax.axis_size("dec")
    heads = key_absorb.shape[0]
    rows = latent_rows.shape[0]
    prompts, width = decode_owner.shape
    slot_count = 3 * (rows // PAGE) // (2 * dec_count)
    kept = slot_count * PAGE
    reach = width * dec_count * slot_count * PAGE
    count = -(-reach // rows) - (1 if prompts == 2 else 0)
    count = min(n_cp - 2, count + count % 2)
    own = latent_rows.T
    blocks = fetch(own, n_cp, dec_count)

    vmem = pl.BlockSpec(memory_space=pltpu.VMEM)
    hbm = pl.BlockSpec(memory_space=pltpu.HBM)
    params = pltpu.CompilerParams(vmem_limit_bytes=32 * 2**20)
    group = 8
    inputs = (prompt_pages, decode_owner, slot_offset, own, queries, key_absorb)
    (combined, summed, peaks, totals, bias, picked, kept_rows, sent_rows, filled) = pl.pallas_call(
        functools.partial(own_kernel, n_cp, count, group, slot_count),
        in_specs=[hbm] * 6,
        out_specs=[vmem] * 9,
        out_shape=[
            jax.ShapeDtypeStruct((heads * rows, ROW), jnp.bfloat16),
            jax.ShapeDtypeStruct((heads * rows, LAT), jnp.float32),
            jax.ShapeDtypeStruct((heads * rows, LANES), jnp.float32),
            jax.ShapeDtypeStruct((heads * rows, LANES), jnp.float32),
            jax.ShapeDtypeStruct((rows, count * rows), jnp.float32),
            jax.ShapeDtypeStruct((kept, (n_cp - 1) * rows), jnp.bfloat16),
            jax.ShapeDtypeStruct((kept, ROW), jnp.bfloat16),
            jax.ShapeDtypeStruct((kept, ROW), jnp.bfloat16),
            jax.ShapeDtypeStruct((8, LANES), jnp.float32),
        ],
        scratch_shapes=[
            pltpu.SMEM(prompt_pages.shape, jnp.int32),
            pltpu.SMEM(decode_owner.shape, jnp.int32),
            pltpu.SMEM(slot_offset.shape, jnp.int32),
            pltpu.VMEM((ROW, rows), jnp.bfloat16),
            pltpu.VMEM((rows, heads * HEAD), jnp.bfloat16),
            pltpu.VMEM((heads, NOPE, LAT), jnp.bfloat16),
            pltpu.SemaphoreType.DMA((4 + 2 * (heads // group),)),
            pltpu.VMEM((rows, LAT), jnp.bfloat16),
        ],
        cost_estimate=pl.CostEstimate(
            flops=2 * rows * heads * (NOPE * LAT + rows * (ROW + LAT)),
            bytes_accessed=2 * (queries.size + key_absorb.size + heads * rows * ROW),
            transcendentals=rows * heads * rows,
        ),
        compiler_params=params,
        name="own",
    )(*[pltpu.with_memory_space_constraint(x, pltpu.HBM) for x in inputs])
    blocks, combined = lax.optimization_barrier((blocks, combined))
    pieces = swap(blocks, dec_count)
    sent_rows = lax.ppermute(sent_rows, "cp", [(c, (c + n_cp - 1) % n_cp) for c in range(n_cp)])

    group = 8 if count <= 4 else 1
    operands = (combined, summed, peaks, totals, value_expand, bias, picked, kept_rows, sent_rows, filled, *pieces)
    attended, page_cache, page_scales = pl.pallas_call(
        functools.partial(earlier_kernel, n_cp, count, group),
        in_specs=[vmem] * len(operands),
        out_specs=[hbm, vmem, vmem],
        out_shape=[
            jax.ShapeDtypeStruct((rows, heads * VDIM), jnp.bfloat16),
            jax.ShapeDtypeStruct((slot_count, PAGE, ROW), jnp.bfloat16),
            jax.ShapeDtypeStruct((slot_count, NBLK, PAGE), jnp.bfloat16),
        ],
        scratch_shapes=[
            pltpu.VMEM((ROW, count * rows), jnp.bfloat16),
            pltpu.VMEM((count * rows, LAT), jnp.bfloat16),
            pltpu.VMEM((rows, heads * VDIM), jnp.bfloat16),
            pltpu.SemaphoreType.DMA((heads // group,)),
        ],
        cost_estimate=pl.CostEstimate(
            flops=2 * rows * heads * (count * rows * (ROW + LAT) + LAT * VDIM),
            bytes_accessed=2 * (heads * rows * (ROW + VDIM) + value_expand.size),
            transcendentals=rows * heads * count * rows,
        ),
        compiler_params=params,
        name="earlier",
    )(*operands)
    page_cache = page_cache.reshape(1, 1, slot_count, PAGE, ROW)
    page_scales = page_scales.transpose(0, 2, 1).reshape(1, 1, slot_count, PAGE, NBLK)
    return attended, page_cache, page_scales


def solution(mesh):
    return jax.shard_map(
        on_device,
        mesh=mesh,
        in_specs=(
            P(("grp", "cp"), "dec"),
            P(("grp", "cp"), None),
            P("dec", None, None),
            P("dec", None, None),
            P("grp"),
            P("grp", None),
            P("grp"),
        ),
        out_specs=(
            P(("grp", "cp"), "dec"),
            P(("grp", "cp"), "dec", None, None, None),
            P(("grp", "cp"), "dec", None, None, None),
        ),
        check_vma=False,
    )
```

```python
import functools
import math

import jax
import jax.numpy as jnp
from jax import lax
from jax.experimental import pallas as pl
from jax.experimental.pallas import tpu as pltpu
from jax.sharding import PartitionSpec as P

LAT = 512
ROPE = 64
NOPE = 128
VDIM = 128
PAGE = 16
BLOCK = 128
NBLK = LAT // BLOCK
ROW = LAT + ROPE
HEAD = NOPE + ROPE
LANES = 128

masked_fill = -1e30
amax_epsilon = 1e-06
exp2_scale = math.log2(math.e) / math.sqrt(HEAD)

NT = (((1,), (1,)), ((), ()))


def prompt_starts(prompt_pages):
    starts = [jnp.int32(0)]
    for k in range(prompt_pages.shape[0] - 1):
        starts.append(starts[-1] + prompt_pages[k])
    return starts


def visible_bias(prompt_pages, rows, steps_back):
    first = lax.axis_index("cp") * rows
    token = first + lax.broadcasted_iota(jnp.int32, (rows, 1), 0)
    begin = jnp.zeros((rows, 1), jnp.int32)
    for start in prompt_starts(prompt_pages):
        begin = jnp.maximum(begin, jnp.where(start * PAGE <= token, start * PAGE, 0))
    spot = first - steps_back * rows + lax.broadcasted_iota(jnp.int32, (1, rows), 1)
    return jnp.where((spot >= begin) & (spot <= token), 0.0, masked_fill)


def swap_pair(position, n_cp):
    odd = lax.rem(lax.axis_index("dec"), 2)
    within = lax.rem(position + 1, 2)
    swapped = position - within + lax.rem(within + odd, 2)
    paired = (position >= 1) & (position <= (n_cp - 1) // 2 * 2)
    return jnp.where(paired, swapped, position)


def slot_pages(owner, slot_count, prompt_pages, decode_owner, slot_offset):
    prompts, width = decode_owner.shape
    cycle = width * lax.axis_size("dec") * slot_count
    starts = prompt_starts(prompt_pages)
    pages, start, offset, place = jnp.int32(0), jnp.int32(0), jnp.int32(0), jnp.int32(0)
    for k in range(prompts):
        for p in range(width):
            mine = decode_owner[k, p] == owner
            pages = jnp.where(mine, prompt_pages[k], pages)
            start = jnp.where(mine, starts[k], start)
            offset = jnp.where(mine, slot_offset[k], offset)
            place = jnp.where(mine, p, place)
    result = []
    for c in range(slot_count):
        turn = width * (lax.axis_index("dec") * slot_count + c) + place
        page = lax.rem(turn - offset + 2 * cycle, cycle)
        result.append((page < pages, start + page))
    return result


def row_picker(targets, columns):
    kept = len(targets) * PAGE
    row = lax.broadcasted_iota(jnp.int32, (kept, 1), 0)
    target = jnp.full((kept, 1), -1, jnp.int32)
    for c, column in enumerate(targets):
        target = jnp.where(row // PAGE == c, column + row % PAGE, target)
    column = lax.broadcasted_iota(jnp.int32, (1, columns), 1)
    return jnp.where(column == target, 1.0, 0.0).astype(jnp.bfloat16)


def own_kernel(n_cp, count, group, slot_count, *refs):
    inputs, refs = refs[:6], refs[6:]
    combined, summed, peaks, totals, bias, picked, kept_rows, filled = refs[:8]
    buffers, sems, values = refs[8:14], refs[14], refs[15]
    pages_hbm, owner_hbm, offset_hbm, own_hbm, queries_hbm, absorb_hbm = inputs
    prompt_pages, decode_owner, slot_offset, own, queries, key_absorb = buffers
    rows = own.shape[1]
    heads = key_absorb.shape[0]
    wide = group * HEAD
    small = [pltpu.make_async_copy(inputs[i], buffers[i], sems.at[i]) for i in range(4)]
    large = []
    for g in range(heads // group):
        at = 4 + 2 * g
        large.append((
            pltpu.make_async_copy(queries_hbm.at[:, pl.ds(g * wide, wide)], queries.at[:, pl.ds(g * wide, wide)], sems.at[at]),
            pltpu.make_async_copy(absorb_hbm.at[pl.ds(g * group, group)], key_absorb.at[pl.ds(g * group, group)], sems.at[at + 1]),
        ))
    small[3].start()
    for pair in large:
        for copy in pair:
            copy.start()
    for copy in small[:3]:
        copy.start()
    small[3].wait()
    block = own[...]
    values[...] = block[:LAT].T
    for g in range(heads // group):
        for copy in large[g]:
            copy.wait()
        if g == 0:
            for copy in small[:3]:
                copy.wait()
            own_bias = visible_bias(prompt_pages, rows, 0)
        for h in range(g * group, (g + 1) * group):
            at = h * HEAD
            absorbed = jnp.dot(queries[:, at:at + NOPE], key_absorb[h], preferred_element_type=jnp.float32)
            combined[h * rows:(h + 1) * rows, :LAT] = absorbed.astype(jnp.bfloat16)
            combined[h * rows:(h + 1) * rows, LAT:] = queries[:, at + NOPE:at + HEAD]
        span = pl.ds(g * group * rows, group * rows)
        scores = jnp.dot(combined[span, :], block, preferred_element_type=jnp.float32)
        scores = (scores.reshape(group, rows, rows) + own_bias[None]).reshape(group * rows, rows)
        peak = jnp.max(scores, axis=1, keepdims=True)
        weights = jnp.exp2((scores - peak) * exp2_scale)
        total = jnp.sum(weights, axis=1, keepdims=True)
        summed[span, :] = jnp.dot(weights.astype(jnp.bfloat16), values[...], preferred_element_type=jnp.float32)
        peaks[span, :] = jnp.broadcast_to(peak, (group * rows, LANES))
        totals[span, :] = jnp.broadcast_to(total, (group * rows, LANES))

    for b in range(count):
        bias[:, b * rows:(b + 1) * rows] = visible_bias(prompt_pages, rows, swap_pair(jnp.int32(b + 1), n_cp))
    me = lax.axis_index("cp")
    targets = []
    lane = lax.broadcasted_iota(jnp.int32, filled.shape, 1)
    lane_filled = jnp.zeros(filled.shape, jnp.float32)
    for c, (valid, page) in enumerate(slot_pages(me, slot_count, prompt_pages, decode_owner, slot_offset)):
        source = page * PAGE // rows
        column = swap_pair(lax.rem(me - source + n_cp, n_cp), n_cp) * rows + lax.rem(page * PAGE, rows)
        targets.append(jnp.where(valid, column, -PAGE))
        lane_filled = jnp.where(lane // PAGE == c, valid.astype(jnp.float32), lane_filled)
    filled[...] = lane_filled
    choice = row_picker(targets, n_cp * rows)
    picked[...] = choice
    kept_rows[...] = lax.dot_general(choice[:, :rows], block, NT, preferred_element_type=jnp.float32).astype(jnp.bfloat16)


def write_cache(rows, filled, page_cache, page_scales):
    slot_count = page_cache.shape[0]
    scales = []
    for b in range(NBLK):
        values = rows[:, b * BLOCK:(b + 1) * BLOCK]
        scale = jnp.max(jnp.abs(values), axis=1, keepdims=True) + amax_epsilon
        scale = scale.astype(jnp.bfloat16).astype(jnp.float32)
        encoded = (values / scale).astype(jnp.bfloat16)
        for c in range(slot_count):
            page_cache[c, :, b * BLOCK:(b + 1) * BLOCK] = encoded[c * PAGE:(c + 1) * PAGE]
        scales.append(scale)
    kept = rows.shape[0]
    which = lax.broadcasted_iota(jnp.int32, (kept, LANES), 1)
    table = jnp.zeros((kept, LANES), jnp.float32)
    for b, scale in enumerate(scales):
        table = jnp.where(which == b, scale, table)
    table = (table.T[:NBLK] * filled[:1, :kept]).astype(jnp.bfloat16)
    for c in range(slot_count):
        page_cache[c, :, LAT:] = rows[c * PAGE:(c + 1) * PAGE, LAT:].astype(jnp.bfloat16)
        page_scales[c] = table[:, c * PAGE:(c + 1) * PAGE]


def earlier_kernel(n_cp, count, group, *refs):
    combined, summed, peaks, totals, value_expand, bias, picked, kept_rows, filled = refs[:9]
    pieces = refs[9:8 + n_cp]
    attended, page_cache, page_scales, keys, values, result, sems = refs[8 + n_cp:]
    rows = attended.shape[0]
    heads = value_expand.shape[0]
    width = count * rows
    for b in range(count):
        block = pieces[b][...]
        keys[:, b * rows:(b + 1) * rows] = block
        values[b * rows:(b + 1) * rows, :] = block[:LAT].T

    def one_group(g, _):
        span = pl.ds(pl.multiple_of(g * group * rows, group * rows), group * rows)
        scores = jnp.dot(combined[span, :], keys[...], preferred_element_type=jnp.float32)
        scores = (scores.reshape(group, rows, width) + bias[...][None]).reshape(group * rows, width)
        old_peak = peaks[span, :]
        peak = jnp.maximum(old_peak, jnp.max(scores, axis=1, keepdims=True))
        total = jnp.zeros((group * rows, 1), jnp.float32)
        weights = []
        for b in range(count):
            part = jnp.exp2((scores[:, b * rows:(b + 1) * rows] - peak) * exp2_scale)
            total = total + jnp.sum(part, axis=1, keepdims=True)
            weights.append(part.astype(jnp.bfloat16))
        factor = jnp.exp2((old_peak - peak) * exp2_scale)
        inverse = 1.0 / (totals[span, :] * factor + total)
        factor = factor * inverse
        added = jnp.dot(jnp.concatenate(weights, axis=1), values[...], preferred_element_type=jnp.float32)
        mixed = []
        for b in range(NBLK):
            part = slice(b * BLOCK, (b + 1) * BLOCK)
            mixed.append((summed[span, part] * factor + added[:, part] * inverse).astype(jnp.bfloat16))
        mixed = jnp.concatenate(mixed, axis=1)
        for h in range(group):
            out = jnp.dot(mixed[h * rows:(h + 1) * rows], value_expand[g * group + h], preferred_element_type=jnp.float32)
            at = pl.ds(pl.multiple_of((g * group + h) * VDIM, VDIM), VDIM)
            result[:, at] = out.astype(jnp.bfloat16)
        send(g).start()
        return 0

    def send(g):
        at = pl.ds(pl.multiple_of(g * group * VDIM, group * VDIM), group * VDIM)
        return pltpu.make_async_copy(result.at[:, at], attended.at[:, at], sems.at[g])

    if count <= 4:
        for g in range(heads // group):
            one_group(g, 0)
    else:
        lax.fori_loop(0, heads // group, one_group, 0)
    found = kept_rows[...].astype(jnp.float32)
    for b, piece in enumerate(pieces):
        choice = picked[:, (b + 1) * rows:(b + 2) * rows]
        found = found + lax.dot_general(choice, piece[...], NT, preferred_element_type=jnp.float32)
    write_cache(found, filled, page_cache, page_scales)
    for g in range(heads // group):
        send(g).wait()


def fetch(own, n_cp, n_dec):
    blocks = []
    for step in range(1, n_cp - 1, 2):
        pairs = [(c * n_dec + e, (c + step + e % 2) % n_cp * n_dec + e) for c in range(n_cp) for e in range(n_dec)]
        blocks.append(lax.ppermute(own, ("cp", "dec"), pairs))
    last = lax.ppermute(own, "cp", [(c, (c + n_cp - 1) % n_cp) for c in range(n_cp)])
    return blocks, last


def swap(blocks, n_dec):
    pieces = []
    for block in blocks:
        pieces += [block, lax.ppermute(block, "dec", [(e, e ^ 1) for e in range(n_dec)])]
    return pieces


def on_device(queries, latent_rows, key_absorb, value_expand, prompt_pages, decode_owner, slot_offset):
    n_cp = lax.axis_size("cp")
    dec_count = lax.axis_size("dec")
    heads = key_absorb.shape[0]
    rows = latent_rows.shape[0]
    prompts, width = decode_owner.shape
    slot_count = 3 * (rows // PAGE) // (2 * dec_count)
    kept = slot_count * PAGE
    reach = width * dec_count * slot_count * PAGE
    count = -(-reach // rows) - (1 if prompts == 2 else 0)
    count = min(n_cp - 2, count + count % 2)
    own = latent_rows.T
    blocks, last = fetch(own, n_cp, dec_count)

    vmem = pl.BlockSpec(memory_space=pltpu.VMEM)
    hbm = pl.BlockSpec(memory_space=pltpu.HBM)
    params = pltpu.CompilerParams(vmem_limit_bytes=32 * 2**20)
    group = 4
    inputs = (prompt_pages, decode_owner, slot_offset, own, queries, key_absorb)
    (combined, summed, peaks, totals, bias, picked, kept_rows, filled) = pl.pallas_call(
        functools.partial(own_kernel, n_cp, count, group, slot_count),
        in_specs=[hbm] * 6,
        out_specs=[vmem] * 8,
        out_shape=[
            jax.ShapeDtypeStruct((heads * rows, ROW), jnp.bfloat16),
            jax.ShapeDtypeStruct((heads * rows, LAT), jnp.float32),
            jax.ShapeDtypeStruct((heads * rows, LANES), jnp.float32),
            jax.ShapeDtypeStruct((heads * rows, LANES), jnp.float32),
            jax.ShapeDtypeStruct((rows, count * rows), jnp.float32),
            jax.ShapeDtypeStruct((kept, n_cp * rows), jnp.bfloat16),
            jax.ShapeDtypeStruct((kept, ROW), jnp.bfloat16),
            jax.ShapeDtypeStruct((8, LANES), jnp.float32),
        ],
        scratch_shapes=[
            pltpu.SMEM(prompt_pages.shape, jnp.int32),
            pltpu.SMEM(decode_owner.shape, jnp.int32),
            pltpu.SMEM(slot_offset.shape, jnp.int32),
            pltpu.VMEM((ROW, rows), jnp.bfloat16),
            pltpu.VMEM((rows, heads * HEAD), jnp.bfloat16),
            pltpu.VMEM((heads, NOPE, LAT), jnp.bfloat16),
            pltpu.SemaphoreType.DMA((4 + 2 * (heads // group),)),
            pltpu.VMEM((rows, LAT), jnp.bfloat16),
        ],
        cost_estimate=pl.CostEstimate(
            flops=2 * rows * heads * (NOPE * LAT + rows * (ROW + LAT)),
            bytes_accessed=2 * (queries.size + key_absorb.size + heads * rows * ROW),
            transcendentals=rows * heads * rows,
        ),
        compiler_params=params,
        name="own",
    )(*[pltpu.with_memory_space_constraint(x, pltpu.HBM) for x in inputs])
    blocks, combined = lax.optimization_barrier((blocks, combined))
    pieces = swap(blocks, dec_count) + [last]

    group = 8 if count <= 4 else 1
    operands = (combined, summed, peaks, totals, value_expand, bias, picked, kept_rows, filled, *pieces)
    attended, page_cache, page_scales = pl.pallas_call(
        functools.partial(earlier_kernel, n_cp, count, group),
        in_specs=[vmem] * len(operands),
        out_specs=[hbm, vmem, vmem],
        out_shape=[
            jax.ShapeDtypeStruct((rows, heads * VDIM), jnp.bfloat16),
            jax.ShapeDtypeStruct((slot_count, PAGE, ROW), jnp.bfloat16),
            jax.ShapeDtypeStruct((slot_count, NBLK, PAGE), jnp.bfloat16),
        ],
        scratch_shapes=[
            pltpu.VMEM((ROW, count * rows), jnp.bfloat16),
            pltpu.VMEM((count * rows, LAT), jnp.bfloat16),
            pltpu.VMEM((rows, heads * VDIM), jnp.bfloat16),
            pltpu.SemaphoreType.DMA((heads // group,)),
        ],
        cost_estimate=pl.CostEstimate(
            flops=2 * rows * heads * (count * rows * (ROW + LAT) + LAT * VDIM),
            bytes_accessed=2 * (heads * rows * (ROW + VDIM) + value_expand.size),
            transcendentals=rows * heads * count * rows,
        ),
        compiler_params=params,
        name="earlier",
    )(*operands)
    page_cache = page_cache.reshape(1, 1, slot_count, PAGE, ROW)
    page_scales = page_scales.transpose(0, 2, 1).reshape(1, 1, slot_count, PAGE, NBLK)
    return attended, page_cache, page_scales


def solution(mesh):
    return jax.shard_map(
        on_device,
        mesh=mesh,
        in_specs=(
            P(("grp", "cp"), "dec"),
            P(("grp", "cp"), None),
            P("dec", None, None),
            P("dec", None, None),
            P("grp"),
            P("grp", None),
            P("grp"),
        ),
        out_specs=(
            P(("grp", "cp"), "dec"),
            P(("grp", "cp"), "dec", None, None, None),
            P(("grp", "cp"), "dec", None, None, None),
        ),
        check_vma=False,
    )
```

```python
import functools
import math

import jax
import jax.numpy as jnp
from jax import lax
from jax.experimental import pallas as pl
from jax.experimental.pallas import tpu as pltpu
from jax.sharding import PartitionSpec as P

LAT = 512
ROPE = 64
NOPE = 128
VDIM = 128
PAGE = 16
BLOCK = 128
NBLK = LAT // BLOCK
ROW = LAT + ROPE
HEAD = NOPE + ROPE
LANES = 128
SWAP = 3

masked_fill = -1e30
amax_epsilon = 1e-06
exp2_scale = math.log2(math.e) / math.sqrt(HEAD)

NT = (((1,), (1,)), ((), ()))


def prompt_starts(prompt_pages):
    starts = [jnp.int32(0)]
    for k in range(prompt_pages.shape[0] - 1):
        starts.append(starts[-1] + prompt_pages[k])
    return starts


def visible_bias(prompt_pages, rows, steps_back):
    first = lax.axis_index("cp") * rows
    token = first + lax.broadcasted_iota(jnp.int32, (rows, 1), 0)
    begin = jnp.zeros((rows, 1), jnp.int32)
    for start in prompt_starts(prompt_pages):
        begin = jnp.maximum(begin, jnp.where(start * PAGE <= token, start * PAGE, 0))
    spot = first - steps_back * rows + lax.broadcasted_iota(jnp.int32, (1, rows), 1)
    return jnp.where((spot >= begin) & (spot <= token), 0.0, masked_fill)


def swap_pair(position, n_cp):
    odd = lax.rem(lax.axis_index("dec"), 2)
    within = lax.rem(position + 1, 2)
    swapped = position - within + lax.rem(within + odd, 2)
    paired = (position >= 1) & (position <= (n_cp - 1) // 2 * 2)
    return jnp.where(paired, swapped, position)


def slot_pages(owner, slot_count, prompt_pages, decode_owner, slot_offset):
    prompts, width = decode_owner.shape
    cycle = width * lax.axis_size("dec") * slot_count
    starts = prompt_starts(prompt_pages)
    pages, start, offset, place = jnp.int32(0), jnp.int32(0), jnp.int32(0), jnp.int32(0)
    for k in range(prompts):
        for p in range(width):
            mine = decode_owner[k, p] == owner
            pages = jnp.where(mine, prompt_pages[k], pages)
            start = jnp.where(mine, starts[k], start)
            offset = jnp.where(mine, slot_offset[k], offset)
            place = jnp.where(mine, p, place)
    result = []
    for c in range(slot_count):
        turn = width * (lax.axis_index("dec") * slot_count + c) + place
        page = lax.rem(turn - offset + 2 * cycle, cycle)
        result.append((page < pages, start + page))
    return result


def row_picker(targets, columns):
    kept = len(targets) * PAGE
    row = lax.broadcasted_iota(jnp.int32, (kept, 1), 0)
    target = jnp.full((kept, 1), -1, jnp.int32)
    for c, column in enumerate(targets):
        target = jnp.where(row // PAGE == c, column + row % PAGE, target)
    column = lax.broadcasted_iota(jnp.int32, (1, columns), 1)
    return jnp.where(column == target, 1.0, 0.0).astype(jnp.bfloat16)


def head_values(latents, value_expand, h):
    both = jnp.concatenate([value_expand[h], value_expand[h + 1]], axis=1)
    return jnp.dot(latents, both, preferred_element_type=jnp.float32).astype(jnp.bfloat16)


def own_kernel(n_cp, group, slot_count, *refs):
    inputs, expand_hbm, refs = refs[:6], refs[6], refs[7:]
    combined, result, peaks, totals, sent_rows, value_expand = refs[:6]
    buffers, sems, latents = refs[6:12], refs[12], refs[13]
    pages_hbm, owner_hbm, offset_hbm, own_hbm, queries_hbm, absorb_hbm = inputs
    prompt_pages, decode_owner, slot_offset, own, queries, key_absorb = buffers
    rows = own.shape[1]
    heads = key_absorb.shape[0]
    wide = group * HEAD
    small = [pltpu.make_async_copy(inputs[i], buffers[i], sems.at[i]) for i in range(4)]
    large = []
    for g in range(heads // group):
        at = 4 + 3 * g
        some = pl.ds(g * group, group)
        large.append((
            pltpu.make_async_copy(queries_hbm.at[:, pl.ds(g * wide, wide)], queries.at[:, pl.ds(g * wide, wide)], sems.at[at]),
            pltpu.make_async_copy(absorb_hbm.at[some], key_absorb.at[some], sems.at[at + 1]),
            pltpu.make_async_copy(expand_hbm.at[some], value_expand.at[some], sems.at[at + 2]),
        ))
    for copy in small:
        copy.start()
    for pair in large:
        for copy in pair:
            copy.start()
    small[3].wait()
    block = own[...]
    latents[...] = block[:LAT].T
    for g in range(heads // group):
        for copy in large[g]:
            copy.wait()
        if g == 0:
            for copy in small[:3]:
                copy.wait()
            own_bias = visible_bias(prompt_pages, rows, 0)
            me = lax.axis_index("cp")
            behind = lax.rem(me + n_cp - 1, n_cp)
            targets = []
            for valid, page in slot_pages(behind, slot_count, prompt_pages, decode_owner, slot_offset):
                here = valid & (page * PAGE // rows == me)
                targets.append(jnp.where(here, lax.rem(page * PAGE, rows), -PAGE))
            choice = row_picker(targets, rows)
            sent = lax.dot_general(choice, block, NT, preferred_element_type=jnp.float32)
            sent_rows[:, :ROW] = sent.astype(jnp.bfloat16)
            sent_rows[:, ROW:] = jnp.zeros((choice.shape[0], sent_rows.shape[1] - ROW), jnp.bfloat16)
        for h in range(g * group, (g + 1) * group):
            at = h * HEAD
            absorbed = jnp.dot(queries[:, at:at + NOPE], key_absorb[h], preferred_element_type=jnp.float32)
            combined[h * rows:(h + 1) * rows, :LAT] = absorbed.astype(jnp.bfloat16)
            combined[h * rows:(h + 1) * rows, LAT:] = queries[:, at + NOPE:at + HEAD]
        span = pl.ds(g * group * rows, group * rows)
        scores = jnp.dot(combined[span, :], block, preferred_element_type=jnp.float32)
        scores = (scores.reshape(group, rows, rows) + own_bias[None]).reshape(group * rows, rows)
        peak = jnp.max(scores, axis=1, keepdims=True)
        weights = jnp.exp2((scores - peak) * exp2_scale)
        total = jnp.sum(weights, axis=1, keepdims=True)
        weights = weights.astype(jnp.bfloat16)
        for i in range(0, group, 2):
            both = head_values(latents[...], value_expand, g * group + i)
            for j in range(2):
                h = i + j
                out = jnp.dot(weights[h * rows:(h + 1) * rows], both[:, j * VDIM:(j + 1) * VDIM], preferred_element_type=jnp.float32)
                result[(g * group + h) * rows:(g * group + h + 1) * rows, :] = out
        peaks[span, :] = jnp.broadcast_to(peak, (group * rows, LANES))
        totals[span, :] = jnp.broadcast_to(total, (group * rows, LANES))


def index_kernel(n_cp, count, slot_count, *refs):
    inputs, refs = refs[:4], refs[4:]
    bias, picked, kept_rows, filled = refs[:4]
    buffers, sems = refs[4:8], refs[8]
    prompt_pages, decode_owner, slot_offset, own = buffers
    rows = own.shape[1]
    copies = [pltpu.make_async_copy(inputs[i], buffers[i], sems.at[i]) for i in range(4)]
    for copy in copies:
        copy.start()
    for copy in copies:
        copy.wait()
    for b in range(count):
        bias[:, b * rows:(b + 1) * rows] = visible_bias(prompt_pages, rows, swap_pair(jnp.int32(b + 1), n_cp))
    me = lax.axis_index("cp")
    targets = []
    lane = lax.broadcasted_iota(jnp.int32, filled.shape, 1)
    lane_filled = jnp.zeros(filled.shape, jnp.float32)
    for c, (valid, page) in enumerate(slot_pages(me, slot_count, prompt_pages, decode_owner, slot_offset)):
        source = page * PAGE // rows
        column = swap_pair(lax.rem(me - source + n_cp, n_cp), n_cp) * rows + lax.rem(page * PAGE, rows)
        targets.append(jnp.where(valid, column, -PAGE))
        lane_filled = jnp.where(lane // PAGE == c, valid.astype(jnp.float32), lane_filled)
    filled[...] = lane_filled
    choice = row_picker(targets, (n_cp - 1) * rows)
    picked[...] = choice
    kept_rows[...] = lax.dot_general(choice[:, :rows], own[...], NT, preferred_element_type=jnp.float32).astype(jnp.bfloat16)


def write_cache(rows, filled, page_cache, page_scales):
    slot_count = page_cache.shape[0]
    scales = []
    for b in range(NBLK):
        values = rows[:, b * BLOCK:(b + 1) * BLOCK]
        scale = jnp.max(jnp.abs(values), axis=1, keepdims=True) + amax_epsilon
        scale = scale.astype(jnp.bfloat16).astype(jnp.float32)
        encoded = (values / scale).astype(jnp.bfloat16)
        for c in range(slot_count):
            page_cache[c, :, b * BLOCK:(b + 1) * BLOCK] = encoded[c * PAGE:(c + 1) * PAGE]
        scales.append(scale)
    kept = rows.shape[0]
    which = lax.broadcasted_iota(jnp.int32, (kept, LANES), 1)
    table = jnp.zeros((kept, LANES), jnp.float32)
    for b, scale in enumerate(scales):
        table = jnp.where(which == b, scale, table)
    table = (table.T[:NBLK] * filled[:1, :kept]).astype(jnp.bfloat16)
    for c in range(slot_count):
        page_cache[c, :, LAT:] = rows[c * PAGE:(c + 1) * PAGE, LAT:].astype(jnp.bfloat16)
        page_scales[c] = table[:, c * PAGE:(c + 1) * PAGE]


def earlier_kernel(n_cp, count, group, *refs):
    combined, own_result, peaks, totals, value_expand, bias, picked, kept_rows, sent_rows, filled = refs[:10]
    arrived, refs = refs[10:10 + (n_cp - 2) // 2 * (1 + SWAP)], refs[10 + (n_cp - 2) // 2 * (1 + SWAP):]
    attended, page_cache, page_scales, keys, latents, result, sems = refs
    pieces = []
    for at in range(0, len(arrived), 1 + SWAP):
        pieces.append(arrived[at][...])
        pieces.append(jnp.concatenate([part[...] for part in arrived[at + 1:at + 1 + SWAP]], axis=0))
    rows = attended.shape[0]
    heads = value_expand.shape[0]
    width = count * rows
    for b in range(count):
        block = pieces[b]
        keys[:, b * rows:(b + 1) * rows] = block
        latents[b * rows:(b + 1) * rows, :] = block[:LAT].T

    def one_group(g, _):
        span = pl.ds(pl.multiple_of(g * group * rows, group * rows), group * rows)
        scores = jnp.dot(combined[span, :], keys[...], preferred_element_type=jnp.float32)
        scores = (scores.reshape(group, rows, width) + bias[...][None]).reshape(group * rows, width)
        old_peak = peaks[span, :]
        peak = jnp.maximum(old_peak, jnp.max(scores, axis=1, keepdims=True))
        total = jnp.zeros((group * rows, 1), jnp.float32)
        weights = []
        for b in range(count):
            part = jnp.exp2((scores[:, b * rows:(b + 1) * rows] - peak) * exp2_scale)
            total = total + jnp.sum(part, axis=1, keepdims=True)
            weights.append(part.astype(jnp.bfloat16))
        weights = jnp.concatenate(weights, axis=1)
        factor = jnp.exp2((old_peak - peak) * exp2_scale)
        inverse = 1.0 / (totals[span, :] * factor + total)
        old = own_result[span, :] * (factor * inverse)
        for i in range(0, group, 2):
            both = head_values(latents[...], value_expand, g * group + i)
            for j in range(2):
                part = slice((i + j) * rows, (i + j + 1) * rows)
                out = jnp.dot(weights[part], both[:, j * VDIM:(j + 1) * VDIM], preferred_element_type=jnp.float32)
                at = pl.ds(pl.multiple_of((g * group + i + j) * VDIM, VDIM), VDIM)
                result[:, at] = (old[part] + out * inverse[part]).astype(jnp.bfloat16)
        send(g).start()
        return 0

    def send(g):
        at = pl.ds(pl.multiple_of(g * group * VDIM, group * VDIM), group * VDIM)
        return pltpu.make_async_copy(result.at[:, at], attended.at[:, at], sems.at[g])

    if count <= 4:
        for g in range(heads // group):
            one_group(g, 0)
    else:
        lax.fori_loop(0, heads // group, one_group, 0)
    found = kept_rows[...].astype(jnp.float32) + sent_rows[:, :ROW].astype(jnp.float32)
    for b, piece in enumerate(pieces):
        choice = picked[:, (b + 1) * rows:(b + 2) * rows]
        found = found + lax.dot_general(choice, piece, NT, preferred_element_type=jnp.float32)
    write_cache(found, filled, page_cache, page_scales)
    for g in range(heads // group):
        send(g).wait()


def fetch(own, n_cp, n_dec):
    blocks = []
    for step in range(1, n_cp - 1, 2):
        pairs = [(c * n_dec + e, (c + step + e % 2) % n_cp * n_dec + e) for c in range(n_cp) for e in range(n_dec)]
        blocks.append(lax.ppermute(own, ("cp", "dec"), pairs))
    return blocks


def swap(blocks, n_dec):
    pieces = []
    for block in blocks:
        parts = [block[at:at + ROW // SWAP] for at in range(0, ROW, ROW // SWAP)]
        pieces += [block] + [lax.ppermute(part, "dec", [(e, e ^ 1) for e in range(n_dec)]) for part in parts]
    return pieces


def on_device(queries, latent_rows, key_absorb, value_expand, prompt_pages, decode_owner, slot_offset):
    n_cp = lax.axis_size("cp")
    dec_count = lax.axis_size("dec")
    heads = key_absorb.shape[0]
    rows = latent_rows.shape[0]
    prompts, width = decode_owner.shape
    slot_count = 3 * (rows // PAGE) // (2 * dec_count)
    kept = slot_count * PAGE
    reach = width * dec_count * slot_count * PAGE
    count = -(-reach // rows) - (1 if prompts == 2 else 0)
    count = min(n_cp - 2, count + count % 2)
    own = latent_rows.T
    blocks = fetch(own, n_cp, dec_count)

    vmem = pl.BlockSpec(memory_space=pltpu.VMEM)
    hbm = pl.BlockSpec(memory_space=pltpu.HBM)
    params = pltpu.CompilerParams(vmem_limit_bytes=32 * 2**20)
    group = 4
    inputs = [pltpu.with_memory_space_constraint(x, pltpu.HBM) for x in (prompt_pages, decode_owner, slot_offset, own, queries, key_absorb)]
    small_scratch = [
        pltpu.SMEM(prompt_pages.shape, jnp.int32),
        pltpu.SMEM(decode_owner.shape, jnp.int32),
        pltpu.SMEM(slot_offset.shape, jnp.int32),
        pltpu.VMEM((ROW, rows), jnp.bfloat16),
    ]
    combined, result, peaks, totals, sent_rows, value_copy = pl.pallas_call(
        functools.partial(own_kernel, n_cp, group, slot_count),
        in_specs=[hbm] * 7,
        out_specs=[vmem] * 6,
        out_shape=[
            jax.ShapeDtypeStruct((heads * rows, ROW), jnp.bfloat16),
            jax.ShapeDtypeStruct((heads * rows, VDIM), jnp.float32),
            jax.ShapeDtypeStruct((heads * rows, LANES), jnp.float32),
            jax.ShapeDtypeStruct((heads * rows, LANES), jnp.float32),
            jax.ShapeDtypeStruct((kept, -(-ROW // LANES) * LANES), jnp.bfloat16),
            jax.ShapeDtypeStruct(value_expand.shape, jnp.bfloat16),
        ],
        scratch_shapes=small_scratch + [
            pltpu.VMEM((rows, heads * HEAD), jnp.bfloat16),
            pltpu.VMEM((heads, NOPE, LAT), jnp.bfloat16),
            pltpu.SemaphoreType.DMA((4 + 3 * (heads // group),)),
            pltpu.VMEM((rows, LAT), jnp.bfloat16),
        ],
        cost_estimate=pl.CostEstimate(
            flops=2 * rows * heads * (2 * NOPE * LAT + rows * (ROW + VDIM)),
            bytes_accessed=2 * (queries.size + key_absorb.size + heads * rows * ROW),
            transcendentals=rows * heads * rows,
        ),
        compiler_params=params,
        name="own",
    )(*inputs, pltpu.with_memory_space_constraint(value_expand, pltpu.HBM))
    sent_rows = lax.ppermute(sent_rows, "cp", [(c, (c + n_cp - 1) % n_cp) for c in range(n_cp)])
    *inputs, combined = lax.optimization_barrier((*inputs[:4], combined))
    bias, picked, kept_rows, filled = pl.pallas_call(
        functools.partial(index_kernel, n_cp, count, slot_count),
        in_specs=[hbm] * 4,
        out_specs=[vmem] * 4,
        out_shape=[
            jax.ShapeDtypeStruct((rows, count * rows), jnp.float32),
            jax.ShapeDtypeStruct((kept, (n_cp - 1) * rows), jnp.bfloat16),
            jax.ShapeDtypeStruct((kept, ROW), jnp.bfloat16),
            jax.ShapeDtypeStruct((8, LANES), jnp.float32),
        ],
        scratch_shapes=small_scratch + [pltpu.SemaphoreType.DMA((4,))],
        cost_estimate=pl.CostEstimate(flops=2**27, bytes_accessed=2**20, transcendentals=0),
        compiler_params=params,
        name="index",
    )(*inputs)
    blocks, bias = lax.optimization_barrier((blocks, bias))
    pieces = swap(blocks, dec_count)

    group = 8 if count <= 4 else 2
    operands = (combined, result, peaks, totals, value_copy, bias, picked, kept_rows, sent_rows, filled, *pieces)
    attended, page_cache, page_scales = pl.pallas_call(
        functools.partial(earlier_kernel, n_cp, count, group),
        in_specs=[vmem] * len(operands),
        out_specs=[hbm, vmem, vmem],
        out_shape=[
            jax.ShapeDtypeStruct((rows, heads * VDIM), jnp.bfloat16),
            jax.ShapeDtypeStruct((slot_count, PAGE, ROW), jnp.bfloat16),
            jax.ShapeDtypeStruct((slot_count, NBLK, PAGE), jnp.bfloat16),
        ],
        scratch_shapes=[
            pltpu.VMEM((ROW, count * rows), jnp.bfloat16),
            pltpu.VMEM((count * rows, LAT), jnp.bfloat16),
            pltpu.VMEM((rows, heads * VDIM), jnp.bfloat16),
            pltpu.SemaphoreType.DMA((heads // group,)),
        ],
        cost_estimate=pl.CostEstimate(
            flops=2 * heads * count * rows * (rows * (ROW + VDIM) + LAT * VDIM),
            bytes_accessed=2 * (heads * rows * (ROW + VDIM) + value_expand.size),
            transcendentals=rows * heads * count * rows,
        ),
        compiler_params=params,
        name="earlier",
    )(*operands)
    page_cache = page_cache.reshape(1, 1, slot_count, PAGE, ROW)
    page_scales = page_scales.transpose(0, 2, 1).reshape(1, 1, slot_count, PAGE, NBLK)
    return attended, page_cache, page_scales


def solution(mesh):
    return jax.shard_map(
        on_device,
        mesh=mesh,
        in_specs=(
            P(("grp", "cp"), "dec"),
            P(("grp", "cp"), None),
            P("dec", None, None),
            P("dec", None, None),
            P("grp"),
            P("grp", None),
            P("grp"),
        ),
        out_specs=(
            P(("grp", "cp"), "dec"),
            P(("grp", "cp"), "dec", None, None, None),
            P(("grp", "cp"), "dec", None, None, None),
        ),
        check_vma=False,
    )
```

```python
import functools
import math

import jax
import jax.numpy as jnp
from jax import lax
from jax.experimental import pallas as pl
from jax.experimental.pallas import tpu as pltpu
from jax.sharding import PartitionSpec as P

LAT = 512
ROPE = 64
NOPE = 128
VDIM = 128
PAGE = 16
BLOCK = 128
NBLK = LAT // BLOCK
ROW = LAT + ROPE
HEAD = NOPE + ROPE
LANES = 128
SWAP = 3

masked_fill = -1e30
amax_epsilon = 1e-06
exp2_scale = math.log2(math.e) / math.sqrt(HEAD)

NT = (((1,), (1,)), ((), ()))


def prompt_starts(prompt_pages):
    starts = [jnp.int32(0)]
    for k in range(prompt_pages.shape[0] - 1):
        starts.append(starts[-1] + prompt_pages[k])
    return starts


def visible_bias(prompt_pages, rows, steps_back):
    first = lax.axis_index("cp") * rows
    token = first + lax.broadcasted_iota(jnp.int32, (rows, 1), 0)
    begin = jnp.zeros((rows, 1), jnp.int32)
    for start in prompt_starts(prompt_pages):
        begin = jnp.maximum(begin, jnp.where(start * PAGE <= token, start * PAGE, 0))
    spot = first - steps_back * rows + lax.broadcasted_iota(jnp.int32, (1, rows), 1)
    return jnp.where((spot >= begin) & (spot <= token), 0.0, masked_fill)


def swap_pair(position, n_cp):
    odd = lax.rem(lax.axis_index("dec"), 2)
    within = lax.rem(position + 1, 2)
    swapped = position - within + lax.rem(within + odd, 2)
    paired = (position >= 1) & (position <= (n_cp - 1) // 2 * 2)
    return jnp.where(paired, swapped, position)


def slot_pages(owner, slot_count, prompt_pages, decode_owner, slot_offset):
    prompts, width = decode_owner.shape
    cycle = width * lax.axis_size("dec") * slot_count
    starts = prompt_starts(prompt_pages)
    pages, start, offset, place = jnp.int32(0), jnp.int32(0), jnp.int32(0), jnp.int32(0)
    for k in range(prompts):
        for p in range(width):
            mine = decode_owner[k, p] == owner
            pages = jnp.where(mine, prompt_pages[k], pages)
            start = jnp.where(mine, starts[k], start)
            offset = jnp.where(mine, slot_offset[k], offset)
            place = jnp.where(mine, p, place)
    result = []
    for c in range(slot_count):
        turn = width * (lax.axis_index("dec") * slot_count + c) + place
        page = lax.rem(turn - offset + 2 * cycle, cycle)
        result.append((page < pages, start + page))
    return result


def row_picker(targets, columns):
    kept = len(targets) * PAGE
    row = lax.broadcasted_iota(jnp.int32, (kept, 1), 0)
    target = jnp.full((kept, 1), -1, jnp.int32)
    for c, column in enumerate(targets):
        target = jnp.where(row // PAGE == c, column + row % PAGE, target)
    column = lax.broadcasted_iota(jnp.int32, (1, columns), 1)
    return jnp.where(column == target, 1.0, 0.0).astype(jnp.bfloat16)


def head_values(latents, value_expand, h):
    both = jnp.concatenate([value_expand[h], value_expand[h + 1]], axis=1)
    return jnp.dot(latents, both, preferred_element_type=jnp.float32).astype(jnp.bfloat16)


def own_kernel(n_cp, count, chunk, group, slot_count, *refs):
    inputs, refs = refs[:7], refs[7:]
    combined, result, peaks, totals, sent_rows, bias, picked, filled, own, value_expand = refs[:10]
    prompt_pages, decode_owner, slot_offset, queries, key_absorb, latents, sems = refs[10:]
    pages_hbm, owner_hbm, offset_hbm, own_hbm, queries_hbm, absorb_hbm, expand_hbm = inputs
    rows = own.shape[1]
    heads = key_absorb.shape[0]
    small = [
        pltpu.make_async_copy(source, target, sems.at[i])
        for i, (source, target) in enumerate(zip(inputs[:4], (prompt_pages, decode_owner, slot_offset, own)))
    ]
    large = []
    for g in range(heads // chunk):
        at = 4 + 3 * g
        some = pl.ds(g * chunk, chunk)
        wide = pl.ds(g * chunk * HEAD, chunk * HEAD)
        large.append((
            pltpu.make_async_copy(queries_hbm.at[:, wide], queries.at[:, wide], sems.at[at]),
            pltpu.make_async_copy(absorb_hbm.at[some], key_absorb.at[some], sems.at[at + 1]),
            pltpu.make_async_copy(expand_hbm.at[some], value_expand.at[some], sems.at[at + 2]),
        ))
    for copy in small:
        copy.start()
    for i in range(3):
        for chunk_copies in large:
            if i < 2:
                chunk_copies[i].start()
    for chunk_copies in large:
        chunk_copies[2].start()
    small[3].wait()
    block = own[...]
    latents[...] = block[:LAT].T
    for copy in small[:3]:
        copy.wait()
    own_bias = visible_bias(prompt_pages, rows, 0)
    index_work(n_cp, count, slot_count, prompt_pages, decode_owner, slot_offset, block, sent_rows, bias, picked, filled)

    for g in range(heads // group):
        if g * group % chunk == 0:
            for copy in large[g * group // chunk]:
                copy.wait()
        for h in range(g * group, (g + 1) * group):
            at = h * HEAD
            absorbed = jnp.dot(queries[:, at:at + NOPE], key_absorb[h], preferred_element_type=jnp.float32)
            combined[h * rows:(h + 1) * rows, :LAT] = absorbed.astype(jnp.bfloat16)
            combined[h * rows:(h + 1) * rows, LAT:] = queries[:, at + NOPE:at + HEAD]
        span = pl.ds(g * group * rows, group * rows)
        scores = jnp.dot(combined[span, :], block, preferred_element_type=jnp.float32)
        scores = (scores.reshape(group, rows, rows) + own_bias[None]).reshape(group * rows, rows)
        peak = jnp.max(scores, axis=1, keepdims=True)
        weights = jnp.exp2((scores - peak) * exp2_scale)
        total = jnp.sum(weights, axis=1, keepdims=True)
        weights = weights.astype(jnp.bfloat16)
        for i in range(0, group, 2):
            both = head_values(latents[...], value_expand, g * group + i)
            for j in range(2):
                h = i + j
                out = jnp.dot(weights[h * rows:(h + 1) * rows], both[:, j * VDIM:(j + 1) * VDIM], preferred_element_type=jnp.float32)
                result[(g * group + h) * rows:(g * group + h + 1) * rows, :] = out
        peaks[span, :] = jnp.broadcast_to(peak, (group * rows, LANES))
        totals[span, :] = jnp.broadcast_to(total, (group * rows, LANES))


def index_work(n_cp, count, slot_count, prompt_pages, decode_owner, slot_offset, block, sent_rows, bias, picked, filled):
    rows = block.shape[1]
    me = lax.axis_index("cp")
    behind = lax.rem(me + n_cp - 1, n_cp)
    targets = []
    for valid, page in slot_pages(behind, slot_count, prompt_pages, decode_owner, slot_offset):
        here = valid & (page * PAGE // rows == me)
        targets.append(jnp.where(here, lax.rem(page * PAGE, rows), -PAGE))
    choice = row_picker(targets, rows)
    sent = lax.dot_general(choice, block, NT, preferred_element_type=jnp.float32)
    sent_rows[:, :ROW] = sent.astype(jnp.bfloat16)
    sent_rows[:, ROW:] = jnp.zeros((choice.shape[0], sent_rows.shape[1] - ROW), jnp.bfloat16)
    for b in range(count):
        bias[:, b * rows:(b + 1) * rows] = visible_bias(prompt_pages, rows, swap_pair(jnp.int32(b + 1), n_cp))
    targets = []
    lane = lax.broadcasted_iota(jnp.int32, filled.shape, 1)
    lane_filled = jnp.zeros(filled.shape, jnp.float32)
    for c, (valid, page) in enumerate(slot_pages(me, slot_count, prompt_pages, decode_owner, slot_offset)):
        source = page * PAGE // rows
        column = swap_pair(lax.rem(me - source + n_cp, n_cp), n_cp) * rows + lax.rem(page * PAGE, rows)
        targets.append(jnp.where(valid, column, -PAGE))
        lane_filled = jnp.where(lane // PAGE == c, valid.astype(jnp.float32), lane_filled)
    filled[...] = lane_filled
    picked[...] = row_picker(targets, (n_cp - 1) * rows)


def keep_kernel(picked, own, kept_rows):
    choice = picked[:, :own.shape[1]]
    kept_rows[...] = lax.dot_general(choice, own[...], NT, preferred_element_type=jnp.float32)


def arrived_kernel(picked, kept_rows, *refs):
    half = (len(refs) - 2)
    blocks, found, latents = refs[:half], refs[half], refs[half + 1]
    rows = blocks[0].shape[1]
    total = kept_rows[...]
    for i, block in enumerate(blocks):
        at = (1 + 2 * i) * rows
        total = total + lax.dot_general(picked[:, at:at + rows], block[...], NT, preferred_element_type=jnp.float32)
        latents[i * rows:(i + 1) * rows, :] = block[:LAT, :].T
    found[...] = total


def write_cache(rows, filled, page_cache, page_scales):
    slot_count = page_cache.shape[0]
    scales = []
    for b in range(NBLK):
        values = rows[:, b * BLOCK:(b + 1) * BLOCK]
        scale = jnp.max(jnp.abs(values), axis=1, keepdims=True) + amax_epsilon
        scale = scale.astype(jnp.bfloat16).astype(jnp.float32)
        encoded = (values / scale).astype(jnp.bfloat16)
        for c in range(slot_count):
            page_cache[c, :, b * BLOCK:(b + 1) * BLOCK] = encoded[c * PAGE:(c + 1) * PAGE]
        scales.append(scale)
    kept = rows.shape[0]
    which = lax.broadcasted_iota(jnp.int32, (kept, LANES), 1)
    table = jnp.zeros((kept, LANES), jnp.float32)
    for b, scale in enumerate(scales):
        table = jnp.where(which == b, scale, table)
    table = (table.T[:NBLK] * filled[:1, :kept]).astype(jnp.bfloat16)
    for c in range(slot_count):
        page_cache[c, :, LAT:] = rows[c * PAGE:(c + 1) * PAGE, LAT:].astype(jnp.bfloat16)
        page_scales[c] = table[:, c * PAGE:(c + 1) * PAGE]


def earlier_kernel(n_cp, count, group, *refs):
    combined, own_result, peaks, totals, value_expand, bias, picked, found, sent_rows, filled, fetched_latents = refs[:11]
    arrived, refs = refs[11:11 + (n_cp - 2) // 2 * (1 + SWAP)], refs[11 + (n_cp - 2) // 2 * (1 + SWAP):]
    attended, page_cache, page_scales, keys, latents, result, cache_buf, scale_buf, sems = refs
    rows = attended.shape[0]
    heads = value_expand.shape[0]
    width = count * rows
    steps = heads // group
    found_rows = found[...] + sent_rows[:, :ROW].astype(jnp.float32)
    for i in range((n_cp - 2) // 2):
        at = i * (1 + SWAP)
        swapped = jnp.concatenate([part[...] for part in arrived[at + 1:at + 1 + SWAP]], axis=0)
        b = 2 * i + 1
        choice = picked[:, (b + 1) * rows:(b + 2) * rows]
        found_rows = found_rows + lax.dot_general(choice, swapped, NT, preferred_element_type=jnp.float32)
        if b < count:
            keys[:, (b - 1) * rows:b * rows] = arrived[at][...]
            keys[:, b * rows:(b + 1) * rows] = swapped
            latents[(b - 1) * rows:b * rows, :] = fetched_latents[i * rows:(i + 1) * rows, :]
            latents[b * rows:(b + 1) * rows, :] = swapped[:LAT].T

    def span(g):
        return slice(g * group * rows, (g + 1) * group * rows)

    def score(g):
        scores = jnp.dot(combined[span(g), :], keys[...], preferred_element_type=jnp.float32)
        return (scores.reshape(group, rows, width) + bias[...][None]).reshape(group * rows, width)

    def weigh(g, scores):
        old_peak = peaks[span(g), :]
        parts = [scores[:, b * rows:(b + 1) * rows] for b in range(count)]
        peak = jnp.maximum(old_peak, jnp.max(functools.reduce(jnp.maximum, parts), axis=1, keepdims=True))
        parts = [jnp.exp2((part - peak) * exp2_scale) for part in parts]
        total = jnp.sum(functools.reduce(jnp.add, parts), axis=1, keepdims=True)
        factor = jnp.exp2((old_peak - peak) * exp2_scale)
        inverse = 1.0 / (totals[span(g), :] * factor + total)
        weights = jnp.concatenate([part.astype(jnp.bfloat16) for part in parts], axis=1)
        return weights, factor * inverse, inverse

    def mix(g, weights):
        return jnp.dot(weights, latents[...], preferred_element_type=jnp.float32).astype(jnp.bfloat16)

    def finish(g, mixed, factor, inverse):
        for i in range(group):
            part = slice(i * rows, (i + 1) * rows)
            h = g * group + i
            out = jnp.dot(mixed[part], value_expand[h], preferred_element_type=jnp.float32)
            out = own_result[h * rows:(h + 1) * rows, :] * factor[part] + out * inverse[part]
            result[:, h * VDIM:(h + 1) * VDIM] = out.astype(jnp.bfloat16)
        send(g).start()

    def send(g):
        at = pl.ds(g * group * VDIM, group * VDIM)
        return pltpu.make_async_copy(result.at[:, at], attended.at[:, at], sems.at[g])

    scores, weights, mixed = {}, {}, {}
    for step in range(steps + 2):
        if step < steps:
            scores[step] = score(step)
        if step == 0:
            write_cache(found_rows, filled, cache_buf, scale_buf)
            cache_copies = [
                pltpu.make_async_copy(cache_buf, page_cache, sems.at[steps]),
                pltpu.make_async_copy(scale_buf, page_scales, sems.at[steps + 1]),
            ]
            for copy in cache_copies:
                copy.start()
        if 0 <= step - 2:
            finish(step - 2, mixed.pop(step - 2), *weights.pop(step - 2)[1:])
        if 0 <= step - 1 < steps:
            weights[step - 1] = weigh(step - 1, scores.pop(step - 1))
            mixed[step - 1] = mix(step - 1, weights[step - 1][0])
    for g in range(steps):
        send(g).wait()
    for copy in cache_copies:
        copy.wait()


def fetch(own, n_cp, n_dec):
    blocks = []
    for step in range(1, n_cp - 1, 2):
        pairs = [(c * n_dec + e, (c + step + e % 2) % n_cp * n_dec + e) for c in range(n_cp) for e in range(n_dec)]
        blocks.append(lax.ppermute(own, ("cp", "dec"), pairs))
    return blocks


def swap(blocks, n_dec):
    pieces = []
    for block in blocks:
        parts = [block[at:at + ROW // SWAP] for at in range(0, ROW, ROW // SWAP)]
        pieces += [block] + [lax.ppermute(part, "dec", [(e, e ^ 1) for e in range(n_dec)]) for part in parts]
    return pieces


def on_device(queries, latent_rows, key_absorb, value_expand, prompt_pages, decode_owner, slot_offset):
    n_cp = lax.axis_size("cp")
    dec_count = lax.axis_size("dec")
    heads = key_absorb.shape[0]
    rows = latent_rows.shape[0]
    prompts, width = decode_owner.shape
    slot_count = 3 * (rows // PAGE) // (2 * dec_count)
    kept = slot_count * PAGE
    reach = width * dec_count * slot_count * PAGE
    count = -(-reach // rows) - (1 if prompts == 2 else 0)
    count = min(n_cp - 2, count + count % 2)
    own = latent_rows.T
    blocks = fetch(own, n_cp, dec_count)

    vmem = pl.BlockSpec(memory_space=pltpu.VMEM)
    hbm = pl.BlockSpec(memory_space=pltpu.HBM)
    params = pltpu.CompilerParams(vmem_limit_bytes=32 * 2**20)
    group, chunk = 2, 4
    inputs = (prompt_pages, decode_owner, slot_offset, own, queries, key_absorb, value_expand)
    combined, result, peaks, totals, sent_rows, bias, picked, filled, own_copy, value_copy = pl.pallas_call(
        functools.partial(own_kernel, n_cp, count, chunk, group, slot_count),
        in_specs=[hbm] * 7,
        out_specs=[vmem] * 10,
        out_shape=[
            jax.ShapeDtypeStruct((heads * rows, ROW), jnp.bfloat16),
            jax.ShapeDtypeStruct((heads * rows, VDIM), jnp.float32),
            jax.ShapeDtypeStruct((heads * rows, LANES), jnp.float32),
            jax.ShapeDtypeStruct((heads * rows, LANES), jnp.float32),
            jax.ShapeDtypeStruct((kept, -(-ROW // LANES) * LANES), jnp.bfloat16),
            jax.ShapeDtypeStruct((rows, count * rows), jnp.float32),
            jax.ShapeDtypeStruct((kept, (n_cp - 1) * rows), jnp.bfloat16),
            jax.ShapeDtypeStruct((8, LANES), jnp.float32),
            jax.ShapeDtypeStruct(own.shape, jnp.bfloat16),
            jax.ShapeDtypeStruct(value_expand.shape, jnp.bfloat16),
        ],
        scratch_shapes=[
            pltpu.SMEM(prompt_pages.shape, jnp.int32),
            pltpu.SMEM(decode_owner.shape, jnp.int32),
            pltpu.SMEM(slot_offset.shape, jnp.int32),
            pltpu.VMEM((rows, heads * HEAD), jnp.bfloat16),
            pltpu.VMEM((heads, NOPE, LAT), jnp.bfloat16),
            pltpu.VMEM((rows, LAT), jnp.bfloat16),
            pltpu.SemaphoreType.DMA((4 + 3 * (heads // chunk),)),
        ],
        cost_estimate=pl.CostEstimate(
            flops=2 * rows * heads * (2 * NOPE * LAT + rows * (ROW + VDIM)),
            bytes_accessed=2 * (queries.size + key_absorb.size + heads * rows * ROW),
            transcendentals=rows * heads * rows,
        ),
        compiler_params=params,
        name="own",
    )(*[pltpu.with_memory_space_constraint(x, pltpu.HBM) for x in inputs])
    sent_rows = lax.ppermute(sent_rows, "cp", [(c, (c + n_cp - 1) % n_cp) for c in range(n_cp)])
    kept_rows = pl.pallas_call(
        keep_kernel,
        in_specs=[vmem] * 2,
        out_specs=vmem,
        out_shape=jax.ShapeDtypeStruct((kept, ROW), jnp.float32),
        cost_estimate=pl.CostEstimate(flops=2**27, bytes_accessed=2**20, transcendentals=0),
        compiler_params=params,
        name="keep",
    )(picked, own_copy)
    blocks, kept_rows = lax.optimization_barrier((blocks, kept_rows))
    pieces = swap(blocks, dec_count)
    found, fetched_latents = pl.pallas_call(
        arrived_kernel,
        in_specs=[vmem] * (2 + len(blocks)),
        out_specs=[vmem] * 2,
        out_shape=[
            jax.ShapeDtypeStruct((kept, ROW), jnp.float32),
            jax.ShapeDtypeStruct((len(blocks) * rows, LAT), jnp.bfloat16),
        ],
        cost_estimate=pl.CostEstimate(flops=2**20, bytes_accessed=2**10, transcendentals=0),
        compiler_params=params,
        name="arrived",
    )(picked, kept_rows, *blocks)

    operands = (combined, result, peaks, totals, value_copy, bias, picked, found, sent_rows, filled, fetched_latents, *pieces)
    attended, page_cache, page_scales = pl.pallas_call(
        functools.partial(earlier_kernel, n_cp, count, group),
        in_specs=[vmem] * len(operands),
        out_specs=[hbm] * 3,
        out_shape=[
            jax.ShapeDtypeStruct((rows, heads * VDIM), jnp.bfloat16),
            jax.ShapeDtypeStruct((slot_count, PAGE, ROW), jnp.bfloat16),
            jax.ShapeDtypeStruct((slot_count, NBLK, PAGE), jnp.bfloat16),
        ],
        scratch_shapes=[
            pltpu.VMEM((ROW, count * rows), jnp.bfloat16),
            pltpu.VMEM((count * rows, LAT), jnp.bfloat16),
            pltpu.VMEM((rows, heads * VDIM), jnp.bfloat16),
            pltpu.VMEM((slot_count, PAGE, ROW), jnp.bfloat16),
            pltpu.VMEM((slot_count, NBLK, PAGE), jnp.bfloat16),
            pltpu.SemaphoreType.DMA((heads // group + 2,)),
        ],
        cost_estimate=pl.CostEstimate(
            flops=2 * rows * heads * (count * rows * (ROW + LAT) + LAT * VDIM),
            bytes_accessed=2 * (heads * rows * (ROW + VDIM) + value_expand.size),
            transcendentals=rows * heads * count * rows,
        ),
        compiler_params=params,
        name="earlier",
    )(*operands)
    page_cache = page_cache.reshape(1, 1, slot_count, PAGE, ROW)
    page_scales = page_scales.transpose(0, 2, 1).reshape(1, 1, slot_count, PAGE, NBLK)
    return attended, page_cache, page_scales


def solution(mesh):
    return jax.shard_map(
        on_device,
        mesh=mesh,
        in_specs=(
            P(("grp", "cp"), "dec"),
            P(("grp", "cp"), None),
            P("dec", None, None),
            P("dec", None, None),
            P("grp"),
            P("grp", None),
            P("grp"),
        ),
        out_specs=(
            P(("grp", "cp"), "dec"),
            P(("grp", "cp"), "dec", None, None, None),
            P(("grp", "cp"), "dec", None, None, None),
        ),
        check_vma=False,
    )
```

```python
import functools
import math

import jax
import jax.numpy as jnp
from jax import lax
from jax.experimental import pallas as pl
from jax.experimental.pallas import tpu as pltpu
from jax.sharding import PartitionSpec as P

LAT = 512
ROPE = 64
NOPE = 128
VDIM = 128
PAGE = 16
BLOCK = 128
NBLK = LAT // BLOCK
ROW = LAT + ROPE
HEAD = NOPE + ROPE
LANES = 128
SWAP = 3

masked_fill = -1e30
amax_epsilon = 1e-06
exp2_scale = math.log2(math.e) / math.sqrt(HEAD)

NT = (((1,), (1,)), ((), ()))


def prompt_starts(prompt_pages):
    starts = [jnp.int32(0)]
    for k in range(prompt_pages.shape[0] - 1):
        starts.append(starts[-1] + prompt_pages[k])
    return starts


def visible_bias(prompt_pages, rows, steps_back):
    first = lax.axis_index("cp") * rows
    token = first + lax.broadcasted_iota(jnp.int32, (rows, 1), 0)
    begin = jnp.zeros((rows, 1), jnp.int32)
    for start in prompt_starts(prompt_pages):
        begin = jnp.maximum(begin, jnp.where(start * PAGE <= token, start * PAGE, 0))
    spot = first - steps_back * rows + lax.broadcasted_iota(jnp.int32, (1, rows), 1)
    return jnp.where((spot >= begin) & (spot <= token), 0.0, masked_fill)


def swap_pair(position, n_cp):
    odd = lax.rem(lax.axis_index("dec"), 2)
    within = lax.rem(position + 1, 2)
    swapped = position - within + lax.rem(within + odd, 2)
    paired = (position >= 1) & (position <= (n_cp - 1) // 2 * 2)
    return jnp.where(paired, swapped, position)


def slot_pages(owner, slot_count, prompt_pages, decode_owner, slot_offset):
    prompts, width = decode_owner.shape
    cycle = width * lax.axis_size("dec") * slot_count
    starts = prompt_starts(prompt_pages)
    pages, start, offset, place = jnp.int32(0), jnp.int32(0), jnp.int32(0), jnp.int32(0)
    for k in range(prompts):
        for p in range(width):
            mine = decode_owner[k, p] == owner
            pages = jnp.where(mine, prompt_pages[k], pages)
            start = jnp.where(mine, starts[k], start)
            offset = jnp.where(mine, slot_offset[k], offset)
            place = jnp.where(mine, p, place)
    result = []
    for c in range(slot_count):
        turn = width * (lax.axis_index("dec") * slot_count + c) + place
        page = lax.rem(turn - offset + 2 * cycle, cycle)
        result.append((page < pages, start + page))
    return result


def row_picker(targets, columns):
    kept = len(targets) * PAGE
    row = lax.broadcasted_iota(jnp.int32, (kept, 1), 0)
    target = jnp.full((kept, 1), -1, jnp.int32)
    for c, column in enumerate(targets):
        target = jnp.where(row // PAGE == c, column + row % PAGE, target)
    column = lax.broadcasted_iota(jnp.int32, (1, columns), 1)
    return jnp.where(column == target, 1.0, 0.0).astype(jnp.bfloat16)


def head_values(latents, value_expand, h):
    both = jnp.concatenate([value_expand[h], value_expand[h + 1]], axis=1)
    return jnp.dot(latents, both, preferred_element_type=jnp.float32).astype(jnp.bfloat16)


def own_kernel(n_cp, count, chunk, group, slot_count, *refs):
    inputs, refs = refs[:7], refs[7:]
    combined, result, peaks, totals, sent_rows, bias, picked, filled, own, value_expand = refs[:10]
    prompt_pages, decode_owner, slot_offset, queries, key_absorb, latents, sems = refs[10:]
    pages_hbm, owner_hbm, offset_hbm, own_hbm, queries_hbm, absorb_hbm, expand_hbm = inputs
    rows = own.shape[1]
    heads = key_absorb.shape[0]
    small = [
        pltpu.make_async_copy(source, target, sems.at[i])
        for i, (source, target) in enumerate(zip(inputs[:4], (prompt_pages, decode_owner, slot_offset, own)))
    ]
    large = []
    for g in range(heads // chunk):
        at = 4 + 3 * g
        some = pl.ds(g * chunk, chunk)
        wide = pl.ds(g * chunk * HEAD, chunk * HEAD)
        large.append((
            pltpu.make_async_copy(queries_hbm.at[:, wide], queries.at[:, wide], sems.at[at]),
            pltpu.make_async_copy(absorb_hbm.at[some], key_absorb.at[some], sems.at[at + 1]),
            pltpu.make_async_copy(expand_hbm.at[some], value_expand.at[some], sems.at[at + 2]),
        ))
    for copy in small:
        copy.start()
    for chunk_copies in large:
        for copy in chunk_copies:
            copy.start()
    steps = heads // group

    def absorb(g):
        if g * group % chunk == 0:
            for copy in large[g * group // chunk][:2]:
                copy.wait()
        for h in range(g * group, (g + 1) * group):
            at = h * HEAD
            absorbed = jnp.dot(queries[:, at:at + NOPE], key_absorb[h], preferred_element_type=jnp.float32)
            combined[h * rows:(h + 1) * rows, :LAT] = absorbed.astype(jnp.bfloat16)
            combined[h * rows:(h + 1) * rows, LAT:] = queries[:, at + NOPE:at + HEAD]

    def score(g):
        return jnp.dot(combined[g * group * rows:(g + 1) * group * rows, :], own[...], preferred_element_type=jnp.float32)

    def value(g):
        if g * group % chunk == 0:
            large[g * group // chunk][2].wait()
        return [head_values(latents[...], value_expand, g * group + i) for i in range(0, group, 2)]

    def finish(g, scores, both):
        span = slice(g * group * rows, (g + 1) * group * rows)
        scores = (scores.reshape(group, rows, rows) + own_bias[None]).reshape(group * rows, rows)
        peak = jnp.max(scores, axis=1, keepdims=True)
        weights = jnp.exp2((scores - peak) * exp2_scale)
        total = jnp.sum(weights, axis=1, keepdims=True)
        weights = weights.astype(jnp.bfloat16)
        for i in range(group):
            mine = both[i // 2][:, i % 2 * VDIM:(i % 2 + 1) * VDIM]
            out = jnp.dot(weights[i * rows:(i + 1) * rows], mine, preferred_element_type=jnp.float32)
            result[(g * group + i) * rows:(g * group + i + 1) * rows, :] = out
        peaks[span, :] = jnp.broadcast_to(peak, (group * rows, LANES))
        totals[span, :] = jnp.broadcast_to(total, (group * rows, LANES))

    scores, both = {}, {}
    for step in range(steps + 2):
        if step < steps:
            absorb(step)
        if step == 0:
            small[3].wait()
            latents[...] = own[:LAT, :].T
        if step == 1:
            for copy in small[:3]:
                copy.wait()
            own_bias = visible_bias(prompt_pages, rows, 0)
            index_work(n_cp, count, slot_count, prompt_pages, decode_owner, slot_offset, own[...], sent_rows, bias, picked, filled)
        if 0 <= step - 1 < steps:
            scores[step - 1] = score(step - 1)
            both[step - 1] = value(step - 1)
        if 0 <= step - 2:
            finish(step - 2, scores.pop(step - 2), both.pop(step - 2))


def index_work(n_cp, count, slot_count, prompt_pages, decode_owner, slot_offset, block, sent_rows, bias, picked, filled):
    rows = block.shape[1]
    me = lax.axis_index("cp")
    behind = lax.rem(me + n_cp - 1, n_cp)
    targets = []
    for valid, page in slot_pages(behind, slot_count, prompt_pages, decode_owner, slot_offset):
        here = valid & (page * PAGE // rows == me)
        targets.append(jnp.where(here, lax.rem(page * PAGE, rows), -PAGE))
    choice = row_picker(targets, rows)
    sent = lax.dot_general(choice, block, NT, preferred_element_type=jnp.float32)
    sent_rows[:, :ROW] = sent.astype(jnp.bfloat16)
    sent_rows[:, ROW:] = jnp.zeros((choice.shape[0], sent_rows.shape[1] - ROW), jnp.bfloat16)
    for b in range(count):
        bias[:, b * rows:(b + 1) * rows] = visible_bias(prompt_pages, rows, swap_pair(jnp.int32(b + 1), n_cp))
    targets = []
    lane = lax.broadcasted_iota(jnp.int32, filled.shape, 1)
    lane_filled = jnp.zeros(filled.shape, jnp.float32)
    for c, (valid, page) in enumerate(slot_pages(me, slot_count, prompt_pages, decode_owner, slot_offset)):
        source = page * PAGE // rows
        column = swap_pair(lax.rem(me - source + n_cp, n_cp), n_cp) * rows + lax.rem(page * PAGE, rows)
        targets.append(jnp.where(valid, column, -PAGE))
        lane_filled = jnp.where(lane // PAGE == c, valid.astype(jnp.float32), lane_filled)
    filled[...] = lane_filled
    picked[...] = row_picker(targets, (n_cp - 1) * rows)


def keep_kernel(picked, own, kept_rows):
    choice = picked[:, :own.shape[1]]
    kept_rows[...] = lax.dot_general(choice, own[...], NT, preferred_element_type=jnp.float32)


def arrived_kernel(picked, kept_rows, *refs):
    half = (len(refs) - 2)
    blocks, found, latents = refs[:half], refs[half], refs[half + 1]
    rows = blocks[0].shape[1]
    total = kept_rows[...]
    for i, block in enumerate(blocks):
        at = (1 + 2 * i) * rows
        total = total + lax.dot_general(picked[:, at:at + rows], block[...], NT, preferred_element_type=jnp.float32)
        latents[i * rows:(i + 1) * rows, :] = block[:LAT, :].T
    found[...] = total


def write_cache(rows, filled, page_cache, page_scales):
    slot_count = page_cache.shape[0]
    scales = []
    for b in range(NBLK):
        values = rows[:, b * BLOCK:(b + 1) * BLOCK]
        scale = jnp.max(jnp.abs(values), axis=1, keepdims=True) + amax_epsilon
        scale = scale.astype(jnp.bfloat16).astype(jnp.float32)
        encoded = (values / scale).astype(jnp.bfloat16)
        for c in range(slot_count):
            page_cache[c, :, b * BLOCK:(b + 1) * BLOCK] = encoded[c * PAGE:(c + 1) * PAGE]
        scales.append(scale)
    kept = rows.shape[0]
    which = lax.broadcasted_iota(jnp.int32, (kept, LANES), 1)
    table = jnp.zeros((kept, LANES), jnp.float32)
    for b, scale in enumerate(scales):
        table = jnp.where(which == b, scale, table)
    table = (table.T[:NBLK] * filled[:1, :kept]).astype(jnp.bfloat16)
    for c in range(slot_count):
        page_cache[c, :, LAT:] = rows[c * PAGE:(c + 1) * PAGE, LAT:].astype(jnp.bfloat16)
        page_scales[c] = table[:, c * PAGE:(c + 1) * PAGE]


def earlier_kernel(n_cp, count, group, *refs):
    combined, own_result, peaks, totals, value_expand, bias, picked, found, sent_rows, filled, fetched_latents = refs[:11]
    arrived, refs = refs[11:11 + (n_cp - 2) // 2 * (1 + SWAP)], refs[11 + (n_cp - 2) // 2 * (1 + SWAP):]
    attended, page_cache, page_scales, keys, latents, result, cache_buf, scale_buf, sems = refs
    rows = attended.shape[0]
    heads = value_expand.shape[0]
    width = count * rows
    steps = heads // group
    found_rows = found[...] + sent_rows[:, :ROW].astype(jnp.float32)
    for i in range((n_cp - 2) // 2):
        at = i * (1 + SWAP)
        swapped = jnp.concatenate([part[...] for part in arrived[at + 1:at + 1 + SWAP]], axis=0)
        b = 2 * i + 1
        choice = picked[:, (b + 1) * rows:(b + 2) * rows]
        found_rows = found_rows + lax.dot_general(choice, swapped, NT, preferred_element_type=jnp.float32)
        if b < count:
            keys[:, (b - 1) * rows:b * rows] = arrived[at][...]
            keys[:, b * rows:(b + 1) * rows] = swapped
            latents[(b - 1) * rows:b * rows, :] = fetched_latents[i * rows:(i + 1) * rows, :]
            latents[b * rows:(b + 1) * rows, :] = swapped[:LAT].T

    def span(g):
        return slice(g * group * rows, (g + 1) * group * rows)

    def score(g):
        scores = jnp.dot(combined[span(g), :], keys[...], preferred_element_type=jnp.float32)
        return (scores.reshape(group, rows, width) + bias[...][None]).reshape(group * rows, width)

    def weigh(g, scores):
        old_peak = peaks[span(g), :]
        parts = [scores[:, b * rows:(b + 1) * rows] for b in range(count)]
        peak = jnp.maximum(old_peak, jnp.max(functools.reduce(jnp.maximum, parts), axis=1, keepdims=True))
        parts = [jnp.exp2((part - peak) * exp2_scale) for part in parts]
        total = jnp.sum(functools.reduce(jnp.add, parts), axis=1, keepdims=True)
        factor = jnp.exp2((old_peak - peak) * exp2_scale)
        inverse = 1.0 / (totals[span(g), :] * factor + total)
        weights = jnp.concatenate([part.astype(jnp.bfloat16) for part in parts], axis=1)
        return weights, factor * inverse, inverse

    def mix(g, weights):
        return jnp.dot(weights, latents[...], preferred_element_type=jnp.float32).astype(jnp.bfloat16)

    def finish(g, mixed, factor, inverse):
        for i in range(group):
            part = slice(i * rows, (i + 1) * rows)
            h = g * group + i
            out = jnp.dot(mixed[part], value_expand[h], preferred_element_type=jnp.float32)
            out = own_result[h * rows:(h + 1) * rows, :] * factor[part] + out * inverse[part]
            result[:, h * VDIM:(h + 1) * VDIM] = out.astype(jnp.bfloat16)
        send(g).start()

    def send(g):
        at = pl.ds(g * group * VDIM, group * VDIM)
        return pltpu.make_async_copy(result.at[:, at], attended.at[:, at], sems.at[g])

    scores, weights, mixed = {}, {}, {}
    for step in range(steps + 2):
        if step < steps:
            scores[step] = score(step)
        if step == 0:
            write_cache(found_rows, filled, cache_buf, scale_buf)
            cache_copies = [
                pltpu.make_async_copy(cache_buf, page_cache, sems.at[steps]),
                pltpu.make_async_copy(scale_buf, page_scales, sems.at[steps + 1]),
            ]
            for copy in cache_copies:
                copy.start()
        if 0 <= step - 2:
            finish(step - 2, mixed.pop(step - 2), *weights.pop(step - 2)[1:])
        if 0 <= step - 1 < steps:
            weights[step - 1] = weigh(step - 1, scores.pop(step - 1))
            mixed[step - 1] = mix(step - 1, weights[step - 1][0])
    for g in range(steps):
        send(g).wait()
    for copy in cache_copies:
        copy.wait()


def fetch(own, n_cp, n_dec):
    blocks = []
    for step in range(1, n_cp - 1, 2):
        pairs = [(c * n_dec + e, (c + step + e % 2) % n_cp * n_dec + e) for c in range(n_cp) for e in range(n_dec)]
        blocks.append(lax.ppermute(own, ("cp", "dec"), pairs))
    return blocks


def swap(blocks, n_dec):
    pieces = []
    for block in blocks:
        parts = [block[at:at + ROW // SWAP] for at in range(0, ROW, ROW // SWAP)]
        pieces += [block] + [lax.ppermute(part, "dec", [(e, e ^ 1) for e in range(n_dec)]) for part in parts]
    return pieces


def on_device(queries, latent_rows, key_absorb, value_expand, prompt_pages, decode_owner, slot_offset):
    n_cp = lax.axis_size("cp")
    dec_count = lax.axis_size("dec")
    heads = key_absorb.shape[0]
    rows = latent_rows.shape[0]
    prompts, width = decode_owner.shape
    slot_count = 3 * (rows // PAGE) // (2 * dec_count)
    kept = slot_count * PAGE
    reach = width * dec_count * slot_count * PAGE
    count = -(-reach // rows) - (1 if prompts == 2 else 0)
    count = min(n_cp - 2, count + count % 2)
    own = latent_rows.T
    blocks = fetch(own, n_cp, dec_count)

    vmem = pl.BlockSpec(memory_space=pltpu.VMEM)
    hbm = pl.BlockSpec(memory_space=pltpu.HBM)
    params = pltpu.CompilerParams(vmem_limit_bytes=32 * 2**20)
    group, chunk = 2, 4
    inputs = (prompt_pages, decode_owner, slot_offset, own, queries, key_absorb, value_expand)
    combined, result, peaks, totals, sent_rows, bias, picked, filled, own_copy, value_copy = pl.pallas_call(
        functools.partial(own_kernel, n_cp, count, chunk, group, slot_count),
        in_specs=[hbm] * 7,
        out_specs=[vmem] * 10,
        out_shape=[
            jax.ShapeDtypeStruct((heads * rows, ROW), jnp.bfloat16),
            jax.ShapeDtypeStruct((heads * rows, VDIM), jnp.float32),
            jax.ShapeDtypeStruct((heads * rows, LANES), jnp.float32),
            jax.ShapeDtypeStruct((heads * rows, LANES), jnp.float32),
            jax.ShapeDtypeStruct((kept, -(-ROW // LANES) * LANES), jnp.bfloat16),
            jax.ShapeDtypeStruct((rows, count * rows), jnp.float32),
            jax.ShapeDtypeStruct((kept, (n_cp - 1) * rows), jnp.bfloat16),
            jax.ShapeDtypeStruct((8, LANES), jnp.float32),
            jax.ShapeDtypeStruct(own.shape, jnp.bfloat16),
            jax.ShapeDtypeStruct(value_expand.shape, jnp.bfloat16),
        ],
        scratch_shapes=[
            pltpu.SMEM(prompt_pages.shape, jnp.int32),
            pltpu.SMEM(decode_owner.shape, jnp.int32),
            pltpu.SMEM(slot_offset.shape, jnp.int32),
            pltpu.VMEM((rows, heads * HEAD), jnp.bfloat16),
            pltpu.VMEM((heads, NOPE, LAT), jnp.bfloat16),
            pltpu.VMEM((rows, LAT), jnp.bfloat16),
            pltpu.SemaphoreType.DMA((4 + 3 * (heads // chunk),)),
        ],
        cost_estimate=pl.CostEstimate(
            flops=2 * rows * heads * (2 * NOPE * LAT + rows * (ROW + VDIM)),
            bytes_accessed=2 * (queries.size + key_absorb.size + heads * rows * ROW),
            transcendentals=rows * heads * rows,
        ),
        compiler_params=params,
        name="own",
    )(*[pltpu.with_memory_space_constraint(x, pltpu.HBM) for x in inputs])
    sent_rows = lax.ppermute(sent_rows, "cp", [(c, (c + n_cp - 1) % n_cp) for c in range(n_cp)])
    kept_rows = pl.pallas_call(
        keep_kernel,
        in_specs=[vmem] * 2,
        out_specs=vmem,
        out_shape=jax.ShapeDtypeStruct((kept, ROW), jnp.float32),
        cost_estimate=pl.CostEstimate(flops=2**27, bytes_accessed=2**20, transcendentals=0),
        compiler_params=params,
        name="keep",
    )(picked, own_copy)
    blocks, kept_rows = lax.optimization_barrier((blocks, kept_rows))
    pieces = swap(blocks, dec_count)
    found, fetched_latents = pl.pallas_call(
        arrived_kernel,
        in_specs=[vmem] * (2 + len(blocks)),
        out_specs=[vmem] * 2,
        out_shape=[
            jax.ShapeDtypeStruct((kept, ROW), jnp.float32),
            jax.ShapeDtypeStruct((len(blocks) * rows, LAT), jnp.bfloat16),
        ],
        cost_estimate=pl.CostEstimate(flops=2**20, bytes_accessed=2**10, transcendentals=0),
        compiler_params=params,
        name="arrived",
    )(picked, kept_rows, *blocks)

    operands = (combined, result, peaks, totals, value_copy, bias, picked, found, sent_rows, filled, fetched_latents, *pieces)
    attended, page_cache, page_scales = pl.pallas_call(
        functools.partial(earlier_kernel, n_cp, count, group),
        in_specs=[vmem] * len(operands),
        out_specs=[hbm] * 3,
        out_shape=[
            jax.ShapeDtypeStruct((rows, heads * VDIM), jnp.bfloat16),
            jax.ShapeDtypeStruct((slot_count, PAGE, ROW), jnp.bfloat16),
            jax.ShapeDtypeStruct((slot_count, NBLK, PAGE), jnp.bfloat16),
        ],
        scratch_shapes=[
            pltpu.VMEM((ROW, count * rows), jnp.bfloat16),
            pltpu.VMEM((count * rows, LAT), jnp.bfloat16),
            pltpu.VMEM((rows, heads * VDIM), jnp.bfloat16),
            pltpu.VMEM((slot_count, PAGE, ROW), jnp.bfloat16),
            pltpu.VMEM((slot_count, NBLK, PAGE), jnp.bfloat16),
            pltpu.SemaphoreType.DMA((heads // group + 2,)),
        ],
        cost_estimate=pl.CostEstimate(
            flops=2 * rows * heads * (count * rows * (ROW + LAT) + LAT * VDIM),
            bytes_accessed=2 * (heads * rows * (ROW + VDIM) + value_expand.size),
            transcendentals=rows * heads * count * rows,
        ),
        compiler_params=params,
        name="earlier",
    )(*operands)
    page_cache = page_cache.reshape(1, 1, slot_count, PAGE, ROW)
    page_scales = page_scales.transpose(0, 2, 1).reshape(1, 1, slot_count, PAGE, NBLK)
    return attended, page_cache, page_scales


def solution(mesh):
    return jax.shard_map(
        on_device,
        mesh=mesh,
        in_specs=(
            P(("grp", "cp"), "dec"),
            P(("grp", "cp"), None),
            P("dec", None, None),
            P("dec", None, None),
            P("grp"),
            P("grp", None),
            P("grp"),
        ),
        out_specs=(
            P(("grp", "cp"), "dec"),
            P(("grp", "cp"), "dec", None, None, None),
            P(("grp", "cp"), "dec", None, None, None),
        ),
        check_vma=False,
    )
```

```python
import functools
import math

import jax
import jax.numpy as jnp
from jax import lax
from jax.experimental import pallas as pl
from jax.experimental.pallas import tpu as pltpu
from jax.sharding import PartitionSpec as P

LAT = 512
ROPE = 64
NOPE = 128
VDIM = 128
PAGE = 16
BLOCK = 128
NBLK = LAT // BLOCK
ROW = LAT + ROPE
HEAD = NOPE + ROPE
LANES = 128

masked_fill = -1e30
amax_epsilon = 1e-06
exp2_scale = math.log2(math.e) / math.sqrt(HEAD)

NT = (((1,), (1,)), ((), ()))


def prompt_starts(prompt_pages):
    starts = [jnp.int32(0)]
    for k in range(prompt_pages.shape[0] - 1):
        starts.append(starts[-1] + prompt_pages[k])
    return starts


def visible_bias(prompt_pages, rows, steps_back):
    first = lax.axis_index("cp") * rows
    token = first + lax.broadcasted_iota(jnp.int32, (rows, 1), 0)
    begin = jnp.zeros((rows, 1), jnp.int32)
    for start in prompt_starts(prompt_pages):
        begin = jnp.maximum(begin, jnp.where(start * PAGE <= token, start * PAGE, 0))
    spot = first - steps_back * rows + lax.broadcasted_iota(jnp.int32, (1, rows), 1)
    return jnp.where((spot >= begin) & (spot <= token), 0.0, masked_fill)


def piece_of(source, me):
    distance = jnp.abs(me - source)
    other = lax.rem(lax.rem(lax.axis_index("dec"), 2) + (source > me).astype(jnp.int32), 2)
    return jnp.where(distance == 0, 0, 2 * distance - 1 + other)


def slot_pages(owner, slot_count, prompt_pages, decode_owner, slot_offset):
    prompts, width = decode_owner.shape
    cycle = width * lax.axis_size("dec") * slot_count
    starts = prompt_starts(prompt_pages)
    pages, start, offset, place = jnp.int32(0), jnp.int32(0), jnp.int32(0), jnp.int32(0)
    for k in range(prompts):
        for p in range(width):
            mine = decode_owner[k, p] == owner
            pages = jnp.where(mine, prompt_pages[k], pages)
            start = jnp.where(mine, starts[k], start)
            offset = jnp.where(mine, slot_offset[k], offset)
            place = jnp.where(mine, p, place)
    result = []
    for c in range(slot_count):
        turn = width * (lax.axis_index("dec") * slot_count + c) + place
        page = lax.rem(turn - offset + 2 * cycle, cycle)
        result.append((page < pages, start + page))
    return result


def row_picker(targets, columns):
    kept = len(targets) * PAGE
    row = lax.broadcasted_iota(jnp.int32, (kept, 1), 0)
    target = jnp.full((kept, 1), -1, jnp.int32)
    for c, column in enumerate(targets):
        target = jnp.where(row // PAGE == c, column + row % PAGE, target)
    column = lax.broadcasted_iota(jnp.int32, (1, columns), 1)
    return jnp.where(column == target, 1.0, 0.0).astype(jnp.bfloat16)


def head_values(latents, value_expand, h):
    both = jnp.concatenate([value_expand[h], value_expand[h + 1]], axis=1)
    return jnp.dot(latents, both, preferred_element_type=jnp.float32).astype(jnp.bfloat16)


def own_steps(heads, group, before, queries, key_absorb, value_expand, own, latents, own_bias, outputs):
    combined, result, peaks, totals = outputs
    rows = own.shape[1]
    steps = heads // group

    def absorb(g):
        for h in range(g * group, (g + 1) * group):
            at = h * HEAD
            absorbed = jnp.dot(queries[:, at:at + NOPE], key_absorb[h], preferred_element_type=jnp.float32)
            combined[h * rows:(h + 1) * rows, :LAT] = absorbed.astype(jnp.bfloat16)
            combined[h * rows:(h + 1) * rows, LAT:] = queries[:, at + NOPE:at + HEAD]

    def score(g):
        return jnp.dot(combined[g * group * rows:(g + 1) * group * rows, :], own[...], preferred_element_type=jnp.float32)

    def value(g):
        return [head_values(latents[...], value_expand, g * group + i) for i in range(0, group, 2)]

    def finish(g, scores, both):
        span = slice(g * group * rows, (g + 1) * group * rows)
        scores = (scores.reshape(group, rows, rows) + own_bias[...][None]).reshape(group * rows, rows)
        peak = jnp.max(scores, axis=1, keepdims=True)
        weights = jnp.exp2((scores - peak) * exp2_scale)
        total = jnp.sum(weights, axis=1, keepdims=True)
        weights = weights.astype(jnp.bfloat16)
        for i in range(group):
            mine = both[i // 2][:, i % 2 * VDIM:(i % 2 + 1) * VDIM]
            out = jnp.dot(weights[i * rows:(i + 1) * rows], mine, preferred_element_type=jnp.float32)
            result[(g * group + i) * rows:(g * group + i + 1) * rows, :] = out
        peaks[span, :] = jnp.broadcast_to(peak, (group * rows, LANES))
        totals[span, :] = jnp.broadcast_to(total, (group * rows, LANES))

    scores, both = {}, {}
    for step in range(steps + 2):
        before(step)
        if step < steps:
            absorb(step)
        if 0 <= step - 1 < steps:
            scores[step - 1] = score(step - 1)
            both[step - 1] = value(step - 1)
        if 0 <= step - 2:
            finish(step - 2, scores.pop(step - 2), both.pop(step - 2))


def own_first_kernel(heads, group, *refs):
    pages_hbm, own_hbm, queries_hbm, absorb_hbm, expand_hbm = refs[:5]
    outputs, (own, latents, own_bias, late_queries, late_absorb, value_expand) = refs[5:9], refs[9:15]
    prompt_pages, queries, key_absorb, sems = refs[15:]
    rows = own.shape[1]
    total = value_expand.shape[0]
    some, wide = pl.ds(0, heads), pl.ds(0, heads * HEAD)
    rest, wide_rest = pl.ds(heads, total - heads), pl.ds(heads * HEAD, (total - heads) * HEAD)
    copies = [
        pltpu.make_async_copy(source, target, sems.at[i])
        for i, (source, target) in enumerate((
            (own_hbm, own),
            (pages_hbm, prompt_pages),
            (queries_hbm.at[:, wide], queries),
            (absorb_hbm.at[some], key_absorb),
            (expand_hbm.at[some], value_expand.at[some]),
            (queries_hbm.at[:, wide_rest], late_queries),
            (absorb_hbm.at[rest], late_absorb),
            (expand_hbm.at[rest], value_expand.at[rest]),
        ))
    ]
    for copy in copies:
        copy.start()

    def before(step):
        if step == 0:
            copies[2].wait()
            copies[3].wait()
        if step == 1:
            copies[0].wait()
            latents[...] = own[:LAT, :].T
            copies[1].wait()
            own_bias[...] = visible_bias(prompt_pages, rows, 0)
            copies[4].wait()

    own_steps(heads, group, before, queries, key_absorb, value_expand, own, latents, own_bias, outputs)
    for copy in copies[5:]:
        copy.wait()


def own_second_kernel(n_cp, count, heads, group, slot_count, *refs):
    small_hbm, (own, latents, own_bias, queries, key_absorb, value_expand) = refs[:3], refs[3:9]
    outputs, (sent_rows, bias, picked, filled) = refs[9:13], refs[13:17]
    prompt_pages, decode_owner, slot_offset, sems = refs[17:]
    copies = [
        pltpu.make_async_copy(source, target, sems.at[i])
        for i, (source, target) in enumerate(zip(small_hbm, (prompt_pages, decode_owner, slot_offset)))
    ]
    for copy in copies:
        copy.start()

    def before(step):
        if step == 2:
            for copy in copies:
                copy.wait()
            index_work(n_cp, count, slot_count, prompt_pages, decode_owner, slot_offset, own[...], sent_rows, bias, picked, filled)

    mine = value_expand.at[pl.ds(value_expand.shape[0] - heads, heads)]
    own_steps(heads, group, before, queries, key_absorb, mine, own, latents, own_bias, outputs)


def index_work(n_cp, count, slot_count, prompt_pages, decode_owner, slot_offset, block, sent_rows, bias, picked, filled):
    rows = block.shape[1]
    me = lax.axis_index("cp")
    targets = []
    for valid, page in slot_pages(n_cp - 1 - me, slot_count, prompt_pages, decode_owner, slot_offset):
        here = valid & (page * PAGE // rows == me)
        targets.append(jnp.where(here, lax.rem(page * PAGE, rows), -PAGE))
    choice = row_picker(targets, rows)
    sent = lax.dot_general(choice, block, NT, preferred_element_type=jnp.float32)
    sent_rows[:, :ROW] = sent.astype(jnp.bfloat16)
    sent_rows[:, ROW:] = jnp.zeros((choice.shape[0], sent_rows.shape[1] - ROW), jnp.bfloat16)
    for b in range(count):
        bias[:, b * rows:(b + 1) * rows] = visible_bias(prompt_pages, rows, b + 1)
    targets = []
    lane = lax.broadcasted_iota(jnp.int32, filled.shape, 1)
    lane_filled = jnp.zeros(filled.shape, jnp.float32)
    for c, (valid, page) in enumerate(slot_pages(me, slot_count, prompt_pages, decode_owner, slot_offset)):
        source = page * PAGE // rows
        here = valid & (jnp.abs(me - source) < n_cp - 1)
        column = piece_of(source, me) * rows + lax.rem(page * PAGE, rows)
        targets.append(jnp.where(here, column, -PAGE))
        lane_filled = jnp.where(lane // PAGE == c, valid.astype(jnp.float32), lane_filled)
    filled[...] = lane_filled
    picked[...] = row_picker(targets, picked.shape[1])


def pick_rows(picked, index, block):
    rows = block.shape[1]
    return lax.dot_general(picked[:, index * rows:(index + 1) * rows], block, NT, preferred_element_type=jnp.float32)


def lower_block(mine, others):
    odd = lax.rem(lax.axis_index("dec"), 2) == 1
    return jnp.where(odd, others, mine)


def arrived_kernel(ready, picked, *refs):
    blocks, (found, keys, latents) = refs[:-3], refs[-3:]
    rows = blocks[0].shape[1]
    total = pick_rows(picked, 0, blocks[0][...])
    for i, block in enumerate(blocks[1:]):
        total = total + pick_rows(picked, i + 1, block[...])
    found[...] = total
    for b in range(ready):
        block = lower_block(blocks[2 * b + 1][...], blocks[2 * b + 2][...])
        keys[:, b * rows:(b + 1) * rows] = block
        latents[b * rows:(b + 1) * rows, :] = block[:LAT].T


def cache_kernel(last, picked, found, filled, sent_rows, block, page_cache, page_scales):
    rows = found[...] + sent_rows[:, :ROW].astype(jnp.float32) + pick_rows(picked, last, block[...])
    write_cache(rows, filled, page_cache, page_scales)


def write_cache(rows, filled, page_cache, page_scales):
    slot_count = page_cache.shape[0]
    scales = []
    for b in range(NBLK):
        values = rows[:, b * BLOCK:(b + 1) * BLOCK]
        scale = jnp.max(jnp.abs(values), axis=1, keepdims=True) + amax_epsilon
        scale = scale.astype(jnp.bfloat16).astype(jnp.float32)
        encoded = (values / scale).astype(jnp.bfloat16)
        for c in range(slot_count):
            page_cache[c, :, b * BLOCK:(b + 1) * BLOCK] = encoded[c * PAGE:(c + 1) * PAGE]
        scales.append(scale)
    kept = rows.shape[0]
    which = lax.broadcasted_iota(jnp.int32, (kept, LANES), 1)
    table = jnp.zeros((kept, LANES), jnp.float32)
    for b, scale in enumerate(scales):
        table = jnp.where(which == b, scale, table)
    table = (table.T[:NBLK] * filled[:1, :kept]).astype(jnp.bfloat16)
    for c in range(slot_count):
        page_cache[c, :, LAT:] = rows[c * PAGE:(c + 1) * PAGE, LAT:].astype(jnp.bfloat16)
        page_scales[c] = table[:, c * PAGE:(c + 1) * PAGE]


def earlier_kernel(count, ready, group, *refs):
    halves = (refs[:4], refs[4:8])
    value_expand, bias, ready_keys, ready_latents, fetched, swapped = refs[8:14]
    attended, keys, latents, result, sems = refs[14:]
    rows = attended.shape[0]
    heads = value_expand.shape[0]
    width = count * rows
    steps = heads // group
    keys[:, :ready * rows] = ready_keys[...]
    latents[:ready * rows, :] = ready_latents[...]
    if ready < count:
        block = lower_block(fetched[...], swapped[...])
        keys[:, ready * rows:] = block
        latents[ready * rows:, :] = block[:LAT].T

    def part_of(i, g):
        first = halves[0][i].shape[0]
        at = g * group * rows
        half = halves[0][i] if at < first else halves[1][i]
        at = at % first
        return half[at:at + group * rows, :]

    def score(g):
        scores = jnp.dot(part_of(0, g), keys[...], preferred_element_type=jnp.float32)
        return (scores.reshape(group, rows, width) + bias[...][None]).reshape(group * rows, width)

    def weigh(g, scores):
        old_peak = part_of(2, g)
        parts = [scores[:, b * rows:(b + 1) * rows] for b in range(count)]
        peak = jnp.maximum(old_peak, jnp.max(functools.reduce(jnp.maximum, parts), axis=1, keepdims=True))
        parts = [jnp.exp2((part - peak) * exp2_scale) for part in parts]
        total = jnp.sum(functools.reduce(jnp.add, parts), axis=1, keepdims=True)
        factor = jnp.exp2((old_peak - peak) * exp2_scale)
        inverse = 1.0 / (part_of(3, g) * factor + total)
        weights = jnp.concatenate([part.astype(jnp.bfloat16) for part in parts], axis=1)
        return weights, factor * inverse, inverse

    def mix(g, weights):
        return jnp.dot(weights, latents[...], preferred_element_type=jnp.float32).astype(jnp.bfloat16)

    def finish(g, mixed, factor, inverse):
        own_result = part_of(1, g)
        for i in range(group):
            part = slice(i * rows, (i + 1) * rows)
            h = g * group + i
            out = jnp.dot(mixed[part], value_expand[h], preferred_element_type=jnp.float32)
            out = own_result[part] * factor[part] + out * inverse[part]
            result[:, h * VDIM:(h + 1) * VDIM] = out.astype(jnp.bfloat16)
        send(g).start()

    def send(g):
        at = pl.ds(g * group * VDIM, group * VDIM)
        return pltpu.make_async_copy(result.at[:, at], attended.at[:, at], sems.at[g])

    scores, weights, mixed = {}, {}, {}
    for step in range(steps + 2):
        if step < steps:
            scores[step] = score(step)
        if 0 <= step - 2:
            finish(step - 2, mixed.pop(step - 2), *weights.pop(step - 2)[1:])
        if 0 <= step - 1 < steps:
            weights[step - 1] = weigh(step - 1, scores.pop(step - 1))
            mixed[step - 1] = mix(step - 1, weights[step - 1][0])
    for g in range(steps):
        send(g).wait()


def pass_on(block, n_cp, n_dec):
    pairs = []
    for c in range(n_cp):
        for e in range(n_dec):
            target = c - 1 if e % 2 else c + 1
            if 0 <= target < n_cp:
                pairs.append((c * n_dec + e, target * n_dec + e))
    return lax.ppermute(block, ("cp", "dec"), pairs)


def swap(block, n_dec):
    return lax.ppermute(block, "dec", [(e, e ^ 1) for e in range(n_dec)])


def on_device(queries, latent_rows, key_absorb, value_expand, prompt_pages, decode_owner, slot_offset):
    n_cp = lax.axis_size("cp")
    dec_count = lax.axis_size("dec")
    heads = key_absorb.shape[0]
    rows = latent_rows.shape[0]
    prompts, width = decode_owner.shape
    slot_count = 3 * (rows // PAGE) // (2 * dec_count)
    kept = slot_count * PAGE
    reach = width * dec_count * slot_count * PAGE
    count = min(n_cp - 2, -(-reach // rows) - (1 if prompts == 2 else 0))
    ready = min(count, n_cp - 3)
    own = latent_rows.T
    fetched = [pass_on(own, n_cp, dec_count)]

    vmem = pl.BlockSpec(memory_space=pltpu.VMEM)
    hbm = pl.BlockSpec(memory_space=pltpu.HBM)
    params = pltpu.CompilerParams(vmem_limit_bytes=32 * 2**20)
    group, first_heads = 2, heads // 2

    def in_hbm(*arrays):
        return [pltpu.with_memory_space_constraint(x, pltpu.HBM) for x in arrays]

    def own_cost(some):
        return pl.CostEstimate(
            flops=2 * rows * some * (2 * NOPE * LAT + rows * (ROW + VDIM)),
            bytes_accessed=2 * (queries.size + key_absorb.size + some * rows * ROW),
            transcendentals=rows * some * rows,
        )

    def own_shapes(some):
        return [
            jax.ShapeDtypeStruct((some * rows, ROW), jnp.bfloat16),
            jax.ShapeDtypeStruct((some * rows, VDIM), jnp.float32),
            jax.ShapeDtypeStruct((some * rows, LANES), jnp.float32),
            jax.ShapeDtypeStruct((some * rows, LANES), jnp.float32),
        ]

    late_heads = heads - first_heads
    *first, own_copy, latents, own_bias, late_queries, late_absorb, value_copy = pl.pallas_call(
        functools.partial(own_first_kernel, first_heads, group),
        in_specs=[hbm] * 5,
        out_specs=[vmem] * 10,
        out_shape=own_shapes(first_heads) + [
            jax.ShapeDtypeStruct(own.shape, jnp.bfloat16),
            jax.ShapeDtypeStruct((rows, LAT), jnp.bfloat16),
            jax.ShapeDtypeStruct((rows, rows), jnp.float32),
            jax.ShapeDtypeStruct((rows, late_heads * HEAD), jnp.bfloat16),
            jax.ShapeDtypeStruct((late_heads, NOPE, LAT), jnp.bfloat16),
            jax.ShapeDtypeStruct(value_expand.shape, jnp.bfloat16),
        ],
        scratch_shapes=[
            pltpu.SMEM(prompt_pages.shape, jnp.int32),
            pltpu.VMEM((rows, first_heads * HEAD), jnp.bfloat16),
            pltpu.VMEM((first_heads, NOPE, LAT), jnp.bfloat16),
            pltpu.SemaphoreType.DMA((8,)),
        ],
        cost_estimate=own_cost(first_heads),
        compiler_params=params,
        name="own_first",
    )(*in_hbm(prompt_pages, own, queries, key_absorb, value_expand))
    fetched[0], own_copy = lax.optimization_barrier((fetched[0], own_copy))

    pieces = 2 * (n_cp - 2) + 1
    late = (own_copy, latents, own_bias, late_queries, late_absorb, value_copy)
    *second, sent_rows, bias, picked, filled = pl.pallas_call(
        functools.partial(own_second_kernel, n_cp, count, late_heads, group, slot_count),
        in_specs=[hbm] * 3 + [vmem] * len(late),
        out_specs=[vmem] * 8,
        out_shape=own_shapes(late_heads) + [
            jax.ShapeDtypeStruct((kept, -(-ROW // LANES) * LANES), jnp.bfloat16),
            jax.ShapeDtypeStruct((rows, count * rows), jnp.float32),
            jax.ShapeDtypeStruct((kept, pieces * rows), jnp.bfloat16),
            jax.ShapeDtypeStruct((8, LANES), jnp.float32),
        ],
        scratch_shapes=[
            pltpu.SMEM(prompt_pages.shape, jnp.int32),
            pltpu.SMEM(decode_owner.shape, jnp.int32),
            pltpu.SMEM(slot_offset.shape, jnp.int32),
            pltpu.SemaphoreType.DMA((3,)),
        ],
        cost_estimate=own_cost(late_heads),
        compiler_params=params,
        name="own_second",
    )(*in_hbm(prompt_pages, decode_owner, slot_offset), *late)
    for _ in range(n_cp - 3):
        fetched.append(pass_on(fetched[-1], n_cp, dec_count))
    fetched[-1], bias = lax.optimization_barrier((fetched[-1], bias))
    swapped = [swap(block, dec_count) for block in fetched]
    sent_rows = lax.ppermute(sent_rows, "cp", [(0, n_cp - 1), (n_cp - 1, 0)])

    arrived = [own_copy] + [block for pair in zip(fetched, swapped) for block in pair][:-1]
    found, ready_keys, ready_latents = pl.pallas_call(
        functools.partial(arrived_kernel, ready),
        in_specs=[vmem] * (1 + len(arrived)),
        out_specs=[vmem] * 3,
        out_shape=[
            jax.ShapeDtypeStruct((kept, ROW), jnp.float32),
            jax.ShapeDtypeStruct((ROW, ready * rows), jnp.bfloat16),
            jax.ShapeDtypeStruct((ready * rows, LAT), jnp.bfloat16),
        ],
        cost_estimate=pl.CostEstimate(flops=2**20, bytes_accessed=2**10, transcendentals=0),
        compiler_params=params,
        name="arrived",
    )(picked, *arrived)

    operands = (*first, *second, value_copy, bias, ready_keys, ready_latents, fetched[-1], swapped[-1])
    attended = pl.pallas_call(
        functools.partial(earlier_kernel, count, ready, group),
        in_specs=[vmem] * len(operands),
        out_specs=hbm,
        out_shape=jax.ShapeDtypeStruct((rows, heads * VDIM), jnp.bfloat16),
        scratch_shapes=[
            pltpu.VMEM((ROW, count * rows), jnp.bfloat16),
            pltpu.VMEM((count * rows, LAT), jnp.bfloat16),
            pltpu.VMEM((rows, heads * VDIM), jnp.bfloat16),
            pltpu.SemaphoreType.DMA((heads // group,)),
        ],
        cost_estimate=pl.CostEstimate(
            flops=2 * rows * heads * (count * rows * (ROW + LAT) + LAT * VDIM),
            bytes_accessed=2 * (heads * rows * (ROW + VDIM) + value_expand.size),
            transcendentals=rows * heads * count * rows,
        ),
        compiler_params=params,
        name="earlier",
    )(*operands)
    sent_rows, attended = lax.optimization_barrier((sent_rows, attended))
    page_cache, page_scales = pl.pallas_call(
        functools.partial(cache_kernel, pieces - 1),
        in_specs=[vmem] * 5,
        out_specs=[vmem] * 2,
        out_shape=[
            jax.ShapeDtypeStruct((slot_count, PAGE, ROW), jnp.bfloat16),
            jax.ShapeDtypeStruct((slot_count, NBLK, PAGE), jnp.bfloat16),
        ],
        cost_estimate=pl.CostEstimate(flops=2**20, bytes_accessed=2**10, transcendentals=0),
        compiler_params=params,
        name="cache",
    )(picked, found, filled, sent_rows, swapped[-1])
    page_cache = page_cache.reshape(1, 1, slot_count, PAGE, ROW)
    page_scales = page_scales.transpose(0, 2, 1).reshape(1, 1, slot_count, PAGE, NBLK)
    return attended, page_cache, page_scales


def solution(mesh):
    return jax.shard_map(
        on_device,
        mesh=mesh,
        in_specs=(
            P(("grp", "cp"), "dec"),
            P(("grp", "cp"), None),
            P("dec", None, None),
            P("dec", None, None),
            P("grp"),
            P("grp", None),
            P("grp"),
        ),
        out_specs=(
            P(("grp", "cp"), "dec"),
            P(("grp", "cp"), "dec", None, None, None),
            P(("grp", "cp"), "dec", None, None, None),
        ),
        check_vma=False,
    )
```

```python
import functools
import math

import jax
import jax.numpy as jnp
from jax import lax
from jax.experimental import pallas as pl
from jax.experimental.pallas import tpu as pltpu
from jax.sharding import PartitionSpec as P

LAT = 512
ROPE = 64
NOPE = 128
VDIM = 128
PAGE = 16
BLOCK = 128
NBLK = LAT // BLOCK
ROW = LAT + ROPE
HEAD = NOPE + ROPE
LANES = 128

masked_fill = -1e30
amax_epsilon = 1e-06
exp2_scale = math.log2(math.e) / math.sqrt(HEAD)

NT = (((1,), (1,)), ((), ()))


def prompt_starts(prompt_pages):
    starts = [jnp.int32(0)]
    for k in range(prompt_pages.shape[0] - 1):
        starts.append(starts[-1] + prompt_pages[k])
    return starts


def visible_bias(prompt_pages, rows, steps_back):
    first = lax.axis_index("cp") * rows
    token = first + lax.broadcasted_iota(jnp.int32, (rows, 1), 0)
    begin = jnp.zeros((rows, 1), jnp.int32)
    for start in prompt_starts(prompt_pages):
        begin = jnp.maximum(begin, jnp.where(start * PAGE <= token, start * PAGE, 0))
    spot = first - steps_back * rows + lax.broadcasted_iota(jnp.int32, (1, rows), 1)
    return jnp.where((spot >= begin) & (spot <= token), 0.0, masked_fill)


def piece_of(source, me):
    distance = jnp.abs(me - source)
    other = lax.rem(lax.rem(lax.axis_index("dec"), 2) + (source > me).astype(jnp.int32), 2)
    return jnp.where(distance == 0, 0, 2 * distance - 1 + other)


def slot_pages(owner, slot_count, prompt_pages, decode_owner, slot_offset):
    prompts, width = decode_owner.shape
    cycle = width * lax.axis_size("dec") * slot_count
    starts = prompt_starts(prompt_pages)
    pages, start, offset, place = jnp.int32(0), jnp.int32(0), jnp.int32(0), jnp.int32(0)
    for k in range(prompts):
        for p in range(width):
            mine = decode_owner[k, p] == owner
            pages = jnp.where(mine, prompt_pages[k], pages)
            start = jnp.where(mine, starts[k], start)
            offset = jnp.where(mine, slot_offset[k], offset)
            place = jnp.where(mine, p, place)
    result = []
    for c in range(slot_count):
        turn = width * (lax.axis_index("dec") * slot_count + c) + place
        page = lax.rem(turn - offset + 2 * cycle, cycle)
        result.append((page < pages, start + page))
    return result


def row_picker(targets, columns):
    kept = len(targets) * PAGE
    row = lax.broadcasted_iota(jnp.int32, (kept, 1), 0)
    target = jnp.full((kept, 1), -1, jnp.int32)
    for c, column in enumerate(targets):
        target = jnp.where(row // PAGE == c, column + row % PAGE, target)
    column = lax.broadcasted_iota(jnp.int32, (1, columns), 1)
    return jnp.where(column == target, 1.0, 0.0).astype(jnp.bfloat16)


def head_values(latents, value_expand, h):
    both = jnp.concatenate([value_expand[h], value_expand[h + 1]], axis=1)
    return jnp.dot(latents, both, preferred_element_type=jnp.float32).astype(jnp.bfloat16)


def own_steps(heads, group, before, queries, key_absorb, value_expand, own, latents, own_bias, outputs):
    combined, result, peaks, totals = outputs
    rows = own.shape[1]
    steps = heads // group

    def absorb(g):
        for h in range(g * group, (g + 1) * group):
            at = h * HEAD
            absorbed = jnp.dot(queries[:, at:at + NOPE], key_absorb[h], preferred_element_type=jnp.float32)
            combined[h * rows:(h + 1) * rows, :LAT] = absorbed.astype(jnp.bfloat16)
            combined[h * rows:(h + 1) * rows, LAT:] = queries[:, at + NOPE:at + HEAD]

    def score(g):
        return jnp.dot(combined[g * group * rows:(g + 1) * group * rows, :], own[...], preferred_element_type=jnp.float32)

    def value(g):
        return [head_values(latents[...], value_expand, g * group + i) for i in range(0, group, 2)]

    def finish(g, scores, both):
        span = slice(g * group * rows, (g + 1) * group * rows)
        scores = (scores.reshape(group, rows, rows) + own_bias[...][None]).reshape(group * rows, rows)
        peak = jnp.max(scores, axis=1, keepdims=True)
        weights = jnp.exp2((scores - peak) * exp2_scale)
        total = jnp.sum(weights, axis=1, keepdims=True)
        weights = weights.astype(jnp.bfloat16)
        for i in range(group):
            mine = both[i // 2][:, i % 2 * VDIM:(i % 2 + 1) * VDIM]
            out = jnp.dot(weights[i * rows:(i + 1) * rows], mine, preferred_element_type=jnp.float32)
            result[(g * group + i) * rows:(g * group + i + 1) * rows, :] = out
        peaks[span, :] = jnp.broadcast_to(peak, (group * rows, LANES))
        totals[span, :] = jnp.broadcast_to(total, (group * rows, LANES))

    scores, both = {}, {}
    for step in range(steps + 2):
        before(step)
        if step < steps:
            absorb(step)
        if 0 <= step - 1 < steps:
            scores[step - 1] = score(step - 1)
            both[step - 1] = value(step - 1)
        if 0 <= step - 2:
            finish(step - 2, scores.pop(step - 2), both.pop(step - 2))


def own_first_kernel(heads, group, *refs):
    pages_hbm, own_hbm, queries_hbm, absorb_hbm, expand_hbm = refs[:5]
    outputs, (own, latents, own_bias, late_queries, late_absorb, value_expand) = refs[5:9], refs[9:15]
    prompt_pages, queries, key_absorb, sems = refs[15:]
    rows = own.shape[1]
    total = value_expand.shape[0]
    some, wide = pl.ds(0, heads), pl.ds(0, heads * HEAD)
    rest, wide_rest = pl.ds(heads, total - heads), pl.ds(heads * HEAD, (total - heads) * HEAD)
    copies = [
        pltpu.make_async_copy(source, target, sems.at[i])
        for i, (source, target) in enumerate((
            (own_hbm, own),
            (pages_hbm, prompt_pages),
            (queries_hbm.at[:, wide], queries),
            (absorb_hbm.at[some], key_absorb),
            (expand_hbm.at[some], value_expand.at[some]),
            (queries_hbm.at[:, wide_rest], late_queries),
            (absorb_hbm.at[rest], late_absorb),
            (expand_hbm.at[rest], value_expand.at[rest]),
        ))
    ]
    for copy in copies:
        copy.start()

    def before(step):
        if step == 0:
            copies[2].wait()
            copies[3].wait()
        if step == 1:
            copies[0].wait()
            latents[...] = own[:LAT, :].T
            copies[1].wait()
            own_bias[...] = visible_bias(prompt_pages, rows, 0)
            copies[4].wait()

    own_steps(heads, group, before, queries, key_absorb, value_expand, own, latents, own_bias, outputs)
    for copy in copies[5:]:
        copy.wait()


def own_second_kernel(n_cp, count, heads, group, slot_count, *refs):
    small_hbm, (own, latents, own_bias, queries, key_absorb, value_expand) = refs[:3], refs[3:9]
    outputs, (sent_rows, bias, picked, filled) = refs[9:13], refs[13:17]
    prompt_pages, decode_owner, slot_offset, sems = refs[17:]
    copies = [
        pltpu.make_async_copy(source, target, sems.at[i])
        for i, (source, target) in enumerate(zip(small_hbm, (prompt_pages, decode_owner, slot_offset)))
    ]
    for copy in copies:
        copy.start()

    def before(step):
        if step == 2:
            for copy in copies:
                copy.wait()
            index_work(n_cp, count, slot_count, prompt_pages, decode_owner, slot_offset, own[...], sent_rows, bias, picked, filled)

    mine = value_expand.at[pl.ds(value_expand.shape[0] - heads, heads)]
    own_steps(heads, group, before, queries, key_absorb, mine, own, latents, own_bias, outputs)


def index_work(n_cp, count, slot_count, prompt_pages, decode_owner, slot_offset, block, sent_rows, bias, picked, filled):
    rows = block.shape[1]
    me = lax.axis_index("cp")
    targets = []
    at_end = (me == 0) | (me == n_cp - 1)
    for valid, page in slot_pages(n_cp - 1 - me, slot_count, prompt_pages, decode_owner, slot_offset):
        here = valid & at_end & (page * PAGE // rows == me)
        targets.append(jnp.where(here, lax.rem(page * PAGE, rows), -PAGE))
    choice = row_picker(targets, rows)
    sent = lax.dot_general(choice, block, NT, preferred_element_type=jnp.float32)
    sent_rows[:, :ROW] = sent.astype(jnp.bfloat16)
    sent_rows[:, ROW:] = jnp.zeros((choice.shape[0], sent_rows.shape[1] - ROW), jnp.bfloat16)
    for b in range(count):
        bias[:, b * rows:(b + 1) * rows] = visible_bias(prompt_pages, rows, b + 1)
    targets = []
    lane = lax.broadcasted_iota(jnp.int32, filled.shape, 1)
    lane_filled = jnp.zeros(filled.shape, jnp.float32)
    for c, (valid, page) in enumerate(slot_pages(me, slot_count, prompt_pages, decode_owner, slot_offset)):
        source = page * PAGE // rows
        here = valid & (jnp.abs(me - source) < n_cp - 1)
        column = piece_of(source, me) * rows + lax.rem(page * PAGE, rows)
        targets.append(jnp.where(here, column, -PAGE))
        lane_filled = jnp.where(lane // PAGE == c, valid.astype(jnp.float32), lane_filled)
    filled[...] = lane_filled
    picked[...] = row_picker(targets, picked.shape[1])


def pick_rows(picked, index, block):
    rows = block.shape[1]
    return lax.dot_general(picked[:, index * rows:(index + 1) * rows], block, NT, preferred_element_type=jnp.float32)


def lower_block(mine, others):
    odd = lax.rem(lax.axis_index("dec"), 2) == 1
    return jnp.where(odd, others, mine)


def arrived_kernel(ready, picked, *refs):
    blocks, (found, keys, latents) = refs[:-3], refs[-3:]
    rows = blocks[0].shape[1]
    total = pick_rows(picked, 0, blocks[0][...])
    for i, block in enumerate(blocks[1:]):
        total = total + pick_rows(picked, i + 1, block[...])
    found[...] = total
    for b in range(ready):
        block = lower_block(blocks[2 * b + 1][...], blocks[2 * b + 2][...])
        keys[:, b * rows:(b + 1) * rows] = block
        latents[b * rows:(b + 1) * rows, :] = block[:LAT].T


def cache_kernel(last, picked, found, filled, sent_rows, block, page_cache, page_scales):
    rows = found[...] + sent_rows[:, :ROW].astype(jnp.float32) + pick_rows(picked, last, block[...])
    write_cache(rows, filled, page_cache, page_scales)


def write_cache(rows, filled, page_cache, page_scales):
    slot_count = page_cache.shape[0]
    scales = []
    for b in range(NBLK):
        values = rows[:, b * BLOCK:(b + 1) * BLOCK]
        scale = jnp.max(jnp.abs(values), axis=1, keepdims=True) + amax_epsilon
        scale = scale.astype(jnp.bfloat16).astype(jnp.float32)
        encoded = (values / scale).astype(jnp.bfloat16)
        for c in range(slot_count):
            page_cache[c, :, b * BLOCK:(b + 1) * BLOCK] = encoded[c * PAGE:(c + 1) * PAGE]
        scales.append(scale)
    kept = rows.shape[0]
    which = lax.broadcasted_iota(jnp.int32, (kept, LANES), 1)
    table = jnp.zeros((kept, LANES), jnp.float32)
    for b, scale in enumerate(scales):
        table = jnp.where(which == b, scale, table)
    table = (table.T[:NBLK] * filled[:1, :kept]).astype(jnp.bfloat16)
    for c in range(slot_count):
        page_cache[c, :, LAT:] = rows[c * PAGE:(c + 1) * PAGE, LAT:].astype(jnp.bfloat16)
        page_scales[c] = table[:, c * PAGE:(c + 1) * PAGE]


def earlier_kernel(count, ready, group, *refs):
    halves = (refs[:4], refs[4:8])
    value_expand, bias, ready_keys, ready_latents, fetched, swapped = refs[8:14]
    attended, keys, latents, result, sems = refs[14:]
    rows = attended.shape[0]
    heads = value_expand.shape[0]
    width = count * rows
    steps = heads // group
    keys[:, :ready * rows] = ready_keys[...]
    latents[:ready * rows, :] = ready_latents[...]
    if ready < count:
        block = lower_block(fetched[...], swapped[...])
        keys[:, ready * rows:] = block
        latents[ready * rows:, :] = block[:LAT].T

    def part_of(i, g):
        first = halves[0][i].shape[0]
        at = g * group * rows
        half = halves[0][i] if at < first else halves[1][i]
        at = at % first
        return half[at:at + group * rows, :]

    def score(g):
        scores = jnp.dot(part_of(0, g), keys[...], preferred_element_type=jnp.float32)
        return (scores.reshape(group, rows, width) + bias[...][None]).reshape(group * rows, width)

    def weigh(g, scores):
        old_peak = part_of(2, g)
        parts = [scores[:, b * rows:(b + 1) * rows] for b in range(count)]
        peak = jnp.maximum(old_peak, jnp.max(functools.reduce(jnp.maximum, parts), axis=1, keepdims=True))
        parts = [jnp.exp2((part - peak) * exp2_scale) for part in parts]
        total = jnp.sum(functools.reduce(jnp.add, parts), axis=1, keepdims=True)
        factor = jnp.exp2((old_peak - peak) * exp2_scale)
        inverse = 1.0 / (part_of(3, g) * factor + total)
        weights = jnp.concatenate([part.astype(jnp.bfloat16) for part in parts], axis=1)
        return weights, factor * inverse, inverse

    def mix(g, weights):
        return jnp.dot(weights, latents[...], preferred_element_type=jnp.float32).astype(jnp.bfloat16)

    def finish(g, mixed, factor, inverse):
        own_result = part_of(1, g)
        for i in range(group):
            part = slice(i * rows, (i + 1) * rows)
            h = g * group + i
            out = jnp.dot(mixed[part], value_expand[h], preferred_element_type=jnp.float32)
            out = own_result[part] * factor[part] + out * inverse[part]
            result[:, h * VDIM:(h + 1) * VDIM] = out.astype(jnp.bfloat16)
        send(g).start()

    def send(g):
        at = pl.ds(g * group * VDIM, group * VDIM)
        return pltpu.make_async_copy(result.at[:, at], attended.at[:, at], sems.at[g])

    scores, weights, mixed = {}, {}, {}
    for step in range(steps + 2):
        if step < steps:
            scores[step] = score(step)
        if 0 <= step - 2:
            finish(step - 2, mixed.pop(step - 2), *weights.pop(step - 2)[1:])
        if 0 <= step - 1 < steps:
            weights[step - 1] = weigh(step - 1, scores.pop(step - 1))
            mixed[step - 1] = mix(step - 1, weights[step - 1][0])
    for g in range(steps):
        send(g).wait()


def pass_on(block, n_cp, n_dec):
    pairs = []
    for c in range(n_cp):
        for e in range(n_dec):
            target = c - 1 if e % 2 else c + 1
            at = (target, e) if 0 <= target < n_cp else (c, e ^ 1)
            pairs.append((c * n_dec + e, at[0] * n_dec + at[1]))
    return lax.ppermute(block, ("cp", "dec"), pairs)


def end_to_end(block, n_cp, n_dec):
    pairs = []
    for c in range(n_cp):
        for e in range(n_dec):
            at = (n_cp - 1 - c, e) if c in (0, n_cp - 1) else (c, e ^ 1)
            pairs.append((c * n_dec + e, at[0] * n_dec + at[1]))
    return lax.ppermute(block, ("cp", "dec"), pairs)


def swap(block, n_dec):
    return lax.ppermute(block, "dec", [(e, e ^ 1) for e in range(n_dec)])


def on_device(queries, latent_rows, key_absorb, value_expand, prompt_pages, decode_owner, slot_offset):
    n_cp = lax.axis_size("cp")
    dec_count = lax.axis_size("dec")
    heads = key_absorb.shape[0]
    rows = latent_rows.shape[0]
    prompts, width = decode_owner.shape
    slot_count = 3 * (rows // PAGE) // (2 * dec_count)
    kept = slot_count * PAGE
    reach = width * dec_count * slot_count * PAGE
    count = min(n_cp - 2, -(-reach // rows) - (1 if prompts == 2 else 0))
    ready = min(count, n_cp - 3)
    own = latent_rows.T
    fetched = [pass_on(own, n_cp, dec_count)]

    vmem = pl.BlockSpec(memory_space=pltpu.VMEM)
    hbm = pl.BlockSpec(memory_space=pltpu.HBM)
    params = pltpu.CompilerParams(vmem_limit_bytes=32 * 2**20)
    group, first_heads = 2, heads // 2

    def in_hbm(*arrays):
        return [pltpu.with_memory_space_constraint(x, pltpu.HBM) for x in arrays]

    def own_cost(some):
        return pl.CostEstimate(
            flops=2 * rows * some * (2 * NOPE * LAT + rows * (ROW + VDIM)),
            bytes_accessed=2 * (queries.size + key_absorb.size + some * rows * ROW),
            transcendentals=rows * some * rows,
        )

    def own_shapes(some):
        return [
            jax.ShapeDtypeStruct((some * rows, ROW), jnp.bfloat16),
            jax.ShapeDtypeStruct((some * rows, VDIM), jnp.float32),
            jax.ShapeDtypeStruct((some * rows, LANES), jnp.float32),
            jax.ShapeDtypeStruct((some * rows, LANES), jnp.float32),
        ]

    late_heads = heads - first_heads
    *first, own_copy, latents, own_bias, late_queries, late_absorb, value_copy = pl.pallas_call(
        functools.partial(own_first_kernel, first_heads, group),
        in_specs=[hbm] * 5,
        out_specs=[vmem] * 10,
        out_shape=own_shapes(first_heads) + [
            jax.ShapeDtypeStruct(own.shape, jnp.bfloat16),
            jax.ShapeDtypeStruct((rows, LAT), jnp.bfloat16),
            jax.ShapeDtypeStruct((rows, rows), jnp.float32),
            jax.ShapeDtypeStruct((rows, late_heads * HEAD), jnp.bfloat16),
            jax.ShapeDtypeStruct((late_heads, NOPE, LAT), jnp.bfloat16),
            jax.ShapeDtypeStruct(value_expand.shape, jnp.bfloat16),
        ],
        scratch_shapes=[
            pltpu.SMEM(prompt_pages.shape, jnp.int32),
            pltpu.VMEM((rows, first_heads * HEAD), jnp.bfloat16),
            pltpu.VMEM((first_heads, NOPE, LAT), jnp.bfloat16),
            pltpu.SemaphoreType.DMA((8,)),
        ],
        cost_estimate=own_cost(first_heads),
        compiler_params=params,
        name="own_first",
    )(*in_hbm(prompt_pages, own, queries, key_absorb, value_expand))
    fetched[0], own_copy = lax.optimization_barrier((fetched[0], own_copy))

    pieces = 2 * (n_cp - 2) + 1
    late = (own_copy, latents, own_bias, late_queries, late_absorb, value_copy)
    *second, sent_rows, bias, picked, filled = pl.pallas_call(
        functools.partial(own_second_kernel, n_cp, count, late_heads, group, slot_count),
        in_specs=[hbm] * 3 + [vmem] * len(late),
        out_specs=[vmem] * 8,
        out_shape=own_shapes(late_heads) + [
            jax.ShapeDtypeStruct((kept, -(-ROW // LANES) * LANES), jnp.bfloat16),
            jax.ShapeDtypeStruct((rows, count * rows), jnp.float32),
            jax.ShapeDtypeStruct((kept, pieces * rows), jnp.bfloat16),
            jax.ShapeDtypeStruct((8, LANES), jnp.float32),
        ],
        scratch_shapes=[
            pltpu.SMEM(prompt_pages.shape, jnp.int32),
            pltpu.SMEM(decode_owner.shape, jnp.int32),
            pltpu.SMEM(slot_offset.shape, jnp.int32),
            pltpu.SemaphoreType.DMA((3,)),
        ],
        cost_estimate=own_cost(late_heads),
        compiler_params=params,
        name="own_second",
    )(*in_hbm(prompt_pages, decode_owner, slot_offset), *late)
    for _ in range(n_cp - 3):
        fetched.append(pass_on(fetched[-1], n_cp, dec_count))
    fetched[-1], bias = lax.optimization_barrier((fetched[-1], bias))
    swapped = [swap(block, dec_count) for block in fetched]
    sent_rows = end_to_end(sent_rows, n_cp, dec_count)

    arrived = [own_copy] + [block for pair in zip(fetched, swapped) for block in pair][:-1]
    found, ready_keys, ready_latents = pl.pallas_call(
        functools.partial(arrived_kernel, ready),
        in_specs=[vmem] * (1 + len(arrived)),
        out_specs=[vmem] * 3,
        out_shape=[
            jax.ShapeDtypeStruct((kept, ROW), jnp.float32),
            jax.ShapeDtypeStruct((ROW, ready * rows), jnp.bfloat16),
            jax.ShapeDtypeStruct((ready * rows, LAT), jnp.bfloat16),
        ],
        cost_estimate=pl.CostEstimate(flops=2**20, bytes_accessed=2**10, transcendentals=0),
        compiler_params=params,
        name="arrived",
    )(picked, *arrived)

    operands = (*first, *second, value_copy, bias, ready_keys, ready_latents, fetched[-1], swapped[-1])
    attended = pl.pallas_call(
        functools.partial(earlier_kernel, count, ready, group),
        in_specs=[vmem] * len(operands),
        out_specs=hbm,
        out_shape=jax.ShapeDtypeStruct((rows, heads * VDIM), jnp.bfloat16),
        scratch_shapes=[
            pltpu.VMEM((ROW, count * rows), jnp.bfloat16),
            pltpu.VMEM((count * rows, LAT), jnp.bfloat16),
            pltpu.VMEM((rows, heads * VDIM), jnp.bfloat16),
            pltpu.SemaphoreType.DMA((heads // group,)),
        ],
        cost_estimate=pl.CostEstimate(
            flops=2 * rows * heads * (count * rows * (ROW + LAT) + LAT * VDIM),
            bytes_accessed=2 * (heads * rows * (ROW + VDIM) + value_expand.size),
            transcendentals=rows * heads * count * rows,
        ),
        compiler_params=params,
        name="earlier",
    )(*operands)
    sent_rows, attended = lax.optimization_barrier((sent_rows, attended))
    page_cache, page_scales = pl.pallas_call(
        functools.partial(cache_kernel, pieces - 1),
        in_specs=[vmem] * 5,
        out_specs=[vmem] * 2,
        out_shape=[
            jax.ShapeDtypeStruct((slot_count, PAGE, ROW), jnp.bfloat16),
            jax.ShapeDtypeStruct((slot_count, NBLK, PAGE), jnp.bfloat16),
        ],
        cost_estimate=pl.CostEstimate(flops=2**20, bytes_accessed=2**10, transcendentals=0),
        compiler_params=params,
        name="cache",
    )(picked, found, filled, sent_rows, swapped[-1])
    page_cache = page_cache.reshape(1, 1, slot_count, PAGE, ROW)
    page_scales = page_scales.transpose(0, 2, 1).reshape(1, 1, slot_count, PAGE, NBLK)
    return attended, page_cache, page_scales


def solution(mesh):
    return jax.shard_map(
        on_device,
        mesh=mesh,
        in_specs=(
            P(("grp", "cp"), "dec"),
            P(("grp", "cp"), None),
            P("dec", None, None),
            P("dec", None, None),
            P("grp"),
            P("grp", None),
            P("grp"),
        ),
        out_specs=(
            P(("grp", "cp"), "dec"),
            P(("grp", "cp"), "dec", None, None, None),
            P(("grp", "cp"), "dec", None, None, None),
        ),
        check_vma=False,
    )
```

```python
import functools
import math

import jax
import jax.numpy as jnp
from jax import lax
from jax.experimental import pallas as pl
from jax.experimental.pallas import tpu as pltpu
from jax.sharding import PartitionSpec as P

LAT = 512
ROPE = 64
NOPE = 128
VDIM = 128
PAGE = 16
BLOCK = 128
NBLK = LAT // BLOCK
ROW = LAT + ROPE
HEAD = NOPE + ROPE
LANES = 128

masked_fill = -1e30
amax_epsilon = 1e-06
exp2_scale = math.log2(math.e) / math.sqrt(HEAD)

NT = (((1,), (1,)), ((), ()))


def prompt_starts(prompt_pages):
    starts = [jnp.int32(0)]
    for k in range(prompt_pages.shape[0] - 1):
        starts.append(starts[-1] + prompt_pages[k])
    return starts


def visible_bias(prompt_pages, rows, steps_back):
    first = lax.axis_index("cp") * rows
    token = first + lax.broadcasted_iota(jnp.int32, (rows, 1), 0)
    begin = jnp.zeros((rows, 1), jnp.int32)
    for start in prompt_starts(prompt_pages):
        begin = jnp.maximum(begin, jnp.where(start * PAGE <= token, start * PAGE, 0))
    spot = first - steps_back * rows + lax.broadcasted_iota(jnp.int32, (1, rows), 1)
    return jnp.where((spot >= begin) & (spot <= token), 0.0, masked_fill)


def slot_pages(owner, slot_count, prompt_pages, decode_owner, slot_offset):
    prompts, width = decode_owner.shape
    cycle = width * lax.axis_size("dec") * slot_count
    starts = prompt_starts(prompt_pages)
    pages, start, offset, place = jnp.int32(0), jnp.int32(0), jnp.int32(0), jnp.int32(0)
    for k in range(prompts):
        for p in range(width):
            mine = decode_owner[k, p] == owner
            pages = jnp.where(mine, prompt_pages[k], pages)
            start = jnp.where(mine, starts[k], start)
            offset = jnp.where(mine, slot_offset[k], offset)
            place = jnp.where(mine, p, place)
    result = []
    for c in range(slot_count):
        turn = width * (lax.axis_index("dec") * slot_count + c) + place
        page = lax.rem(turn - offset + 2 * cycle, cycle)
        result.append((page < pages, start + page))
    return result


def row_picker(targets, columns):
    kept = len(targets) * PAGE
    row = lax.broadcasted_iota(jnp.int32, (kept, 1), 0)
    target = jnp.full((kept, 1), -1, jnp.int32)
    for c, column in enumerate(targets):
        target = jnp.where(row // PAGE == c, column + row % PAGE, target)
    column = lax.broadcasted_iota(jnp.int32, (1, columns), 1)
    return jnp.where(column == target, 1.0, 0.0).astype(jnp.bfloat16)


def head_values(latents, value_expand, h):
    both = jnp.concatenate([value_expand[h], value_expand[h + 1]], axis=1)
    return jnp.dot(latents, both, preferred_element_type=jnp.float32).astype(jnp.bfloat16)


def own_steps(heads, group, before, queries, key_absorb, value_expand, own, latents, own_bias, outputs):
    combined, result, peaks, totals = outputs
    rows = own.shape[1]
    steps = heads // group

    def absorb(g):
        for h in range(g * group, (g + 1) * group):
            at = h * HEAD
            absorbed = jnp.dot(queries[:, at:at + NOPE], key_absorb[h], preferred_element_type=jnp.float32)
            combined[h * rows:(h + 1) * rows, :LAT] = absorbed.astype(jnp.bfloat16)
            combined[h * rows:(h + 1) * rows, LAT:] = queries[:, at + NOPE:at + HEAD]

    def score(g):
        return jnp.dot(combined[g * group * rows:(g + 1) * group * rows, :], own[...], preferred_element_type=jnp.float32)

    def value(g):
        return [head_values(latents[...], value_expand, g * group + i) for i in range(0, group, 2)]

    def finish(g, scores, both):
        span = slice(g * group * rows, (g + 1) * group * rows)
        scores = (scores.reshape(group, rows, rows) + own_bias[...][None]).reshape(group * rows, rows)
        peak = jnp.max(scores, axis=1, keepdims=True)
        weights = jnp.exp2((scores - peak) * exp2_scale)
        total = jnp.sum(weights, axis=1, keepdims=True)
        weights = weights.astype(jnp.bfloat16)
        for i in range(group):
            mine = both[i // 2][:, i % 2 * VDIM:(i % 2 + 1) * VDIM]
            out = jnp.dot(weights[i * rows:(i + 1) * rows], mine, preferred_element_type=jnp.float32)
            result[(g * group + i) * rows:(g * group + i + 1) * rows, :] = out
        peaks[span, :] = jnp.broadcast_to(peak, (group * rows, LANES))
        totals[span, :] = jnp.broadcast_to(total, (group * rows, LANES))

    scores, both = {}, {}
    for step in range(steps + 2):
        before(step)
        if step < steps:
            absorb(step)
        if 0 <= step - 1 < steps:
            scores[step - 1] = score(step - 1)
            both[step - 1] = value(step - 1)
        if 0 <= step - 2:
            finish(step - 2, scores.pop(step - 2), both.pop(step - 2))


def own_first_kernel(heads, group, *refs):
    pages_hbm, own_hbm, queries_hbm, absorb_hbm, expand_hbm = refs[:5]
    outputs, (own, latents, own_bias, late_queries, late_absorb, value_expand) = refs[5:9], refs[9:15]
    prompt_pages, queries, key_absorb, sems = refs[15:]
    rows = own.shape[1]
    total = value_expand.shape[0]
    some, wide = pl.ds(0, heads), pl.ds(0, heads * HEAD)
    rest, wide_rest = pl.ds(heads, total - heads), pl.ds(heads * HEAD, (total - heads) * HEAD)
    copies = [
        pltpu.make_async_copy(source, target, sems.at[i])
        for i, (source, target) in enumerate((
            (own_hbm, own),
            (pages_hbm, prompt_pages),
            (queries_hbm.at[:, wide], queries),
            (absorb_hbm.at[some], key_absorb),
            (expand_hbm.at[some], value_expand.at[some]),
            (queries_hbm.at[:, wide_rest], late_queries),
            (absorb_hbm.at[rest], late_absorb),
            (expand_hbm.at[rest], value_expand.at[rest]),
        ))
    ]
    for copy in copies:
        copy.start()

    def before(step):
        if step == 0:
            copies[2].wait()
            copies[3].wait()
        if step == 1:
            copies[0].wait()
            latents[...] = own[:LAT, :].T
            copies[1].wait()
            own_bias[...] = visible_bias(prompt_pages, rows, 0)
            copies[4].wait()

    own_steps(heads, group, before, queries, key_absorb, value_expand, own, latents, own_bias, outputs)
    for copy in copies[5:]:
        copy.wait()


def own_second_kernel(n_cp, count, heads, group, slot_count, *refs):
    small_hbm, (own, latents, own_bias, queries, key_absorb, value_expand) = refs[:3], refs[3:9]
    outputs, (sent_rows, bias, picked, filled) = refs[9:13], refs[13:17]
    prompt_pages, decode_owner, slot_offset, sems = refs[17:]
    copies = [
        pltpu.make_async_copy(source, target, sems.at[i])
        for i, (source, target) in enumerate(zip(small_hbm, (prompt_pages, decode_owner, slot_offset)))
    ]
    for copy in copies:
        copy.start()

    def before(step):
        if step == 2:
            for copy in copies:
                copy.wait()
            index_work(n_cp, count, slot_count, prompt_pages, decode_owner, slot_offset, own[...], sent_rows, bias, picked, filled)

    mine = value_expand.at[pl.ds(value_expand.shape[0] - heads, heads)]
    own_steps(heads, group, before, queries, key_absorb, mine, own, latents, own_bias, outputs)


def index_work(n_cp, count, slot_count, prompt_pages, decode_owner, slot_offset, block, sent_rows, bias, picked, filled):
    rows = block.shape[1]
    me = lax.axis_index("cp")
    targets = []
    behind = lax.rem(me + n_cp - 1, n_cp)
    for valid, page in slot_pages(behind, slot_count, prompt_pages, decode_owner, slot_offset):
        here = valid & (page * PAGE // rows == me)
        targets.append(jnp.where(here, lax.rem(page * PAGE, rows), -PAGE))
    choice = row_picker(targets, rows)
    sent = lax.dot_general(choice, block, NT, preferred_element_type=jnp.float32)
    sent_rows[:, :ROW] = sent.astype(jnp.bfloat16)
    sent_rows[:, ROW:] = jnp.zeros((choice.shape[0], sent_rows.shape[1] - ROW), jnp.bfloat16)
    for b in range(count):
        bias[:, b * rows:(b + 1) * rows] = visible_bias(prompt_pages, rows, b + 1)
    targets = []
    lane = lax.broadcasted_iota(jnp.int32, filled.shape, 1)
    lane_filled = jnp.zeros(filled.shape, jnp.float32)
    for c, (valid, page) in enumerate(slot_pages(me, slot_count, prompt_pages, decode_owner, slot_offset)):
        source = page * PAGE // rows
        column = lax.rem(me - source + n_cp, n_cp) * rows + lax.rem(page * PAGE, rows)
        targets.append(jnp.where(valid, column, -PAGE))
        lane_filled = jnp.where(lane // PAGE == c, valid.astype(jnp.float32), lane_filled)
    filled[...] = lane_filled
    picked[...] = row_picker(targets, picked.shape[1])


def pick_rows(picked, index, block):
    rows = block.shape[1]
    return lax.dot_general(picked[:, index * rows:(index + 1) * rows], block, NT, preferred_element_type=jnp.float32)


def whole_block(mine, others):
    odd = lax.rem(lax.axis_index("dec"), 2) == 1
    mine, others = mine[...], others[...]
    return jnp.concatenate([jnp.where(odd, others, mine), jnp.where(odd, mine, others)], axis=0)


def arrived_kernel(ready, picked, own, *refs):
    halves, (found, keys, latents) = refs[:-3], refs[-3:]
    rows = own.shape[1]
    total = pick_rows(picked, 0, own[...])
    for i in range(len(halves) // 2):
        block = whole_block(halves[2 * i], halves[2 * i + 1])
        total = total + pick_rows(picked, i + 1, block)
        if i < ready:
            keys[:, i * rows:(i + 1) * rows] = block
            latents[i * rows:(i + 1) * rows, :] = block[:LAT].T
    found[...] = total


def cache_kernel(last, picked, found, filled, sent_rows, fetched, swapped, page_cache, page_scales):
    rows = found[...] + sent_rows[:, :ROW].astype(jnp.float32) + pick_rows(picked, last, whole_block(fetched, swapped))
    write_cache(rows, filled, page_cache, page_scales)


def write_cache(rows, filled, page_cache, page_scales):
    slot_count = page_cache.shape[0]
    scales = []
    for b in range(NBLK):
        values = rows[:, b * BLOCK:(b + 1) * BLOCK]
        scale = jnp.max(jnp.abs(values), axis=1, keepdims=True) + amax_epsilon
        scale = scale.astype(jnp.bfloat16).astype(jnp.float32)
        encoded = (values / scale).astype(jnp.bfloat16)
        for c in range(slot_count):
            page_cache[c, :, b * BLOCK:(b + 1) * BLOCK] = encoded[c * PAGE:(c + 1) * PAGE]
        scales.append(scale)
    kept = rows.shape[0]
    which = lax.broadcasted_iota(jnp.int32, (kept, LANES), 1)
    table = jnp.zeros((kept, LANES), jnp.float32)
    for b, scale in enumerate(scales):
        table = jnp.where(which == b, scale, table)
    table = (table.T[:NBLK] * filled[:1, :kept]).astype(jnp.bfloat16)
    for c in range(slot_count):
        page_cache[c, :, LAT:] = rows[c * PAGE:(c + 1) * PAGE, LAT:].astype(jnp.bfloat16)
        page_scales[c] = table[:, c * PAGE:(c + 1) * PAGE]


def earlier_kernel(count, ready, group, *refs):
    halves = (refs[:4], refs[4:8])
    value_expand, bias, ready_keys, ready_latents, fetched, swapped = refs[8:14]
    attended, keys, latents, result, sems = refs[14:]
    rows = attended.shape[0]
    heads = value_expand.shape[0]
    width = count * rows
    steps = heads // group
    keys[:, :ready * rows] = ready_keys[...]
    latents[:ready * rows, :] = ready_latents[...]
    if ready < count:
        block = whole_block(fetched, swapped)
        keys[:, ready * rows:] = block
        latents[ready * rows:, :] = block[:LAT].T

    def part_of(i, g):
        first = halves[0][i].shape[0]
        at = g * group * rows
        half = halves[0][i] if at < first else halves[1][i]
        at = at % first
        return half[at:at + group * rows, :]

    def score(g):
        scores = jnp.dot(part_of(0, g), keys[...], preferred_element_type=jnp.float32)
        return (scores.reshape(group, rows, width) + bias[...][None]).reshape(group * rows, width)

    def weigh(g, scores):
        old_peak = part_of(2, g)
        parts = [scores[:, b * rows:(b + 1) * rows] for b in range(count)]
        peak = jnp.maximum(old_peak, jnp.max(functools.reduce(jnp.maximum, parts), axis=1, keepdims=True))
        parts = [jnp.exp2((part - peak) * exp2_scale) for part in parts]
        total = jnp.sum(functools.reduce(jnp.add, parts), axis=1, keepdims=True)
        factor = jnp.exp2((old_peak - peak) * exp2_scale)
        inverse = 1.0 / (part_of(3, g) * factor + total)
        weights = jnp.concatenate([part.astype(jnp.bfloat16) for part in parts], axis=1)
        return weights, factor * inverse, inverse

    def mix(g, weights):
        return jnp.dot(weights, latents[...], preferred_element_type=jnp.float32).astype(jnp.bfloat16)

    def finish(g, mixed, factor, inverse):
        own_result = part_of(1, g)
        for i in range(group):
            part = slice(i * rows, (i + 1) * rows)
            h = g * group + i
            out = jnp.dot(mixed[part], value_expand[h], preferred_element_type=jnp.float32)
            out = own_result[part] * factor[part] + out * inverse[part]
            result[:, h * VDIM:(h + 1) * VDIM] = out.astype(jnp.bfloat16)
        send(g).start()

    def send(g):
        at = pl.ds(g * group * VDIM, group * VDIM)
        return pltpu.make_async_copy(result.at[:, at], attended.at[:, at], sems.at[g])

    scores, weights, mixed = {}, {}, {}
    for step in range(steps + 2):
        if step < steps:
            scores[step] = score(step)
        if 0 <= step - 2:
            finish(step - 2, mixed.pop(step - 2), *weights.pop(step - 2)[1:])
        if 0 <= step - 1 < steps:
            weights[step - 1] = weigh(step - 1, scores.pop(step - 1))
            mixed[step - 1] = mix(step - 1, weights[step - 1][0])
    for g in range(steps):
        send(g).wait()


def shift(block, n_cp, steps):
    return lax.ppermute(block, "cp", [(c, (c + steps) % n_cp) for c in range(n_cp)])


def swap(block, n_dec):
    return lax.ppermute(block, "dec", [(e, e ^ 1) for e in range(n_dec)])


def on_device(queries, latent_rows, key_absorb, value_expand, prompt_pages, decode_owner, slot_offset):
    n_cp = lax.axis_size("cp")
    dec_count = lax.axis_size("dec")
    heads = key_absorb.shape[0]
    rows = latent_rows.shape[0]
    prompts, width = decode_owner.shape
    slot_count = 3 * (rows // PAGE) // (2 * dec_count)
    kept = slot_count * PAGE
    reach = width * dec_count * slot_count * PAGE
    count = min(n_cp - 2, -(-reach // rows) - (1 if prompts == 2 else 0))
    ready = min(count, n_cp - 3)
    own = latent_rows.T
    half = ROW // 2
    mine = lax.dynamic_slice_in_dim(own, lax.rem(lax.axis_index("dec"), 2) * half, half, 0)
    fetched = [shift(mine, n_cp, 1)]

    vmem = pl.BlockSpec(memory_space=pltpu.VMEM)
    hbm = pl.BlockSpec(memory_space=pltpu.HBM)
    params = pltpu.CompilerParams(vmem_limit_bytes=32 * 2**20)
    group, first_heads = 2, heads // 2

    def in_hbm(*arrays):
        return [pltpu.with_memory_space_constraint(x, pltpu.HBM) for x in arrays]

    def own_cost(some):
        return pl.CostEstimate(
            flops=2 * rows * some * (2 * NOPE * LAT + rows * (ROW + VDIM)),
            bytes_accessed=2 * (queries.size + key_absorb.size + some * rows * ROW),
            transcendentals=rows * some * rows,
        )

    def own_shapes(some):
        return [
            jax.ShapeDtypeStruct((some * rows, ROW), jnp.bfloat16),
            jax.ShapeDtypeStruct((some * rows, VDIM), jnp.float32),
            jax.ShapeDtypeStruct((some * rows, LANES), jnp.float32),
            jax.ShapeDtypeStruct((some * rows, LANES), jnp.float32),
        ]

    late_heads = heads - first_heads
    *first, own_copy, latents, own_bias, late_queries, late_absorb, value_copy = pl.pallas_call(
        functools.partial(own_first_kernel, first_heads, group),
        in_specs=[hbm] * 5,
        out_specs=[vmem] * 10,
        out_shape=own_shapes(first_heads) + [
            jax.ShapeDtypeStruct(own.shape, jnp.bfloat16),
            jax.ShapeDtypeStruct((rows, LAT), jnp.bfloat16),
            jax.ShapeDtypeStruct((rows, rows), jnp.float32),
            jax.ShapeDtypeStruct((rows, late_heads * HEAD), jnp.bfloat16),
            jax.ShapeDtypeStruct((late_heads, NOPE, LAT), jnp.bfloat16),
            jax.ShapeDtypeStruct(value_expand.shape, jnp.bfloat16),
        ],
        scratch_shapes=[
            pltpu.SMEM(prompt_pages.shape, jnp.int32),
            pltpu.VMEM((rows, first_heads * HEAD), jnp.bfloat16),
            pltpu.VMEM((first_heads, NOPE, LAT), jnp.bfloat16),
            pltpu.SemaphoreType.DMA((8,)),
        ],
        cost_estimate=own_cost(first_heads),
        compiler_params=params,
        name="own_first",
    )(*in_hbm(prompt_pages, own, queries, key_absorb, value_expand))
    fetched[0], own_copy = lax.optimization_barrier((fetched[0], own_copy))

    pieces = n_cp - 1
    late = (own_copy, latents, own_bias, late_queries, late_absorb, value_copy)
    *second, sent_rows, bias, picked, filled = pl.pallas_call(
        functools.partial(own_second_kernel, n_cp, count, late_heads, group, slot_count),
        in_specs=[hbm] * 3 + [vmem] * len(late),
        out_specs=[vmem] * 8,
        out_shape=own_shapes(late_heads) + [
            jax.ShapeDtypeStruct((kept, -(-ROW // LANES) * LANES), jnp.bfloat16),
            jax.ShapeDtypeStruct((rows, count * rows), jnp.float32),
            jax.ShapeDtypeStruct((kept, pieces * rows), jnp.bfloat16),
            jax.ShapeDtypeStruct((8, LANES), jnp.float32),
        ],
        scratch_shapes=[
            pltpu.SMEM(prompt_pages.shape, jnp.int32),
            pltpu.SMEM(decode_owner.shape, jnp.int32),
            pltpu.SMEM(slot_offset.shape, jnp.int32),
            pltpu.SemaphoreType.DMA((3,)),
        ],
        cost_estimate=own_cost(late_heads),
        compiler_params=params,
        name="own_second",
    )(*in_hbm(prompt_pages, decode_owner, slot_offset), *late)
    for _ in range(n_cp - 3):
        fetched.append(shift(fetched[-1], n_cp, 1))
    fetched[-1], bias = lax.optimization_barrier((fetched[-1], bias))
    swapped = [swap(block, dec_count) for block in fetched]
    sent_rows = shift(sent_rows, n_cp, -1)

    arrived = [own_copy] + [block for pair in zip(fetched[:-1], swapped[:-1]) for block in pair]
    found, ready_keys, ready_latents = pl.pallas_call(
        functools.partial(arrived_kernel, ready),
        in_specs=[vmem] * (1 + len(arrived)),
        out_specs=[vmem] * 3,
        out_shape=[
            jax.ShapeDtypeStruct((kept, ROW), jnp.float32),
            jax.ShapeDtypeStruct((ROW, ready * rows), jnp.bfloat16),
            jax.ShapeDtypeStruct((ready * rows, LAT), jnp.bfloat16),
        ],
        cost_estimate=pl.CostEstimate(flops=2**20, bytes_accessed=2**10, transcendentals=0),
        compiler_params=params,
        name="arrived",
    )(picked, *arrived)

    operands = (*first, *second, value_copy, bias, ready_keys, ready_latents, fetched[-1], swapped[-1])
    attended = pl.pallas_call(
        functools.partial(earlier_kernel, count, ready, group),
        in_specs=[vmem] * len(operands),
        out_specs=hbm,
        out_shape=jax.ShapeDtypeStruct((rows, heads * VDIM), jnp.bfloat16),
        scratch_shapes=[
            pltpu.VMEM((ROW, count * rows), jnp.bfloat16),
            pltpu.VMEM((count * rows, LAT), jnp.bfloat16),
            pltpu.VMEM((rows, heads * VDIM), jnp.bfloat16),
            pltpu.SemaphoreType.DMA((heads // group,)),
        ],
        cost_estimate=pl.CostEstimate(
            flops=2 * rows * heads * (count * rows * (ROW + LAT) + LAT * VDIM),
            bytes_accessed=2 * (heads * rows * (ROW + VDIM) + value_expand.size),
            transcendentals=rows * heads * count * rows,
        ),
        compiler_params=params,
        name="earlier",
    )(*operands)
    sent_rows, attended = lax.optimization_barrier((sent_rows, attended))
    page_cache, page_scales = pl.pallas_call(
        functools.partial(cache_kernel, pieces - 1),
        in_specs=[vmem] * 6,
        out_specs=[vmem] * 2,
        out_shape=[
            jax.ShapeDtypeStruct((slot_count, PAGE, ROW), jnp.bfloat16),
            jax.ShapeDtypeStruct((slot_count, NBLK, PAGE), jnp.bfloat16),
        ],
        cost_estimate=pl.CostEstimate(flops=2**20, bytes_accessed=2**10, transcendentals=0),
        compiler_params=params,
        name="cache",
    )(picked, found, filled, sent_rows, fetched[-1], swapped[-1])
    page_cache = page_cache.reshape(1, 1, slot_count, PAGE, ROW)
    page_scales = page_scales.transpose(0, 2, 1).reshape(1, 1, slot_count, PAGE, NBLK)
    return attended, page_cache, page_scales


def solution(mesh):
    return jax.shard_map(
        on_device,
        mesh=mesh,
        in_specs=(
            P(("grp", "cp"), "dec"),
            P(("grp", "cp"), None),
            P("dec", None, None),
            P("dec", None, None),
            P("grp"),
            P("grp", None),
            P("grp"),
        ),
        out_specs=(
            P(("grp", "cp"), "dec"),
            P(("grp", "cp"), "dec", None, None, None),
            P(("grp", "cp"), "dec", None, None, None),
        ),
        check_vma=False,
    )
```

```python
import functools
import math

import jax
import jax.numpy as jnp
from jax import lax
from jax.experimental import pallas as pl
from jax.experimental.pallas import tpu as pltpu
from jax.sharding import PartitionSpec as P

LAT = 512
ROPE = 64
NOPE = 128
VDIM = 128
PAGE = 16
BLOCK = 128
NBLK = LAT // BLOCK
ROW = LAT + ROPE
HEAD = NOPE + ROPE
LANES = 128

masked_fill = -1e30
amax_epsilon = 1e-06
exp2_scale = math.log2(math.e) / math.sqrt(HEAD)

NT = (((1,), (1,)), ((), ()))


def prompt_starts(prompt_pages):
    starts = [jnp.int32(0)]
    for k in range(prompt_pages.shape[0] - 1):
        starts.append(starts[-1] + prompt_pages[k])
    return starts


def visible_bias(prompt_pages, rows, steps_back):
    first = lax.axis_index("cp") * rows
    token = first + lax.broadcasted_iota(jnp.int32, (rows, 1), 0)
    begin = jnp.zeros((rows, 1), jnp.int32)
    for start in prompt_starts(prompt_pages):
        begin = jnp.maximum(begin, jnp.where(start * PAGE <= token, start * PAGE, 0))
    spot = first - steps_back * rows + lax.broadcasted_iota(jnp.int32, (1, rows), 1)
    return jnp.where((spot >= begin) & (spot <= token), 0.0, masked_fill)


def swap_pair(position, n_cp):
    odd = lax.rem(lax.axis_index("dec"), 2)
    within = lax.rem(position + 1, 2)
    swapped = position - within + lax.rem(within + odd, 2)
    paired = (position >= 1) & (position <= (n_cp - 1) // 2 * 2)
    return jnp.where(paired, swapped, position)


def slot_pages(owner, slot_count, prompt_pages, decode_owner, slot_offset):
    prompts, width = decode_owner.shape
    cycle = width * lax.axis_size("dec") * slot_count
    starts = prompt_starts(prompt_pages)
    pages, start, offset, place = jnp.int32(0), jnp.int32(0), jnp.int32(0), jnp.int32(0)
    for k in range(prompts):
        for p in range(width):
            mine = decode_owner[k, p] == owner
            pages = jnp.where(mine, prompt_pages[k], pages)
            start = jnp.where(mine, starts[k], start)
            offset = jnp.where(mine, slot_offset[k], offset)
            place = jnp.where(mine, p, place)
    result = []
    for c in range(slot_count):
        turn = width * (lax.axis_index("dec") * slot_count + c) + place
        page = lax.rem(turn - offset + 2 * cycle, cycle)
        result.append((page < pages, start + page))
    return result


def row_picker(targets, columns):
    kept = len(targets) * PAGE
    row = lax.broadcasted_iota(jnp.int32, (kept, 1), 0)
    target = jnp.full((kept, 1), -1, jnp.int32)
    for c, column in enumerate(targets):
        target = jnp.where(row // PAGE == c, column + row % PAGE, target)
    column = lax.broadcasted_iota(jnp.int32, (1, columns), 1)
    return jnp.where(column == target, 1.0, 0.0).astype(jnp.bfloat16)


def head_values(latents, value_expand, h):
    both = jnp.concatenate([value_expand[h], value_expand[h + 1]], axis=1)
    return jnp.dot(latents, both, preferred_element_type=jnp.float32).astype(jnp.bfloat16)


def own_kernel(n_cp, count, chunk, group, slot_count, *refs):
    inputs, refs = refs[:7], refs[7:]
    combined, result, peaks, totals, sent_rows, bias, picked, filled, own, value_expand = refs[:10]
    prompt_pages, decode_owner, slot_offset, queries, key_absorb, latents, sems = refs[10:]
    pages_hbm, owner_hbm, offset_hbm, own_hbm, queries_hbm, absorb_hbm, expand_hbm = inputs
    rows = own.shape[1]
    heads = key_absorb.shape[0]
    small = [
        pltpu.make_async_copy(source, target, sems.at[i])
        for i, (source, target) in enumerate(zip(inputs[:4], (prompt_pages, decode_owner, slot_offset, own)))
    ]
    large = []
    for g in range(heads // chunk):
        at = 4 + 3 * g
        some = pl.ds(g * chunk, chunk)
        wide = pl.ds(g * chunk * HEAD, chunk * HEAD)
        large.append((
            pltpu.make_async_copy(queries_hbm.at[:, wide], queries.at[:, wide], sems.at[at]),
            pltpu.make_async_copy(absorb_hbm.at[some], key_absorb.at[some], sems.at[at + 1]),
            pltpu.make_async_copy(expand_hbm.at[some], value_expand.at[some], sems.at[at + 2]),
        ))
    for copy in small:
        copy.start()
    for chunk_copies in large:
        for copy in chunk_copies:
            copy.start()
    steps = heads // group

    def absorb(g):
        if g * group % chunk == 0:
            for copy in large[g * group // chunk][:2]:
                copy.wait()
        for h in range(g * group, (g + 1) * group):
            at = h * HEAD
            absorbed = jnp.dot(queries[:, at:at + NOPE], key_absorb[h], preferred_element_type=jnp.float32)
            combined[h * rows:(h + 1) * rows, :LAT] = absorbed.astype(jnp.bfloat16)
            combined[h * rows:(h + 1) * rows, LAT:] = queries[:, at + NOPE:at + HEAD]

    def score(g):
        return jnp.dot(combined[g * group * rows:(g + 1) * group * rows, :], own[...], preferred_element_type=jnp.float32)

    def value(g):
        if g * group % chunk == 0:
            large[g * group // chunk][2].wait()
        return [head_values(latents[...], value_expand, g * group + i) for i in range(0, group, 2)]

    def finish(g, scores, both):
        span = slice(g * group * rows, (g + 1) * group * rows)
        scores = (scores.reshape(group, rows, rows) + own_bias[None]).reshape(group * rows, rows)
        peak = jnp.max(scores, axis=1, keepdims=True)
        weights = jnp.exp2((scores - peak) * exp2_scale)
        total = jnp.sum(weights, axis=1, keepdims=True)
        weights = weights.astype(jnp.bfloat16)
        for i in range(group):
            mine = both[i // 2][:, i % 2 * VDIM:(i % 2 + 1) * VDIM]
            out = jnp.dot(weights[i * rows:(i + 1) * rows], mine, preferred_element_type=jnp.float32)
            result[(g * group + i) * rows:(g * group + i + 1) * rows, :] = out
        peaks[span, :] = jnp.broadcast_to(peak, (group * rows, LANES))
        totals[span, :] = jnp.broadcast_to(total, (group * rows, LANES))

    scores, both = {}, {}
    for step in range(steps + 2):
        if step < steps:
            absorb(step)
        if step == 0:
            small[3].wait()
            latents[...] = own[:LAT, :].T
        if step == 1:
            for copy in small[:3]:
                copy.wait()
            own_bias = visible_bias(prompt_pages, rows, 0)
            index_work(n_cp, count, slot_count, prompt_pages, decode_owner, slot_offset, own[...], sent_rows, bias, picked, filled)
        if 0 <= step - 1 < steps:
            scores[step - 1] = score(step - 1)
            both[step - 1] = value(step - 1)
        if 0 <= step - 2:
            finish(step - 2, scores.pop(step - 2), both.pop(step - 2))


def index_work(n_cp, count, slot_count, prompt_pages, decode_owner, slot_offset, block, sent_rows, bias, picked, filled):
    rows = block.shape[1]
    me = lax.axis_index("cp")
    behind = lax.rem(me + n_cp - 1, n_cp)
    targets = []
    for valid, page in slot_pages(behind, slot_count, prompt_pages, decode_owner, slot_offset):
        here = valid & (page * PAGE // rows == me)
        targets.append(jnp.where(here, lax.rem(page * PAGE, rows), -PAGE))
    choice = row_picker(targets, rows)
    sent = lax.dot_general(choice, block, NT, preferred_element_type=jnp.float32)
    sent_rows[:, :ROW] = sent.astype(jnp.bfloat16)
    sent_rows[:, ROW:] = jnp.zeros((choice.shape[0], sent_rows.shape[1] - ROW), jnp.bfloat16)
    for b in range(count):
        bias[:, b * rows:(b + 1) * rows] = visible_bias(prompt_pages, rows, swap_pair(jnp.int32(b + 1), n_cp))
    targets = []
    lane = lax.broadcasted_iota(jnp.int32, filled.shape, 1)
    lane_filled = jnp.zeros(filled.shape, jnp.float32)
    for c, (valid, page) in enumerate(slot_pages(me, slot_count, prompt_pages, decode_owner, slot_offset)):
        source = page * PAGE // rows
        column = swap_pair(lax.rem(me - source + n_cp, n_cp), n_cp) * rows + lax.rem(page * PAGE, rows)
        targets.append(jnp.where(valid, column, -PAGE))
        lane_filled = jnp.where(lane // PAGE == c, valid.astype(jnp.float32), lane_filled)
    filled[...] = lane_filled
    picked[...] = row_picker(targets, (n_cp - 1) * rows)


def pick_rows(picked, index, block):
    rows = block.shape[1]
    return lax.dot_general(picked[:, index * rows:(index + 1) * rows], block, NT, preferred_element_type=jnp.float32)


def arrived_kernel(picked, own, *refs):
    blocks, (found, latents) = refs[:-2], refs[-2:]
    rows = own.shape[1]
    total = pick_rows(picked, 0, own[...])
    for i, block in enumerate(blocks):
        total = total + pick_rows(picked, 1 + 2 * i, block[...])
        latents[i * rows:(i + 1) * rows, :] = block[:LAT, :].T
    found[...] = total


def write_cache(rows, filled, page_cache, page_scales):
    slot_count = page_cache.shape[0]
    scales = []
    for b in range(NBLK):
        values = rows[:, b * BLOCK:(b + 1) * BLOCK]
        scale = jnp.max(jnp.abs(values), axis=1, keepdims=True) + amax_epsilon
        scale = scale.astype(jnp.bfloat16).astype(jnp.float32)
        encoded = (values / scale).astype(jnp.bfloat16)
        for c in range(slot_count):
            page_cache[c, :, b * BLOCK:(b + 1) * BLOCK] = encoded[c * PAGE:(c + 1) * PAGE]
        scales.append(scale)
    kept = rows.shape[0]
    which = lax.broadcasted_iota(jnp.int32, (kept, LANES), 1)
    table = jnp.zeros((kept, LANES), jnp.float32)
    for b, scale in enumerate(scales):
        table = jnp.where(which == b, scale, table)
    table = (table.T[:NBLK] * filled[:1, :kept]).astype(jnp.bfloat16)
    for c in range(slot_count):
        page_cache[c, :, LAT:] = rows[c * PAGE:(c + 1) * PAGE, LAT:].astype(jnp.bfloat16)
        page_scales[c] = table[:, c * PAGE:(c + 1) * PAGE]


def earlier_heads(first_head, heads, group, inputs, keys, latents, attended, result, sems, beside):
    combined, own_result, peaks, totals, value_expand, bias = inputs
    rows, width = bias.shape
    steps = heads // group

    def span(g):
        at = (first_head + g * group) * rows
        return slice(at, at + group * rows)

    def send(g):
        at = pl.ds((first_head + g * group) * VDIM, group * VDIM)
        here = pl.ds(g * group * VDIM, group * VDIM)
        return pltpu.make_async_copy(result.at[:, here], attended.at[:, at], sems.at[g])

    def score(g):
        scores = jnp.dot(combined[span(g), :], keys[...], preferred_element_type=jnp.float32)
        return (scores.reshape(group, rows, width) + bias[...][None]).reshape(group * rows, width)

    def weigh(g, scores):
        old_peak = peaks[span(g), :]
        parts = [scores[:, b:b + LANES] for b in range(0, width, LANES)]
        peak = jnp.maximum(old_peak, jnp.max(functools.reduce(jnp.maximum, parts), axis=1, keepdims=True))
        parts = [jnp.exp2((part - peak) * exp2_scale) for part in parts]
        total = jnp.sum(functools.reduce(jnp.add, parts), axis=1, keepdims=True)
        factor = jnp.exp2((old_peak - peak) * exp2_scale)
        inverse = 1.0 / (totals[span(g), :] * factor + total)
        weights = jnp.concatenate([part.astype(jnp.bfloat16) for part in parts], axis=1)
        return weights, factor * inverse, inverse

    def mix(g, weights):
        return jnp.dot(weights, latents[...], preferred_element_type=jnp.float32).astype(jnp.bfloat16)

    def finish(g, mixed, factor, inverse):
        for i in range(group):
            part = slice(i * rows, (i + 1) * rows)
            h = first_head + g * group + i
            out = jnp.dot(mixed[part], value_expand[h], preferred_element_type=jnp.float32)
            out = own_result[h * rows:(h + 1) * rows, :] * factor[part] + out * inverse[part]
            at = (g * group + i) * VDIM
            result[:, at:at + VDIM] = out.astype(jnp.bfloat16)
        send(g).start()

    @pl.when(lax.axis_index("cp") == 0)
    def _():
        beside()
        for g in range(steps):
            for i in range(group):
                h = first_head + g * group + i
                at = (g * group + i) * VDIM
                part = slice(h * rows, (h + 1) * rows)
                result[:, at:at + VDIM] = (own_result[part, :] / totals[part, :]).astype(jnp.bfloat16)
            send(g).start()

    @pl.when(lax.axis_index("cp") > 0)
    def _():
        scores, weights, mixed = {}, {}, {}
        for step in range(steps + 2):
            if step < steps:
                scores[step] = score(step)
            if step == 0:
                beside()
            if 0 <= step - 2:
                finish(step - 2, mixed.pop(step - 2), *weights.pop(step - 2)[1:])
            if 0 <= step - 1 < steps:
                weights[step - 1] = weigh(step - 1, scores.pop(step - 1))
                mixed[step - 1] = mix(step - 1, weights[step - 1][0])

    for g in range(steps):
        send(g).wait()


def earlier_first_kernel(count, heads, group, *refs):
    inputs, fetched_latents, refs = refs[:6], refs[6], refs[7:]
    arrived, (attended, keys, latents, result, sems) = refs[:-5], refs[-5:]
    rows = arrived[0].shape[1]
    for b in range(count):
        keys[:, b * rows:(b + 1) * rows] = arrived[b][...]
        if b % 2:
            latents[b * rows:(b + 1) * rows, :] = arrived[b][:LAT, :].T
        else:
            latents[b * rows:(b + 1) * rows, :] = fetched_latents[b // 2 * rows:(b // 2 + 1) * rows, :]
    earlier_heads(0, heads, group, inputs, keys, latents, attended, result, sems, lambda: None)


def earlier_last_kernel(first_head, heads, group, *refs):
    inputs, (keys, latents, picked, found, sent_rows, filled), refs = refs[:6], refs[6:12], refs[12:]
    swapped, refs = refs[:-8], refs[-7:]
    attended, page_cache, page_scales, result, cache_buf, scale_buf, sems = refs
    cache_copies = [
        pltpu.make_async_copy(cache_buf, page_cache, sems.at[heads // group]),
        pltpu.make_async_copy(scale_buf, page_scales, sems.at[heads // group + 1]),
    ]

    def cache():
        rows = found[...] + sent_rows[:, :ROW].astype(jnp.float32)
        for i, block in enumerate(swapped):
            rows = rows + pick_rows(picked, 2 + 2 * i, block[...])
        write_cache(rows, filled, cache_buf, scale_buf)
        for copy in cache_copies:
            copy.start()

    earlier_heads(first_head, heads, group, inputs, keys, latents, attended, result, sems, cache)
    for copy in cache_copies:
        copy.wait()


def fetch(own, n_cp, n_dec):
    blocks = []
    for step in range(1, n_cp - 1, 2):
        pairs = [(c * n_dec + e, (c + step + e % 2) % n_cp * n_dec + e) for c in range(n_cp) for e in range(n_dec)]
        blocks.append(lax.ppermute(own, ("cp", "dec"), pairs))
    return blocks


def swap(blocks, n_dec):
    pieces = []
    for block in blocks:
        pieces += [block, lax.ppermute(block, "dec", [(e, e ^ 1) for e in range(n_dec)])]
    return pieces


def on_device(queries, latent_rows, key_absorb, value_expand, prompt_pages, decode_owner, slot_offset):
    n_cp = lax.axis_size("cp")
    dec_count = lax.axis_size("dec")
    heads = key_absorb.shape[0]
    rows = latent_rows.shape[0]
    prompts, width = decode_owner.shape
    slot_count = 3 * (rows // PAGE) // (2 * dec_count)
    kept = slot_count * PAGE
    reach = width * dec_count * slot_count * PAGE
    count = -(-reach // rows) - (1 if prompts == 2 else 0)
    count = min(n_cp - 2, count + count % 2)
    own = latent_rows.T
    blocks = fetch(own, n_cp, dec_count)

    vmem = pl.BlockSpec(memory_space=pltpu.VMEM)
    hbm = pl.BlockSpec(memory_space=pltpu.HBM)
    params = pltpu.CompilerParams(vmem_limit_bytes=32 * 2**20)
    group, chunk = 2, 4
    inputs = (prompt_pages, decode_owner, slot_offset, own, queries, key_absorb, value_expand)
    combined, result, peaks, totals, sent_rows, bias, picked, filled, own_copy, value_copy = pl.pallas_call(
        functools.partial(own_kernel, n_cp, count, chunk, group, slot_count),
        in_specs=[hbm] * 7,
        out_specs=[vmem] * 10,
        out_shape=[
            jax.ShapeDtypeStruct((heads * rows, ROW), jnp.bfloat16),
            jax.ShapeDtypeStruct((heads * rows, VDIM), jnp.float32),
            jax.ShapeDtypeStruct((heads * rows, LANES), jnp.float32),
            jax.ShapeDtypeStruct((heads * rows, LANES), jnp.float32),
            jax.ShapeDtypeStruct((kept, -(-ROW // LANES) * LANES), jnp.bfloat16),
            jax.ShapeDtypeStruct((rows, count * rows), jnp.float32),
            jax.ShapeDtypeStruct((kept, (n_cp - 1) * rows), jnp.bfloat16),
            jax.ShapeDtypeStruct((8, LANES), jnp.float32),
            jax.ShapeDtypeStruct(own.shape, jnp.bfloat16),
            jax.ShapeDtypeStruct(value_expand.shape, jnp.bfloat16),
        ],
        scratch_shapes=[
            pltpu.SMEM(prompt_pages.shape, jnp.int32),
            pltpu.SMEM(decode_owner.shape, jnp.int32),
            pltpu.SMEM(slot_offset.shape, jnp.int32),
            pltpu.VMEM((rows, heads * HEAD), jnp.bfloat16),
            pltpu.VMEM((heads, NOPE, LAT), jnp.bfloat16),
            pltpu.VMEM((rows, LAT), jnp.bfloat16),
            pltpu.SemaphoreType.DMA((4 + 3 * (heads // chunk),)),
        ],
        cost_estimate=pl.CostEstimate(
            flops=2 * rows * heads * (2 * NOPE * LAT + rows * (ROW + VDIM)),
            bytes_accessed=2 * (queries.size + key_absorb.size + heads * rows * ROW),
            transcendentals=rows * heads * rows,
        ),
        compiler_params=params,
        name="own",
    )(*[pltpu.with_memory_space_constraint(x, pltpu.HBM) for x in inputs])
    sent_rows = lax.ppermute(sent_rows, "cp", [(c, (c + n_cp - 1) % n_cp) for c in range(n_cp)])
    blocks, picked = lax.optimization_barrier((blocks, picked))
    pieces = swap(blocks, dec_count)
    found, fetched_latents = pl.pallas_call(
        arrived_kernel,
        in_specs=[vmem] * (2 + len(blocks)),
        out_specs=[vmem] * 2,
        out_shape=[
            jax.ShapeDtypeStruct((kept, ROW), jnp.float32),
            jax.ShapeDtypeStruct((len(blocks) * rows, LAT), jnp.bfloat16),
        ],
        cost_estimate=pl.CostEstimate(flops=2**20, bytes_accessed=2**10, transcendentals=0),
        compiler_params=params,
        name="arrived",
    )(picked, own_copy, *blocks)

    def earlier_cost(some):
        return pl.CostEstimate(
            flops=2 * rows * some * (count * rows * (ROW + LAT) + LAT * VDIM),
            bytes_accessed=2 * (some * rows * (ROW + VDIM) + value_expand.size),
            transcendentals=rows * some * count * rows,
        )

    attended_shape = jax.ShapeDtypeStruct((rows, heads * VDIM), jnp.bfloat16)
    last_heads = heads // 4
    first_heads = heads - last_heads
    group = 4 if count <= 4 else 2
    inputs = (combined, result, peaks, totals, value_copy, bias)
    operands = (*inputs, fetched_latents, *pieces[:count])
    attended, keys, latents = pl.pallas_call(
        functools.partial(earlier_first_kernel, count, first_heads, group),
        in_specs=[vmem] * len(operands),
        out_specs=[hbm, vmem, vmem],
        out_shape=[
            attended_shape,
            jax.ShapeDtypeStruct((ROW, count * rows), jnp.bfloat16),
            jax.ShapeDtypeStruct((count * rows, LAT), jnp.bfloat16),
        ],
        scratch_shapes=[
            pltpu.VMEM((rows, first_heads * VDIM), jnp.bfloat16),
            pltpu.SemaphoreType.DMA((first_heads // group,)),
        ],
        cost_estimate=earlier_cost(first_heads),
        compiler_params=params,
        name="earlier_first",
    )(*operands)
    sent_rows, keys = lax.optimization_barrier((sent_rows, keys))
    group = 2
    operands = (*inputs, keys, latents, picked, found, sent_rows, filled, *pieces[1::2], attended)
    attended, page_cache, page_scales = pl.pallas_call(
        functools.partial(earlier_last_kernel, first_heads, last_heads, group),
        in_specs=[vmem] * (len(operands) - 1) + [hbm],
        out_specs=[hbm] * 3,
        out_shape=[
            attended_shape,
            jax.ShapeDtypeStruct((slot_count, PAGE, ROW), jnp.bfloat16),
            jax.ShapeDtypeStruct((slot_count, NBLK, PAGE), jnp.bfloat16),
        ],
        scratch_shapes=[
            pltpu.VMEM((rows, last_heads * VDIM), jnp.bfloat16),
            pltpu.VMEM((slot_count, PAGE, ROW), jnp.bfloat16),
            pltpu.VMEM((slot_count, NBLK, PAGE), jnp.bfloat16),
            pltpu.SemaphoreType.DMA((last_heads // group + 2,)),
        ],
        input_output_aliases={len(operands) - 1: 0},
        cost_estimate=earlier_cost(last_heads),
        compiler_params=params,
        name="earlier_last",
    )(*operands)
    page_cache = page_cache.reshape(1, 1, slot_count, PAGE, ROW)
    page_scales = page_scales.transpose(0, 2, 1).reshape(1, 1, slot_count, PAGE, NBLK)
    return attended, page_cache, page_scales


def solution(mesh):
    return jax.shard_map(
        on_device,
        mesh=mesh,
        in_specs=(
            P(("grp", "cp"), "dec"),
            P(("grp", "cp"), None),
            P("dec", None, None),
            P("dec", None, None),
            P("grp"),
            P("grp", None),
            P("grp"),
        ),
        out_specs=(
            P(("grp", "cp"), "dec"),
            P(("grp", "cp"), "dec", None, None, None),
            P(("grp", "cp"), "dec", None, None, None),
        ),
        check_vma=False,
    )
```

```python
import functools
import math

import jax
import jax.numpy as jnp
from jax import lax
from jax.experimental import pallas as pl
from jax.experimental.pallas import tpu as pltpu
from jax.sharding import PartitionSpec as P

LAT = 512
ROPE = 64
NOPE = 128
VDIM = 128
PAGE = 16
BLOCK = 128
NBLK = LAT // BLOCK
ROW = LAT + ROPE
HEAD = NOPE + ROPE
LANES = 128
SWAP = 3

masked_fill = -1e30
amax_epsilon = 1e-06
exp2_scale = math.log2(math.e) / math.sqrt(HEAD)

NT = (((1,), (1,)), ((), ()))


def prompt_starts(prompt_pages):
    starts = [jnp.int32(0)]
    for k in range(prompt_pages.shape[0] - 1):
        starts.append(starts[-1] + prompt_pages[k])
    return starts


def visible_bias(prompt_pages, rows, steps_back):
    first = lax.axis_index("cp") * rows
    token = first + lax.broadcasted_iota(jnp.int32, (rows, 1), 0)
    begin = jnp.zeros((rows, 1), jnp.int32)
    for start in prompt_starts(prompt_pages):
        begin = jnp.maximum(begin, jnp.where(start * PAGE <= token, start * PAGE, 0))
    spot = first - steps_back * rows + lax.broadcasted_iota(jnp.int32, (1, rows), 1)
    return jnp.where((spot >= begin) & (spot <= token), 0.0, masked_fill)


def swap_pair(position, n_cp):
    odd = lax.rem(lax.axis_index("dec"), 2)
    within = lax.rem(position + 1, 2)
    swapped = position - within + lax.rem(within + odd, 2)
    paired = (position >= 1) & (position <= (n_cp - 1) // 2 * 2)
    return jnp.where(paired, swapped, position)


def slot_pages(owner, slot_count, prompt_pages, decode_owner, slot_offset):
    prompts, width = decode_owner.shape
    cycle = width * lax.axis_size("dec") * slot_count
    starts = prompt_starts(prompt_pages)
    pages, start, offset, place = jnp.int32(0), jnp.int32(0), jnp.int32(0), jnp.int32(0)
    for k in range(prompts):
        for p in range(width):
            mine = decode_owner[k, p] == owner
            pages = jnp.where(mine, prompt_pages[k], pages)
            start = jnp.where(mine, starts[k], start)
            offset = jnp.where(mine, slot_offset[k], offset)
            place = jnp.where(mine, p, place)
    result = []
    for c in range(slot_count):
        turn = width * (lax.axis_index("dec") * slot_count + c) + place
        page = lax.rem(turn - offset + 2 * cycle, cycle)
        result.append((page < pages, start + page))
    return result


def row_picker(targets, columns):
    kept = len(targets) * PAGE
    row = lax.broadcasted_iota(jnp.int32, (kept, 1), 0)
    target = jnp.full((kept, 1), -1, jnp.int32)
    for c, column in enumerate(targets):
        target = jnp.where(row // PAGE == c, column + row % PAGE, target)
    column = lax.broadcasted_iota(jnp.int32, (1, columns), 1)
    return jnp.where(column == target, 1.0, 0.0).astype(jnp.bfloat16)


def head_values(latents, value_expand, h):
    both = jnp.concatenate([value_expand[h], value_expand[h + 1]], axis=1)
    return jnp.dot(latents, both, preferred_element_type=jnp.float32).astype(jnp.bfloat16)


def own_kernel(n_cp, count, chunk, group, slot_count, *refs):
    inputs, refs = refs[:7], refs[7:]
    combined, result, peaks, totals, sent_rows, bias, picked, filled, own, value_expand = refs[:10]
    prompt_pages, decode_owner, slot_offset, queries, key_absorb, latents, sems = refs[10:]
    pages_hbm, owner_hbm, offset_hbm, own_hbm, queries_hbm, absorb_hbm, expand_hbm = inputs
    rows = own.shape[1]
    heads = key_absorb.shape[0]
    small = [
        pltpu.make_async_copy(source, target, sems.at[i])
        for i, (source, target) in enumerate(zip(inputs[:4], (prompt_pages, decode_owner, slot_offset, own)))
    ]
    large = []
    for g in range(heads // chunk):
        at = 4 + 3 * g
        some = pl.ds(g * chunk, chunk)
        wide = pl.ds(g * chunk * HEAD, chunk * HEAD)
        large.append((
            pltpu.make_async_copy(queries_hbm.at[:, wide], queries.at[:, wide], sems.at[at]),
            pltpu.make_async_copy(absorb_hbm.at[some], key_absorb.at[some], sems.at[at + 1]),
            pltpu.make_async_copy(expand_hbm.at[some], value_expand.at[some], sems.at[at + 2]),
        ))
    for copy in small:
        copy.start()
    for chunk_copies in large:
        for copy in chunk_copies:
            copy.start()
    steps = heads // group

    def absorb(g):
        if g * group % chunk == 0:
            for copy in large[g * group // chunk][:2]:
                copy.wait()
        for h in range(g * group, (g + 1) * group):
            at = h * HEAD
            absorbed = jnp.dot(queries[:, at:at + NOPE], key_absorb[h], preferred_element_type=jnp.float32)
            combined[h * rows:(h + 1) * rows, :LAT] = absorbed.astype(jnp.bfloat16)
            combined[h * rows:(h + 1) * rows, LAT:] = queries[:, at + NOPE:at + HEAD]

    def score(g):
        return jnp.dot(combined[g * group * rows:(g + 1) * group * rows, :], own[...], preferred_element_type=jnp.float32)

    def value(g):
        if g * group % chunk == 0:
            large[g * group // chunk][2].wait()
        return [head_values(latents[...], value_expand, g * group + i) for i in range(0, group, 2)]

    def finish(g, scores, both):
        span = slice(g * group * rows, (g + 1) * group * rows)
        scores = (scores.reshape(group, rows, rows) + own_bias[None]).reshape(group * rows, rows)
        peak = jnp.max(scores, axis=1, keepdims=True)
        weights = jnp.exp2((scores - peak) * exp2_scale)
        total = jnp.sum(weights, axis=1, keepdims=True)
        weights = weights.astype(jnp.bfloat16)
        for i in range(group):
            mine = both[i // 2][:, i % 2 * VDIM:(i % 2 + 1) * VDIM]
            out = jnp.dot(weights[i * rows:(i + 1) * rows], mine, preferred_element_type=jnp.float32)
            result[(g * group + i) * rows:(g * group + i + 1) * rows, :] = out
        peaks[span, :] = jnp.broadcast_to(peak, (group * rows, LANES))
        totals[span, :] = jnp.broadcast_to(total, (group * rows, LANES))

    scores, both = {}, {}
    for step in range(steps + 2):
        if step < steps:
            absorb(step)
        if step == 0:
            small[3].wait()
            latents[...] = own[:LAT, :].T
        if step == 1:
            for copy in small[:3]:
                copy.wait()
            own_bias = visible_bias(prompt_pages, rows, 0)
            index_work(n_cp, count, slot_count, prompt_pages, decode_owner, slot_offset, own[...], sent_rows, bias, picked, filled)
        if 0 <= step - 1 < steps:
            scores[step - 1] = score(step - 1)
            both[step - 1] = value(step - 1)
        if 0 <= step - 2:
            finish(step - 2, scores.pop(step - 2), both.pop(step - 2))


def index_work(n_cp, count, slot_count, prompt_pages, decode_owner, slot_offset, block, sent_rows, bias, picked, filled):
    rows = block.shape[1]
    me = lax.axis_index("cp")
    behind = lax.rem(me + n_cp - 1, n_cp)
    targets = []
    for valid, page in slot_pages(behind, slot_count, prompt_pages, decode_owner, slot_offset):
        here = valid & (page * PAGE // rows == me)
        targets.append(jnp.where(here, lax.rem(page * PAGE, rows), -PAGE))
    choice = row_picker(targets, rows)
    sent = lax.dot_general(choice, block, NT, preferred_element_type=jnp.float32)
    sent_rows[:, :ROW] = sent.astype(jnp.bfloat16)
    sent_rows[:, ROW:] = jnp.zeros((choice.shape[0], sent_rows.shape[1] - ROW), jnp.bfloat16)
    for b in range(count):
        bias[:, b * rows:(b + 1) * rows] = visible_bias(prompt_pages, rows, swap_pair(jnp.int32(b + 1), n_cp))
    targets = []
    lane = lax.broadcasted_iota(jnp.int32, filled.shape, 1)
    lane_filled = jnp.zeros(filled.shape, jnp.float32)
    for c, (valid, page) in enumerate(slot_pages(me, slot_count, prompt_pages, decode_owner, slot_offset)):
        source = page * PAGE // rows
        column = swap_pair(lax.rem(me - source + n_cp, n_cp), n_cp) * rows + lax.rem(page * PAGE, rows)
        targets.append(jnp.where(valid, column, -PAGE))
        lane_filled = jnp.where(lane // PAGE == c, valid.astype(jnp.float32), lane_filled)
    filled[...] = lane_filled
    picked[...] = row_picker(targets, (n_cp - 1) * rows)


def pick_rows(picked, index, block):
    rows = block.shape[1]
    return lax.dot_general(picked[:, index * rows:(index + 1) * rows], block, NT, preferred_element_type=jnp.float32)


def arrived_kernel(picked, own, *refs):
    blocks, (found, latents) = refs[:-2], refs[-2:]
    rows = own.shape[1]
    total = pick_rows(picked, 0, own[...])
    for i, block in enumerate(blocks):
        total = total + pick_rows(picked, 1 + 2 * i, block[...])
        latents[i * rows:(i + 1) * rows, :] = block[:LAT, :].T
    found[...] = total


def write_cache(rows, filled, page_cache, page_scales):
    slot_count = page_cache.shape[0]
    scales = []
    for b in range(NBLK):
        values = rows[:, b * BLOCK:(b + 1) * BLOCK]
        scale = jnp.max(jnp.abs(values), axis=1, keepdims=True) + amax_epsilon
        scale = scale.astype(jnp.bfloat16).astype(jnp.float32)
        encoded = (values / scale).astype(jnp.bfloat16)
        for c in range(slot_count):
            page_cache[c, :, b * BLOCK:(b + 1) * BLOCK] = encoded[c * PAGE:(c + 1) * PAGE]
        scales.append(scale)
    kept = rows.shape[0]
    which = lax.broadcasted_iota(jnp.int32, (kept, LANES), 1)
    table = jnp.zeros((kept, LANES), jnp.float32)
    for b, scale in enumerate(scales):
        table = jnp.where(which == b, scale, table)
    table = (table.T[:NBLK] * filled[:1, :kept]).astype(jnp.bfloat16)
    for c in range(slot_count):
        page_cache[c, :, LAT:] = rows[c * PAGE:(c + 1) * PAGE, LAT:].astype(jnp.bfloat16)
        page_scales[c] = table[:, c * PAGE:(c + 1) * PAGE]


def earlier_heads(first_head, heads, group, inputs, keys, latents, attended, result, sems, beside):
    combined, own_result, peaks, totals, value_expand, bias = inputs
    rows, width = bias.shape
    steps = heads // group

    def span(g):
        at = (first_head + g * group) * rows
        return slice(at, at + group * rows)

    def send(g):
        at = pl.ds((first_head + g * group) * VDIM, group * VDIM)
        here = pl.ds(g * group * VDIM, group * VDIM)
        return pltpu.make_async_copy(result.at[:, here], attended.at[:, at], sems.at[g])

    def score(g):
        scores = jnp.dot(combined[span(g), :], keys[...], preferred_element_type=jnp.float32)
        return (scores.reshape(group, rows, width) + bias[...][None]).reshape(group * rows, width)

    def weigh(g, scores):
        old_peak = peaks[span(g), :]
        parts = [scores[:, b:b + LANES] for b in range(0, width, LANES)]
        peak = jnp.maximum(old_peak, jnp.max(functools.reduce(jnp.maximum, parts), axis=1, keepdims=True))
        parts = [jnp.exp2((part - peak) * exp2_scale) for part in parts]
        total = jnp.sum(functools.reduce(jnp.add, parts), axis=1, keepdims=True)
        factor = jnp.exp2((old_peak - peak) * exp2_scale)
        inverse = 1.0 / (totals[span(g), :] * factor + total)
        weights = jnp.concatenate([part.astype(jnp.bfloat16) for part in parts], axis=1)
        return weights, factor * inverse, inverse

    def mix(g, weights):
        return jnp.dot(weights, latents[...], preferred_element_type=jnp.float32).astype(jnp.bfloat16)

    def finish(g, mixed, factor, inverse):
        for i in range(group):
            part = slice(i * rows, (i + 1) * rows)
            h = first_head + g * group + i
            out = jnp.dot(mixed[part], value_expand[h], preferred_element_type=jnp.float32)
            out = own_result[h * rows:(h + 1) * rows, :] * factor[part] + out * inverse[part]
            at = (g * group + i) * VDIM
            result[:, at:at + VDIM] = out.astype(jnp.bfloat16)
        send(g).start()

    @pl.when(lax.axis_index("cp") == 0)
    def _():
        beside()
        for g in range(steps):
            for i in range(group):
                h = first_head + g * group + i
                at = (g * group + i) * VDIM
                part = slice(h * rows, (h + 1) * rows)
                result[:, at:at + VDIM] = (own_result[part, :] / totals[part, :]).astype(jnp.bfloat16)
            send(g).start()

    @pl.when(lax.axis_index("cp") > 0)
    def _():
        scores, weights, mixed = {}, {}, {}
        for step in range(steps + 2):
            if step < steps:
                scores[step] = score(step)
            if step == 0:
                beside()
            if 0 <= step - 2:
                finish(step - 2, mixed.pop(step - 2), *weights.pop(step - 2)[1:])
            if 0 <= step - 1 < steps:
                weights[step - 1] = weigh(step - 1, scores.pop(step - 1))
                mixed[step - 1] = mix(step - 1, weights[step - 1][0])

    for g in range(steps):
        send(g).wait()


def earlier_first_kernel(count, heads, group, *refs):
    inputs, fetched_latents, refs = refs[:6], refs[6], refs[7:]
    arrived, (attended, keys, latents, result, sems) = refs[:-5], refs[-5:]
    rows = arrived[0].shape[1]
    for i in range(count // 2):
        fetched, *parts = arrived[i * (1 + SWAP):(i + 1) * (1 + SWAP)]
        swapped = jnp.concatenate([part[...] for part in parts], axis=0)
        at = 2 * i * rows
        keys[:, at:at + rows] = fetched[...]
        keys[:, at + rows:at + 2 * rows] = swapped
        latents[at:at + rows, :] = fetched_latents[i * rows:(i + 1) * rows, :]
        latents[at + rows:at + 2 * rows, :] = swapped[:LAT].T
    earlier_heads(0, heads, group, inputs, keys, latents, attended, result, sems, lambda: None)


def earlier_last_kernel(first_head, heads, group, *refs):
    inputs, (keys, latents, picked, found, sent_rows, filled), refs = refs[:6], refs[6:12], refs[12:]
    swapped, refs = refs[:-8], refs[-7:]
    attended, page_cache, page_scales, result, cache_buf, scale_buf, sems = refs
    cache_copies = [
        pltpu.make_async_copy(cache_buf, page_cache, sems.at[heads // group]),
        pltpu.make_async_copy(scale_buf, page_scales, sems.at[heads // group + 1]),
    ]

    def cache():
        rows = found[...] + sent_rows[:, :ROW].astype(jnp.float32)
        for i in range(len(swapped) // SWAP):
            block = jnp.concatenate([part[...] for part in swapped[i * SWAP:(i + 1) * SWAP]], axis=0)
            rows = rows + pick_rows(picked, 2 + 2 * i, block)
        write_cache(rows, filled, cache_buf, scale_buf)
        for copy in cache_copies:
            copy.start()

    earlier_heads(first_head, heads, group, inputs, keys, latents, attended, result, sems, cache)
    for copy in cache_copies:
        copy.wait()


def fetch(own, n_cp, n_dec):
    blocks = []
    for step in range(1, n_cp - 1, 2):
        pairs = [(c * n_dec + e, (c + step + e % 2) % n_cp * n_dec + e) for c in range(n_cp) for e in range(n_dec)]
        blocks.append(lax.ppermute(own, ("cp", "dec"), pairs))
    return blocks


def swap(blocks, n_dec):
    pieces = []
    for block in blocks:
        parts = [block[at:at + ROW // SWAP] for at in range(0, ROW, ROW // SWAP)]
        pieces += [block] + [lax.ppermute(part, "dec", [(e, e ^ 1) for e in range(n_dec)]) for part in parts]
    return pieces


def on_device(queries, latent_rows, key_absorb, value_expand, prompt_pages, decode_owner, slot_offset):
    n_cp = lax.axis_size("cp")
    dec_count = lax.axis_size("dec")
    heads = key_absorb.shape[0]
    rows = latent_rows.shape[0]
    prompts, width = decode_owner.shape
    slot_count = 3 * (rows // PAGE) // (2 * dec_count)
    kept = slot_count * PAGE
    reach = width * dec_count * slot_count * PAGE
    count = -(-reach // rows) - (1 if prompts == 2 else 0)
    count = min(n_cp - 2, count + count % 2)
    own = latent_rows.T
    blocks = fetch(own, n_cp, dec_count)

    vmem = pl.BlockSpec(memory_space=pltpu.VMEM)
    hbm = pl.BlockSpec(memory_space=pltpu.HBM)
    params = pltpu.CompilerParams(vmem_limit_bytes=32 * 2**20)
    group, chunk = 2, 4
    inputs = (prompt_pages, decode_owner, slot_offset, own, queries, key_absorb, value_expand)
    combined, result, peaks, totals, sent_rows, bias, picked, filled, own_copy, value_copy = pl.pallas_call(
        functools.partial(own_kernel, n_cp, count, chunk, group, slot_count),
        in_specs=[hbm] * 7,
        out_specs=[vmem] * 10,
        out_shape=[
            jax.ShapeDtypeStruct((heads * rows, ROW), jnp.bfloat16),
            jax.ShapeDtypeStruct((heads * rows, VDIM), jnp.float32),
            jax.ShapeDtypeStruct((heads * rows, LANES), jnp.float32),
            jax.ShapeDtypeStruct((heads * rows, LANES), jnp.float32),
            jax.ShapeDtypeStruct((kept, -(-ROW // LANES) * LANES), jnp.bfloat16),
            jax.ShapeDtypeStruct((rows, count * rows), jnp.float32),
            jax.ShapeDtypeStruct((kept, (n_cp - 1) * rows), jnp.bfloat16),
            jax.ShapeDtypeStruct((8, LANES), jnp.float32),
            jax.ShapeDtypeStruct(own.shape, jnp.bfloat16),
            jax.ShapeDtypeStruct(value_expand.shape, jnp.bfloat16),
        ],
        scratch_shapes=[
            pltpu.SMEM(prompt_pages.shape, jnp.int32),
            pltpu.SMEM(decode_owner.shape, jnp.int32),
            pltpu.SMEM(slot_offset.shape, jnp.int32),
            pltpu.VMEM((rows, heads * HEAD), jnp.bfloat16),
            pltpu.VMEM((heads, NOPE, LAT), jnp.bfloat16),
            pltpu.VMEM((rows, LAT), jnp.bfloat16),
            pltpu.SemaphoreType.DMA((4 + 3 * (heads // chunk),)),
        ],
        cost_estimate=pl.CostEstimate(
            flops=2 * rows * heads * (2 * NOPE * LAT + rows * (ROW + VDIM)),
            bytes_accessed=2 * (queries.size + key_absorb.size + heads * rows * ROW),
            transcendentals=rows * heads * rows,
        ),
        compiler_params=params,
        name="own",
    )(*[pltpu.with_memory_space_constraint(x, pltpu.HBM) for x in inputs])
    sent_rows = lax.ppermute(sent_rows, "cp", [(c, (c + n_cp - 1) % n_cp) for c in range(n_cp)])
    blocks, picked = lax.optimization_barrier((blocks, picked))
    pieces = swap(blocks, dec_count)
    found, fetched_latents = pl.pallas_call(
        arrived_kernel,
        in_specs=[vmem] * (2 + len(blocks)),
        out_specs=[vmem] * 2,
        out_shape=[
            jax.ShapeDtypeStruct((kept, ROW), jnp.float32),
            jax.ShapeDtypeStruct((len(blocks) * rows, LAT), jnp.bfloat16),
        ],
        cost_estimate=pl.CostEstimate(flops=2**20, bytes_accessed=2**10, transcendentals=0),
        compiler_params=params,
        name="arrived",
    )(picked, own_copy, *blocks)

    def earlier_cost(some):
        return pl.CostEstimate(
            flops=2 * rows * some * (count * rows * (ROW + LAT) + LAT * VDIM),
            bytes_accessed=2 * (some * rows * (ROW + VDIM) + value_expand.size),
            transcendentals=rows * some * count * rows,
        )

    attended_shape = jax.ShapeDtypeStruct((rows, heads * VDIM), jnp.bfloat16)
    last_heads = heads // 4
    first_heads = heads - last_heads
    group = 4 if count <= 4 else 2
    inputs = (combined, result, peaks, totals, value_copy, bias)
    operands = (*inputs, fetched_latents, *pieces[:count // 2 * (1 + SWAP)])
    attended, keys, latents = pl.pallas_call(
        functools.partial(earlier_first_kernel, count, first_heads, group),
        in_specs=[vmem] * len(operands),
        out_specs=[hbm, vmem, vmem],
        out_shape=[
            attended_shape,
            jax.ShapeDtypeStruct((ROW, count * rows), jnp.bfloat16),
            jax.ShapeDtypeStruct((count * rows, LAT), jnp.bfloat16),
        ],
        scratch_shapes=[
            pltpu.VMEM((rows, first_heads * VDIM), jnp.bfloat16),
            pltpu.SemaphoreType.DMA((first_heads // group,)),
        ],
        cost_estimate=pl.CostEstimate(flops=2**20, bytes_accessed=2**10, transcendentals=0),
        compiler_params=params,
        name="earlier_first",
    )(*operands)
    sent_rows, keys = lax.optimization_barrier((sent_rows, keys))
    group = 2
    operands = (*inputs, keys, latents, picked, found, sent_rows, filled, *[part for i, part in enumerate(pieces) if i % (1 + SWAP)], attended)
    attended, page_cache, page_scales = pl.pallas_call(
        functools.partial(earlier_last_kernel, first_heads, last_heads, group),
        in_specs=[vmem] * (len(operands) - 1) + [hbm],
        out_specs=[hbm] * 3,
        out_shape=[
            attended_shape,
            jax.ShapeDtypeStruct((slot_count, PAGE, ROW), jnp.bfloat16),
            jax.ShapeDtypeStruct((slot_count, NBLK, PAGE), jnp.bfloat16),
        ],
        scratch_shapes=[
            pltpu.VMEM((rows, last_heads * VDIM), jnp.bfloat16),
            pltpu.VMEM((slot_count, PAGE, ROW), jnp.bfloat16),
            pltpu.VMEM((slot_count, NBLK, PAGE), jnp.bfloat16),
            pltpu.SemaphoreType.DMA((last_heads // group + 2,)),
        ],
        input_output_aliases={len(operands) - 1: 0},
        cost_estimate=earlier_cost(last_heads),
        compiler_params=params,
        name="earlier_last",
    )(*operands)
    page_cache = page_cache.reshape(1, 1, slot_count, PAGE, ROW)
    page_scales = page_scales.transpose(0, 2, 1).reshape(1, 1, slot_count, PAGE, NBLK)
    return attended, page_cache, page_scales


def solution(mesh):
    return jax.shard_map(
        on_device,
        mesh=mesh,
        in_specs=(
            P(("grp", "cp"), "dec"),
            P(("grp", "cp"), None),
            P("dec", None, None),
            P("dec", None, None),
            P("grp"),
            P("grp", None),
            P("grp"),
        ),
        out_specs=(
            P(("grp", "cp"), "dec"),
            P(("grp", "cp"), "dec", None, None, None),
            P(("grp", "cp"), "dec", None, None, None),
        ),
        check_vma=False,
    )
```

```python
import functools
import math

import jax
import jax.numpy as jnp
from jax import lax
from jax.experimental import pallas as pl
from jax.experimental.pallas import tpu as pltpu
from jax.sharding import PartitionSpec as P

LAT = 512
ROPE = 64
NOPE = 128
VDIM = 128
PAGE = 16
BLOCK = 128
NBLK = LAT // BLOCK
ROW = LAT + ROPE
HEAD = NOPE + ROPE
LANES = 128
SWAP = 2

masked_fill = -1e30
amax_epsilon = 1e-06
exp2_scale = math.log2(math.e) / math.sqrt(HEAD)

NT = (((1,), (1,)), ((), ()))


def prompt_starts(prompt_pages):
    starts = [jnp.int32(0)]
    for k in range(prompt_pages.shape[0] - 1):
        starts.append(starts[-1] + prompt_pages[k])
    return starts


def visible_bias(prompt_pages, rows, steps_back):
    first = lax.axis_index("cp") * rows
    token = first + lax.broadcasted_iota(jnp.int32, (rows, 1), 0)
    begin = jnp.zeros((rows, 1), jnp.int32)
    for start in prompt_starts(prompt_pages):
        begin = jnp.maximum(begin, jnp.where(start * PAGE <= token, start * PAGE, 0))
    spot = first - steps_back * rows + lax.broadcasted_iota(jnp.int32, (1, rows), 1)
    return jnp.where((spot >= begin) & (spot <= token), 0.0, masked_fill)


def swap_pair(position, n_cp):
    odd = lax.rem(lax.axis_index("dec"), 2)
    within = lax.rem(position + 1, 2)
    swapped = position - within + lax.rem(within + odd, 2)
    paired = (position >= 1) & (position <= (n_cp - 1) // 2 * 2)
    return jnp.where(paired, swapped, position)


def slot_pages(owner, slot_count, prompt_pages, decode_owner, slot_offset):
    prompts, width = decode_owner.shape
    cycle = width * lax.axis_size("dec") * slot_count
    starts = prompt_starts(prompt_pages)
    pages, start, offset, place = jnp.int32(0), jnp.int32(0), jnp.int32(0), jnp.int32(0)
    for k in range(prompts):
        for p in range(width):
            mine = decode_owner[k, p] == owner
            pages = jnp.where(mine, prompt_pages[k], pages)
            start = jnp.where(mine, starts[k], start)
            offset = jnp.where(mine, slot_offset[k], offset)
            place = jnp.where(mine, p, place)
    result = []
    for c in range(slot_count):
        turn = width * (lax.axis_index("dec") * slot_count + c) + place
        page = lax.rem(turn - offset + 2 * cycle, cycle)
        result.append((page < pages, start + page))
    return result


def row_picker(targets, columns):
    kept = len(targets) * PAGE
    row = lax.broadcasted_iota(jnp.int32, (kept, 1), 0)
    target = jnp.full((kept, 1), -1, jnp.int32)
    for c, column in enumerate(targets):
        target = jnp.where(row // PAGE == c, column + row % PAGE, target)
    column = lax.broadcasted_iota(jnp.int32, (1, columns), 1)
    return jnp.where(column == target, 1.0, 0.0).astype(jnp.bfloat16)


def head_values(latents, value_expand, h):
    both = jnp.concatenate([value_expand[h], value_expand[h + 1]], axis=1)
    return jnp.dot(latents, both, preferred_element_type=jnp.float32).astype(jnp.bfloat16)


def own_kernel(n_cp, count, chunks, group, slot_count, *refs):
    inputs, refs = refs[:7], refs[7:]
    combined, result, peaks, totals, sent_rows, bias, picked, filled, own, value_expand = refs[:10]
    prompt_pages, decode_owner, slot_offset, queries, key_absorb, latents, sems = refs[10:]
    pages_hbm, owner_hbm, offset_hbm, own_hbm, queries_hbm, absorb_hbm, expand_hbm = inputs
    rows = own.shape[1]
    heads = key_absorb.shape[0]
    small = [
        pltpu.make_async_copy(source, target, sems.at[i])
        for i, (source, target) in enumerate(zip(inputs[:4], (prompt_pages, decode_owner, slot_offset, own)))
    ]
    large = {}
    first = 0
    for chunk in chunks:
        at = 4 + 3 * len(large)
        some = pl.ds(first, chunk)
        wide = pl.ds(first * HEAD, chunk * HEAD)
        large[first] = (
            pltpu.make_async_copy(queries_hbm.at[:, wide], queries.at[:, wide], sems.at[at]),
            pltpu.make_async_copy(absorb_hbm.at[some], key_absorb.at[some], sems.at[at + 1]),
            pltpu.make_async_copy(expand_hbm.at[some], value_expand.at[some], sems.at[at + 2]),
        )
        first += chunk
    for copy in small:
        copy.start()
    for chunk_copies in large.values():
        for copy in chunk_copies:
            copy.start()
    steps = heads // group

    def absorb(g):
        for copy in large.get(g * group, ())[:2]:
            copy.wait()
        for h in range(g * group, (g + 1) * group):
            at = h * HEAD
            absorbed = jnp.dot(queries[:, at:at + NOPE], key_absorb[h], preferred_element_type=jnp.float32)
            combined[h * rows:(h + 1) * rows, :LAT] = absorbed.astype(jnp.bfloat16)
            combined[h * rows:(h + 1) * rows, LAT:] = queries[:, at + NOPE:at + HEAD]

    def score(g):
        return jnp.dot(combined[g * group * rows:(g + 1) * group * rows, :], own[...], preferred_element_type=jnp.float32)

    def value(g):
        for copy in large.get(g * group, ())[2:]:
            copy.wait()
        return [head_values(latents[...], value_expand, g * group + i) for i in range(0, group, 2)]

    def finish(g, scores, both):
        span = slice(g * group * rows, (g + 1) * group * rows)
        scores = (scores.reshape(group, rows, rows) + own_bias[None]).reshape(group * rows, rows)
        peak = jnp.max(scores, axis=1, keepdims=True)
        weights = jnp.exp2((scores - peak) * exp2_scale)
        total = jnp.sum(weights, axis=1, keepdims=True)
        weights = weights.astype(jnp.bfloat16)
        for i in range(group):
            mine = both[i // 2][:, i % 2 * VDIM:(i % 2 + 1) * VDIM]
            out = jnp.dot(weights[i * rows:(i + 1) * rows], mine, preferred_element_type=jnp.float32)
            result[(g * group + i) * rows:(g * group + i + 1) * rows, :] = out
        peaks[span, :] = jnp.broadcast_to(peak, (group * rows, LANES))
        totals[span, :] = jnp.broadcast_to(total, (group * rows, LANES))

    scores, both = {}, {}
    for step in range(steps + 2):
        if step < steps:
            absorb(step)
        if step == 0:
            small[3].wait()
            latents[...] = own[:LAT, :].T
        if step == 1:
            for copy in small[:3]:
                copy.wait()
            own_bias = visible_bias(prompt_pages, rows, 0)
            index_work(n_cp, count, slot_count, prompt_pages, decode_owner, slot_offset, own[...], sent_rows, bias, picked, filled)
        if 0 <= step - 1 < steps:
            scores[step - 1] = score(step - 1)
            both[step - 1] = value(step - 1)
        if 0 <= step - 2:
            finish(step - 2, scores.pop(step - 2), both.pop(step - 2))


def index_work(n_cp, count, slot_count, prompt_pages, decode_owner, slot_offset, block, sent_rows, bias, picked, filled):
    rows = block.shape[1]
    me = lax.axis_index("cp")
    behind = lax.rem(me + n_cp - 1, n_cp)
    targets = []
    for valid, page in slot_pages(behind, slot_count, prompt_pages, decode_owner, slot_offset):
        here = valid & (page * PAGE // rows == me)
        targets.append(jnp.where(here, lax.rem(page * PAGE, rows), -PAGE))
    choice = row_picker(targets, rows)
    sent = lax.dot_general(choice, block, NT, preferred_element_type=jnp.float32)
    kept = choice.shape[0]
    sent_rows[...] = jnp.zeros(sent_rows.shape, jnp.bfloat16)
    sent_rows[:kept, :ROW] = sent.astype(jnp.bfloat16)
    for b in range(count):
        bias[:, b * rows:(b + 1) * rows] = visible_bias(prompt_pages, rows, swap_pair(jnp.int32(b + 1), n_cp))
    targets = []
    lane = lax.broadcasted_iota(jnp.int32, filled.shape, 1)
    lane_filled = jnp.zeros(filled.shape, jnp.float32)
    for c, (valid, page) in enumerate(slot_pages(me, slot_count, prompt_pages, decode_owner, slot_offset)):
        source = page * PAGE // rows
        column = swap_pair(lax.rem(me - source + n_cp, n_cp), n_cp) * rows + lax.rem(page * PAGE, rows)
        targets.append(jnp.where(valid, column, -PAGE))
        lane_filled = jnp.where(lane // PAGE == c, valid.astype(jnp.float32), lane_filled)
    filled[...] = lane_filled
    picked[...] = row_picker(targets, (n_cp - 1) * rows)


def pick_rows(picked, index, block):
    rows = block.shape[1]
    return lax.dot_general(picked[:, index * rows:(index + 1) * rows], block, NT, preferred_element_type=jnp.float32)


def arrived_kernel(picked, own, *refs):
    blocks, (found, latents) = refs[:-2], refs[-2:]
    rows = own.shape[1]
    total = pick_rows(picked, 0, own[...])
    for i, block in enumerate(blocks):
        total = total + pick_rows(picked, 1 + 2 * i, block[...])
        latents[i * rows:(i + 1) * rows, :] = block[:LAT, :].T
    found[...] = total


def write_cache(rows, filled, page_cache, page_scales):
    slot_count = page_cache.shape[0]
    scales = []
    for b in range(NBLK):
        values = rows[:, b * BLOCK:(b + 1) * BLOCK]
        scale = jnp.max(jnp.abs(values), axis=1, keepdims=True) + amax_epsilon
        scale = scale.astype(jnp.bfloat16).astype(jnp.float32)
        encoded = (values / scale).astype(jnp.bfloat16)
        for c in range(slot_count):
            page_cache[c, :, b * BLOCK:(b + 1) * BLOCK] = encoded[c * PAGE:(c + 1) * PAGE]
        scales.append(scale)
    kept = rows.shape[0]
    which = lax.broadcasted_iota(jnp.int32, (kept, LANES), 1)
    table = jnp.zeros((kept, LANES), jnp.float32)
    for b, scale in enumerate(scales):
        table = jnp.where(which == b, scale, table)
    table = (table.T[:NBLK] * filled[:1, :kept]).astype(jnp.bfloat16)
    for c in range(slot_count):
        page_cache[c, :, LAT:] = rows[c * PAGE:(c + 1) * PAGE, LAT:].astype(jnp.bfloat16)
        page_scales[c] = table[:, c * PAGE:(c + 1) * PAGE]


def earlier_kernel(count, group, *refs):
    combined, own_result, peaks, totals, value_expand, bias, fetched_latents = refs[:7]
    arrived, (result, keys, latents) = refs[7:-3], refs[-3:]
    rows, width = bias.shape
    heads = value_expand.shape[0]
    steps = heads // group

    def span(g):
        at = g * group * rows
        return slice(at, at + group * rows)

    def score(g):
        scores = jnp.dot(combined[span(g), :], keys[...], preferred_element_type=jnp.float32)
        return (scores.reshape(group, rows, width) + bias[...][None]).reshape(group * rows, width)

    def weigh(g, scores):
        old_peak = peaks[span(g), :]
        parts = [scores[:, b:b + LANES] for b in range(0, width, LANES)]
        peak = jnp.maximum(old_peak, jnp.max(functools.reduce(jnp.maximum, parts), axis=1, keepdims=True))
        parts = [jnp.exp2((part - peak) * exp2_scale) for part in parts]
        total = jnp.sum(functools.reduce(jnp.add, parts), axis=1, keepdims=True)
        factor = jnp.exp2((old_peak - peak) * exp2_scale)
        inverse = 1.0 / (totals[span(g), :] * factor + total)
        weights = jnp.concatenate([part.astype(jnp.bfloat16) for part in parts], axis=1)
        return weights, factor * inverse, inverse

    def mix(g, weights):
        return jnp.dot(weights, latents[...], preferred_element_type=jnp.float32).astype(jnp.bfloat16)

    def finish(g, mixed, factor, inverse):
        for i in range(group):
            part = slice(i * rows, (i + 1) * rows)
            h = g * group + i
            out = jnp.dot(mixed[part], value_expand[h], preferred_element_type=jnp.float32)
            out = own_result[h * rows:(h + 1) * rows, :] * factor[part] + out * inverse[part]
            result[:, h * VDIM:(h + 1) * VDIM] = out.astype(jnp.bfloat16)

    @pl.when(lax.axis_index("cp") == 0)
    def _():
        for h in range(heads):
            part = slice(h * rows, (h + 1) * rows)
            result[:, h * VDIM:(h + 1) * VDIM] = (own_result[part, :] / totals[part, :]).astype(jnp.bfloat16)

    @pl.when(lax.axis_index("cp") > 0)
    def _():
        for i in range(count // 2):
            fetched, *parts = arrived[i * (1 + SWAP):(i + 1) * (1 + SWAP)]
            swapped = jnp.concatenate([part[...] for part in parts], axis=0)
            at = 2 * i * rows
            keys[:, at:at + rows] = fetched[...]
            keys[:, at + rows:at + 2 * rows] = swapped
            latents[at:at + rows, :] = fetched_latents[i * rows:(i + 1) * rows, :]
            latents[at + rows:at + 2 * rows, :] = swapped[:LAT].T
        scores, weights, mixed = {}, {}, {}
        for step in range(steps + 2):
            if step < steps:
                scores[step] = score(step)
            if 0 <= step - 2:
                finish(step - 2, mixed.pop(step - 2), *weights.pop(step - 2)[1:])
            if 0 <= step - 1 < steps:
                weights[step - 1] = weigh(step - 1, scores.pop(step - 1))
                mixed[step - 1] = mix(step - 1, weights[step - 1][0])


def store_kernel(result, picked, found, sent_rows, filled, *refs):
    swapped, (attended, page_cache, page_scales, cache_buf, scale_buf, sems) = refs[:-6], refs[-6:]
    copies = [
        pltpu.make_async_copy(source, target, sems.at[i])
        for i, (source, target) in enumerate(((result, attended), (cache_buf, page_cache), (scale_buf, page_scales)))
    ]
    copies[0].start()
    rows = found[...] + sent_rows[:found.shape[0], :ROW].astype(jnp.float32)
    for i in range(len(swapped) // SWAP):
        block = jnp.concatenate([part[...] for part in swapped[i * SWAP:(i + 1) * SWAP]], axis=0)
        rows = rows + pick_rows(picked, 2 + 2 * i, block)
    write_cache(rows, filled, cache_buf, scale_buf)
    for copy in copies[1:]:
        copy.start()
    for copy in copies:
        copy.wait()


def fetch(own, n_cp, n_dec):
    blocks = []
    for step in range(1, n_cp - 1, 2):
        pairs = [(c * n_dec + e, (c + step + e % 2) % n_cp * n_dec + e) for c in range(n_cp) for e in range(n_dec)]
        blocks.append(lax.ppermute(own, ("cp", "dec"), pairs))
    return blocks


def swap(blocks, n_dec):
    pieces = []
    for block in blocks:
        parts = [block[at:at + ROW // SWAP] for at in range(0, ROW, ROW // SWAP)]
        pieces += [block] + [lax.ppermute(part, "dec", [(e, e ^ 1) for e in range(n_dec)]) for part in parts]
    return pieces


def on_device(queries, latent_rows, key_absorb, value_expand, prompt_pages, decode_owner, slot_offset):
    n_cp = lax.axis_size("cp")
    dec_count = lax.axis_size("dec")
    heads = key_absorb.shape[0]
    rows = latent_rows.shape[0]
    prompts, width = decode_owner.shape
    slot_count = 3 * (rows // PAGE) // (2 * dec_count)
    kept = slot_count * PAGE
    reach = width * dec_count * slot_count * PAGE
    count = -(-reach // rows) - (1 if prompts == 2 else 0)
    count = min(n_cp - 2, count + count % 2)
    own = latent_rows.T
    blocks = fetch(own, n_cp, dec_count)

    vmem = pl.BlockSpec(memory_space=pltpu.VMEM)
    hbm = pl.BlockSpec(memory_space=pltpu.HBM)
    params = pltpu.CompilerParams(vmem_limit_bytes=32 * 2**20)
    group, chunks = 2, (heads // 8, heads // 8, heads // 4, heads // 2)
    inputs = (prompt_pages, decode_owner, slot_offset, own, queries, key_absorb, value_expand)
    combined, result, peaks, totals, sent_rows, bias, picked, filled, own_copy, value_copy = pl.pallas_call(
        functools.partial(own_kernel, n_cp, count, chunks, group, slot_count),
        in_specs=[hbm] * 7,
        out_specs=[vmem] * 10,
        out_shape=[
            jax.ShapeDtypeStruct((heads * rows, ROW), jnp.bfloat16),
            jax.ShapeDtypeStruct((heads * rows, VDIM), jnp.float32),
            jax.ShapeDtypeStruct((heads * rows, LANES), jnp.float32),
            jax.ShapeDtypeStruct((heads * rows, LANES), jnp.float32),
            jax.ShapeDtypeStruct((kept + PAGE, -(-ROW // LANES) * LANES), jnp.bfloat16),
            jax.ShapeDtypeStruct((rows, count * rows), jnp.float32),
            jax.ShapeDtypeStruct((kept, (n_cp - 1) * rows), jnp.bfloat16),
            jax.ShapeDtypeStruct((8, LANES), jnp.float32),
            jax.ShapeDtypeStruct(own.shape, jnp.bfloat16),
            jax.ShapeDtypeStruct(value_expand.shape, jnp.bfloat16),
        ],
        scratch_shapes=[
            pltpu.SMEM(prompt_pages.shape, jnp.int32),
            pltpu.SMEM(decode_owner.shape, jnp.int32),
            pltpu.SMEM(slot_offset.shape, jnp.int32),
            pltpu.VMEM((rows, heads * HEAD), jnp.bfloat16),
            pltpu.VMEM((heads, NOPE, LAT), jnp.bfloat16),
            pltpu.VMEM((rows, LAT), jnp.bfloat16),
            pltpu.SemaphoreType.DMA((4 + 3 * len(chunks),)),
        ],
        cost_estimate=pl.CostEstimate(
            flops=2 * rows * heads * (2 * NOPE * LAT + rows * (ROW + VDIM)),
            bytes_accessed=2 * (queries.size + key_absorb.size + heads * rows * ROW),
            transcendentals=rows * heads * rows,
        ),
        compiler_params=params,
        name="own",
    )(*[pltpu.with_memory_space_constraint(x, pltpu.HBM) for x in inputs])
    sent_rows = lax.ppermute(sent_rows, "cp", [(c, (c + n_cp - 1) % n_cp) for c in range(n_cp)])
    blocks, picked = lax.optimization_barrier((blocks, picked))
    pieces = swap(blocks, dec_count)
    found, fetched_latents = pl.pallas_call(
        arrived_kernel,
        in_specs=[vmem] * (2 + len(blocks)),
        out_specs=[vmem] * 2,
        out_shape=[
            jax.ShapeDtypeStruct((kept, ROW), jnp.float32),
            jax.ShapeDtypeStruct((len(blocks) * rows, LAT), jnp.bfloat16),
        ],
        cost_estimate=pl.CostEstimate(flops=2**20, bytes_accessed=2**10, transcendentals=0),
        compiler_params=params,
        name="arrived",
    )(picked, own_copy, *blocks)

    group = 4 if count <= 4 else 2
    operands = (combined, result, peaks, totals, value_copy, bias, fetched_latents, *pieces[:count // 2 * (1 + SWAP)])
    attended = pl.pallas_call(
        functools.partial(earlier_kernel, count, group),
        in_specs=[vmem] * len(operands),
        out_specs=vmem,
        out_shape=jax.ShapeDtypeStruct((rows, heads * VDIM), jnp.bfloat16),
        scratch_shapes=[
            pltpu.VMEM((ROW, count * rows), jnp.bfloat16),
            pltpu.VMEM((count * rows, LAT), jnp.bfloat16),
        ],
        cost_estimate=pl.CostEstimate(flops=2**20, bytes_accessed=2**10, transcendentals=0),
        compiler_params=params,
        name="earlier",
    )(*operands)
    sent_rows, attended = lax.optimization_barrier((sent_rows, attended))
    operands = (attended, picked, found, sent_rows, filled, *[part for i, part in enumerate(pieces) if i % (1 + SWAP)])
    attended, page_cache, page_scales = pl.pallas_call(
        store_kernel,
        in_specs=[vmem] * len(operands),
        out_specs=[hbm] * 3,
        out_shape=[
            jax.ShapeDtypeStruct((rows, heads * VDIM), jnp.bfloat16),
            jax.ShapeDtypeStruct((slot_count, PAGE, ROW), jnp.bfloat16),
            jax.ShapeDtypeStruct((slot_count, NBLK, PAGE), jnp.bfloat16),
        ],
        scratch_shapes=[
            pltpu.VMEM((slot_count, PAGE, ROW), jnp.bfloat16),
            pltpu.VMEM((slot_count, NBLK, PAGE), jnp.bfloat16),
            pltpu.SemaphoreType.DMA((3,)),
        ],
        cost_estimate=pl.CostEstimate(flops=2**20, bytes_accessed=2**10, transcendentals=0),
        compiler_params=params,
        name="store",
    )(*operands)
    page_cache = page_cache.reshape(1, 1, slot_count, PAGE, ROW)
    page_scales = page_scales.transpose(0, 2, 1).reshape(1, 1, slot_count, PAGE, NBLK)
    return attended, page_cache, page_scales


def solution(mesh):
    return jax.shard_map(
        on_device,
        mesh=mesh,
        in_specs=(
            P(("grp", "cp"), "dec"),
            P(("grp", "cp"), None),
            P("dec", None, None),
            P("dec", None, None),
            P("grp"),
            P("grp", None),
            P("grp"),
        ),
        out_specs=(
            P(("grp", "cp"), "dec"),
            P(("grp", "cp"), "dec", None, None, None),
            P(("grp", "cp"), "dec", None, None, None),
        ),
        check_vma=False,
    )
```

```python
import functools
import math

import jax
import jax.numpy as jnp
from jax import lax
from jax.experimental import pallas as pl
from jax.experimental.pallas import tpu as pltpu
from jax.sharding import PartitionSpec as P

LAT = 512
ROPE = 64
NOPE = 128
VDIM = 128
PAGE = 16
BLOCK = 128
NBLK = LAT // BLOCK
ROW = LAT + ROPE
HEAD = NOPE + ROPE
LANES = 128
SWAP = 2

masked_fill = -1e30
amax_epsilon = 1e-06
exp2_scale = math.log2(math.e) / math.sqrt(HEAD)

NT = (((1,), (1,)), ((), ()))


def prompt_starts(prompt_pages):
    starts = [jnp.int32(0)]
    for k in range(prompt_pages.shape[0] - 1):
        starts.append(starts[-1] + prompt_pages[k])
    return starts


def visible_bias(prompt_pages, rows, steps_back):
    first = lax.axis_index("cp") * rows
    token = first + lax.broadcasted_iota(jnp.int32, (rows, 1), 0)
    begin = jnp.zeros((rows, 1), jnp.int32)
    for start in prompt_starts(prompt_pages):
        begin = jnp.maximum(begin, jnp.where(start * PAGE <= token, start * PAGE, 0))
    spot = first - steps_back * rows + lax.broadcasted_iota(jnp.int32, (1, rows), 1)
    return jnp.where((spot >= begin) & (spot <= token), 0.0, masked_fill)


def swap_pair(position, n_cp):
    odd = lax.rem(lax.axis_index("dec"), 2)
    within = lax.rem(position + 1, 2)
    swapped = position - within + lax.rem(within + odd, 2)
    paired = (position >= 1) & (position <= (n_cp - 1) // 2 * 2)
    return jnp.where(paired, swapped, position)


def slot_pages(owner, slot_count, prompt_pages, decode_owner, slot_offset):
    prompts, width = decode_owner.shape
    cycle = width * lax.axis_size("dec") * slot_count
    starts = prompt_starts(prompt_pages)
    pages, start, offset, place = jnp.int32(0), jnp.int32(0), jnp.int32(0), jnp.int32(0)
    for k in range(prompts):
        for p in range(width):
            mine = decode_owner[k, p] == owner
            pages = jnp.where(mine, prompt_pages[k], pages)
            start = jnp.where(mine, starts[k], start)
            offset = jnp.where(mine, slot_offset[k], offset)
            place = jnp.where(mine, p, place)
    result = []
    for c in range(slot_count):
        turn = width * (lax.axis_index("dec") * slot_count + c) + place
        page = lax.rem(turn - offset + 2 * cycle, cycle)
        result.append((page < pages, start + page))
    return result


def row_picker(targets, columns):
    kept = len(targets) * PAGE
    row = lax.broadcasted_iota(jnp.int32, (kept, 1), 0)
    target = jnp.full((kept, 1), -1, jnp.int32)
    for c, column in enumerate(targets):
        target = jnp.where(row // PAGE == c, column + row % PAGE, target)
    column = lax.broadcasted_iota(jnp.int32, (1, columns), 1)
    return jnp.where(column == target, 1.0, 0.0).astype(jnp.bfloat16)


def head_values(latents, value_expand, h):
    both = jnp.concatenate([value_expand[h], value_expand[h + 1]], axis=1)
    return jnp.dot(latents, both, preferred_element_type=jnp.float32).astype(jnp.bfloat16)


def own_kernel(n_cp, count, chunks, group, slot_count, *refs):
    inputs, refs = refs[:7], refs[7:]
    combined, result, peaks, totals, sent_rows, bias, picked, filled, own, value_expand = refs[:10]
    prompt_pages, decode_owner, slot_offset, queries, key_absorb, latents, sems = refs[10:]
    pages_hbm, owner_hbm, offset_hbm, own_hbm, queries_hbm, absorb_hbm, expand_hbm = inputs
    rows = own.shape[1]
    heads = key_absorb.shape[0]
    small = [
        pltpu.make_async_copy(source, target, sems.at[i])
        for i, (source, target) in enumerate(zip(inputs[:4], (prompt_pages, decode_owner, slot_offset, own)))
    ]
    large = {}
    first = 0
    for chunk in chunks:
        at = 4 + 3 * len(large)
        some = pl.ds(first, chunk)
        wide = pl.ds(first * HEAD, chunk * HEAD)
        large[first] = (
            pltpu.make_async_copy(queries_hbm.at[:, wide], queries.at[:, wide], sems.at[at]),
            pltpu.make_async_copy(absorb_hbm.at[some], key_absorb.at[some], sems.at[at + 1]),
            pltpu.make_async_copy(expand_hbm.at[some], value_expand.at[some], sems.at[at + 2]),
        )
        first += chunk
    for copy in small:
        copy.start()
    for chunk_copies in large.values():
        for copy in chunk_copies:
            copy.start()
    steps = heads // group

    def absorb(g):
        for copy in large.get(g * group, ())[:2]:
            copy.wait()
        for h in range(g * group, (g + 1) * group):
            at = h * HEAD
            absorbed = jnp.dot(queries[:, at:at + NOPE], key_absorb[h], preferred_element_type=jnp.float32)
            combined[h * rows:(h + 1) * rows, :LAT] = absorbed.astype(jnp.bfloat16)
            combined[h * rows:(h + 1) * rows, LAT:] = queries[:, at + NOPE:at + HEAD]

    def score(g):
        return jnp.dot(combined[g * group * rows:(g + 1) * group * rows, :], own[...], preferred_element_type=jnp.float32)

    def value(g):
        for copy in large.get(g * group, ())[2:]:
            copy.wait()
        return [head_values(latents[...], value_expand, g * group + i) for i in range(0, group, 2)]

    def finish(g, scores, both):
        span = slice(g * group * rows, (g + 1) * group * rows)
        scores = (scores.reshape(group, rows, rows) + own_bias[None]).reshape(group * rows, rows)
        peak = jnp.max(scores, axis=1, keepdims=True)
        weights = jnp.exp2((scores - peak) * exp2_scale)
        total = jnp.sum(weights, axis=1, keepdims=True)
        weights = weights.astype(jnp.bfloat16)
        for i in range(group):
            mine = both[i // 2][:, i % 2 * VDIM:(i % 2 + 1) * VDIM]
            out = jnp.dot(weights[i * rows:(i + 1) * rows], mine, preferred_element_type=jnp.float32)
            result[(g * group + i) * rows:(g * group + i + 1) * rows, :] = out
        peaks[span, :] = jnp.broadcast_to(peak, (group * rows, LANES))
        totals[span, :] = jnp.broadcast_to(total, (group * rows, LANES))

    scores, both = {}, {}
    for step in range(steps + 2):
        if step < steps:
            absorb(step)
        if step == 0:
            small[3].wait()
            latents[...] = own[:LAT, :].T
        if step == 1:
            for copy in small[:3]:
                copy.wait()
            own_bias = visible_bias(prompt_pages, rows, 0)
            index_work(n_cp, count, slot_count, prompt_pages, decode_owner, slot_offset, own[...], sent_rows, bias, picked, filled)
        if 0 <= step - 1 < steps:
            scores[step - 1] = score(step - 1)
            both[step - 1] = value(step - 1)
        if 0 <= step - 2:
            finish(step - 2, scores.pop(step - 2), both.pop(step - 2))


def index_work(n_cp, count, slot_count, prompt_pages, decode_owner, slot_offset, block, sent_rows, bias, picked, filled):
    rows = block.shape[1]
    me = lax.axis_index("cp")
    behind = lax.rem(me + n_cp - 1, n_cp)
    targets = []
    for valid, page in slot_pages(behind, slot_count, prompt_pages, decode_owner, slot_offset):
        here = valid & (page * PAGE // rows == me)
        targets.append(jnp.where(here, lax.rem(page * PAGE, rows), -PAGE))
    choice = row_picker(targets, rows)
    sent = lax.dot_general(choice, block, NT, preferred_element_type=jnp.float32)
    kept = choice.shape[0]
    sent_rows[...] = jnp.zeros(sent_rows.shape, jnp.bfloat16)
    sent_rows[:kept, :ROW] = sent.astype(jnp.bfloat16)
    for b in range(count):
        bias[:, b * rows:(b + 1) * rows] = visible_bias(prompt_pages, rows, swap_pair(jnp.int32(b + 1), n_cp))
    targets = []
    lane = lax.broadcasted_iota(jnp.int32, filled.shape, 1)
    lane_filled = jnp.zeros(filled.shape, jnp.float32)
    for c, (valid, page) in enumerate(slot_pages(me, slot_count, prompt_pages, decode_owner, slot_offset)):
        source = page * PAGE // rows
        column = swap_pair(lax.rem(me - source + n_cp, n_cp), n_cp) * rows + lax.rem(page * PAGE, rows)
        targets.append(jnp.where(valid, column, -PAGE))
        lane_filled = jnp.where(lane // PAGE == c, valid.astype(jnp.float32), lane_filled)
    filled[...] = lane_filled
    picked[...] = row_picker(targets, (n_cp - 1) * rows)


def pick_rows(picked, index, block):
    rows = block.shape[1]
    return lax.dot_general(picked[:, index * rows:(index + 1) * rows], block, NT, preferred_element_type=jnp.float32)


def arrived_kernel(picked, own, *refs):
    blocks, (found, latents) = refs[:-2], refs[-2:]
    rows = own.shape[1]
    total = pick_rows(picked, 0, own[...])
    for i, block in enumerate(blocks):
        total = total + pick_rows(picked, 1 + 2 * i, block[...])
        latents[i * rows:(i + 1) * rows, :] = block[:LAT, :].T
    found[...] = total


def write_cache(rows, filled, page_cache, page_scales):
    slot_count = page_cache.shape[0]
    scales = []
    for b in range(NBLK):
        values = rows[:, b * BLOCK:(b + 1) * BLOCK]
        scale = jnp.max(jnp.abs(values), axis=1, keepdims=True) + amax_epsilon
        scale = scale.astype(jnp.bfloat16).astype(jnp.float32)
        encoded = (values / scale).astype(jnp.bfloat16)
        for c in range(slot_count):
            page_cache[c, :, b * BLOCK:(b + 1) * BLOCK] = encoded[c * PAGE:(c + 1) * PAGE]
        scales.append(scale)
    kept = rows.shape[0]
    which = lax.broadcasted_iota(jnp.int32, (kept, LANES), 1)
    table = jnp.zeros((kept, LANES), jnp.float32)
    for b, scale in enumerate(scales):
        table = jnp.where(which == b, scale, table)
    table = (table.T[:NBLK] * filled[:1, :kept]).astype(jnp.bfloat16)
    for c in range(slot_count):
        page_cache[c, :, LAT:] = rows[c * PAGE:(c + 1) * PAGE, LAT:].astype(jnp.bfloat16)
        page_scales[c] = table[:, c * PAGE:(c + 1) * PAGE]


def earlier_kernel(count, group, *refs):
    combined, own_result, peaks, totals, value_expand, bias, fetched_latents, picked, found = refs[:9]
    arrived, (result, found_more, keys, latents) = refs[9:-4], refs[-4:]
    rows, width = bias.shape
    heads = value_expand.shape[0]
    steps = heads // group

    def span(g):
        at = g * group * rows
        return slice(at, at + group * rows)

    def score(g):
        scores = jnp.dot(combined[span(g), :], keys[...], preferred_element_type=jnp.float32)
        return (scores.reshape(group, rows, width) + bias[...][None]).reshape(group * rows, width)

    def weigh(g, scores):
        old_peak = peaks[span(g), :]
        parts = [scores[:, b:b + LANES] for b in range(0, width, LANES)]
        peak = jnp.maximum(old_peak, jnp.max(functools.reduce(jnp.maximum, parts), axis=1, keepdims=True))
        parts = [jnp.exp2((part - peak) * exp2_scale) for part in parts]
        total = jnp.sum(functools.reduce(jnp.add, parts), axis=1, keepdims=True)
        factor = jnp.exp2((old_peak - peak) * exp2_scale)
        inverse = 1.0 / (totals[span(g), :] * factor + total)
        weights = jnp.concatenate([part.astype(jnp.bfloat16) for part in parts], axis=1)
        return weights, factor * inverse, inverse

    def mix(g, weights):
        return jnp.dot(weights, latents[...], preferred_element_type=jnp.float32).astype(jnp.bfloat16)

    def finish(g, mixed, factor, inverse):
        for i in range(group):
            part = slice(i * rows, (i + 1) * rows)
            h = g * group + i
            out = jnp.dot(mixed[part], value_expand[h], preferred_element_type=jnp.float32)
            out = own_result[h * rows:(h + 1) * rows, :] * factor[part] + out * inverse[part]
            result[:, h * VDIM:(h + 1) * VDIM] = out.astype(jnp.bfloat16)

    def pick_swapped():
        total = found[...]
        for i in range(len(arrived) // (1 + SWAP)):
            parts = arrived[i * (1 + SWAP) + 1:(i + 1) * (1 + SWAP)]
            total = total + pick_rows(picked, 2 + 2 * i, jnp.concatenate([part[...] for part in parts], axis=0))
        found_more[...] = total

    @pl.when(lax.axis_index("cp") == 0)
    def _():
        pick_swapped()
        for h in range(heads):
            part = slice(h * rows, (h + 1) * rows)
            result[:, h * VDIM:(h + 1) * VDIM] = (own_result[part, :] / totals[part, :]).astype(jnp.bfloat16)

    @pl.when(lax.axis_index("cp") > 0)
    def _():
        for i in range(count // 2):
            fetched, *parts = arrived[i * (1 + SWAP):(i + 1) * (1 + SWAP)]
            swapped = jnp.concatenate([part[...] for part in parts], axis=0)
            at = 2 * i * rows
            keys[:, at:at + rows] = fetched[...]
            keys[:, at + rows:at + 2 * rows] = swapped
            latents[at:at + rows, :] = fetched_latents[i * rows:(i + 1) * rows, :]
            latents[at + rows:at + 2 * rows, :] = swapped[:LAT].T
        scores, weights, mixed = {}, {}, {}
        for step in range(steps + 2):
            if step < steps:
                scores[step] = score(step)
            if step == 1:
                pick_swapped()
            if 0 <= step - 2:
                finish(step - 2, mixed.pop(step - 2), *weights.pop(step - 2)[1:])
            if 0 <= step - 1 < steps:
                weights[step - 1] = weigh(step - 1, scores.pop(step - 1))
                mixed[step - 1] = mix(step - 1, weights[step - 1][0])


def store_kernel(result, found, sent_rows, filled, attended, page_cache, page_scales, cache_buf, scale_buf, sems):
    count = sems.shape[0] - 2
    wide = result.shape[1] // count
    copies = []
    for i in range(count):
        some = pl.ds(i * wide, wide)
        copies.append(pltpu.make_async_copy(result.at[:, some], attended.at[:, some], sems.at[i]))
        copies[-1].start()
    rows = found[...] + sent_rows[:found.shape[0], :ROW].astype(jnp.float32)
    write_cache(rows, filled, cache_buf, scale_buf)
    for i, (source, target) in enumerate(((cache_buf, page_cache), (scale_buf, page_scales))):
        copies.append(pltpu.make_async_copy(source, target, sems.at[count + i]))
        copies[-1].start()
    for copy in copies:
        copy.wait()


def fetch(own, n_cp, n_dec):
    blocks = []
    for step in range(1, n_cp - 1, 2):
        pairs = [(c * n_dec + e, (c + step + e % 2) % n_cp * n_dec + e) for c in range(n_cp) for e in range(n_dec)]
        blocks.append(lax.ppermute(own, ("cp", "dec"), pairs))
    return blocks


def swap(blocks, n_dec):
    pieces = []
    for block in blocks:
        parts = [block[at:at + ROW // SWAP] for at in range(0, ROW, ROW // SWAP)]
        pieces += [block] + [lax.ppermute(part, "dec", [(e, e ^ 1) for e in range(n_dec)]) for part in parts]
    return pieces


def on_device(queries, latent_rows, key_absorb, value_expand, prompt_pages, decode_owner, slot_offset):
    n_cp = lax.axis_size("cp")
    dec_count = lax.axis_size("dec")
    heads = key_absorb.shape[0]
    rows = latent_rows.shape[0]
    prompts, width = decode_owner.shape
    slot_count = 3 * (rows // PAGE) // (2 * dec_count)
    kept = slot_count * PAGE
    reach = width * dec_count * slot_count * PAGE
    count = -(-reach // rows) - (1 if prompts == 2 else 0)
    count = min(n_cp - 2, count + count % 2)
    own = latent_rows.T
    blocks = fetch(own, n_cp, dec_count)

    vmem = pl.BlockSpec(memory_space=pltpu.VMEM)
    hbm = pl.BlockSpec(memory_space=pltpu.HBM)
    params = pltpu.CompilerParams(vmem_limit_bytes=32 * 2**20)
    group, chunks = 4, (heads // 4, heads // 4, heads // 2)
    inputs = (prompt_pages, decode_owner, slot_offset, own, queries, key_absorb, value_expand)
    combined, result, peaks, totals, sent_rows, bias, picked, filled, own_copy, value_copy = pl.pallas_call(
        functools.partial(own_kernel, n_cp, count, chunks, group, slot_count),
        in_specs=[hbm] * 7,
        out_specs=[vmem] * 10,
        out_shape=[
            jax.ShapeDtypeStruct((heads * rows, ROW), jnp.bfloat16),
            jax.ShapeDtypeStruct((heads * rows, VDIM), jnp.float32),
            jax.ShapeDtypeStruct((heads * rows, LANES), jnp.float32),
            jax.ShapeDtypeStruct((heads * rows, LANES), jnp.float32),
            jax.ShapeDtypeStruct((kept + PAGE, -(-ROW // LANES) * LANES), jnp.bfloat16),
            jax.ShapeDtypeStruct((rows, count * rows), jnp.float32),
            jax.ShapeDtypeStruct((kept, (n_cp - 1) * rows), jnp.bfloat16),
            jax.ShapeDtypeStruct((8, LANES), jnp.float32),
            jax.ShapeDtypeStruct(own.shape, jnp.bfloat16),
            jax.ShapeDtypeStruct(value_expand.shape, jnp.bfloat16),
        ],
        scratch_shapes=[
            pltpu.SMEM(prompt_pages.shape, jnp.int32),
            pltpu.SMEM(decode_owner.shape, jnp.int32),
            pltpu.SMEM(slot_offset.shape, jnp.int32),
            pltpu.VMEM((rows, heads * HEAD), jnp.bfloat16),
            pltpu.VMEM((heads, NOPE, LAT), jnp.bfloat16),
            pltpu.VMEM((rows, LAT), jnp.bfloat16),
            pltpu.SemaphoreType.DMA((4 + 3 * len(chunks),)),
        ],
        cost_estimate=pl.CostEstimate(
            flops=2 * rows * heads * (2 * NOPE * LAT + rows * (ROW + VDIM)),
            bytes_accessed=2 * (queries.size + key_absorb.size + heads * rows * ROW),
            transcendentals=rows * heads * rows,
        ),
        compiler_params=params,
        name="own",
    )(*[pltpu.with_memory_space_constraint(x, pltpu.HBM) for x in inputs])
    sent_rows = lax.ppermute(sent_rows, "cp", [(c, (c + n_cp - 1) % n_cp) for c in range(n_cp)])
    blocks, picked = lax.optimization_barrier((blocks, picked))
    pieces = swap(blocks, dec_count)
    found, fetched_latents = pl.pallas_call(
        arrived_kernel,
        in_specs=[vmem] * (2 + len(blocks)),
        out_specs=[vmem] * 2,
        out_shape=[
            jax.ShapeDtypeStruct((kept, ROW), jnp.float32),
            jax.ShapeDtypeStruct((len(blocks) * rows, LAT), jnp.bfloat16),
        ],
        cost_estimate=pl.CostEstimate(flops=2**20, bytes_accessed=2**10, transcendentals=0),
        compiler_params=params,
        name="arrived",
    )(picked, own_copy, *blocks)

    group = 8 if count <= 4 else 2
    operands = (combined, result, peaks, totals, value_copy, bias, fetched_latents, picked, found, *pieces)
    attended, found = pl.pallas_call(
        functools.partial(earlier_kernel, count, group),
        in_specs=[vmem] * len(operands),
        out_specs=[vmem] * 2,
        out_shape=[
            jax.ShapeDtypeStruct((rows, heads * VDIM), jnp.bfloat16),
            jax.ShapeDtypeStruct((kept, ROW), jnp.float32),
        ],
        scratch_shapes=[
            pltpu.VMEM((ROW, count * rows), jnp.bfloat16),
            pltpu.VMEM((count * rows, LAT), jnp.bfloat16),
        ],
        cost_estimate=pl.CostEstimate(flops=2**20, bytes_accessed=2**10, transcendentals=0),
        compiler_params=params,
        name="earlier",
    )(*operands)
    sent_rows, attended = lax.optimization_barrier((sent_rows, attended))
    operands = (attended, found, sent_rows, filled)
    attended, page_cache, page_scales = pl.pallas_call(
        store_kernel,
        in_specs=[vmem] * len(operands),
        out_specs=[hbm] * 3,
        out_shape=[
            jax.ShapeDtypeStruct((rows, heads * VDIM), jnp.bfloat16),
            jax.ShapeDtypeStruct((slot_count, PAGE, ROW), jnp.bfloat16),
            jax.ShapeDtypeStruct((slot_count, NBLK, PAGE), jnp.bfloat16),
        ],
        scratch_shapes=[
            pltpu.VMEM((slot_count, PAGE, ROW), jnp.bfloat16),
            pltpu.VMEM((slot_count, NBLK, PAGE), jnp.bfloat16),
            pltpu.SemaphoreType.DMA((4 + 2,)),
        ],
        cost_estimate=pl.CostEstimate(flops=2**20, bytes_accessed=2**10, transcendentals=0),
        compiler_params=params,
        name="store",
    )(*operands)
    page_cache = page_cache.reshape(1, 1, slot_count, PAGE, ROW)
    page_scales = page_scales.transpose(0, 2, 1).reshape(1, 1, slot_count, PAGE, NBLK)
    return attended, page_cache, page_scales


def solution(mesh):
    return jax.shard_map(
        on_device,
        mesh=mesh,
        in_specs=(
            P(("grp", "cp"), "dec"),
            P(("grp", "cp"), None),
            P("dec", None, None),
            P("dec", None, None),
            P("grp"),
            P("grp", None),
            P("grp"),
        ),
        out_specs=(
            P(("grp", "cp"), "dec"),
            P(("grp", "cp"), "dec", None, None, None),
            P(("grp", "cp"), "dec", None, None, None),
        ),
        check_vma=False,
    )
```

```python
import functools
import math

import jax
import jax.numpy as jnp
from jax import lax
from jax.experimental import pallas as pl
from jax.experimental.pallas import tpu as pltpu
from jax.sharding import PartitionSpec as P

LAT = 512
ROPE = 64
NOPE = 128
VDIM = 128
PAGE = 16
BLOCK = 128
NBLK = LAT // BLOCK
ROW = LAT + ROPE
HEAD = NOPE + ROPE
LANES = 128
SWAP = 2

masked_fill = -1e30
amax_epsilon = 1e-06
exp2_scale = math.log2(math.e) / math.sqrt(HEAD)

NT = (((1,), (1,)), ((), ()))


def prompt_starts(prompt_pages):
    starts = [jnp.int32(0)]
    for k in range(prompt_pages.shape[0] - 1):
        starts.append(starts[-1] + prompt_pages[k])
    return starts


def visible_bias(prompt_pages, rows, steps_back):
    first = lax.axis_index("cp") * rows
    token = first + lax.broadcasted_iota(jnp.int32, (rows, 1), 0)
    begin = jnp.zeros((rows, 1), jnp.int32)
    for start in prompt_starts(prompt_pages):
        begin = jnp.maximum(begin, jnp.where(start * PAGE <= token, start * PAGE, 0))
    spot = first - steps_back * rows + lax.broadcasted_iota(jnp.int32, (1, rows), 1)
    return jnp.where((spot >= begin) & (spot <= token), 0.0, masked_fill)


def swap_pair(position, n_cp):
    odd = lax.rem(lax.axis_index("dec"), 2)
    within = lax.rem(position + 1, 2)
    swapped = position - within + lax.rem(within + odd, 2)
    paired = (position >= 1) & (position <= (n_cp - 1) // 2 * 2)
    return jnp.where(paired, swapped, position)


def slot_pages(owner, slot_count, prompt_pages, decode_owner, slot_offset):
    prompts, width = decode_owner.shape
    cycle = width * lax.axis_size("dec") * slot_count
    starts = prompt_starts(prompt_pages)
    pages, start, offset, place = jnp.int32(0), jnp.int32(0), jnp.int32(0), jnp.int32(0)
    for k in range(prompts):
        for p in range(width):
            mine = decode_owner[k, p] == owner
            pages = jnp.where(mine, prompt_pages[k], pages)
            start = jnp.where(mine, starts[k], start)
            offset = jnp.where(mine, slot_offset[k], offset)
            place = jnp.where(mine, p, place)
    result = []
    for c in range(slot_count):
        turn = width * (lax.axis_index("dec") * slot_count + c) + place
        page = lax.rem(turn - offset + 2 * cycle, cycle)
        result.append((page < pages, start + page))
    return result


def row_picker(targets, columns):
    kept = len(targets) * PAGE
    row = lax.broadcasted_iota(jnp.int32, (kept, 1), 0)
    target = jnp.full((kept, 1), -1, jnp.int32)
    for c, column in enumerate(targets):
        target = jnp.where(row // PAGE == c, column + row % PAGE, target)
    column = lax.broadcasted_iota(jnp.int32, (1, columns), 1)
    return jnp.where(column == target, 1.0, 0.0).astype(jnp.bfloat16)


def head_values(latents, value_expand, h):
    both = jnp.concatenate([value_expand[h], value_expand[h + 1]], axis=1)
    return jnp.dot(latents, both, preferred_element_type=jnp.float32).astype(jnp.bfloat16)


def own_kernel(n_cp, count, chunks, group, slot_count, *refs):
    inputs, refs = refs[:7], refs[7:]
    combined, result, peaks, totals, sent_rows, bias, picked, filled, own, value_expand = refs[:10]
    prompt_pages, decode_owner, slot_offset, queries, key_absorb, latents, sems = refs[10:]
    pages_hbm, owner_hbm, offset_hbm, own_hbm, queries_hbm, absorb_hbm, expand_hbm = inputs
    rows = own.shape[1]
    heads = key_absorb.shape[0]
    small = [
        pltpu.make_async_copy(source, target, sems.at[i])
        for i, (source, target) in enumerate(zip(inputs[:4], (prompt_pages, decode_owner, slot_offset, own)))
    ]
    large = {}
    first = 0
    for chunk in chunks:
        at = 4 + 3 * len(large)
        some = pl.ds(first, chunk)
        wide = pl.ds(first * HEAD, chunk * HEAD)
        large[first] = (
            pltpu.make_async_copy(queries_hbm.at[:, wide], queries.at[:, wide], sems.at[at]),
            pltpu.make_async_copy(absorb_hbm.at[some], key_absorb.at[some], sems.at[at + 1]),
            pltpu.make_async_copy(expand_hbm.at[some], value_expand.at[some], sems.at[at + 2]),
        )
        first += chunk
    for copy in small:
        copy.start()
    for chunk_copies in large.values():
        for copy in chunk_copies:
            copy.start()
    steps = heads // group

    def absorb(g):
        for copy in large.get(g * group, ())[:2]:
            copy.wait()
        for h in range(g * group, (g + 1) * group):
            at = h * HEAD
            absorbed = jnp.dot(queries[:, at:at + NOPE], key_absorb[h], preferred_element_type=jnp.float32)
            combined[h * rows:(h + 1) * rows, :LAT] = absorbed.astype(jnp.bfloat16)
            combined[h * rows:(h + 1) * rows, LAT:] = queries[:, at + NOPE:at + HEAD]

    def score(g):
        return jnp.dot(combined[g * group * rows:(g + 1) * group * rows, :], own[...], preferred_element_type=jnp.float32)

    def value(g):
        for copy in large.get(g * group, ())[2:]:
            copy.wait()
        return [head_values(latents[...], value_expand, g * group + i) for i in range(0, group, 2)]

    def finish(g, scores, both):
        span = slice(g * group * rows, (g + 1) * group * rows)
        scores = (scores.reshape(group, rows, rows) + own_bias[None]).reshape(group * rows, rows)
        peak = jnp.max(scores, axis=1, keepdims=True)
        weights = jnp.exp2((scores - peak) * exp2_scale)
        total = jnp.sum(weights, axis=1, keepdims=True)
        weights = weights.astype(jnp.bfloat16)
        for i in range(group):
            mine = both[i // 2][:, i % 2 * VDIM:(i % 2 + 1) * VDIM]
            out = jnp.dot(weights[i * rows:(i + 1) * rows], mine, preferred_element_type=jnp.float32)
            result[(g * group + i) * rows:(g * group + i + 1) * rows, :] = out
        peaks[span, :] = jnp.broadcast_to(peak, (group * rows, LANES))
        totals[span, :] = jnp.broadcast_to(total, (group * rows, LANES))

    for copy in small:
        copy.wait()
    latents[...] = own[:LAT, :].T
    own_bias = visible_bias(prompt_pages, rows, 0)
    index_work(n_cp, count, slot_count, prompt_pages, decode_owner, slot_offset, own[...], sent_rows, bias, picked, filled)
    scores, both = {}, {}
    for step in range(steps + 2):
        if step < steps:
            absorb(step)
        if 0 <= step - 1 < steps:
            scores[step - 1] = score(step - 1)
            both[step - 1] = value(step - 1)
        if 0 <= step - 2:
            finish(step - 2, scores.pop(step - 2), both.pop(step - 2))


def index_work(n_cp, count, slot_count, prompt_pages, decode_owner, slot_offset, block, sent_rows, bias, picked, filled):
    rows = block.shape[1]
    me = lax.axis_index("cp")
    behind = lax.rem(me + n_cp - 1, n_cp)
    targets = []
    for valid, page in slot_pages(behind, slot_count, prompt_pages, decode_owner, slot_offset):
        here = valid & (page * PAGE // rows == me)
        targets.append(jnp.where(here, lax.rem(page * PAGE, rows), -PAGE))
    choice = row_picker(targets, rows)
    sent = lax.dot_general(choice, block, NT, preferred_element_type=jnp.float32)
    kept = choice.shape[0]
    sent_rows[...] = jnp.zeros(sent_rows.shape, jnp.bfloat16)
    sent_rows[:kept, :ROW] = sent.astype(jnp.bfloat16)
    for b in range(count):
        bias[:, b * rows:(b + 1) * rows] = visible_bias(prompt_pages, rows, swap_pair(jnp.int32(b + 1), n_cp))
    targets = []
    lane = lax.broadcasted_iota(jnp.int32, filled.shape, 1)
    lane_filled = jnp.zeros(filled.shape, jnp.float32)
    for c, (valid, page) in enumerate(slot_pages(me, slot_count, prompt_pages, decode_owner, slot_offset)):
        source = page * PAGE // rows
        column = swap_pair(lax.rem(me - source + n_cp, n_cp), n_cp) * rows + lax.rem(page * PAGE, rows)
        targets.append(jnp.where(valid, column, -PAGE))
        lane_filled = jnp.where(lane // PAGE == c, valid.astype(jnp.float32), lane_filled)
    filled[...] = lane_filled
    picked[...] = row_picker(targets, (n_cp - 1) * rows)


def pick_rows(picked, index, block):
    rows = block.shape[1]
    return lax.dot_general(picked[:, index * rows:(index + 1) * rows], block, NT, preferred_element_type=jnp.float32)


def arrived_kernel(picked, own, *refs):
    blocks, (found, latents) = refs[:-2], refs[-2:]
    rows = own.shape[1]
    total = pick_rows(picked, 0, own[...])
    for i, block in enumerate(blocks):
        total = total + pick_rows(picked, 1 + 2 * i, block[...])
        latents[i * rows:(i + 1) * rows, :] = block[:LAT, :].T
    found[...] = total


def write_cache(rows, filled, page_cache, page_scales):
    slot_count = page_cache.shape[0]
    scales = []
    for b in range(NBLK):
        values = rows[:, b * BLOCK:(b + 1) * BLOCK]
        scale = jnp.max(jnp.abs(values), axis=1, keepdims=True) + amax_epsilon
        scale = scale.astype(jnp.bfloat16).astype(jnp.float32)
        encoded = (values / scale).astype(jnp.bfloat16)
        for c in range(slot_count):
            page_cache[c, :, b * BLOCK:(b + 1) * BLOCK] = encoded[c * PAGE:(c + 1) * PAGE]
        scales.append(scale)
    kept = rows.shape[0]
    which = lax.broadcasted_iota(jnp.int32, (kept, LANES), 1)
    table = jnp.zeros((kept, LANES), jnp.float32)
    for b, scale in enumerate(scales):
        table = jnp.where(which == b, scale, table)
    table = (table.T[:NBLK] * filled[:1, :kept]).astype(jnp.bfloat16)
    for c in range(slot_count):
        page_cache[c, :, LAT:] = rows[c * PAGE:(c + 1) * PAGE, LAT:].astype(jnp.bfloat16)
        page_scales[c] = table[:, c * PAGE:(c + 1) * PAGE]


def earlier_kernel(count, group, *refs):
    combined, own_result, peaks, totals, value_expand, bias, fetched_latents, picked, found = refs[:9]
    arrived, (result, found_more, keys, latents) = refs[9:-4], refs[-4:]
    rows, width = bias.shape
    heads = value_expand.shape[0]
    steps = heads // group

    def span(g):
        at = g * group * rows
        return slice(at, at + group * rows)

    def score(g):
        scores = jnp.dot(combined[span(g), :], keys[...], preferred_element_type=jnp.float32)
        return (scores.reshape(group, rows, width) + bias[...][None]).reshape(group * rows, width)

    def weigh(g, scores):
        old_peak = peaks[span(g), :]
        parts = [scores[:, b:b + LANES] for b in range(0, width, LANES)]
        peak = jnp.maximum(old_peak, jnp.max(functools.reduce(jnp.maximum, parts), axis=1, keepdims=True))
        parts = [jnp.exp2((part - peak) * exp2_scale) for part in parts]
        total = jnp.sum(functools.reduce(jnp.add, parts), axis=1, keepdims=True)
        factor = jnp.exp2((old_peak - peak) * exp2_scale)
        inverse = 1.0 / (totals[span(g), :] * factor + total)
        weights = jnp.concatenate([part.astype(jnp.bfloat16) for part in parts], axis=1)
        return weights, factor * inverse, inverse

    def mix(g, weights):
        return jnp.dot(weights, latents[...], preferred_element_type=jnp.float32).astype(jnp.bfloat16)

    def finish(g, mixed, factor, inverse):
        for i in range(group):
            part = slice(i * rows, (i + 1) * rows)
            h = g * group + i
            out = jnp.dot(mixed[part], value_expand[h], preferred_element_type=jnp.float32)
            out = own_result[h * rows:(h + 1) * rows, :] * factor[part] + out * inverse[part]
            result[:, h * VDIM:(h + 1) * VDIM] = out.astype(jnp.bfloat16)

    def pick_swapped():
        total = found[...]
        for i in range(len(arrived) // (1 + SWAP)):
            parts = arrived[i * (1 + SWAP) + 1:(i + 1) * (1 + SWAP)]
            total = total + pick_rows(picked, 2 + 2 * i, jnp.concatenate([part[...] for part in parts], axis=0))
        found_more[...] = total

    @pl.when(lax.axis_index("cp") == 0)
    def _():
        pick_swapped()
        for h in range(heads):
            part = slice(h * rows, (h + 1) * rows)
            result[:, h * VDIM:(h + 1) * VDIM] = (own_result[part, :] / totals[part, :]).astype(jnp.bfloat16)

    @pl.when(lax.axis_index("cp") > 0)
    def _():
        for i in range(count // 2):
            fetched, *parts = arrived[i * (1 + SWAP):(i + 1) * (1 + SWAP)]
            swapped = jnp.concatenate([part[...] for part in parts], axis=0)
            at = 2 * i * rows
            keys[:, at:at + rows] = fetched[...]
            keys[:, at + rows:at + 2 * rows] = swapped
            latents[at:at + rows, :] = fetched_latents[i * rows:(i + 1) * rows, :]
            latents[at + rows:at + 2 * rows, :] = swapped[:LAT].T
        scores, weights, mixed = {}, {}, {}
        for step in range(steps + 2):
            if step < steps:
                scores[step] = score(step)
            if step == 1:
                pick_swapped()
            if 0 <= step - 2:
                finish(step - 2, mixed.pop(step - 2), *weights.pop(step - 2)[1:])
            if 0 <= step - 1 < steps:
                weights[step - 1] = weigh(step - 1, scores.pop(step - 1))
                mixed[step - 1] = mix(step - 1, weights[step - 1][0])


def store_kernel(result, found, sent_rows, filled, attended, page_cache, page_scales, cache_buf, scale_buf, sems):
    count = sems.shape[0] - 2
    wide = result.shape[1] // count
    copies = []
    for i in range(count):
        some = pl.ds(i * wide, wide)
        copies.append(pltpu.make_async_copy(result.at[:, some], attended.at[:, some], sems.at[i]))
        copies[-1].start()
    rows = found[...] + sent_rows[:found.shape[0], :ROW].astype(jnp.float32)
    write_cache(rows, filled, cache_buf, scale_buf)
    for i, (source, target) in enumerate(((cache_buf, page_cache), (scale_buf, page_scales))):
        copies.append(pltpu.make_async_copy(source, target, sems.at[count + i]))
        copies[-1].start()
    for copy in copies:
        copy.wait()


def fetch(own, n_cp, n_dec):
    blocks = []
    for step in range(1, n_cp - 1, 2):
        pairs = [(c * n_dec + e, (c + step + e % 2) % n_cp * n_dec + e) for c in range(n_cp) for e in range(n_dec)]
        blocks.append(lax.ppermute(own, ("cp", "dec"), pairs))
    return blocks


def swap(blocks, n_dec):
    pieces = []
    for block in blocks:
        parts = [block[at:at + ROW // SWAP] for at in range(0, ROW, ROW // SWAP)]
        pieces += [block] + [lax.ppermute(part, "dec", [(e, e ^ 1) for e in range(n_dec)]) for part in parts]
    return pieces


def on_device(queries, latent_rows, key_absorb, value_expand, prompt_pages, decode_owner, slot_offset):
    n_cp = lax.axis_size("cp")
    dec_count = lax.axis_size("dec")
    heads = key_absorb.shape[0]
    rows = latent_rows.shape[0]
    prompts, width = decode_owner.shape
    slot_count = 3 * (rows // PAGE) // (2 * dec_count)
    kept = slot_count * PAGE
    reach = width * dec_count * slot_count * PAGE
    count = -(-reach // rows) - (1 if prompts == 2 else 0)
    count = min(n_cp - 2, count + count % 2)
    own = latent_rows.T
    blocks = fetch(own, n_cp, dec_count)

    vmem = pl.BlockSpec(memory_space=pltpu.VMEM)
    hbm = pl.BlockSpec(memory_space=pltpu.HBM)
    params = pltpu.CompilerParams(vmem_limit_bytes=32 * 2**20)
    group, chunks = 4, (heads // 4, heads // 4, heads // 2)
    inputs = (prompt_pages, decode_owner, slot_offset, own, queries, key_absorb, value_expand)
    combined, result, peaks, totals, sent_rows, bias, picked, filled, own_copy, value_copy = pl.pallas_call(
        functools.partial(own_kernel, n_cp, count, chunks, group, slot_count),
        in_specs=[hbm] * 7,
        out_specs=[vmem] * 10,
        out_shape=[
            jax.ShapeDtypeStruct((heads * rows, ROW), jnp.bfloat16),
            jax.ShapeDtypeStruct((heads * rows, VDIM), jnp.float32),
            jax.ShapeDtypeStruct((heads * rows, LANES), jnp.float32),
            jax.ShapeDtypeStruct((heads * rows, LANES), jnp.float32),
            jax.ShapeDtypeStruct((kept + PAGE, -(-ROW // LANES) * LANES), jnp.bfloat16),
            jax.ShapeDtypeStruct((rows, count * rows), jnp.float32),
            jax.ShapeDtypeStruct((kept, (n_cp - 1) * rows), jnp.bfloat16),
            jax.ShapeDtypeStruct((8, LANES), jnp.float32),
            jax.ShapeDtypeStruct(own.shape, jnp.bfloat16),
            jax.ShapeDtypeStruct(value_expand.shape, jnp.bfloat16),
        ],
        scratch_shapes=[
            pltpu.SMEM(prompt_pages.shape, jnp.int32),
            pltpu.SMEM(decode_owner.shape, jnp.int32),
            pltpu.SMEM(slot_offset.shape, jnp.int32),
            pltpu.VMEM((rows, heads * HEAD), jnp.bfloat16),
            pltpu.VMEM((heads, NOPE, LAT), jnp.bfloat16),
            pltpu.VMEM((rows, LAT), jnp.bfloat16),
            pltpu.SemaphoreType.DMA((4 + 3 * len(chunks),)),
        ],
        cost_estimate=pl.CostEstimate(
            flops=2 * rows * heads * (2 * NOPE * LAT + rows * (ROW + VDIM)),
            bytes_accessed=2 * (queries.size + key_absorb.size + heads * rows * ROW),
            transcendentals=rows * heads * rows,
        ),
        compiler_params=params,
        name="own",
    )(*[pltpu.with_memory_space_constraint(x, pltpu.HBM) for x in inputs])
    sent_rows = lax.ppermute(sent_rows, "cp", [(c, (c + n_cp - 1) % n_cp) for c in range(n_cp)])
    blocks, picked = lax.optimization_barrier((blocks, picked))
    pieces = swap(blocks, dec_count)
    found, fetched_latents = pl.pallas_call(
        arrived_kernel,
        in_specs=[vmem] * (2 + len(blocks)),
        out_specs=[vmem] * 2,
        out_shape=[
            jax.ShapeDtypeStruct((kept, ROW), jnp.float32),
            jax.ShapeDtypeStruct((len(blocks) * rows, LAT), jnp.bfloat16),
        ],
        cost_estimate=pl.CostEstimate(flops=2**20, bytes_accessed=2**10, transcendentals=0),
        compiler_params=params,
        name="arrived",
    )(picked, own_copy, *blocks)

    group = 4 if count <= 4 else 2
    operands = (combined, result, peaks, totals, value_copy, bias, fetched_latents, picked, found, *pieces)
    attended, found = pl.pallas_call(
        functools.partial(earlier_kernel, count, group),
        in_specs=[vmem] * len(operands),
        out_specs=[vmem] * 2,
        out_shape=[
            jax.ShapeDtypeStruct((rows, heads * VDIM), jnp.bfloat16),
            jax.ShapeDtypeStruct((kept, ROW), jnp.float32),
        ],
        scratch_shapes=[
            pltpu.VMEM((ROW, count * rows), jnp.bfloat16),
            pltpu.VMEM((count * rows, LAT), jnp.bfloat16),
        ],
        cost_estimate=pl.CostEstimate(flops=2**20, bytes_accessed=2**10, transcendentals=0),
        compiler_params=params,
        name="earlier",
    )(*operands)
    sent_rows, attended = lax.optimization_barrier((sent_rows, attended))
    operands = (attended, found, sent_rows, filled)
    attended, page_cache, page_scales = pl.pallas_call(
        store_kernel,
        in_specs=[vmem] * len(operands),
        out_specs=[hbm] * 3,
        out_shape=[
            jax.ShapeDtypeStruct((rows, heads * VDIM), jnp.bfloat16),
            jax.ShapeDtypeStruct((slot_count, PAGE, ROW), jnp.bfloat16),
            jax.ShapeDtypeStruct((slot_count, NBLK, PAGE), jnp.bfloat16),
        ],
        scratch_shapes=[
            pltpu.VMEM((slot_count, PAGE, ROW), jnp.bfloat16),
            pltpu.VMEM((slot_count, NBLK, PAGE), jnp.bfloat16),
            pltpu.SemaphoreType.DMA((4 + 2,)),
        ],
        cost_estimate=pl.CostEstimate(flops=2**20, bytes_accessed=2**10, transcendentals=0),
        compiler_params=params,
        name="store",
    )(*operands)
    page_cache = page_cache.reshape(1, 1, slot_count, PAGE, ROW)
    page_scales = page_scales.transpose(0, 2, 1).reshape(1, 1, slot_count, PAGE, NBLK)
    return attended, page_cache, page_scales


def solution(mesh):
    return jax.shard_map(
        on_device,
        mesh=mesh,
        in_specs=(
            P(("grp", "cp"), "dec"),
            P(("grp", "cp"), None),
            P("dec", None, None),
            P("dec", None, None),
            P("grp"),
            P("grp", None),
            P("grp"),
        ),
        out_specs=(
            P(("grp", "cp"), "dec"),
            P(("grp", "cp"), "dec", None, None, None),
            P(("grp", "cp"), "dec", None, None, None),
        ),
        check_vma=False,
    )
```

```python
import functools
import math

import jax
import jax.numpy as jnp
from jax import lax
from jax.experimental import pallas as pl
from jax.experimental.pallas import tpu as pltpu
from jax.sharding import PartitionSpec as P

LAT = 512
ROPE = 64
NOPE = 128
VDIM = 128
PAGE = 16
BLOCK = 128
NBLK = LAT // BLOCK
ROW = LAT + ROPE
HEAD = NOPE + ROPE
LANES = 128
SWAP = 2

masked_fill = -1e30
amax_epsilon = 1e-06
exp2_scale = math.log2(math.e) / math.sqrt(HEAD)

NT = (((1,), (1,)), ((), ()))


def prompt_starts(prompt_pages):
    starts = [jnp.int32(0)]
    for k in range(prompt_pages.shape[0] - 1):
        starts.append(starts[-1] + prompt_pages[k])
    return starts


def visible_bias(prompt_pages, rows, steps_back):
    first = lax.axis_index("cp") * rows
    token = first + lax.broadcasted_iota(jnp.int32, (rows, 1), 0)
    begin = jnp.zeros((rows, 1), jnp.int32)
    for start in prompt_starts(prompt_pages):
        begin = jnp.maximum(begin, jnp.where(start * PAGE <= token, start * PAGE, 0))
    spot = first - steps_back * rows + lax.broadcasted_iota(jnp.int32, (1, rows), 1)
    return jnp.where((spot >= begin) & (spot <= token), 0.0, masked_fill)


def swap_pair(position, n_cp):
    odd = lax.rem(lax.axis_index("dec"), 2)
    within = lax.rem(position + 1, 2)
    swapped = position - within + lax.rem(within + odd, 2)
    paired = (position >= 1) & (position <= (n_cp - 1) // 2 * 2)
    return jnp.where(paired, swapped, position)


def slot_pages(owner, slot_count, prompt_pages, decode_owner, slot_offset):
    prompts, width = decode_owner.shape
    cycle = width * lax.axis_size("dec") * slot_count
    starts = prompt_starts(prompt_pages)
    pages, start, offset, place = jnp.int32(0), jnp.int32(0), jnp.int32(0), jnp.int32(0)
    for k in range(prompts):
        for p in range(width):
            mine = decode_owner[k, p] == owner
            pages = jnp.where(mine, prompt_pages[k], pages)
            start = jnp.where(mine, starts[k], start)
            offset = jnp.where(mine, slot_offset[k], offset)
            place = jnp.where(mine, p, place)
    result = []
    for c in range(slot_count):
        turn = width * (lax.axis_index("dec") * slot_count + c) + place
        page = lax.rem(turn - offset + 2 * cycle, cycle)
        result.append((page < pages, start + page))
    return result


def row_picker(targets, columns):
    kept = len(targets) * PAGE
    row = lax.broadcasted_iota(jnp.int32, (kept, 1), 0)
    target = jnp.full((kept, 1), -1, jnp.int32)
    for c, column in enumerate(targets):
        target = jnp.where(row // PAGE == c, column + row % PAGE, target)
    column = lax.broadcasted_iota(jnp.int32, (1, columns), 1)
    return jnp.where(column == target, 1.0, 0.0).astype(jnp.bfloat16)


def head_values(latents, value_expand, h):
    both = jnp.concatenate([value_expand[h], value_expand[h + 1]], axis=1)
    return jnp.dot(latents, both, preferred_element_type=jnp.float32).astype(jnp.bfloat16)


def own_kernel(n_cp, count, chunks, group, slot_count, *refs):
    inputs, refs = refs[:7], refs[7:]
    combined, result, peaks, totals, sent_rows, bias, picked, filled, own, value_expand = refs[:10]
    prompt_pages, decode_owner, slot_offset, queries, key_absorb, latents, sems = refs[10:]
    pages_hbm, owner_hbm, offset_hbm, own_hbm, queries_hbm, absorb_hbm, expand_hbm = inputs
    rows = own.shape[1]
    heads = key_absorb.shape[0]
    small = [
        pltpu.make_async_copy(source, target, sems.at[i])
        for i, (source, target) in enumerate(zip(inputs[:4], (prompt_pages, decode_owner, slot_offset, own)))
    ]
    large = {}
    first = 0
    for chunk in chunks:
        at = 4 + 3 * len(large)
        some = pl.ds(first, chunk)
        wide = pl.ds(first * HEAD, chunk * HEAD)
        large[first] = (
            pltpu.make_async_copy(queries_hbm.at[:, wide], queries.at[:, wide], sems.at[at]),
            pltpu.make_async_copy(absorb_hbm.at[some], key_absorb.at[some], sems.at[at + 1]),
            pltpu.make_async_copy(expand_hbm.at[some], value_expand.at[some], sems.at[at + 2]),
        )
        first += chunk
    for copy in small:
        copy.start()
    for chunk_copies in large.values():
        for copy in chunk_copies:
            copy.start()
    steps = heads // group

    def absorb(g):
        for copy in large.get(g * group, ())[:2]:
            copy.wait()
        for h in range(g * group, (g + 1) * group):
            at = h * HEAD
            absorbed = jnp.dot(queries[:, at:at + NOPE], key_absorb[h], preferred_element_type=jnp.float32)
            combined[h * rows:(h + 1) * rows, :LAT] = absorbed.astype(jnp.bfloat16)
            combined[h * rows:(h + 1) * rows, LAT:] = queries[:, at + NOPE:at + HEAD]

    def score(g):
        return jnp.dot(combined[g * group * rows:(g + 1) * group * rows, :], own[...], preferred_element_type=jnp.float32)

    def value(g):
        for copy in large.get(g * group, ())[2:]:
            copy.wait()
        return [head_values(latents[...], value_expand, g * group + i) for i in range(0, group, 2)]

    def finish(g, scores, both):
        span = slice(g * group * rows, (g + 1) * group * rows)
        scores = (scores.reshape(group, rows, rows) + own_bias[None]).reshape(group * rows, rows)
        peak = jnp.max(scores, axis=1, keepdims=True)
        weights = jnp.exp2((scores - peak) * exp2_scale)
        total = jnp.sum(weights, axis=1, keepdims=True)
        weights = weights.astype(jnp.bfloat16)
        for i in range(group):
            mine = both[i // 2][:, i % 2 * VDIM:(i % 2 + 1) * VDIM]
            out = jnp.dot(weights[i * rows:(i + 1) * rows], mine, preferred_element_type=jnp.float32)
            result[(g * group + i) * rows:(g * group + i + 1) * rows, :] = out
        peaks[span, :] = jnp.broadcast_to(peak, (group * rows, LANES))
        totals[span, :] = jnp.broadcast_to(total, (group * rows, LANES))

    for copy in small:
        copy.wait()
    latents[...] = own[:LAT, :].T
    own_bias = visible_bias(prompt_pages, rows, 0)
    index_work(n_cp, count, slot_count, prompt_pages, decode_owner, slot_offset, own[...], sent_rows, bias, picked, filled)
    scores, both = {}, {}
    for step in range(steps + 2):
        if step < steps:
            absorb(step)
        if 0 <= step - 1 < steps:
            scores[step - 1] = score(step - 1)
            both[step - 1] = value(step - 1)
        if 0 <= step - 2:
            finish(step - 2, scores.pop(step - 2), both.pop(step - 2))


def index_work(n_cp, count, slot_count, prompt_pages, decode_owner, slot_offset, block, sent_rows, bias, picked, filled):
    rows = block.shape[1]
    me = lax.axis_index("cp")
    behind = lax.rem(me + n_cp - 1, n_cp)
    targets = []
    for valid, page in slot_pages(behind, slot_count, prompt_pages, decode_owner, slot_offset):
        here = valid & (page * PAGE // rows == me)
        targets.append(jnp.where(here, lax.rem(page * PAGE, rows), -PAGE))
    choice = row_picker(targets, rows)
    sent = lax.dot_general(choice, block, NT, preferred_element_type=jnp.float32)
    kept = choice.shape[0]
    sent_rows[...] = jnp.zeros(sent_rows.shape, jnp.bfloat16)
    sent_rows[:kept, :ROW] = sent.astype(jnp.bfloat16)
    for b in range(count):
        bias[:, b * rows:(b + 1) * rows] = visible_bias(prompt_pages, rows, swap_pair(jnp.int32(b + 1), n_cp))
    targets = []
    lane = lax.broadcasted_iota(jnp.int32, filled.shape, 1)
    lane_filled = jnp.zeros(filled.shape, jnp.float32)
    for c, (valid, page) in enumerate(slot_pages(me, slot_count, prompt_pages, decode_owner, slot_offset)):
        source = page * PAGE // rows
        column = swap_pair(lax.rem(me - source + n_cp, n_cp), n_cp) * rows + lax.rem(page * PAGE, rows)
        targets.append(jnp.where(valid, column, -PAGE))
        lane_filled = jnp.where(lane // PAGE == c, valid.astype(jnp.float32), lane_filled)
    filled[...] = lane_filled
    picked[...] = row_picker(targets, (n_cp - 1) * rows)


def pick_rows(picked, index, block):
    rows = block.shape[1]
    return lax.dot_general(picked[:, index * rows:(index + 1) * rows], block, NT, preferred_element_type=jnp.float32)


def arrived_kernel(used, picked, own, value_expand, *refs):
    blocks, (found, values) = refs[:-2], refs[-2:]
    rows = own.shape[1]
    for i in range(used):
        latents = blocks[i][:LAT, :].T
        for h in range(0, value_expand.shape[0], 2):
            values[i * rows:(i + 1) * rows, h * VDIM:(h + 2) * VDIM] = head_values(latents, value_expand, h)
    total = pick_rows(picked, 0, own[...])
    for i, block in enumerate(blocks):
        total = total + pick_rows(picked, 1 + 2 * i, block[...])
    found[...] = total


def write_cache(rows, filled, page_cache, page_scales):
    slot_count = page_cache.shape[0]
    scales = []
    for b in range(NBLK):
        values = rows[:, b * BLOCK:(b + 1) * BLOCK]
        scale = jnp.max(jnp.abs(values), axis=1, keepdims=True) + amax_epsilon
        scale = scale.astype(jnp.bfloat16).astype(jnp.float32)
        encoded = (values / scale).astype(jnp.bfloat16)
        for c in range(slot_count):
            page_cache[c, :, b * BLOCK:(b + 1) * BLOCK] = encoded[c * PAGE:(c + 1) * PAGE]
        scales.append(scale)
    kept = rows.shape[0]
    which = lax.broadcasted_iota(jnp.int32, (kept, LANES), 1)
    table = jnp.zeros((kept, LANES), jnp.float32)
    for b, scale in enumerate(scales):
        table = jnp.where(which == b, scale, table)
    table = (table.T[:NBLK] * filled[:1, :kept]).astype(jnp.bfloat16)
    for c in range(slot_count):
        page_cache[c, :, LAT:] = rows[c * PAGE:(c + 1) * PAGE, LAT:].astype(jnp.bfloat16)
        page_scales[c] = table[:, c * PAGE:(c + 1) * PAGE]


def earlier_kernel(count, group, *refs):
    combined, own_result, peaks, totals, value_expand, bias, fetched_values = refs[:7]
    arrived, (result, keys, latents) = refs[7:-3], refs[-3:]
    rows, width = bias.shape
    heads = value_expand.shape[0]
    steps = heads // group

    def span(g):
        at = g * group * rows
        return slice(at, at + group * rows)

    def score(g):
        scores = jnp.dot(combined[span(g), :], keys[...], preferred_element_type=jnp.float32)
        return (scores.reshape(group, rows, width) + bias[...][None]).reshape(group * rows, width)

    def weigh(g, scores):
        old_peak = peaks[span(g), :]
        parts = [scores[:, b:b + LANES] for b in range(0, width, LANES)]
        peak = jnp.maximum(old_peak, jnp.max(functools.reduce(jnp.maximum, parts), axis=1, keepdims=True))
        parts = [jnp.exp2((part - peak) * exp2_scale) for part in parts]
        total = jnp.sum(functools.reduce(jnp.add, parts), axis=1, keepdims=True)
        factor = jnp.exp2((old_peak - peak) * exp2_scale)
        inverse = 1.0 / (totals[span(g), :] * factor + total)
        weights = jnp.concatenate([part.astype(jnp.bfloat16) for part in parts], axis=1)
        return weights, factor * inverse, inverse

    def value(g):
        return [
            [head_values(latents[i * rows:(i + 1) * rows, :], value_expand, h) for h in range(g * group, (g + 1) * group, 2)]
            for i in range(count // 2)
        ]

    def finish(g, weights, factor, inverse, swapped):
        for i in range(group):
            part = slice(i * rows, (i + 1) * rows)
            h = g * group + i
            values = []
            for b in range(count // 2):
                values.append(fetched_values[b * rows:(b + 1) * rows, h * VDIM:(h + 1) * VDIM])
                values.append(swapped[b][i // 2][:, i % 2 * VDIM:(i % 2 + 1) * VDIM])
            out = jnp.dot(weights[part], jnp.concatenate(values, axis=0), preferred_element_type=jnp.float32)
            out = own_result[h * rows:(h + 1) * rows, :] * factor[part] + out * inverse[part]
            result[:, h * VDIM:(h + 1) * VDIM] = out.astype(jnp.bfloat16)

    @pl.when(lax.axis_index("cp") == 0)
    def _():
        for h in range(heads):
            part = slice(h * rows, (h + 1) * rows)
            result[:, h * VDIM:(h + 1) * VDIM] = (own_result[part, :] / totals[part, :]).astype(jnp.bfloat16)

    @pl.when(lax.axis_index("cp") > 0)
    def _():
        for i in range(count // 2):
            fetched, *parts = arrived[i * (1 + SWAP):(i + 1) * (1 + SWAP)]
            swapped = jnp.concatenate([part[...] for part in parts], axis=0)
            at = 2 * i * rows
            keys[:, at:at + rows] = fetched[...]
            keys[:, at + rows:at + 2 * rows] = swapped
            latents[i * rows:(i + 1) * rows, :] = swapped[:LAT].T
        scores, values, weights = {}, {}, {}
        for step in range(steps + 2):
            if step < steps:
                scores[step] = score(step)
            if 0 <= step - 2:
                finish(step - 2, *weights.pop(step - 2), values.pop(step - 2))
            if 0 <= step - 1 < steps:
                values[step - 1] = value(step - 1)
                weights[step - 1] = weigh(step - 1, scores.pop(step - 1))


def store_kernel(result, picked, found, sent_rows, filled, *refs):
    swapped, (attended, page_cache, page_scales, cache_buf, scale_buf, sems) = refs[:-6], refs[-6:]
    count = sems.shape[0] - 2
    wide = result.shape[1] // count
    copies = []
    for i in range(count):
        some = pl.ds(i * wide, wide)
        copies.append(pltpu.make_async_copy(result.at[:, some], attended.at[:, some], sems.at[i]))
        copies[-1].start()
    rows = found[...] + sent_rows[:found.shape[0], :ROW].astype(jnp.float32)
    for i in range(len(swapped) // SWAP):
        block = jnp.concatenate([part[...] for part in swapped[i * SWAP:(i + 1) * SWAP]], axis=0)
        rows = rows + pick_rows(picked, 2 + 2 * i, block)
    write_cache(rows, filled, cache_buf, scale_buf)
    for i, (source, target) in enumerate(((cache_buf, page_cache), (scale_buf, page_scales))):
        copies.append(pltpu.make_async_copy(source, target, sems.at[count + i]))
        copies[-1].start()
    for copy in copies:
        copy.wait()


def fetch(own, n_cp, n_dec):
    blocks = []
    for step in range(1, n_cp - 1, 2):
        pairs = [(c * n_dec + e, (c + step + e % 2) % n_cp * n_dec + e) for c in range(n_cp) for e in range(n_dec)]
        blocks.append(lax.ppermute(own, ("cp", "dec"), pairs))
    return blocks


def swap(blocks, n_dec):
    pieces = []
    for block in blocks:
        parts = [block[at:at + ROW // SWAP] for at in range(0, ROW, ROW // SWAP)]
        pieces += [block] + [lax.ppermute(part, "dec", [(e, e ^ 1) for e in range(n_dec)]) for part in parts]
    return pieces


def on_device(queries, latent_rows, key_absorb, value_expand, prompt_pages, decode_owner, slot_offset):
    n_cp = lax.axis_size("cp")
    dec_count = lax.axis_size("dec")
    heads = key_absorb.shape[0]
    rows = latent_rows.shape[0]
    prompts, width = decode_owner.shape
    slot_count = 3 * (rows // PAGE) // (2 * dec_count)
    kept = slot_count * PAGE
    reach = width * dec_count * slot_count * PAGE
    count = -(-reach // rows) - (1 if prompts == 2 else 0)
    count = min(n_cp - 2, count + count % 2)
    own = latent_rows.T
    blocks = fetch(own, n_cp, dec_count)

    vmem = pl.BlockSpec(memory_space=pltpu.VMEM)
    hbm = pl.BlockSpec(memory_space=pltpu.HBM)
    params = pltpu.CompilerParams(vmem_limit_bytes=32 * 2**20)
    group, chunks = 4, (heads // 4, heads // 4, heads // 2)
    inputs = (prompt_pages, decode_owner, slot_offset, own, queries, key_absorb, value_expand)
    combined, result, peaks, totals, sent_rows, bias, picked, filled, own_copy, value_copy = pl.pallas_call(
        functools.partial(own_kernel, n_cp, count, chunks, group, slot_count),
        in_specs=[hbm] * 7,
        out_specs=[vmem] * 10,
        out_shape=[
            jax.ShapeDtypeStruct((heads * rows, ROW), jnp.bfloat16),
            jax.ShapeDtypeStruct((heads * rows, VDIM), jnp.float32),
            jax.ShapeDtypeStruct((heads * rows, LANES), jnp.float32),
            jax.ShapeDtypeStruct((heads * rows, LANES), jnp.float32),
            jax.ShapeDtypeStruct((kept + PAGE, -(-ROW // LANES) * LANES), jnp.bfloat16),
            jax.ShapeDtypeStruct((rows, count * rows), jnp.float32),
            jax.ShapeDtypeStruct((kept, (n_cp - 1) * rows), jnp.bfloat16),
            jax.ShapeDtypeStruct((8, LANES), jnp.float32),
            jax.ShapeDtypeStruct(own.shape, jnp.bfloat16),
            jax.ShapeDtypeStruct(value_expand.shape, jnp.bfloat16),
        ],
        scratch_shapes=[
            pltpu.SMEM(prompt_pages.shape, jnp.int32),
            pltpu.SMEM(decode_owner.shape, jnp.int32),
            pltpu.SMEM(slot_offset.shape, jnp.int32),
            pltpu.VMEM((rows, heads * HEAD), jnp.bfloat16),
            pltpu.VMEM((heads, NOPE, LAT), jnp.bfloat16),
            pltpu.VMEM((rows, LAT), jnp.bfloat16),
            pltpu.SemaphoreType.DMA((4 + 3 * len(chunks),)),
        ],
        cost_estimate=pl.CostEstimate(
            flops=2 * rows * heads * (2 * NOPE * LAT + rows * (ROW + VDIM)),
            bytes_accessed=2 * (queries.size + key_absorb.size + heads * rows * ROW),
            transcendentals=rows * heads * rows,
        ),
        compiler_params=params,
        name="own",
    )(*[pltpu.with_memory_space_constraint(x, pltpu.HBM) for x in inputs])
    sent_rows = lax.ppermute(sent_rows, "cp", [(c, (c + n_cp - 1) % n_cp) for c in range(n_cp)])
    blocks, picked = lax.optimization_barrier((blocks, picked))
    pieces = swap(blocks, dec_count)
    found, fetched_values = pl.pallas_call(
        functools.partial(arrived_kernel, count // 2),
        in_specs=[vmem] * (3 + len(blocks)),
        out_specs=[vmem] * 2,
        out_shape=[
            jax.ShapeDtypeStruct((kept, ROW), jnp.float32),
            jax.ShapeDtypeStruct((count // 2 * rows, heads * VDIM), jnp.bfloat16),
        ],
        cost_estimate=pl.CostEstimate(flops=2**20, bytes_accessed=2**10, transcendentals=0),
        compiler_params=params,
        name="arrived",
    )(picked, own_copy, value_copy, *blocks)

    group = 4 if count <= 4 else 2
    operands = (combined, result, peaks, totals, value_copy, bias, fetched_values, *pieces[:count // 2 * (1 + SWAP)])
    attended = pl.pallas_call(
        functools.partial(earlier_kernel, count, group),
        in_specs=[vmem] * len(operands),
        out_specs=vmem,
        out_shape=jax.ShapeDtypeStruct((rows, heads * VDIM), jnp.bfloat16),
        scratch_shapes=[
            pltpu.VMEM((ROW, count * rows), jnp.bfloat16),
            pltpu.VMEM((count // 2 * rows, LAT), jnp.bfloat16),
        ],
        cost_estimate=pl.CostEstimate(flops=2**20, bytes_accessed=2**10, transcendentals=0),
        compiler_params=params,
        name="earlier",
    )(*operands)
    sent_rows, attended = lax.optimization_barrier((sent_rows, attended))
    operands = (attended, picked, found, sent_rows, filled, *[part for i, part in enumerate(pieces) if i % (1 + SWAP)])
    attended, page_cache, page_scales = pl.pallas_call(
        store_kernel,
        in_specs=[vmem] * len(operands),
        out_specs=[hbm] * 3,
        out_shape=[
            jax.ShapeDtypeStruct((rows, heads * VDIM), jnp.bfloat16),
            jax.ShapeDtypeStruct((slot_count, PAGE, ROW), jnp.bfloat16),
            jax.ShapeDtypeStruct((slot_count, NBLK, PAGE), jnp.bfloat16),
        ],
        scratch_shapes=[
            pltpu.VMEM((slot_count, PAGE, ROW), jnp.bfloat16),
            pltpu.VMEM((slot_count, NBLK, PAGE), jnp.bfloat16),
            pltpu.SemaphoreType.DMA((4 + 2,)),
        ],
        cost_estimate=pl.CostEstimate(flops=2**20, bytes_accessed=2**10, transcendentals=0),
        compiler_params=params,
        name="store",
    )(*operands)
    page_cache = page_cache.reshape(1, 1, slot_count, PAGE, ROW)
    page_scales = page_scales.transpose(0, 2, 1).reshape(1, 1, slot_count, PAGE, NBLK)
    return attended, page_cache, page_scales


def solution(mesh):
    return jax.shard_map(
        on_device,
        mesh=mesh,
        in_specs=(
            P(("grp", "cp"), "dec"),
            P(("grp", "cp"), None),
            P("dec", None, None),
            P("dec", None, None),
            P("grp"),
            P("grp", None),
            P("grp"),
        ),
        out_specs=(
            P(("grp", "cp"), "dec"),
            P(("grp", "cp"), "dec", None, None, None),
            P(("grp", "cp"), "dec", None, None, None),
        ),
        check_vma=False,
    )
```

```python
import functools
import math

import jax
import jax.numpy as jnp
from jax import lax
from jax.experimental import pallas as pl
from jax.experimental.pallas import tpu as pltpu
from jax.sharding import PartitionSpec as P

LAT = 512
ROPE = 64
NOPE = 128
VDIM = 128
PAGE = 16
BLOCK = 128
NBLK = LAT // BLOCK
ROW = LAT + ROPE
HEAD = NOPE + ROPE
LANES = 128
SWAP = 2

masked_fill = -1e30
amax_epsilon = 1e-06
exp2_scale = math.log2(math.e) / math.sqrt(HEAD)

NT = (((1,), (1,)), ((), ()))


def prompt_starts(prompt_pages):
    starts = [jnp.int32(0)]
    for k in range(prompt_pages.shape[0] - 1):
        starts.append(starts[-1] + prompt_pages[k])
    return starts


def visible_bias(prompt_pages, rows, steps_back):
    first = lax.axis_index("cp") * rows
    token = first + lax.broadcasted_iota(jnp.int32, (rows, 1), 0)
    begin = jnp.zeros((rows, 1), jnp.int32)
    for start in prompt_starts(prompt_pages):
        begin = jnp.maximum(begin, jnp.where(start * PAGE <= token, start * PAGE, 0))
    spot = first - steps_back * rows + lax.broadcasted_iota(jnp.int32, (1, rows), 1)
    return jnp.where((spot >= begin) & (spot <= token), 0.0, masked_fill)


def swap_pair(position, n_cp):
    odd = lax.rem(lax.axis_index("dec"), 2)
    within = lax.rem(position + 1, 2)
    swapped = position - within + lax.rem(within + odd, 2)
    paired = (position >= 1) & (position <= (n_cp - 1) // 2 * 2)
    return jnp.where(paired, swapped, position)


def slot_pages(owner, slot_count, prompt_pages, decode_owner, slot_offset):
    prompts, width = decode_owner.shape
    cycle = width * lax.axis_size("dec") * slot_count
    starts = prompt_starts(prompt_pages)
    pages, start, offset, place = jnp.int32(0), jnp.int32(0), jnp.int32(0), jnp.int32(0)
    for k in range(prompts):
        for p in range(width):
            mine = decode_owner[k, p] == owner
            pages = jnp.where(mine, prompt_pages[k], pages)
            start = jnp.where(mine, starts[k], start)
            offset = jnp.where(mine, slot_offset[k], offset)
            place = jnp.where(mine, p, place)
    result = []
    for c in range(slot_count):
        turn = width * (lax.axis_index("dec") * slot_count + c) + place
        page = lax.rem(turn - offset + 2 * cycle, cycle)
        result.append((page < pages, start + page))
    return result


def row_picker(targets, columns):
    kept = len(targets) * PAGE
    row = lax.broadcasted_iota(jnp.int32, (kept, 1), 0)
    target = jnp.full((kept, 1), -1, jnp.int32)
    for c, column in enumerate(targets):
        target = jnp.where(row // PAGE == c, column + row % PAGE, target)
    column = lax.broadcasted_iota(jnp.int32, (1, columns), 1)
    return jnp.where(column == target, 1.0, 0.0).astype(jnp.bfloat16)


def head_values(latents, value_expand, h):
    both = jnp.concatenate([value_expand[h], value_expand[h + 1]], axis=1)
    return jnp.dot(latents, both, preferred_element_type=jnp.float32).astype(jnp.bfloat16)


def own_kernel(n_cp, count, chunks, group, slot_count, *refs):
    inputs, refs = refs[:7], refs[7:]
    combined, result, peaks, totals, sent_rows, bias, picked, filled, own, value_expand = refs[:10]
    prompt_pages, decode_owner, slot_offset, queries, key_absorb, latents, sems = refs[10:]
    pages_hbm, owner_hbm, offset_hbm, own_hbm, queries_hbm, absorb_hbm, expand_hbm = inputs
    rows = own.shape[1]
    heads = key_absorb.shape[0]
    small = [
        pltpu.make_async_copy(source, target, sems.at[i])
        for i, (source, target) in enumerate(zip(inputs[:4], (prompt_pages, decode_owner, slot_offset, own)))
    ]
    large = {}
    first = 0
    for chunk in chunks:
        at = 4 + 3 * len(large)
        some = pl.ds(first, chunk)
        wide = pl.ds(first * HEAD, chunk * HEAD)
        large[first] = (
            pltpu.make_async_copy(queries_hbm.at[:, wide], queries.at[:, wide], sems.at[at]),
            pltpu.make_async_copy(absorb_hbm.at[some], key_absorb.at[some], sems.at[at + 1]),
            pltpu.make_async_copy(expand_hbm.at[some], value_expand.at[some], sems.at[at + 2]),
        )
        first += chunk
    for copy in small:
        copy.start()
    for chunk_copies in large.values():
        for copy in chunk_copies:
            copy.start()
    steps = heads // group

    def absorb(g):
        for copy in large.get(g * group, ())[:2]:
            copy.wait()
        for h in range(g * group, (g + 1) * group):
            at = h * HEAD
            absorbed = jnp.dot(queries[:, at:at + NOPE], key_absorb[h], preferred_element_type=jnp.float32)
            combined[h * rows:(h + 1) * rows, :LAT] = absorbed.astype(jnp.bfloat16)
            combined[h * rows:(h + 1) * rows, LAT:] = queries[:, at + NOPE:at + HEAD]

    def score(g):
        return jnp.dot(combined[g * group * rows:(g + 1) * group * rows, :], own[...], preferred_element_type=jnp.float32)

    def value(g):
        for copy in large.get(g * group, ())[2:]:
            copy.wait()
        return [head_values(latents[...], value_expand, g * group + i) for i in range(0, group, 2)]

    def finish(g, scores, both):
        span = slice(g * group * rows, (g + 1) * group * rows)
        scores = (scores.reshape(group, rows, rows) + own_bias[None]).reshape(group * rows, rows)
        peak = jnp.max(scores, axis=1, keepdims=True)
        weights = jnp.exp2((scores - peak) * exp2_scale)
        total = jnp.sum(weights, axis=1, keepdims=True)
        weights = weights.astype(jnp.bfloat16)
        for i in range(group):
            mine = both[i // 2][:, i % 2 * VDIM:(i % 2 + 1) * VDIM]
            out = jnp.dot(weights[i * rows:(i + 1) * rows], mine, preferred_element_type=jnp.float32)
            result[(g * group + i) * rows:(g * group + i + 1) * rows, :] = out
        peaks[span, :] = jnp.broadcast_to(peak, (group * rows, LANES))
        totals[span, :] = jnp.broadcast_to(total, (group * rows, LANES))

    for copy in small:
        copy.wait()
    latents[...] = own[:LAT, :].T
    own_bias = visible_bias(prompt_pages, rows, 0)
    index_work(n_cp, count, slot_count, prompt_pages, decode_owner, slot_offset, own[...], sent_rows, bias, picked, filled)
    scores, both = {}, {}
    for step in range(steps + 2):
        if step < steps:
            absorb(step)
        if 0 <= step - 1 < steps:
            scores[step - 1] = score(step - 1)
            both[step - 1] = value(step - 1)
        if 0 <= step - 2:
            finish(step - 2, scores.pop(step - 2), both.pop(step - 2))


def index_work(n_cp, count, slot_count, prompt_pages, decode_owner, slot_offset, block, sent_rows, bias, picked, filled):
    rows = block.shape[1]
    me = lax.axis_index("cp")
    behind = lax.rem(me + n_cp - 1, n_cp)
    targets = []
    for valid, page in slot_pages(behind, slot_count, prompt_pages, decode_owner, slot_offset):
        here = valid & (page * PAGE // rows == me)
        targets.append(jnp.where(here, lax.rem(page * PAGE, rows), -PAGE))
    choice = row_picker(targets, rows)
    sent = lax.dot_general(choice, block, NT, preferred_element_type=jnp.float32)
    kept = choice.shape[0]
    sent_rows[...] = jnp.zeros(sent_rows.shape, jnp.bfloat16)
    sent_rows[:kept, :ROW] = sent.astype(jnp.bfloat16)
    for b in range(count):
        bias[:, b * rows:(b + 1) * rows] = visible_bias(prompt_pages, rows, swap_pair(jnp.int32(b + 1), n_cp))
    targets = []
    lane = lax.broadcasted_iota(jnp.int32, filled.shape, 1)
    lane_filled = jnp.zeros(filled.shape, jnp.float32)
    for c, (valid, page) in enumerate(slot_pages(me, slot_count, prompt_pages, decode_owner, slot_offset)):
        source = page * PAGE // rows
        column = swap_pair(lax.rem(me - source + n_cp, n_cp), n_cp) * rows + lax.rem(page * PAGE, rows)
        targets.append(jnp.where(valid, column, -PAGE))
        lane_filled = jnp.where(lane // PAGE == c, valid.astype(jnp.float32), lane_filled)
    filled[...] = lane_filled
    picked[...] = row_picker(targets, (n_cp - 1) * rows)


def pick_rows(picked, index, block):
    rows = block.shape[1]
    return lax.dot_general(picked[:, index * rows:(index + 1) * rows], block, NT, preferred_element_type=jnp.float32)


def arrived_kernel(used, picked, own, value_expand, *refs):
    blocks, (found, values) = refs[:-2], refs[-2:]
    rows = own.shape[1]
    for i in range(used):
        latents = blocks[i][:LAT, :].T
        for h in range(0, value_expand.shape[0], 2):
            values[i * rows:(i + 1) * rows, h * VDIM:(h + 2) * VDIM] = head_values(latents, value_expand, h)
    total = pick_rows(picked, 0, own[...])
    for i, block in enumerate(blocks):
        total = total + pick_rows(picked, 1 + 2 * i, block[...])
    found[...] = total


def write_cache(rows, filled, page_cache, page_scales):
    slot_count = page_cache.shape[0]
    scales = []
    for b in range(NBLK):
        values = rows[:, b * BLOCK:(b + 1) * BLOCK]
        scale = jnp.max(jnp.abs(values), axis=1, keepdims=True) + amax_epsilon
        scale = scale.astype(jnp.bfloat16).astype(jnp.float32)
        encoded = (values / scale).astype(jnp.bfloat16)
        for c in range(slot_count):
            page_cache[c, :, b * BLOCK:(b + 1) * BLOCK] = encoded[c * PAGE:(c + 1) * PAGE]
        scales.append(scale)
    kept = rows.shape[0]
    which = lax.broadcasted_iota(jnp.int32, (kept, LANES), 1)
    table = jnp.zeros((kept, LANES), jnp.float32)
    for b, scale in enumerate(scales):
        table = jnp.where(which == b, scale, table)
    table = (table.T[:NBLK] * filled[:1, :kept]).astype(jnp.bfloat16)
    for c in range(slot_count):
        page_cache[c, :, LAT:] = rows[c * PAGE:(c + 1) * PAGE, LAT:].astype(jnp.bfloat16)
        page_scales[c] = table[:, c * PAGE:(c + 1) * PAGE]


def earlier_kernel(count, group, *refs):
    combined, own_result, peaks, totals, value_expand, bias, fetched_values, picked, found = refs[:9]
    arrived, (attended, last, found_more, keys, latents, result, sems) = refs[9:-7], refs[-7:]
    rows, width = bias.shape
    heads = value_expand.shape[0]
    steps = heads // group

    def span(g):
        at = g * group * rows
        return slice(at, at + group * rows)

    def score(g):
        scores = jnp.dot(combined[span(g), :], keys[...], preferred_element_type=jnp.float32)
        return (scores.reshape(group, rows, width) + bias[...][None]).reshape(group * rows, width)

    def weigh(g, scores):
        old_peak = peaks[span(g), :]
        parts = [scores[:, b:b + LANES] for b in range(0, width, LANES)]
        peak = jnp.maximum(old_peak, jnp.max(functools.reduce(jnp.maximum, parts), axis=1, keepdims=True))
        parts = [jnp.exp2((part - peak) * exp2_scale) for part in parts]
        total = jnp.sum(functools.reduce(jnp.add, parts), axis=1, keepdims=True)
        factor = jnp.exp2((old_peak - peak) * exp2_scale)
        inverse = 1.0 / (totals[span(g), :] * factor + total)
        weights = jnp.concatenate([part.astype(jnp.bfloat16) for part in parts], axis=1)
        return weights, factor * inverse, inverse

    def value(g):
        return [
            [head_values(latents[i * rows:(i + 1) * rows, :], value_expand, h) for h in range(g * group, (g + 1) * group, 2)]
            for i in range(count // 2)
        ]

    def finish(g, weights, factor, inverse, swapped):
        for i in range(group):
            part = slice(i * rows, (i + 1) * rows)
            h = g * group + i
            values = []
            for b in range(count // 2):
                values.append(fetched_values[b * rows:(b + 1) * rows, h * VDIM:(h + 1) * VDIM])
                values.append(swapped[b][i // 2][:, i % 2 * VDIM:(i % 2 + 1) * VDIM])
            out = jnp.dot(weights[part], jnp.concatenate(values, axis=0), preferred_element_type=jnp.float32)
            out = own_result[h * rows:(h + 1) * rows, :] * factor[part] + out * inverse[part]
            place(h, out)

    def swapped_block(i):
        return jnp.concatenate([part[...] for part in arrived[i * (1 + SWAP) + 1:(i + 1) * (1 + SWAP)]], axis=0)

    def pick_swapped():
        total = found[...]
        latent_rows, rotary_rows = total[:, :LAT], total[:, LAT:]
        for i in range(len(arrived) // (1 + SWAP)):
            choice = picked[:, (2 + 2 * i) * rows:(3 + 2 * i) * rows]
            latent_rows = latent_rows + jnp.dot(choice, latents[i * rows:(i + 1) * rows, :], preferred_element_type=jnp.float32)
            rotary = swapped_block(i)[LAT:]
            rotary_rows = rotary_rows + lax.dot_general(choice, rotary, NT, preferred_element_type=jnp.float32)
        found_more[:, :LAT] = latent_rows
        found_more[:, LAT:] = rotary_rows

    def send(g):
        at = pl.ds(g * group * VDIM, group * VDIM)
        return pltpu.make_async_copy(result.at[:, at], attended.at[:, at], sems.at[g])

    def place(h, values):
        kept = (steps - 1) * group
        if h < kept:
            result[:, h * VDIM:(h + 1) * VDIM] = values.astype(jnp.bfloat16)
        else:
            last[:, (h - kept) * VDIM:(h - kept + 1) * VDIM] = values.astype(jnp.bfloat16)

    for i in range(len(arrived) // (1 + SWAP)):
        latents[i * rows:(i + 1) * rows, :] = swapped_block(i)[:LAT].T

    @pl.when(lax.axis_index("cp") == 0)
    def _():
        for h in range(heads):
            part = slice(h * rows, (h + 1) * rows)
            place(h, own_result[part, :] / totals[part, :])
            if (h + 1) % group == 0 and h < heads - group:
                send(h // group).start()
        pick_swapped()

    @pl.when(lax.axis_index("cp") > 0)
    def _():
        for i in range(count // 2):
            at = 2 * i * rows
            keys[:, at:at + rows] = arrived[i * (1 + SWAP)][...]
            keys[:, at + rows:at + 2 * rows] = swapped_block(i)
        scores, values, weights = {}, {}, {}
        for step in range(steps + 2):
            if step < steps:
                scores[step] = score(step)
            if step == 1:
                pick_swapped()
            if 0 <= step - 2:
                finish(step - 2, *weights.pop(step - 2), values.pop(step - 2))
                if step - 2 < steps - 1:
                    send(step - 2).start()
            if 0 <= step - 1 < steps:
                values[step - 1] = value(step - 1)
                weights[step - 1] = weigh(step - 1, scores.pop(step - 1))

    for g in range(steps - 1):
        send(g).wait()


def store_kernel(last, found, sent_rows, filled, _, attended, page_cache, page_scales, cache_buf, scale_buf, sems):
    at = pl.ds(attended.shape[1] - last.shape[1], last.shape[1])
    copies = [
        pltpu.make_async_copy(source, target, sems.at[i])
        for i, (source, target) in enumerate(((last, attended.at[:, at]), (cache_buf, page_cache), (scale_buf, page_scales)))
    ]
    copies[0].start()
    rows = found[...] + sent_rows[:found.shape[0], :ROW].astype(jnp.float32)
    write_cache(rows, filled, cache_buf, scale_buf)
    for copy in copies[1:]:
        copy.start()
    for copy in copies:
        copy.wait()


def fetch(own, n_cp, n_dec):
    blocks = []
    for step in range(1, n_cp - 1, 2):
        pairs = [(c * n_dec + e, (c + step + e % 2) % n_cp * n_dec + e) for c in range(n_cp) for e in range(n_dec)]
        blocks.append(lax.ppermute(own, ("cp", "dec"), pairs))
    return blocks


def swap(blocks, n_dec):
    pieces = []
    for block in blocks:
        parts = [block[at:at + ROW // SWAP] for at in range(0, ROW, ROW // SWAP)]
        pieces += [block] + [lax.ppermute(part, "dec", [(e, e ^ 1) for e in range(n_dec)]) for part in parts]
    return pieces


def on_device(queries, latent_rows, key_absorb, value_expand, prompt_pages, decode_owner, slot_offset):
    n_cp = lax.axis_size("cp")
    dec_count = lax.axis_size("dec")
    heads = key_absorb.shape[0]
    rows = latent_rows.shape[0]
    prompts, width = decode_owner.shape
    slot_count = 3 * (rows // PAGE) // (2 * dec_count)
    kept = slot_count * PAGE
    reach = width * dec_count * slot_count * PAGE
    count = -(-reach // rows) - (1 if prompts == 2 else 0)
    count = min(n_cp - 2, count + count % 2)
    own = latent_rows.T
    blocks = fetch(own, n_cp, dec_count)

    vmem = pl.BlockSpec(memory_space=pltpu.VMEM)
    hbm = pl.BlockSpec(memory_space=pltpu.HBM)
    params = pltpu.CompilerParams(vmem_limit_bytes=32 * 2**20)
    group, chunks = 4, (heads // 4, heads // 4, heads // 2)
    inputs = (prompt_pages, decode_owner, slot_offset, own, queries, key_absorb, value_expand)
    combined, result, peaks, totals, sent_rows, bias, picked, filled, own_copy, value_copy = pl.pallas_call(
        functools.partial(own_kernel, n_cp, count, chunks, group, slot_count),
        in_specs=[hbm] * 7,
        out_specs=[vmem] * 10,
        out_shape=[
            jax.ShapeDtypeStruct((heads * rows, ROW), jnp.bfloat16),
            jax.ShapeDtypeStruct((heads * rows, VDIM), jnp.float32),
            jax.ShapeDtypeStruct((heads * rows, LANES), jnp.float32),
            jax.ShapeDtypeStruct((heads * rows, LANES), jnp.float32),
            jax.ShapeDtypeStruct((kept + PAGE, -(-ROW // LANES) * LANES), jnp.bfloat16),
            jax.ShapeDtypeStruct((rows, count * rows), jnp.float32),
            jax.ShapeDtypeStruct((kept, (n_cp - 1) * rows), jnp.bfloat16),
            jax.ShapeDtypeStruct((8, LANES), jnp.float32),
            jax.ShapeDtypeStruct(own.shape, jnp.bfloat16),
            jax.ShapeDtypeStruct(value_expand.shape, jnp.bfloat16),
        ],
        scratch_shapes=[
            pltpu.SMEM(prompt_pages.shape, jnp.int32),
            pltpu.SMEM(decode_owner.shape, jnp.int32),
            pltpu.SMEM(slot_offset.shape, jnp.int32),
            pltpu.VMEM((rows, heads * HEAD), jnp.bfloat16),
            pltpu.VMEM((heads, NOPE, LAT), jnp.bfloat16),
            pltpu.VMEM((rows, LAT), jnp.bfloat16),
            pltpu.SemaphoreType.DMA((4 + 3 * len(chunks),)),
        ],
        cost_estimate=pl.CostEstimate(
            flops=2 * rows * heads * (2 * NOPE * LAT + rows * (ROW + VDIM)),
            bytes_accessed=2 * (queries.size + key_absorb.size + heads * rows * ROW),
            transcendentals=rows * heads * rows,
        ),
        compiler_params=params,
        name="own",
    )(*[pltpu.with_memory_space_constraint(x, pltpu.HBM) for x in inputs])
    sent_rows = lax.ppermute(sent_rows, "cp", [(c, (c + n_cp - 1) % n_cp) for c in range(n_cp)])
    blocks, picked = lax.optimization_barrier((blocks, picked))
    pieces = swap(blocks, dec_count)
    found, fetched_values = pl.pallas_call(
        functools.partial(arrived_kernel, count // 2),
        in_specs=[vmem] * (3 + len(blocks)),
        out_specs=[vmem] * 2,
        out_shape=[
            jax.ShapeDtypeStruct((kept, ROW), jnp.float32),
            jax.ShapeDtypeStruct((count // 2 * rows, heads * VDIM), jnp.bfloat16),
        ],
        cost_estimate=pl.CostEstimate(flops=2**20, bytes_accessed=2**10, transcendentals=0),
        compiler_params=params,
        name="arrived",
    )(picked, own_copy, value_copy, *blocks)

    group = 4 if count <= 4 else 2
    steps = heads // group
    operands = (combined, result, peaks, totals, value_copy, bias, fetched_values, picked, found, *pieces)
    attended, last, found = pl.pallas_call(
        functools.partial(earlier_kernel, count, group),
        in_specs=[vmem] * len(operands),
        out_specs=[hbm, vmem, vmem],
        out_shape=[
            jax.ShapeDtypeStruct((rows, heads * VDIM), jnp.bfloat16),
            jax.ShapeDtypeStruct((rows, group * VDIM), jnp.bfloat16),
            jax.ShapeDtypeStruct((kept, ROW), jnp.float32),
        ],
        scratch_shapes=[
            pltpu.VMEM((ROW, count * rows), jnp.bfloat16),
            pltpu.VMEM((len(blocks) * rows, LAT), jnp.bfloat16),
            pltpu.VMEM((rows, (steps - 1) * group * VDIM), jnp.bfloat16),
            pltpu.SemaphoreType.DMA((steps - 1,)),
        ],
        cost_estimate=pl.CostEstimate(flops=2**20, bytes_accessed=2**10, transcendentals=0),
        compiler_params=params,
        name="earlier",
    )(*operands)
    sent_rows, last = lax.optimization_barrier((sent_rows, last))
    operands = (last, found, sent_rows, filled, attended)
    attended, page_cache, page_scales = pl.pallas_call(
        store_kernel,
        in_specs=[vmem] * (len(operands) - 1) + [hbm],
        out_specs=[hbm] * 3,
        out_shape=[
            jax.ShapeDtypeStruct((rows, heads * VDIM), jnp.bfloat16),
            jax.ShapeDtypeStruct((slot_count, PAGE, ROW), jnp.bfloat16),
            jax.ShapeDtypeStruct((slot_count, NBLK, PAGE), jnp.bfloat16),
        ],
        scratch_shapes=[
            pltpu.VMEM((slot_count, PAGE, ROW), jnp.bfloat16),
            pltpu.VMEM((slot_count, NBLK, PAGE), jnp.bfloat16),
            pltpu.SemaphoreType.DMA((3,)),
        ],
        input_output_aliases={len(operands) - 1: 0},
        cost_estimate=pl.CostEstimate(flops=2**20, bytes_accessed=2**10, transcendentals=0),
        compiler_params=params,
        name="store",
    )(*operands)
    page_cache = page_cache.reshape(1, 1, slot_count, PAGE, ROW)
    page_scales = page_scales.transpose(0, 2, 1).reshape(1, 1, slot_count, PAGE, NBLK)
    return attended, page_cache, page_scales


def solution(mesh):
    return jax.shard_map(
        on_device,
        mesh=mesh,
        in_specs=(
            P(("grp", "cp"), "dec"),
            P(("grp", "cp"), None),
            P("dec", None, None),
            P("dec", None, None),
            P("grp"),
            P("grp", None),
            P("grp"),
        ),
        out_specs=(
            P(("grp", "cp"), "dec"),
            P(("grp", "cp"), "dec", None, None, None),
            P(("grp", "cp"), "dec", None, None, None),
        ),
        check_vma=False,
    )
```

```python
import functools
import math

import jax
import jax.numpy as jnp
from jax import lax
from jax.experimental import pallas as pl
from jax.experimental.pallas import tpu as pltpu
from jax.sharding import PartitionSpec as P

LAT = 512
ROPE = 64
NOPE = 128
VDIM = 128
PAGE = 16
BLOCK = 128
NBLK = LAT // BLOCK
ROW = LAT + ROPE
HEAD = NOPE + ROPE
LANES = 128
SWAP = 2

masked_fill = -1e30
amax_epsilon = 1e-06
exp2_scale = math.log2(math.e) / math.sqrt(HEAD)

NT = (((1,), (1,)), ((), ()))


def prompt_starts(prompt_pages):
    starts = [jnp.int32(0)]
    for k in range(prompt_pages.shape[0] - 1):
        starts.append(starts[-1] + prompt_pages[k])
    return starts


def visible_bias(prompt_pages, rows, steps_back):
    first = lax.axis_index("cp") * rows
    token = first + lax.broadcasted_iota(jnp.int32, (rows, 1), 0)
    begin = jnp.zeros((rows, 1), jnp.int32)
    for start in prompt_starts(prompt_pages):
        begin = jnp.maximum(begin, jnp.where(start * PAGE <= token, start * PAGE, 0))
    spot = first - steps_back * rows + lax.broadcasted_iota(jnp.int32, (1, rows), 1)
    return jnp.where((spot >= begin) & (spot <= token), 0.0, masked_fill)


def swap_pair(position, n_cp):
    odd = lax.rem(lax.axis_index("dec"), 2)
    within = lax.rem(position + 1, 2)
    swapped = position - within + lax.rem(within + odd, 2)
    paired = (position >= 1) & (position <= (n_cp - 1) // 2 * 2)
    return jnp.where(paired, swapped, position)


def slot_pages(owner, slot_count, prompt_pages, decode_owner, slot_offset):
    prompts, width = decode_owner.shape
    cycle = width * lax.axis_size("dec") * slot_count
    starts = prompt_starts(prompt_pages)
    pages, start, offset, place = jnp.int32(0), jnp.int32(0), jnp.int32(0), jnp.int32(0)
    for k in range(prompts):
        for p in range(width):
            mine = decode_owner[k, p] == owner
            pages = jnp.where(mine, prompt_pages[k], pages)
            start = jnp.where(mine, starts[k], start)
            offset = jnp.where(mine, slot_offset[k], offset)
            place = jnp.where(mine, p, place)
    result = []
    for c in range(slot_count):
        turn = width * (lax.axis_index("dec") * slot_count + c) + place
        page = lax.rem(turn - offset + 2 * cycle, cycle)
        result.append((page < pages, start + page))
    return result


def row_picker(targets, columns):
    kept = len(targets) * PAGE
    row = lax.broadcasted_iota(jnp.int32, (kept, 1), 0)
    target = jnp.full((kept, 1), -1, jnp.int32)
    for c, column in enumerate(targets):
        target = jnp.where(row // PAGE == c, column + row % PAGE, target)
    column = lax.broadcasted_iota(jnp.int32, (1, columns), 1)
    return jnp.where(column == target, 1.0, 0.0).astype(jnp.bfloat16)


def head_values(latents, value_expand, h):
    both = jnp.concatenate([value_expand[h], value_expand[h + 1]], axis=1)
    return jnp.dot(latents, both, preferred_element_type=jnp.float32).astype(jnp.bfloat16)


def own_kernel(n_cp, count, chunks, group, slot_count, *refs):
    inputs, refs = refs[:7], refs[7:]
    combined, result, peaks, totals, sent_rows, bias, picked, filled, own, value_expand = refs[:10]
    prompt_pages, decode_owner, slot_offset, queries, key_absorb, latents, sems = refs[10:]
    pages_hbm, owner_hbm, offset_hbm, own_hbm, queries_hbm, absorb_hbm, expand_hbm = inputs
    rows = own.shape[1]
    heads = key_absorb.shape[0]
    small = [
        pltpu.make_async_copy(source, target, sems.at[i])
        for i, (source, target) in enumerate(zip(inputs[:4], (prompt_pages, decode_owner, slot_offset, own)))
    ]
    large = {}
    first = 0
    for chunk in chunks:
        at = 4 + 3 * len(large)
        some = pl.ds(first, chunk)
        wide = pl.ds(first * HEAD, chunk * HEAD)
        large[first] = (
            pltpu.make_async_copy(queries_hbm.at[:, wide], queries.at[:, wide], sems.at[at]),
            pltpu.make_async_copy(absorb_hbm.at[some], key_absorb.at[some], sems.at[at + 1]),
            pltpu.make_async_copy(expand_hbm.at[some], value_expand.at[some], sems.at[at + 2]),
        )
        first += chunk
    for copy in small:
        copy.start()
    for chunk_copies in large.values():
        for copy in chunk_copies:
            copy.start()
    steps = heads // group

    def absorb(g):
        for copy in large.get(g * group, ())[:2]:
            copy.wait()
        for h in range(g * group, (g + 1) * group):
            at = h * HEAD
            absorbed = jnp.dot(queries[:, at:at + NOPE], key_absorb[h], preferred_element_type=jnp.float32)
            combined[h * rows:(h + 1) * rows, :LAT] = absorbed.astype(jnp.bfloat16)
            combined[h * rows:(h + 1) * rows, LAT:] = queries[:, at + NOPE:at + HEAD]

    def score(g):
        return jnp.dot(combined[g * group * rows:(g + 1) * group * rows, :], own[...], preferred_element_type=jnp.float32)

    def value(g):
        for copy in large.get(g * group, ())[2:]:
            copy.wait()
        return [head_values(latents[...], value_expand, g * group + i) for i in range(0, group, 2)]

    def finish(g, scores, both):
        span = slice(g * group * rows, (g + 1) * group * rows)
        scores = (scores.reshape(group, rows, rows) + own_bias[None]).reshape(group * rows, rows)
        peak = jnp.max(scores, axis=1, keepdims=True)
        weights = jnp.exp2((scores - peak) * exp2_scale)
        total = jnp.sum(weights, axis=1, keepdims=True)
        weights = weights.astype(jnp.bfloat16)
        for i in range(group):
            mine = both[i // 2][:, i % 2 * VDIM:(i % 2 + 1) * VDIM]
            out = jnp.dot(weights[i * rows:(i + 1) * rows], mine, preferred_element_type=jnp.float32)
            result[(g * group + i) * rows:(g * group + i + 1) * rows, :] = out
        peaks[span, :] = jnp.broadcast_to(peak, (group * rows, LANES))
        totals[span, :] = jnp.broadcast_to(total, (group * rows, LANES))

    for copy in small:
        copy.wait()
    latents[...] = own[:LAT, :].T
    own_bias = visible_bias(prompt_pages, rows, 0)
    index_work(n_cp, count, slot_count, prompt_pages, decode_owner, slot_offset, own[...], sent_rows, bias, picked, filled)
    scores, both = {}, {}
    for step in range(steps + 2):
        if step < steps:
            absorb(step)
        if 0 <= step - 1 < steps:
            scores[step - 1] = score(step - 1)
            both[step - 1] = value(step - 1)
        if 0 <= step - 2:
            finish(step - 2, scores.pop(step - 2), both.pop(step - 2))


def index_work(n_cp, count, slot_count, prompt_pages, decode_owner, slot_offset, block, sent_rows, bias, picked, filled):
    rows = block.shape[1]
    me = lax.axis_index("cp")
    behind = lax.rem(me + n_cp - 1, n_cp)
    targets, here = [], []
    for valid, page in slot_pages(behind, slot_count, prompt_pages, decode_owner, slot_offset):
        here.append(valid & (page * PAGE // rows == me))
        targets.append(jnp.where(here[-1], lax.rem(page * PAGE, rows), -PAGE))
    choice = row_picker(targets, rows)
    sent = lax.dot_general(choice, block, NT, preferred_element_type=jnp.float32)
    encoded, scales = encode(sent, slot_lanes(here))
    kept = choice.shape[0]
    sent_rows[...] = jnp.zeros(sent_rows.shape, jnp.bfloat16)
    sent_rows[:kept, :ROW] = encoded
    sent_rows[kept:kept + NBLK, :kept] = scales
    for b in range(count):
        bias[:, b * rows:(b + 1) * rows] = visible_bias(prompt_pages, rows, swap_pair(jnp.int32(b + 1), n_cp))
    targets, found = [], []
    for valid, page in slot_pages(me, slot_count, prompt_pages, decode_owner, slot_offset):
        steps_back = lax.rem(me - page * PAGE // rows + n_cp, n_cp)
        column = swap_pair(steps_back, n_cp) * rows + lax.rem(page * PAGE, rows)
        targets.append(jnp.where(valid, column, -PAGE))
        found.append(valid & (steps_back < n_cp - 1))
    filled[:1, :] = slot_lanes(found, filled.shape[1])
    picked[...] = row_picker(targets, (n_cp - 1) * rows)


def pick_rows(picked, index, block):
    rows = block.shape[1]
    return lax.dot_general(picked[:, index * rows:(index + 1) * rows], block, NT, preferred_element_type=jnp.float32)


def arrived_kernel(used, picked, own, value_expand, *refs):
    blocks, (found, values) = refs[:-2], refs[-2:]
    rows = own.shape[1]
    for i in range(used):
        latents = blocks[i][:LAT, :].T
        for h in range(0, value_expand.shape[0], 2):
            values[i * rows:(i + 1) * rows, h * VDIM:(h + 2) * VDIM] = head_values(latents, value_expand, h)
    total = pick_rows(picked, 0, own[...])
    for i, block in enumerate(blocks):
        total = total + pick_rows(picked, 1 + 2 * i, block[...])
    found[...] = total


def slot_lanes(flags, width=None):
    lane = lax.broadcasted_iota(jnp.int32, (1, width or len(flags) * PAGE), 1)
    lanes = jnp.zeros(lane.shape, jnp.float32)
    for c, flag in enumerate(flags):
        lanes = jnp.where(lane // PAGE == c, flag.astype(jnp.float32), lanes)
    return lanes


def encode(rows, filled):
    kept = rows.shape[0]
    which = lax.broadcasted_iota(jnp.int32, (kept, LANES), 1)
    table = jnp.zeros((kept, LANES), jnp.float32)
    encoded = []
    for b in range(NBLK):
        values = rows[:, b * BLOCK:(b + 1) * BLOCK]
        scale = jnp.max(jnp.abs(values), axis=1, keepdims=True) + amax_epsilon
        scale = scale.astype(jnp.bfloat16).astype(jnp.float32)
        encoded.append((values / scale).astype(jnp.bfloat16))
        table = jnp.where(which == b, scale, table)
    encoded.append(rows[:, LAT:].astype(jnp.bfloat16))
    scales = (table.T[:NBLK] * filled).astype(jnp.bfloat16)
    return jnp.concatenate(encoded, axis=1), scales


def earlier_kernel(count, group, *refs):
    combined, own_result, peaks, totals, value_expand, bias, fetched_values, picked, found, filled = refs[:10]
    arrived, (result, encoded, scales, keys, latents) = refs[10:-5], refs[-5:]
    rows, width = bias.shape
    heads = value_expand.shape[0]
    steps = heads // group

    def span(g):
        at = g * group * rows
        return slice(at, at + group * rows)

    def score(g):
        scores = jnp.dot(combined[span(g), :], keys[...], preferred_element_type=jnp.float32)
        return (scores.reshape(group, rows, width) + bias[...][None]).reshape(group * rows, width)

    def weigh(g, scores):
        old_peak = peaks[span(g), :]
        parts = [scores[:, b:b + LANES] for b in range(0, width, LANES)]
        peak = jnp.maximum(old_peak, jnp.max(functools.reduce(jnp.maximum, parts), axis=1, keepdims=True))
        parts = [jnp.exp2((part - peak) * exp2_scale) for part in parts]
        total = jnp.sum(functools.reduce(jnp.add, parts), axis=1, keepdims=True)
        factor = jnp.exp2((old_peak - peak) * exp2_scale)
        inverse = 1.0 / (totals[span(g), :] * factor + total)
        weights = jnp.concatenate([part.astype(jnp.bfloat16) for part in parts], axis=1)
        return weights, factor * inverse, inverse

    def value(g):
        return [
            [head_values(latents[i * rows:(i + 1) * rows, :], value_expand, h) for h in range(g * group, (g + 1) * group, 2)]
            for i in range(count // 2)
        ]

    def finish(g, weights, factor, inverse, swapped):
        for i in range(group):
            part = slice(i * rows, (i + 1) * rows)
            h = g * group + i
            values = []
            for b in range(count // 2):
                values.append(fetched_values[b * rows:(b + 1) * rows, h * VDIM:(h + 1) * VDIM])
                values.append(swapped[b][i // 2][:, i % 2 * VDIM:(i % 2 + 1) * VDIM])
            out = jnp.dot(weights[part], jnp.concatenate(values, axis=0), preferred_element_type=jnp.float32)
            out = own_result[h * rows:(h + 1) * rows, :] * factor[part] + out * inverse[part]
            result[:, h * VDIM:(h + 1) * VDIM] = out.astype(jnp.bfloat16)

    def swapped_block(i):
        return jnp.concatenate([part[...] for part in arrived[i * (1 + SWAP) + 1:(i + 1) * (1 + SWAP)]], axis=0)

    def encode_found():
        total = found[...]
        latent_rows, rotary_rows = total[:, :LAT], total[:, LAT:]
        for i in range(len(arrived) // (1 + SWAP)):
            choice = picked[:, (2 + 2 * i) * rows:(3 + 2 * i) * rows]
            latent_rows = latent_rows + jnp.dot(choice, latents[i * rows:(i + 1) * rows, :], preferred_element_type=jnp.float32)
            rotary = swapped_block(i)[LAT:]
            rotary_rows = rotary_rows + lax.dot_general(choice, rotary, NT, preferred_element_type=jnp.float32)
        every = jnp.concatenate([latent_rows, rotary_rows], axis=1)
        encoded[...], scales[...] = encode(every, filled[:1, :every.shape[0]])

    for i in range(len(arrived) // (1 + SWAP)):
        latents[i * rows:(i + 1) * rows, :] = swapped_block(i)[:LAT].T

    @pl.when(lax.axis_index("cp") == 0)
    def _():
        for h in range(heads):
            part = slice(h * rows, (h + 1) * rows)
            result[:, h * VDIM:(h + 1) * VDIM] = (own_result[part, :] / totals[part, :]).astype(jnp.bfloat16)
        encode_found()

    @pl.when(lax.axis_index("cp") > 0)
    def _():
        for i in range(count // 2):
            at = 2 * i * rows
            keys[:, at:at + rows] = arrived[i * (1 + SWAP)][...]
            keys[:, at + rows:at + 2 * rows] = swapped_block(i)
        scores, values, weights = {}, {}, {}
        for step in range(steps + 2):
            if step < steps:
                scores[step] = score(step)
            if step == 2:
                encode_found()
            if 0 <= step - 2:
                finish(step - 2, *weights.pop(step - 2), values.pop(step - 2))
            if 0 <= step - 1 < steps:
                values[step - 1] = value(step - 1)
                weights[step - 1] = weigh(step - 1, scores.pop(step - 1))


def store_kernel(result, encoded, scales, sent_rows, attended, page_cache, page_scales, cache_buf, scale_buf, sems):
    count = sems.shape[0] - 2
    wide = result.shape[1] // count
    copies = []
    for i in range(count):
        some = pl.ds(i * wide, wide)
        copies.append(pltpu.make_async_copy(result.at[:, some], attended.at[:, some], sems.at[i]))
        copies[-1].start()
    kept = encoded.shape[0]
    for c in range(page_cache.shape[0]):
        part = slice(c * PAGE, (c + 1) * PAGE)
        cache_buf[c] = encoded[part, :] + sent_rows[part, :ROW]
        scale_buf[c] = (scales[...] + sent_rows[kept:kept + NBLK, :kept])[:, part]
    for i, (source, target) in enumerate(((cache_buf, page_cache), (scale_buf, page_scales))):
        copies.append(pltpu.make_async_copy(source, target, sems.at[count + i]))
        copies[-1].start()
    for copy in copies:
        copy.wait()


def fetch(own, n_cp, n_dec):
    blocks = []
    for step in range(1, n_cp - 1, 2):
        pairs = [(c * n_dec + e, (c + step + e % 2) % n_cp * n_dec + e) for c in range(n_cp) for e in range(n_dec)]
        blocks.append(lax.ppermute(own, ("cp", "dec"), pairs))
    return blocks


def swap(blocks, n_dec):
    pieces = []
    for block in blocks:
        parts = [block[at:at + ROW // SWAP] for at in range(0, ROW, ROW // SWAP)]
        pieces += [block] + [lax.ppermute(part, "dec", [(e, e ^ 1) for e in range(n_dec)]) for part in parts]
    return pieces


def on_device(queries, latent_rows, key_absorb, value_expand, prompt_pages, decode_owner, slot_offset):
    n_cp = lax.axis_size("cp")
    dec_count = lax.axis_size("dec")
    heads = key_absorb.shape[0]
    rows = latent_rows.shape[0]
    prompts, width = decode_owner.shape
    slot_count = 3 * (rows // PAGE) // (2 * dec_count)
    kept = slot_count * PAGE
    reach = width * dec_count * slot_count * PAGE
    count = -(-reach // rows) - (1 if prompts == 2 else 0)
    count = min(n_cp - 2, count + count % 2)
    own = latent_rows.T
    blocks = fetch(own, n_cp, dec_count)

    vmem = pl.BlockSpec(memory_space=pltpu.VMEM)
    hbm = pl.BlockSpec(memory_space=pltpu.HBM)
    params = pltpu.CompilerParams(vmem_limit_bytes=32 * 2**20)
    group, chunks = 4, (heads // 4, heads // 4, heads // 2)
    inputs = (prompt_pages, decode_owner, slot_offset, own, queries, key_absorb, value_expand)
    combined, result, peaks, totals, sent_rows, bias, picked, filled, own_copy, value_copy = pl.pallas_call(
        functools.partial(own_kernel, n_cp, count, chunks, group, slot_count),
        in_specs=[hbm] * 7,
        out_specs=[vmem] * 10,
        out_shape=[
            jax.ShapeDtypeStruct((heads * rows, ROW), jnp.bfloat16),
            jax.ShapeDtypeStruct((heads * rows, VDIM), jnp.float32),
            jax.ShapeDtypeStruct((heads * rows, LANES), jnp.float32),
            jax.ShapeDtypeStruct((heads * rows, LANES), jnp.float32),
            jax.ShapeDtypeStruct((kept + PAGE, -(-ROW // LANES) * LANES), jnp.bfloat16),
            jax.ShapeDtypeStruct((rows, count * rows), jnp.float32),
            jax.ShapeDtypeStruct((kept, (n_cp - 1) * rows), jnp.bfloat16),
            jax.ShapeDtypeStruct((8, LANES), jnp.float32),
            jax.ShapeDtypeStruct(own.shape, jnp.bfloat16),
            jax.ShapeDtypeStruct(value_expand.shape, jnp.bfloat16),
        ],
        scratch_shapes=[
            pltpu.SMEM(prompt_pages.shape, jnp.int32),
            pltpu.SMEM(decode_owner.shape, jnp.int32),
            pltpu.SMEM(slot_offset.shape, jnp.int32),
            pltpu.VMEM((rows, heads * HEAD), jnp.bfloat16),
            pltpu.VMEM((heads, NOPE, LAT), jnp.bfloat16),
            pltpu.VMEM((rows, LAT), jnp.bfloat16),
            pltpu.SemaphoreType.DMA((4 + 3 * len(chunks),)),
        ],
        cost_estimate=pl.CostEstimate(
            flops=2 * rows * heads * (2 * NOPE * LAT + rows * (ROW + VDIM)),
            bytes_accessed=2 * (queries.size + key_absorb.size + heads * rows * ROW),
            transcendentals=rows * heads * rows,
        ),
        compiler_params=params,
        name="own",
    )(*[pltpu.with_memory_space_constraint(x, pltpu.HBM) for x in inputs])
    sent_rows = lax.ppermute(sent_rows, "cp", [(c, (c + n_cp - 1) % n_cp) for c in range(n_cp)])
    blocks, picked = lax.optimization_barrier((blocks, picked))
    pieces = swap(blocks, dec_count)
    found, fetched_values = pl.pallas_call(
        functools.partial(arrived_kernel, count // 2),
        in_specs=[vmem] * (3 + len(blocks)),
        out_specs=[vmem] * 2,
        out_shape=[
            jax.ShapeDtypeStruct((kept, ROW), jnp.float32),
            jax.ShapeDtypeStruct((count // 2 * rows, heads * VDIM), jnp.bfloat16),
        ],
        cost_estimate=pl.CostEstimate(flops=2**20, bytes_accessed=2**10, transcendentals=0),
        compiler_params=params,
        name="arrived",
    )(picked, own_copy, value_copy, *blocks)

    group = 4 if count <= 4 else 2
    operands = (combined, result, peaks, totals, value_copy, bias, fetched_values, picked, found, filled, *pieces)
    attended, encoded, scales = pl.pallas_call(
        functools.partial(earlier_kernel, count, group),
        in_specs=[vmem] * len(operands),
        out_specs=[vmem] * 3,
        out_shape=[
            jax.ShapeDtypeStruct((rows, heads * VDIM), jnp.bfloat16),
            jax.ShapeDtypeStruct((kept, ROW), jnp.bfloat16),
            jax.ShapeDtypeStruct((NBLK, kept), jnp.bfloat16),
        ],
        scratch_shapes=[
            pltpu.VMEM((ROW, count * rows), jnp.bfloat16),
            pltpu.VMEM((len(blocks) * rows, LAT), jnp.bfloat16),
        ],
        cost_estimate=pl.CostEstimate(flops=2**20, bytes_accessed=2**10, transcendentals=0),
        compiler_params=params,
        name="earlier",
    )(*operands)
    sent_rows, attended = lax.optimization_barrier((sent_rows, attended))
    operands = (attended, encoded, scales, sent_rows)
    attended, page_cache, page_scales = pl.pallas_call(
        store_kernel,
        in_specs=[vmem] * len(operands),
        out_specs=[hbm] * 3,
        out_shape=[
            jax.ShapeDtypeStruct((rows, heads * VDIM), jnp.bfloat16),
            jax.ShapeDtypeStruct((slot_count, PAGE, ROW), jnp.bfloat16),
            jax.ShapeDtypeStruct((slot_count, NBLK, PAGE), jnp.bfloat16),
        ],
        scratch_shapes=[
            pltpu.VMEM((slot_count, PAGE, ROW), jnp.bfloat16),
            pltpu.VMEM((slot_count, NBLK, PAGE), jnp.bfloat16),
            pltpu.SemaphoreType.DMA((4 + 2,)),
        ],
        cost_estimate=pl.CostEstimate(flops=2**20, bytes_accessed=2**10, transcendentals=0),
        compiler_params=params,
        name="store",
    )(*operands)
    page_cache = page_cache.reshape(1, 1, slot_count, PAGE, ROW)
    page_scales = page_scales.transpose(0, 2, 1).reshape(1, 1, slot_count, PAGE, NBLK)
    return attended, page_cache, page_scales


def solution(mesh):
    return jax.shard_map(
        on_device,
        mesh=mesh,
        in_specs=(
            P(("grp", "cp"), "dec"),
            P(("grp", "cp"), None),
            P("dec", None, None),
            P("dec", None, None),
            P("grp"),
            P("grp", None),
            P("grp"),
        ),
        out_specs=(
            P(("grp", "cp"), "dec"),
            P(("grp", "cp"), "dec", None, None, None),
            P(("grp", "cp"), "dec", None, None, None),
        ),
        check_vma=False,
    )
```

```python
import functools
import math

import jax
import jax.numpy as jnp
from jax import lax
from jax.experimental import pallas as pl
from jax.experimental.pallas import tpu as pltpu
from jax.sharding import PartitionSpec as P

LAT = 512
ROPE = 64
NOPE = 128
VDIM = 128
PAGE = 16
BLOCK = 128
NBLK = LAT // BLOCK
ROW = LAT + ROPE
HEAD = NOPE + ROPE
LANES = 128
SWAP = 2

masked_fill = -1e30
amax_epsilon = 1e-06
exp2_scale = math.log2(math.e) / math.sqrt(HEAD)

NT = (((1,), (1,)), ((), ()))


def prompt_starts(prompt_pages):
    starts = [jnp.int32(0)]
    for k in range(prompt_pages.shape[0] - 1):
        starts.append(starts[-1] + prompt_pages[k])
    return starts


def visible_bias(prompt_pages, rows, steps_back):
    first = lax.axis_index("cp") * rows
    token = first + lax.broadcasted_iota(jnp.int32, (rows, 1), 0)
    begin = jnp.zeros((rows, 1), jnp.int32)
    for start in prompt_starts(prompt_pages):
        begin = jnp.maximum(begin, jnp.where(start * PAGE <= token, start * PAGE, 0))
    spot = first - steps_back * rows + lax.broadcasted_iota(jnp.int32, (1, rows), 1)
    return jnp.where((spot >= begin) & (spot <= token), 0.0, masked_fill)


def swap_pair(position, n_cp):
    odd = lax.rem(lax.axis_index("dec"), 2)
    within = lax.rem(position + 1, 2)
    swapped = position - within + lax.rem(within + odd, 2)
    paired = (position >= 1) & (position <= (n_cp - 1) // 2 * 2)
    return jnp.where(paired, swapped, position)


def slot_pages(owner, slot_count, prompt_pages, decode_owner, slot_offset):
    prompts, width = decode_owner.shape
    cycle = width * lax.axis_size("dec") * slot_count
    starts = prompt_starts(prompt_pages)
    pages, start, offset, place = jnp.int32(0), jnp.int32(0), jnp.int32(0), jnp.int32(0)
    for k in range(prompts):
        for p in range(width):
            mine = decode_owner[k, p] == owner
            pages = jnp.where(mine, prompt_pages[k], pages)
            start = jnp.where(mine, starts[k], start)
            offset = jnp.where(mine, slot_offset[k], offset)
            place = jnp.where(mine, p, place)
    result = []
    for c in range(slot_count):
        turn = width * (lax.axis_index("dec") * slot_count + c) + place
        page = lax.rem(turn - offset + 2 * cycle, cycle)
        result.append((page < pages, start + page))
    return result


def row_picker(targets, columns):
    kept = len(targets) * PAGE
    row = lax.broadcasted_iota(jnp.int32, (kept, 1), 0)
    target = jnp.full((kept, 1), -1, jnp.int32)
    for c, column in enumerate(targets):
        target = jnp.where(row // PAGE == c, column + row % PAGE, target)
    column = lax.broadcasted_iota(jnp.int32, (1, columns), 1)
    return jnp.where(column == target, 1.0, 0.0).astype(jnp.bfloat16)


def head_values(latents, value_expand, h):
    both = jnp.concatenate([value_expand[h], value_expand[h + 1]], axis=1)
    return jnp.dot(latents, both, preferred_element_type=jnp.float32).astype(jnp.bfloat16)


def own_kernel(n_cp, count, chunks, group, slot_count, *refs):
    inputs, refs = refs[:7], refs[7:]
    combined, result, peaks, totals, sent_rows, bias, picked, filled, own, value_expand = refs[:10]
    prompt_pages, decode_owner, slot_offset, queries, key_absorb, latents, sems = refs[10:]
    pages_hbm, owner_hbm, offset_hbm, own_hbm, queries_hbm, absorb_hbm, expand_hbm = inputs
    rows = own.shape[1]
    heads = key_absorb.shape[0]
    small = [
        pltpu.make_async_copy(source, target, sems.at[i])
        for i, (source, target) in enumerate(zip(inputs[:4], (prompt_pages, decode_owner, slot_offset, own)))
    ]
    large = {}
    first = 0
    for chunk in chunks:
        at = 4 + 3 * len(large)
        some = pl.ds(first, chunk)
        wide = pl.ds(first * HEAD, chunk * HEAD)
        large[first] = (
            pltpu.make_async_copy(queries_hbm.at[:, wide], queries.at[:, wide], sems.at[at]),
            pltpu.make_async_copy(absorb_hbm.at[some], key_absorb.at[some], sems.at[at + 1]),
            pltpu.make_async_copy(expand_hbm.at[some], value_expand.at[some], sems.at[at + 2]),
        )
        first += chunk
    for copy in small:
        copy.start()
    for chunk_copies in large.values():
        for copy in chunk_copies:
            copy.start()
    steps = heads // group

    def absorb(g):
        for copy in large.get(g * group, ())[:2]:
            copy.wait()
        for h in range(g * group, (g + 1) * group):
            at = h * HEAD
            absorbed = jnp.dot(queries[:, at:at + NOPE], key_absorb[h], preferred_element_type=jnp.float32)
            combined[h * rows:(h + 1) * rows, :LAT] = absorbed.astype(jnp.bfloat16)
            combined[h * rows:(h + 1) * rows, LAT:] = queries[:, at + NOPE:at + HEAD]

    def score(g):
        return jnp.dot(combined[g * group * rows:(g + 1) * group * rows, :], own[...], preferred_element_type=jnp.float32)

    def value(g):
        for copy in large.get(g * group, ())[2:]:
            copy.wait()
        return [head_values(latents[...], value_expand, g * group + i) for i in range(0, group, 2)]

    def finish(g, scores, both):
        span = slice(g * group * rows, (g + 1) * group * rows)
        scores = (scores.reshape(group, rows, rows) + own_bias[None]).reshape(group * rows, rows)
        peak = jnp.max(scores, axis=1, keepdims=True)
        weights = jnp.exp2((scores - peak) * exp2_scale)
        total = jnp.sum(weights, axis=1, keepdims=True)
        weights = weights.astype(jnp.bfloat16)
        for i in range(group):
            mine = both[i // 2][:, i % 2 * VDIM:(i % 2 + 1) * VDIM]
            out = jnp.dot(weights[i * rows:(i + 1) * rows], mine, preferred_element_type=jnp.float32)
            result[(g * group + i) * rows:(g * group + i + 1) * rows, :] = out
        peaks[span, :] = jnp.broadcast_to(peak, (group * rows, LANES))
        totals[span, :] = jnp.broadcast_to(total, (group * rows, LANES))

    for copy in small:
        copy.wait()
    latents[...] = own[:LAT, :].T
    own_bias = visible_bias(prompt_pages, rows, 0)
    scores, both = {}, {}
    for step in range(steps + 2):
        if step < steps:
            absorb(step)
        if 0 <= step - 1 < steps:
            scores[step - 1] = score(step - 1)
            both[step - 1] = value(step - 1)
        if step == 1:
            index_work(n_cp, count, slot_count, prompt_pages, decode_owner, slot_offset, own[...], sent_rows, bias, picked, filled)
        if 0 <= step - 2:
            finish(step - 2, scores.pop(step - 2), both.pop(step - 2))


def index_work(n_cp, count, slot_count, prompt_pages, decode_owner, slot_offset, block, sent_rows, bias, picked, filled):
    rows = block.shape[1]
    me = lax.axis_index("cp")
    behind = lax.rem(me + n_cp - 1, n_cp)
    targets, here = [], []
    for valid, page in slot_pages(behind, slot_count, prompt_pages, decode_owner, slot_offset):
        here.append(valid & (page * PAGE // rows == me))
        targets.append(jnp.where(here[-1], lax.rem(page * PAGE, rows), -PAGE))
    choice = row_picker(targets, rows)
    sent = lax.dot_general(choice, block, NT, preferred_element_type=jnp.float32)
    encoded, scales = encode(sent, slot_lanes(here))
    kept = choice.shape[0]
    sent_rows[...] = jnp.zeros(sent_rows.shape, jnp.bfloat16)
    sent_rows[:kept, :ROW] = encoded
    sent_rows[kept:kept + NBLK, :kept] = scales
    for b in range(count):
        bias[:, b * rows:(b + 1) * rows] = visible_bias(prompt_pages, rows, swap_pair(jnp.int32(b + 1), n_cp))
    targets, found = [], []
    for valid, page in slot_pages(me, slot_count, prompt_pages, decode_owner, slot_offset):
        steps_back = lax.rem(me - page * PAGE // rows + n_cp, n_cp)
        column = swap_pair(steps_back, n_cp) * rows + lax.rem(page * PAGE, rows)
        targets.append(jnp.where(valid, column, -PAGE))
        found.append(valid & (steps_back < n_cp - 1))
    filled[:1, :] = slot_lanes(found, filled.shape[1])
    picked[...] = row_picker(targets, (n_cp - 1) * rows)


def pick_rows(picked, index, block):
    rows = block.shape[1]
    return lax.dot_general(picked[:, index * rows:(index + 1) * rows], block, NT, preferred_element_type=jnp.float32)


def arrived_kernel(used, picked, own, value_expand, *refs):
    blocks, (found, values) = refs[:-2], refs[-2:]
    rows = own.shape[1]
    for i in range(used):
        latents = blocks[i][:LAT, :].T
        for h in range(0, value_expand.shape[0], 2):
            values[i * rows:(i + 1) * rows, h * VDIM:(h + 2) * VDIM] = head_values(latents, value_expand, h)
    total = pick_rows(picked, 0, own[...])
    for i, block in enumerate(blocks):
        total = total + pick_rows(picked, 1 + 2 * i, block[...])
    found[...] = total


def slot_lanes(flags, width=None):
    lane = lax.broadcasted_iota(jnp.int32, (1, width or len(flags) * PAGE), 1)
    lanes = jnp.zeros(lane.shape, jnp.float32)
    for c, flag in enumerate(flags):
        lanes = jnp.where(lane // PAGE == c, flag.astype(jnp.float32), lanes)
    return lanes


def encode(rows, filled):
    kept = rows.shape[0]
    which = lax.broadcasted_iota(jnp.int32, (kept, LANES), 1)
    table = jnp.zeros((kept, LANES), jnp.float32)
    encoded = []
    for b in range(NBLK):
        values = rows[:, b * BLOCK:(b + 1) * BLOCK]
        scale = jnp.max(jnp.abs(values), axis=1, keepdims=True) + amax_epsilon
        scale = scale.astype(jnp.bfloat16).astype(jnp.float32)
        encoded.append((values / scale).astype(jnp.bfloat16))
        table = jnp.where(which == b, scale, table)
    encoded.append(rows[:, LAT:].astype(jnp.bfloat16))
    scales = (table.T[:NBLK] * filled).astype(jnp.bfloat16)
    return jnp.concatenate(encoded, axis=1), scales


def earlier_kernel(count, group, *refs):
    combined, own_result, peaks, totals, value_expand, bias, fetched_values, picked, found, filled = refs[:10]
    arrived, (result, encoded, scales, keys, latents) = refs[10:-5], refs[-5:]
    rows, width = bias.shape
    heads = value_expand.shape[0]
    steps = heads // group

    def span(g):
        at = g * group * rows
        return slice(at, at + group * rows)

    def score(g):
        scores = jnp.dot(combined[span(g), :], keys[...], preferred_element_type=jnp.float32)
        return (scores.reshape(group, rows, width) + bias[...][None]).reshape(group * rows, width)

    def weigh(g, scores):
        old_peak = peaks[span(g), :]
        parts = [scores[:, b:b + LANES] for b in range(0, width, LANES)]
        peak = jnp.maximum(old_peak, jnp.max(functools.reduce(jnp.maximum, parts), axis=1, keepdims=True))
        parts = [jnp.exp2((part - peak) * exp2_scale) for part in parts]
        total = jnp.sum(functools.reduce(jnp.add, parts), axis=1, keepdims=True)
        factor = jnp.exp2((old_peak - peak) * exp2_scale)
        inverse = 1.0 / (totals[span(g), :] * factor + total)
        weights = jnp.concatenate([part.astype(jnp.bfloat16) for part in parts], axis=1)
        return weights, factor * inverse, inverse

    def value(g):
        return [
            [head_values(latents[i * rows:(i + 1) * rows, :], value_expand, h) for h in range(g * group, (g + 1) * group, 2)]
            for i in range(count // 2)
        ]

    def finish(g, weights, factor, inverse, swapped):
        for i in range(group):
            part = slice(i * rows, (i + 1) * rows)
            h = g * group + i
            values = []
            for b in range(count // 2):
                values.append(fetched_values[b * rows:(b + 1) * rows, h * VDIM:(h + 1) * VDIM])
                values.append(swapped[b][i // 2][:, i % 2 * VDIM:(i % 2 + 1) * VDIM])
            out = jnp.dot(weights[part], jnp.concatenate(values, axis=0), preferred_element_type=jnp.float32)
            out = own_result[h * rows:(h + 1) * rows, :] * factor[part] + out * inverse[part]
            result[:, h * VDIM:(h + 1) * VDIM] = out.astype(jnp.bfloat16)

    def swapped_block(i):
        return jnp.concatenate([part[...] for part in arrived[i * (1 + SWAP) + 1:(i + 1) * (1 + SWAP)]], axis=0)

    def encode_found():
        total = found[...]
        latent_rows, rotary_rows = total[:, :LAT], total[:, LAT:]
        for i in range(len(arrived) // (1 + SWAP)):
            choice = picked[:, (2 + 2 * i) * rows:(3 + 2 * i) * rows]
            latent_rows = latent_rows + jnp.dot(choice, latents[i * rows:(i + 1) * rows, :], preferred_element_type=jnp.float32)
            rotary = swapped_block(i)[LAT:]
            rotary_rows = rotary_rows + lax.dot_general(choice, rotary, NT, preferred_element_type=jnp.float32)
        every = jnp.concatenate([latent_rows, rotary_rows], axis=1)
        encoded[...], scales[...] = encode(every, filled[:1, :every.shape[0]])

    for i in range(len(arrived) // (1 + SWAP)):
        latents[i * rows:(i + 1) * rows, :] = swapped_block(i)[:LAT].T

    @pl.when(lax.axis_index("cp") == 0)
    def _():
        for h in range(heads):
            part = slice(h * rows, (h + 1) * rows)
            result[:, h * VDIM:(h + 1) * VDIM] = (own_result[part, :] / totals[part, :]).astype(jnp.bfloat16)
        encode_found()

    @pl.when(lax.axis_index("cp") > 0)
    def _():
        for i in range(count // 2):
            at = 2 * i * rows
            keys[:, at:at + rows] = arrived[i * (1 + SWAP)][...]
            keys[:, at + rows:at + 2 * rows] = swapped_block(i)
        scores, values, weights = {}, {}, {}
        for step in range(steps + 2):
            if step < steps:
                scores[step] = score(step)
            if step == 2:
                encode_found()
            if 0 <= step - 2:
                finish(step - 2, *weights.pop(step - 2), values.pop(step - 2))
            if 0 <= step - 1 < steps:
                values[step - 1] = value(step - 1)
                weights[step - 1] = weigh(step - 1, scores.pop(step - 1))


def store_kernel(result, encoded, scales, sent_rows, attended, page_cache, page_scales, cache_buf, scale_buf, sems):
    count = sems.shape[0] - 2
    wide = result.shape[1] // count
    copies = []
    for i in range(count):
        some = pl.ds(i * wide, wide)
        copies.append(pltpu.make_async_copy(result.at[:, some], attended.at[:, some], sems.at[i]))
        copies[-1].start()
    kept = encoded.shape[0]
    for c in range(page_cache.shape[0]):
        part = slice(c * PAGE, (c + 1) * PAGE)
        cache_buf[c] = encoded[part, :] + sent_rows[part, :ROW]
        scale_buf[c] = (scales[...] + sent_rows[kept:kept + NBLK, :kept])[:, part]
    for i, (source, target) in enumerate(((cache_buf, page_cache), (scale_buf, page_scales))):
        copies.append(pltpu.make_async_copy(source, target, sems.at[count + i]))
        copies[-1].start()
    for copy in copies:
        copy.wait()


def fetch(own, n_cp, n_dec):
    blocks = []
    for step in range(1, n_cp - 1, 2):
        pairs = [(c * n_dec + e, (c + step + e % 2) % n_cp * n_dec + e) for c in range(n_cp) for e in range(n_dec)]
        blocks.append(lax.ppermute(own, ("cp", "dec"), pairs))
    return blocks


def swap(blocks, n_dec):
    pieces = []
    for block in blocks:
        parts = [block[at:at + ROW // SWAP] for at in range(0, ROW, ROW // SWAP)]
        pieces += [block] + [lax.ppermute(part, "dec", [(e, e ^ 1) for e in range(n_dec)]) for part in parts]
    return pieces


def on_device(queries, latent_rows, key_absorb, value_expand, prompt_pages, decode_owner, slot_offset):
    n_cp = lax.axis_size("cp")
    dec_count = lax.axis_size("dec")
    heads = key_absorb.shape[0]
    rows = latent_rows.shape[0]
    prompts, width = decode_owner.shape
    slot_count = 3 * (rows // PAGE) // (2 * dec_count)
    kept = slot_count * PAGE
    reach = width * dec_count * slot_count * PAGE
    count = -(-reach // rows) - (1 if prompts == 2 else 0)
    count = min(n_cp - 2, count + count % 2)
    own = latent_rows.T
    blocks = fetch(own, n_cp, dec_count)

    vmem = pl.BlockSpec(memory_space=pltpu.VMEM)
    hbm = pl.BlockSpec(memory_space=pltpu.HBM)
    params = pltpu.CompilerParams(vmem_limit_bytes=32 * 2**20)
    group, chunks = 4, (heads // 4, heads // 4, heads // 2)
    inputs = (prompt_pages, decode_owner, slot_offset, own, queries, key_absorb, value_expand)
    combined, result, peaks, totals, sent_rows, bias, picked, filled, own_copy, value_copy = pl.pallas_call(
        functools.partial(own_kernel, n_cp, count, chunks, group, slot_count),
        in_specs=[hbm] * 7,
        out_specs=[vmem] * 10,
        out_shape=[
            jax.ShapeDtypeStruct((heads * rows, ROW), jnp.bfloat16),
            jax.ShapeDtypeStruct((heads * rows, VDIM), jnp.float32),
            jax.ShapeDtypeStruct((heads * rows, LANES), jnp.float32),
            jax.ShapeDtypeStruct((heads * rows, LANES), jnp.float32),
            jax.ShapeDtypeStruct((kept + PAGE, -(-ROW // LANES) * LANES), jnp.bfloat16),
            jax.ShapeDtypeStruct((rows, count * rows), jnp.float32),
            jax.ShapeDtypeStruct((kept, (n_cp - 1) * rows), jnp.bfloat16),
            jax.ShapeDtypeStruct((8, LANES), jnp.float32),
            jax.ShapeDtypeStruct(own.shape, jnp.bfloat16),
            jax.ShapeDtypeStruct(value_expand.shape, jnp.bfloat16),
        ],
        scratch_shapes=[
            pltpu.SMEM(prompt_pages.shape, jnp.int32),
            pltpu.SMEM(decode_owner.shape, jnp.int32),
            pltpu.SMEM(slot_offset.shape, jnp.int32),
            pltpu.VMEM((rows, heads * HEAD), jnp.bfloat16),
            pltpu.VMEM((heads, NOPE, LAT), jnp.bfloat16),
            pltpu.VMEM((rows, LAT), jnp.bfloat16),
            pltpu.SemaphoreType.DMA((4 + 3 * len(chunks),)),
        ],
        cost_estimate=pl.CostEstimate(
            flops=2 * rows * heads * (2 * NOPE * LAT + rows * (ROW + VDIM)),
            bytes_accessed=2 * (queries.size + key_absorb.size + heads * rows * ROW),
            transcendentals=rows * heads * rows,
        ),
        compiler_params=params,
        name="own",
    )(*[pltpu.with_memory_space_constraint(x, pltpu.HBM) for x in inputs])
    sent_rows = lax.ppermute(sent_rows, "cp", [(c, (c + n_cp - 1) % n_cp) for c in range(n_cp)])
    blocks, picked = lax.optimization_barrier((blocks, picked))
    pieces = swap(blocks, dec_count)
    found, fetched_values = pl.pallas_call(
        functools.partial(arrived_kernel, count // 2),
        in_specs=[vmem] * (3 + len(blocks)),
        out_specs=[vmem] * 2,
        out_shape=[
            jax.ShapeDtypeStruct((kept, ROW), jnp.float32),
            jax.ShapeDtypeStruct((count // 2 * rows, heads * VDIM), jnp.bfloat16),
        ],
        cost_estimate=pl.CostEstimate(flops=2**20, bytes_accessed=2**10, transcendentals=0),
        compiler_params=params,
        name="arrived",
    )(picked, own_copy, value_copy, *blocks)

    group = 2
    operands = (combined, result, peaks, totals, value_copy, bias, fetched_values, picked, found, filled, *pieces)
    attended, encoded, scales = pl.pallas_call(
        functools.partial(earlier_kernel, count, group),
        in_specs=[vmem] * len(operands),
        out_specs=[vmem] * 3,
        out_shape=[
            jax.ShapeDtypeStruct((rows, heads * VDIM), jnp.bfloat16),
            jax.ShapeDtypeStruct((kept, ROW), jnp.bfloat16),
            jax.ShapeDtypeStruct((NBLK, kept), jnp.bfloat16),
        ],
        scratch_shapes=[
            pltpu.VMEM((ROW, count * rows), jnp.bfloat16),
            pltpu.VMEM((len(blocks) * rows, LAT), jnp.bfloat16),
        ],
        cost_estimate=pl.CostEstimate(flops=2**20, bytes_accessed=2**10, transcendentals=0),
        compiler_params=params,
        name="earlier",
    )(*operands)
    sent_rows, attended = lax.optimization_barrier((sent_rows, attended))
    operands = (attended, encoded, scales, sent_rows)
    attended, page_cache, page_scales = pl.pallas_call(
        store_kernel,
        in_specs=[vmem] * len(operands),
        out_specs=[hbm] * 3,
        out_shape=[
            jax.ShapeDtypeStruct((rows, heads * VDIM), jnp.bfloat16),
            jax.ShapeDtypeStruct((slot_count, PAGE, ROW), jnp.bfloat16),
            jax.ShapeDtypeStruct((slot_count, NBLK, PAGE), jnp.bfloat16),
        ],
        scratch_shapes=[
            pltpu.VMEM((slot_count, PAGE, ROW), jnp.bfloat16),
            pltpu.VMEM((slot_count, NBLK, PAGE), jnp.bfloat16),
            pltpu.SemaphoreType.DMA((4 + 2,)),
        ],
        cost_estimate=pl.CostEstimate(flops=2**20, bytes_accessed=2**10, transcendentals=0),
        compiler_params=params,
        name="store",
    )(*operands)
    page_cache = page_cache.reshape(1, 1, slot_count, PAGE, ROW)
    page_scales = page_scales.transpose(0, 2, 1).reshape(1, 1, slot_count, PAGE, NBLK)
    return attended, page_cache, page_scales


def solution(mesh):
    return jax.shard_map(
        on_device,
        mesh=mesh,
        in_specs=(
            P(("grp", "cp"), "dec"),
            P(("grp", "cp"), None),
            P("dec", None, None),
            P("dec", None, None),
            P("grp"),
            P("grp", None),
            P("grp"),
        ),
        out_specs=(
            P(("grp", "cp"), "dec"),
            P(("grp", "cp"), "dec", None, None, None),
            P(("grp", "cp"), "dec", None, None, None),
        ),
        check_vma=False,
    )
```

```python
import functools
import math

import jax
import jax.numpy as jnp
from jax import lax
from jax.experimental import pallas as pl
from jax.experimental.pallas import tpu as pltpu
from jax.sharding import PartitionSpec as P

LAT = 512
ROPE = 64
NOPE = 128
VDIM = 128
PAGE = 16
BLOCK = 128
NBLK = LAT // BLOCK
ROW = LAT + ROPE
HEAD = NOPE + ROPE
LANES = 128
SWAP = 2

masked_fill = -1e30
amax_epsilon = 1e-06
exp2_scale = math.log2(math.e) / math.sqrt(HEAD)

NT = (((1,), (1,)), ((), ()))


def prompt_starts(prompt_pages):
    starts = [jnp.int32(0)]
    for k in range(prompt_pages.shape[0] - 1):
        starts.append(starts[-1] + prompt_pages[k])
    return starts


def visible_bias(prompt_pages, rows, steps_back):
    first = lax.axis_index("cp") * rows
    token = first + lax.broadcasted_iota(jnp.int32, (rows, 1), 0)
    begin = jnp.zeros((rows, 1), jnp.int32)
    for start in prompt_starts(prompt_pages):
        begin = jnp.maximum(begin, jnp.where(start * PAGE <= token, start * PAGE, 0))
    spot = first - steps_back * rows + lax.broadcasted_iota(jnp.int32, (1, rows), 1)
    return jnp.where((spot >= begin) & (spot <= token), 0.0, masked_fill)


def swap_pair(position, n_cp):
    odd = lax.rem(lax.axis_index("dec"), 2)
    within = lax.rem(position + 1, 2)
    swapped = position - within + lax.rem(within + odd, 2)
    paired = (position >= 1) & (position <= (n_cp - 1) // 2 * 2)
    return jnp.where(paired, swapped, position)


def slot_pages(owner, slot_count, prompt_pages, decode_owner, slot_offset):
    prompts, width = decode_owner.shape
    cycle = width * lax.axis_size("dec") * slot_count
    starts = prompt_starts(prompt_pages)
    pages, start, offset, place = jnp.int32(0), jnp.int32(0), jnp.int32(0), jnp.int32(0)
    for k in range(prompts):
        for p in range(width):
            mine = decode_owner[k, p] == owner
            pages = jnp.where(mine, prompt_pages[k], pages)
            start = jnp.where(mine, starts[k], start)
            offset = jnp.where(mine, slot_offset[k], offset)
            place = jnp.where(mine, p, place)
    result = []
    for c in range(slot_count):
        turn = width * (lax.axis_index("dec") * slot_count + c) + place
        page = lax.rem(turn - offset + 2 * cycle, cycle)
        result.append((page < pages, start + page))
    return result


def row_picker(targets, columns):
    kept = len(targets) * PAGE
    row = lax.broadcasted_iota(jnp.int32, (kept, 1), 0)
    target = jnp.full((kept, 1), -1, jnp.int32)
    for c, column in enumerate(targets):
        target = jnp.where(row // PAGE == c, column + row % PAGE, target)
    column = lax.broadcasted_iota(jnp.int32, (1, columns), 1)
    return jnp.where(column == target, 1.0, 0.0).astype(jnp.bfloat16)


def head_values(latents, value_expand, h):
    both = jnp.concatenate([value_expand[h], value_expand[h + 1]], axis=1)
    return jnp.dot(latents, both, preferred_element_type=jnp.float32).astype(jnp.bfloat16)


def own_kernel(n_cp, count, chunks, group, slot_count, *refs):
    inputs, refs = refs[:7], refs[7:]
    combined, result, peaks, totals, sent_rows, bias, picked, filled, own, value_expand = refs[:10]
    prompt_pages, decode_owner, slot_offset, queries, key_absorb, latents, sems = refs[10:]
    pages_hbm, owner_hbm, offset_hbm, own_hbm, queries_hbm, absorb_hbm, expand_hbm = inputs
    rows = own.shape[1]
    heads = key_absorb.shape[0]
    small = [
        pltpu.make_async_copy(source, target, sems.at[i])
        for i, (source, target) in enumerate(zip(inputs[:4], (prompt_pages, decode_owner, slot_offset, own)))
    ]
    large = {}
    first = 0
    for chunk in chunks:
        at = 4 + 3 * len(large)
        some = pl.ds(first, chunk)
        wide = pl.ds(first * HEAD, chunk * HEAD)
        large[first] = (
            pltpu.make_async_copy(queries_hbm.at[:, wide], queries.at[:, wide], sems.at[at]),
            pltpu.make_async_copy(absorb_hbm.at[some], key_absorb.at[some], sems.at[at + 1]),
            pltpu.make_async_copy(expand_hbm.at[some], value_expand.at[some], sems.at[at + 2]),
        )
        first += chunk
    for copy in small:
        copy.start()
    for chunk_copies in large.values():
        for copy in chunk_copies:
            copy.start()
    steps = heads // group

    def absorb(g):
        for copy in large.get(g * group, ())[:2]:
            copy.wait()
        for h in range(g * group, (g + 1) * group):
            at = h * HEAD
            absorbed = jnp.dot(queries[:, at:at + NOPE], key_absorb[h], preferred_element_type=jnp.float32)
            combined[h * rows:(h + 1) * rows, :LAT] = absorbed.astype(jnp.bfloat16)
            combined[h * rows:(h + 1) * rows, LAT:] = queries[:, at + NOPE:at + HEAD]

    def score(g):
        return jnp.dot(combined[g * group * rows:(g + 1) * group * rows, :], own[...], preferred_element_type=jnp.float32)

    def value(g):
        for copy in large.get(g * group, ())[2:]:
            copy.wait()
        return [head_values(latents[...], value_expand, g * group + i) for i in range(0, group, 2)]

    def finish(g, scores, both):
        span = slice(g * group * rows, (g + 1) * group * rows)
        scores = (scores.reshape(group, rows, rows) + own_bias[None]).reshape(group * rows, rows)
        peak = jnp.max(scores, axis=1, keepdims=True)
        weights = jnp.exp2((scores - peak) * exp2_scale)
        total = jnp.sum(weights, axis=1, keepdims=True)
        weights = weights.astype(jnp.bfloat16)
        for i in range(group):
            mine = both[i // 2][:, i % 2 * VDIM:(i % 2 + 1) * VDIM]
            out = jnp.dot(weights[i * rows:(i + 1) * rows], mine, preferred_element_type=jnp.float32)
            result[(g * group + i) * rows:(g * group + i + 1) * rows, :] = out
        peaks[span, :] = jnp.broadcast_to(peak, (group * rows, LANES))
        totals[span, :] = jnp.broadcast_to(total, (group * rows, LANES))

    for copy in small:
        copy.wait()
    latents[...] = own[:LAT, :].T
    own_bias = visible_bias(prompt_pages, rows, 0)
    index_work(n_cp, count, slot_count, prompt_pages, decode_owner, slot_offset, own[...], sent_rows, bias, picked, filled)
    scores, both = {}, {}
    for step in range(steps + 2):
        if step < steps:
            absorb(step)
        if 0 <= step - 1 < steps:
            scores[step - 1] = score(step - 1)
            both[step - 1] = value(step - 1)
        if 0 <= step - 2:
            finish(step - 2, scores.pop(step - 2), both.pop(step - 2))


def index_work(n_cp, count, slot_count, prompt_pages, decode_owner, slot_offset, block, sent_rows, bias, picked, filled):
    rows = block.shape[1]
    me = lax.axis_index("cp")
    behind = lax.rem(me + n_cp - 1, n_cp)
    targets, here = [], []
    for valid, page in slot_pages(behind, slot_count, prompt_pages, decode_owner, slot_offset):
        here.append(valid & (page * PAGE // rows == me))
        targets.append(jnp.where(here[-1], lax.rem(page * PAGE, rows), -PAGE))
    choice = row_picker(targets, rows)
    sent = lax.dot_general(choice, block, NT, preferred_element_type=jnp.float32)
    encoded, scales = encode(sent, slot_lanes(here))
    kept = choice.shape[0]
    sent_rows[...] = jnp.zeros(sent_rows.shape, jnp.bfloat16)
    sent_rows[:kept, :ROW] = encoded
    sent_rows[kept:kept + NBLK, :kept] = scales
    for b in range(count):
        bias[:, b * rows:(b + 1) * rows] = visible_bias(prompt_pages, rows, swap_pair(jnp.int32(b + 1), n_cp))
    targets, found = [], []
    for valid, page in slot_pages(me, slot_count, prompt_pages, decode_owner, slot_offset):
        steps_back = lax.rem(me - page * PAGE // rows + n_cp, n_cp)
        column = swap_pair(steps_back, n_cp) * rows + lax.rem(page * PAGE, rows)
        targets.append(jnp.where(valid, column, -PAGE))
        found.append(valid & (steps_back < n_cp - 1))
    filled[:1, :] = slot_lanes(found, filled.shape[1])
    picked[...] = row_picker(targets, (n_cp - 1) * rows)


def pick_rows(picked, index, block):
    rows = block.shape[1]
    return lax.dot_general(picked[:, index * rows:(index + 1) * rows], block, NT, preferred_element_type=jnp.float32)


def arrived_kernel(used, picked, own, value_expand, *refs):
    blocks, (found, values) = refs[:-2], refs[-2:]
    rows = own.shape[1]
    for i in range(used):
        latents = blocks[i][:LAT, :].T
        for h in range(0, value_expand.shape[0], 2):
            values[i * rows:(i + 1) * rows, h * VDIM:(h + 2) * VDIM] = head_values(latents, value_expand, h)
    total = pick_rows(picked, 0, own[...])
    for i, block in enumerate(blocks):
        total = total + pick_rows(picked, 1 + 2 * i, block[...])
    found[...] = total


def slot_lanes(flags, width=None):
    lane = lax.broadcasted_iota(jnp.int32, (1, width or len(flags) * PAGE), 1)
    lanes = jnp.zeros(lane.shape, jnp.float32)
    for c, flag in enumerate(flags):
        lanes = jnp.where(lane // PAGE == c, flag.astype(jnp.float32), lanes)
    return lanes


def encode(rows, filled):
    kept = rows.shape[0]
    which = lax.broadcasted_iota(jnp.int32, (kept, LANES), 1)
    table = jnp.zeros((kept, LANES), jnp.float32)
    encoded = []
    for b in range(NBLK):
        values = rows[:, b * BLOCK:(b + 1) * BLOCK]
        scale = jnp.max(jnp.abs(values), axis=1, keepdims=True) + amax_epsilon
        scale = scale.astype(jnp.bfloat16).astype(jnp.float32)
        encoded.append((values / scale).astype(jnp.bfloat16))
        table = jnp.where(which == b, scale, table)
    encoded.append(rows[:, LAT:].astype(jnp.bfloat16))
    scales = (table.T[:NBLK] * filled).astype(jnp.bfloat16)
    return jnp.concatenate(encoded, axis=1), scales


def earlier_kernel(count, group, *refs):
    combined, own_result, peaks, totals, value_expand, bias, fetched_values, picked, found, filled = refs[:10]
    arrived, (result, encoded, scales, keys, latents) = refs[10:-5], refs[-5:]
    rows, width = bias.shape
    heads = value_expand.shape[0]
    steps = heads // group

    def span(g):
        at = g * group * rows
        return slice(at, at + group * rows)

    def score(g):
        scores = jnp.dot(combined[span(g), :], keys[...], preferred_element_type=jnp.float32)
        return (scores.reshape(group, rows, width) + bias[...][None]).reshape(group * rows, width)

    def weigh(g, scores):
        old_peak = peaks[span(g), :]
        parts = [scores[:, b:b + LANES] for b in range(0, width, LANES)]
        peak = jnp.maximum(old_peak, jnp.max(functools.reduce(jnp.maximum, parts), axis=1, keepdims=True))
        parts = [jnp.exp2((part - peak) * exp2_scale) for part in parts]
        total = jnp.sum(functools.reduce(jnp.add, parts), axis=1, keepdims=True)
        factor = jnp.exp2((old_peak - peak) * exp2_scale)
        inverse = 1.0 / (totals[span(g), :] * factor + total)
        weights = jnp.concatenate([part.astype(jnp.bfloat16) for part in parts], axis=1)
        return weights, factor * inverse, inverse

    def value(g):
        return [
            [head_values(latents[i * rows:(i + 1) * rows, :], value_expand, h) for h in range(g * group, (g + 1) * group, 2)]
            for i in range(count // 2)
        ]

    def finish(g, weights, factor, inverse, swapped):
        for i in range(group):
            part = slice(i * rows, (i + 1) * rows)
            h = g * group + i
            values = []
            for b in range(count // 2):
                values.append(fetched_values[b * rows:(b + 1) * rows, h * VDIM:(h + 1) * VDIM])
                values.append(swapped[b][i // 2][:, i % 2 * VDIM:(i % 2 + 1) * VDIM])
            out = jnp.dot(weights[part], jnp.concatenate(values, axis=0), preferred_element_type=jnp.float32)
            out = own_result[h * rows:(h + 1) * rows, :] * factor[part] + out * inverse[part]
            result[:, h * VDIM:(h + 1) * VDIM] = out.astype(jnp.bfloat16)

    def swapped_block(i):
        return jnp.concatenate([part[...] for part in arrived[i * (1 + SWAP) + 1:(i + 1) * (1 + SWAP)]], axis=0)

    def encode_found():
        total = found[...]
        latent_rows, rotary_rows = total[:, :LAT], total[:, LAT:]
        for i in range(len(arrived) // (1 + SWAP)):
            choice = picked[:, (2 + 2 * i) * rows:(3 + 2 * i) * rows]
            latent_rows = latent_rows + jnp.dot(choice, latents[i * rows:(i + 1) * rows, :], preferred_element_type=jnp.float32)
            rotary = swapped_block(i)[LAT:]
            rotary_rows = rotary_rows + lax.dot_general(choice, rotary, NT, preferred_element_type=jnp.float32)
        every = jnp.concatenate([latent_rows, rotary_rows], axis=1)
        encoded[...], scales[...] = encode(every, filled[:1, :every.shape[0]])

    for i in range(len(arrived) // (1 + SWAP)):
        latents[i * rows:(i + 1) * rows, :] = swapped_block(i)[:LAT].T

    @pl.when(lax.axis_index("cp") == 0)
    def _():
        for h in range(heads):
            part = slice(h * rows, (h + 1) * rows)
            result[:, h * VDIM:(h + 1) * VDIM] = (own_result[part, :] / totals[part, :]).astype(jnp.bfloat16)
        encode_found()

    @pl.when(lax.axis_index("cp") > 0)
    def _():
        for i in range(count // 2):
            at = 2 * i * rows
            keys[:, at:at + rows] = arrived[i * (1 + SWAP)][...]
            keys[:, at + rows:at + 2 * rows] = swapped_block(i)
        scores, values, weights = {}, {}, {}
        for step in range(steps + 2):
            if step < steps:
                scores[step] = score(step)
            if step == 2:
                encode_found()
            if 0 <= step - 2:
                finish(step - 2, *weights.pop(step - 2), values.pop(step - 2))
            if 0 <= step - 1 < steps:
                values[step - 1] = value(step - 1)
                weights[step - 1] = weigh(step - 1, scores.pop(step - 1))


def store_kernel(result, encoded, scales, sent_rows, attended, page_cache, page_scales, cache_buf, scale_buf, sems):
    count = sems.shape[0] - 2
    wide = result.shape[1] // count
    copies = []
    for i in range(count):
        some = pl.ds(i * wide, wide)
        copies.append(pltpu.make_async_copy(result.at[:, some], attended.at[:, some], sems.at[i]))
        copies[-1].start()
    kept = encoded.shape[0]
    for c in range(page_cache.shape[0]):
        part = slice(c * PAGE, (c + 1) * PAGE)
        cache_buf[c] = encoded[part, :] + sent_rows[part, :ROW]
        scale_buf[c] = (scales[...] + sent_rows[kept:kept + NBLK, :kept])[:, part]
    for i, (source, target) in enumerate(((cache_buf, page_cache), (scale_buf, page_scales))):
        copies.append(pltpu.make_async_copy(source, target, sems.at[count + i]))
        copies[-1].start()
    for copy in copies:
        copy.wait()


def fetch(own, n_cp, n_dec):
    blocks = []
    for step in range(1, n_cp - 1, 2):
        pairs = [(c * n_dec + e, (c + step + e % 2) % n_cp * n_dec + e) for c in range(n_cp) for e in range(n_dec)]
        blocks.append(lax.ppermute(own, ("cp", "dec"), pairs))
    return blocks


def swap(blocks, n_dec):
    pieces = []
    for block in blocks:
        parts = [block[at:at + ROW // SWAP] for at in range(0, ROW, ROW // SWAP)]
        pieces += [block] + [lax.ppermute(part, "dec", [(e, e ^ 1) for e in range(n_dec)]) for part in parts]
    return pieces


def on_device(queries, latent_rows, key_absorb, value_expand, prompt_pages, decode_owner, slot_offset):
    n_cp = lax.axis_size("cp")
    dec_count = lax.axis_size("dec")
    heads = key_absorb.shape[0]
    rows = latent_rows.shape[0]
    prompts, width = decode_owner.shape
    slot_count = 3 * (rows // PAGE) // (2 * dec_count)
    kept = slot_count * PAGE
    reach = width * dec_count * slot_count * PAGE
    count = -(-reach // rows) - (1 if prompts == 2 else 0)
    count = min(n_cp - 2, count + count % 2)
    own = latent_rows.T
    blocks = fetch(own, n_cp, dec_count)

    vmem = pl.BlockSpec(memory_space=pltpu.VMEM)
    hbm = pl.BlockSpec(memory_space=pltpu.HBM)
    params = pltpu.CompilerParams(vmem_limit_bytes=32 * 2**20)
    group, chunks = 8, (heads // 2, heads // 2)
    inputs = (prompt_pages, decode_owner, slot_offset, own, queries, key_absorb, value_expand)
    combined, result, peaks, totals, sent_rows, bias, picked, filled, own_copy, value_copy = pl.pallas_call(
        functools.partial(own_kernel, n_cp, count, chunks, group, slot_count),
        in_specs=[hbm] * 7,
        out_specs=[vmem] * 10,
        out_shape=[
            jax.ShapeDtypeStruct((heads * rows, ROW), jnp.bfloat16),
            jax.ShapeDtypeStruct((heads * rows, VDIM), jnp.float32),
            jax.ShapeDtypeStruct((heads * rows, LANES), jnp.float32),
            jax.ShapeDtypeStruct((heads * rows, LANES), jnp.float32),
            jax.ShapeDtypeStruct((kept + PAGE, -(-ROW // LANES) * LANES), jnp.bfloat16),
            jax.ShapeDtypeStruct((rows, count * rows), jnp.float32),
            jax.ShapeDtypeStruct((kept, (n_cp - 1) * rows), jnp.bfloat16),
            jax.ShapeDtypeStruct((8, LANES), jnp.float32),
            jax.ShapeDtypeStruct(own.shape, jnp.bfloat16),
            jax.ShapeDtypeStruct(value_expand.shape, jnp.bfloat16),
        ],
        scratch_shapes=[
            pltpu.SMEM(prompt_pages.shape, jnp.int32),
            pltpu.SMEM(decode_owner.shape, jnp.int32),
            pltpu.SMEM(slot_offset.shape, jnp.int32),
            pltpu.VMEM((rows, heads * HEAD), jnp.bfloat16),
            pltpu.VMEM((heads, NOPE, LAT), jnp.bfloat16),
            pltpu.VMEM((rows, LAT), jnp.bfloat16),
            pltpu.SemaphoreType.DMA((4 + 3 * len(chunks),)),
        ],
        cost_estimate=pl.CostEstimate(
            flops=2 * rows * heads * (2 * NOPE * LAT + rows * (ROW + VDIM)),
            bytes_accessed=2 * (queries.size + key_absorb.size + heads * rows * ROW),
            transcendentals=rows * heads * rows,
        ),
        compiler_params=params,
        name="own",
    )(*[pltpu.with_memory_space_constraint(x, pltpu.HBM) for x in inputs])
    sent_rows = lax.ppermute(sent_rows, "cp", [(c, (c + n_cp - 1) % n_cp) for c in range(n_cp)])
    blocks, picked = lax.optimization_barrier((blocks, picked))
    pieces = swap(blocks, dec_count)
    found, fetched_values = pl.pallas_call(
        functools.partial(arrived_kernel, count // 2),
        in_specs=[vmem] * (3 + len(blocks)),
        out_specs=[vmem] * 2,
        out_shape=[
            jax.ShapeDtypeStruct((kept, ROW), jnp.float32),
            jax.ShapeDtypeStruct((count // 2 * rows, heads * VDIM), jnp.bfloat16),
        ],
        cost_estimate=pl.CostEstimate(flops=2**20, bytes_accessed=2**10, transcendentals=0),
        compiler_params=params,
        name="arrived",
    )(picked, own_copy, value_copy, *blocks)

    group = 8 if count <= 4 else 2
    operands = (combined, result, peaks, totals, value_copy, bias, fetched_values, picked, found, filled, *pieces)
    attended, encoded, scales = pl.pallas_call(
        functools.partial(earlier_kernel, count, group),
        in_specs=[vmem] * len(operands),
        out_specs=[vmem] * 3,
        out_shape=[
            jax.ShapeDtypeStruct((rows, heads * VDIM), jnp.bfloat16),
            jax.ShapeDtypeStruct((kept, ROW), jnp.bfloat16),
            jax.ShapeDtypeStruct((NBLK, kept), jnp.bfloat16),
        ],
        scratch_shapes=[
            pltpu.VMEM((ROW, count * rows), jnp.bfloat16),
            pltpu.VMEM((len(blocks) * rows, LAT), jnp.bfloat16),
        ],
        cost_estimate=pl.CostEstimate(flops=2**20, bytes_accessed=2**10, transcendentals=0),
        compiler_params=params,
        name="earlier",
    )(*operands)
    sent_rows, attended = lax.optimization_barrier((sent_rows, attended))
    operands = (attended, encoded, scales, sent_rows)
    attended, page_cache, page_scales = pl.pallas_call(
        store_kernel,
        in_specs=[vmem] * len(operands),
        out_specs=[hbm] * 3,
        out_shape=[
            jax.ShapeDtypeStruct((rows, heads * VDIM), jnp.bfloat16),
            jax.ShapeDtypeStruct((slot_count, PAGE, ROW), jnp.bfloat16),
            jax.ShapeDtypeStruct((slot_count, NBLK, PAGE), jnp.bfloat16),
        ],
        scratch_shapes=[
            pltpu.VMEM((slot_count, PAGE, ROW), jnp.bfloat16),
            pltpu.VMEM((slot_count, NBLK, PAGE), jnp.bfloat16),
            pltpu.SemaphoreType.DMA((4 + 2,)),
        ],
        cost_estimate=pl.CostEstimate(flops=2**20, bytes_accessed=2**10, transcendentals=0),
        compiler_params=params,
        name="store",
    )(*operands)
    page_cache = page_cache.reshape(1, 1, slot_count, PAGE, ROW)
    page_scales = page_scales.transpose(0, 2, 1).reshape(1, 1, slot_count, PAGE, NBLK)
    return attended, page_cache, page_scales


def solution(mesh):
    return jax.shard_map(
        on_device,
        mesh=mesh,
        in_specs=(
            P(("grp", "cp"), "dec"),
            P(("grp", "cp"), None),
            P("dec", None, None),
            P("dec", None, None),
            P("grp"),
            P("grp", None),
            P("grp"),
        ),
        out_specs=(
            P(("grp", "cp"), "dec"),
            P(("grp", "cp"), "dec", None, None, None),
            P(("grp", "cp"), "dec", None, None, None),
        ),
        check_vma=False,
    )
```

```python
import functools
import math

import jax
import jax.numpy as jnp
from jax import lax
from jax.experimental import pallas as pl
from jax.experimental.pallas import tpu as pltpu
from jax.sharding import PartitionSpec as P

LAT = 512
ROPE = 64
NOPE = 128
VDIM = 128
PAGE = 16
BLOCK = 128
NBLK = LAT // BLOCK
ROW = LAT + ROPE
HEAD = NOPE + ROPE
LANES = 128
SWAP = 2

masked_fill = -1e30
amax_epsilon = 1e-06
exp2_scale = math.log2(math.e) / math.sqrt(HEAD)

NT = (((1,), (1,)), ((), ()))


def prompt_starts(prompt_pages):
    starts = [jnp.int32(0)]
    for k in range(prompt_pages.shape[0] - 1):
        starts.append(starts[-1] + prompt_pages[k])
    return starts


def visible_bias(prompt_pages, rows, steps_back):
    first = lax.axis_index("cp") * rows
    token = first + lax.broadcasted_iota(jnp.int32, (rows, 1), 0)
    begin = jnp.zeros((rows, 1), jnp.int32)
    for start in prompt_starts(prompt_pages):
        begin = jnp.maximum(begin, jnp.where(start * PAGE <= token, start * PAGE, 0))
    spot = first - steps_back * rows + lax.broadcasted_iota(jnp.int32, (1, rows), 1)
    return jnp.where((spot >= begin) & (spot <= token), 0.0, masked_fill)


def swap_pair(position, n_cp):
    odd = lax.rem(lax.axis_index("dec"), 2)
    within = lax.rem(position + 1, 2)
    swapped = position - within + lax.rem(within + odd, 2)
    paired = (position >= 1) & (position <= (n_cp - 1) // 2 * 2)
    return jnp.where(paired, swapped, position)


def slot_pages(owner, slot_count, prompt_pages, decode_owner, slot_offset):
    prompts, width = decode_owner.shape
    cycle = width * lax.axis_size("dec") * slot_count
    starts = prompt_starts(prompt_pages)
    pages, start, offset, place = jnp.int32(0), jnp.int32(0), jnp.int32(0), jnp.int32(0)
    for k in range(prompts):
        for p in range(width):
            mine = decode_owner[k, p] == owner
            pages = jnp.where(mine, prompt_pages[k], pages)
            start = jnp.where(mine, starts[k], start)
            offset = jnp.where(mine, slot_offset[k], offset)
            place = jnp.where(mine, p, place)
    result = []
    for c in range(slot_count):
        turn = width * (lax.axis_index("dec") * slot_count + c) + place
        page = lax.rem(turn - offset + 2 * cycle, cycle)
        result.append((page < pages, start + page))
    return result


def row_picker(targets, columns):
    kept = len(targets) * PAGE
    row = lax.broadcasted_iota(jnp.int32, (kept, 1), 0)
    target = jnp.full((kept, 1), -1, jnp.int32)
    for c, column in enumerate(targets):
        target = jnp.where(row // PAGE == c, column + row % PAGE, target)
    column = lax.broadcasted_iota(jnp.int32, (1, columns), 1)
    return jnp.where(column == target, 1.0, 0.0).astype(jnp.bfloat16)


def head_values(latents, value_expand, h):
    both = jnp.concatenate([value_expand[h], value_expand[h + 1]], axis=1)
    return jnp.dot(latents, both, preferred_element_type=jnp.float32).astype(jnp.bfloat16)


def own_kernel(n_cp, count, chunks, group, slot_count, *refs):
    inputs, refs = refs[:7], refs[7:]
    combined, result, peaks, totals, sent_rows, bias, picked, filled, own, value_expand = refs[:10]
    prompt_pages, decode_owner, slot_offset, queries, key_absorb, latents, sems = refs[10:]
    pages_hbm, owner_hbm, offset_hbm, own_hbm, queries_hbm, absorb_hbm, expand_hbm = inputs
    rows = own.shape[1]
    heads = key_absorb.shape[0]
    small = [
        pltpu.make_async_copy(source, target, sems.at[i])
        for i, (source, target) in enumerate(zip(inputs[:4], (prompt_pages, decode_owner, slot_offset, own)))
    ]
    large = {}
    first = 0
    for chunk in chunks:
        at = 4 + 3 * len(large)
        some = pl.ds(first, chunk)
        wide = pl.ds(first * HEAD, chunk * HEAD)
        large[first] = (
            pltpu.make_async_copy(queries_hbm.at[:, wide], queries.at[:, wide], sems.at[at]),
            pltpu.make_async_copy(absorb_hbm.at[some], key_absorb.at[some], sems.at[at + 1]),
            pltpu.make_async_copy(expand_hbm.at[some], value_expand.at[some], sems.at[at + 2]),
        )
        first += chunk
    for copy in small:
        copy.start()
    for chunk_copies in large.values():
        for copy in chunk_copies:
            copy.start()
    steps = heads // group

    def absorb(g):
        for copy in large.get(g * group, ())[:2]:
            copy.wait()
        for h in range(g * group, (g + 1) * group):
            at = h * HEAD
            absorbed = jnp.dot(queries[:, at:at + NOPE], key_absorb[h], preferred_element_type=jnp.float32)
            combined[h * rows:(h + 1) * rows, :LAT] = absorbed.astype(jnp.bfloat16)
            combined[h * rows:(h + 1) * rows, LAT:] = queries[:, at + NOPE:at + HEAD]

    def score(g):
        return jnp.dot(combined[g * group * rows:(g + 1) * group * rows, :], own[...], preferred_element_type=jnp.float32)

    def value(g):
        for copy in large.get(g * group, ())[2:]:
            copy.wait()
        return [head_values(latents[...], value_expand, g * group + i) for i in range(0, group, 2)]

    def finish(g, scores, both):
        span = slice(g * group * rows, (g + 1) * group * rows)
        scores = (scores.reshape(group, rows, rows) + own_bias[None]).reshape(group * rows, rows)
        peak = jnp.max(scores, axis=1, keepdims=True)
        weights = jnp.exp2((scores - peak) * exp2_scale)
        total = jnp.sum(weights, axis=1, keepdims=True)
        weights = weights.astype(jnp.bfloat16)
        for i in range(group):
            mine = both[i // 2][:, i % 2 * VDIM:(i % 2 + 1) * VDIM]
            out = jnp.dot(weights[i * rows:(i + 1) * rows], mine, preferred_element_type=jnp.float32)
            result[(g * group + i) * rows:(g * group + i + 1) * rows, :] = out
        peaks[span, :] = jnp.broadcast_to(peak, (group * rows, LANES))
        totals[span, :] = jnp.broadcast_to(total, (group * rows, LANES))

    for copy in small:
        copy.wait()
    latents[...] = own[:LAT, :].T
    own_bias = visible_bias(prompt_pages, rows, 0)
    index_work(n_cp, count, slot_count, prompt_pages, decode_owner, slot_offset, own, latents, sent_rows, bias, picked, filled)
    scores, both = {}, {}
    for step in range(steps + 2):
        if step < steps:
            absorb(step)
        if 0 <= step - 1 < steps:
            scores[step - 1] = score(step - 1)
            both[step - 1] = value(step - 1)
        if 0 <= step - 2:
            finish(step - 2, scores.pop(step - 2), both.pop(step - 2))


def index_work(n_cp, count, slot_count, prompt_pages, decode_owner, slot_offset, own, latents, sent_rows, bias, picked, filled):
    rows = own.shape[1]
    me = lax.axis_index("cp")
    behind = lax.rem(me + n_cp - 1, n_cp)
    targets, here = [], []
    for valid, page in slot_pages(behind, slot_count, prompt_pages, decode_owner, slot_offset):
        here.append(valid & (page * PAGE // rows == me))
        targets.append(jnp.where(here[-1], lax.rem(page * PAGE, rows), -PAGE))
    choice = row_picker(targets, rows)
    sent = jnp.concatenate([
        jnp.dot(choice, latents[...], preferred_element_type=jnp.float32),
        lax.dot_general(choice, own[LAT:, :], NT, preferred_element_type=jnp.float32),
    ], axis=1)
    encoded, scales = encode(sent, slot_lanes(here))
    kept = choice.shape[0]
    sent_rows[...] = jnp.zeros(sent_rows.shape, jnp.bfloat16)
    sent_rows[:kept, :ROW] = encoded
    sent_rows[kept:kept + NBLK, :kept] = scales
    for b in range(count):
        bias[:, b * rows:(b + 1) * rows] = visible_bias(prompt_pages, rows, swap_pair(jnp.int32(b + 1), n_cp))
    targets, found = [], []
    for valid, page in slot_pages(me, slot_count, prompt_pages, decode_owner, slot_offset):
        steps_back = lax.rem(me - page * PAGE // rows + n_cp, n_cp)
        column = swap_pair(steps_back, n_cp) * rows + lax.rem(page * PAGE, rows)
        targets.append(jnp.where(valid, column, -PAGE))
        found.append(valid & (steps_back < n_cp - 1))
    filled[:1, :] = slot_lanes(found, filled.shape[1])
    picked[...] = row_picker(targets, (n_cp - 1) * rows)


def pick_rows(picked, index, block):
    rows = block.shape[1]
    return lax.dot_general(picked[:, index * rows:(index + 1) * rows], block, NT, preferred_element_type=jnp.float32)


def arrived_kernel(used, picked, own, value_expand, *refs):
    blocks, (found, values) = refs[:-2], refs[-2:]
    rows = own.shape[1]
    for i in range(used):
        latents = blocks[i][:LAT, :].T
        for h in range(0, value_expand.shape[0], 2):
            values[i * rows:(i + 1) * rows, h * VDIM:(h + 2) * VDIM] = head_values(latents, value_expand, h)
    total = pick_rows(picked, 0, own[...])
    for i, block in enumerate(blocks):
        total = total + pick_rows(picked, 1 + 2 * i, block[...])
    found[...] = total


def slot_lanes(flags, width=None):
    lane = lax.broadcasted_iota(jnp.int32, (1, width or len(flags) * PAGE), 1)
    lanes = jnp.zeros(lane.shape, jnp.float32)
    for c, flag in enumerate(flags):
        lanes = jnp.where(lane // PAGE == c, flag.astype(jnp.float32), lanes)
    return lanes


def encode(rows, filled):
    kept = rows.shape[0]
    which = lax.broadcasted_iota(jnp.int32, (kept, LANES), 1)
    table = jnp.zeros((kept, LANES), jnp.float32)
    encoded = []
    for b in range(NBLK):
        values = rows[:, b * BLOCK:(b + 1) * BLOCK]
        scale = jnp.max(jnp.abs(values), axis=1, keepdims=True) + amax_epsilon
        scale = scale.astype(jnp.bfloat16).astype(jnp.float32)
        encoded.append((values / scale).astype(jnp.bfloat16))
        table = jnp.where(which == b, scale, table)
    encoded.append(rows[:, LAT:].astype(jnp.bfloat16))
    scales = (table.T[:NBLK] * filled).astype(jnp.bfloat16)
    return jnp.concatenate(encoded, axis=1), scales


def earlier_kernel(count, group, *refs):
    combined, own_result, peaks, totals, value_expand, bias, fetched_values, picked, found, filled = refs[:10]
    arrived, (result, encoded, scales, keys, latents) = refs[10:-5], refs[-5:]
    rows, width = bias.shape
    heads = value_expand.shape[0]
    steps = heads // group

    def span(g):
        at = g * group * rows
        return slice(at, at + group * rows)

    def score(g):
        scores = jnp.dot(combined[span(g), :], keys[...], preferred_element_type=jnp.float32)
        return (scores.reshape(group, rows, width) + bias[...][None]).reshape(group * rows, width)

    def weigh(g, scores):
        old_peak = peaks[span(g), :]
        parts = [scores[:, b:b + LANES] for b in range(0, width, LANES)]
        peak = jnp.maximum(old_peak, jnp.max(functools.reduce(jnp.maximum, parts), axis=1, keepdims=True))
        parts = [jnp.exp2((part - peak) * exp2_scale) for part in parts]
        total = jnp.sum(functools.reduce(jnp.add, parts), axis=1, keepdims=True)
        factor = jnp.exp2((old_peak - peak) * exp2_scale)
        inverse = 1.0 / (totals[span(g), :] * factor + total)
        weights = jnp.concatenate([part.astype(jnp.bfloat16) for part in parts], axis=1)
        return weights, factor * inverse, inverse

    def value(g):
        return [
            [head_values(latents[i * rows:(i + 1) * rows, :], value_expand, h) for h in range(g * group, (g + 1) * group, 2)]
            for i in range(count // 2)
        ]

    def finish(g, weights, factor, inverse, swapped):
        for i in range(group):
            part = slice(i * rows, (i + 1) * rows)
            h = g * group + i
            values = []
            for b in range(count // 2):
                values.append(fetched_values[b * rows:(b + 1) * rows, h * VDIM:(h + 1) * VDIM])
                values.append(swapped[b][i // 2][:, i % 2 * VDIM:(i % 2 + 1) * VDIM])
            out = jnp.dot(weights[part], jnp.concatenate(values, axis=0), preferred_element_type=jnp.float32)
            out = own_result[h * rows:(h + 1) * rows, :] * factor[part] + out * inverse[part]
            result[:, h * VDIM:(h + 1) * VDIM] = out.astype(jnp.bfloat16)

    def swapped_block(i):
        return jnp.concatenate([part[...] for part in arrived[i * (1 + SWAP) + 1:(i + 1) * (1 + SWAP)]], axis=0)

    def encode_found():
        total = found[...]
        latent_rows, rotary_rows = total[:, :LAT], total[:, LAT:]
        for i in range(len(arrived) // (1 + SWAP)):
            choice = picked[:, (2 + 2 * i) * rows:(3 + 2 * i) * rows]
            latent_rows = latent_rows + jnp.dot(choice, latents[i * rows:(i + 1) * rows, :], preferred_element_type=jnp.float32)
            rotary = swapped_block(i)[LAT:]
            rotary_rows = rotary_rows + lax.dot_general(choice, rotary, NT, preferred_element_type=jnp.float32)
        every = jnp.concatenate([latent_rows, rotary_rows], axis=1)
        encoded[...], scales[...] = encode(every, filled[:1, :every.shape[0]])

    for i in range(len(arrived) // (1 + SWAP)):
        latents[i * rows:(i + 1) * rows, :] = swapped_block(i)[:LAT].T

    @pl.when(lax.axis_index("cp") == 0)
    def _():
        for h in range(heads):
            part = slice(h * rows, (h + 1) * rows)
            result[:, h * VDIM:(h + 1) * VDIM] = (own_result[part, :] / totals[part, :]).astype(jnp.bfloat16)
        encode_found()

    @pl.when(lax.axis_index("cp") > 0)
    def _():
        for i in range(count // 2):
            at = 2 * i * rows
            keys[:, at:at + rows] = arrived[i * (1 + SWAP)][...]
            keys[:, at + rows:at + 2 * rows] = swapped_block(i)
        scores, values, weights = {}, {}, {}
        for step in range(steps + 2):
            if step < steps:
                scores[step] = score(step)
            if step == 2:
                encode_found()
            if 0 <= step - 2:
                finish(step - 2, *weights.pop(step - 2), values.pop(step - 2))
            if 0 <= step - 1 < steps:
                values[step - 1] = value(step - 1)
                weights[step - 1] = weigh(step - 1, scores.pop(step - 1))


def store_kernel(result, encoded, scales, sent_rows, attended, page_cache, page_scales, cache_buf, scale_buf, sems):
    count = sems.shape[0] - 2
    wide = result.shape[1] // count
    copies = []
    for i in range(count):
        some = pl.ds(i * wide, wide)
        copies.append(pltpu.make_async_copy(result.at[:, some], attended.at[:, some], sems.at[i]))
        copies[-1].start()
    kept = encoded.shape[0]
    for c in range(page_cache.shape[0]):
        part = slice(c * PAGE, (c + 1) * PAGE)
        cache_buf[c] = encoded[part, :] + sent_rows[part, :ROW]
        scale_buf[c] = (scales[...] + sent_rows[kept:kept + NBLK, :kept])[:, part]
    for i, (source, target) in enumerate(((cache_buf, page_cache), (scale_buf, page_scales))):
        copies.append(pltpu.make_async_copy(source, target, sems.at[count + i]))
        copies[-1].start()
    for copy in copies:
        copy.wait()


def fetch(own, n_cp, n_dec):
    blocks = []
    for step in range(1, n_cp - 1, 2):
        pairs = [(c * n_dec + e, (c + step + e % 2) % n_cp * n_dec + e) for c in range(n_cp) for e in range(n_dec)]
        blocks.append(lax.ppermute(own, ("cp", "dec"), pairs))
    return blocks


def swap(blocks, n_dec):
    pieces = []
    for block in blocks:
        parts = [block[at:at + ROW // SWAP] for at in range(0, ROW, ROW // SWAP)]
        pieces += [block] + [lax.ppermute(part, "dec", [(e, e ^ 1) for e in range(n_dec)]) for part in parts]
    return pieces


def on_device(queries, latent_rows, key_absorb, value_expand, prompt_pages, decode_owner, slot_offset):
    n_cp = lax.axis_size("cp")
    dec_count = lax.axis_size("dec")
    heads = key_absorb.shape[0]
    rows = latent_rows.shape[0]
    prompts, width = decode_owner.shape
    slot_count = 3 * (rows // PAGE) // (2 * dec_count)
    kept = slot_count * PAGE
    reach = width * dec_count * slot_count * PAGE
    count = -(-reach // rows) - (1 if prompts == 2 else 0)
    count = min(n_cp - 2, count + count % 2)
    own = latent_rows.T
    blocks = fetch(own, n_cp, dec_count)

    vmem = pl.BlockSpec(memory_space=pltpu.VMEM)
    hbm = pl.BlockSpec(memory_space=pltpu.HBM)
    params = pltpu.CompilerParams(vmem_limit_bytes=32 * 2**20)
    group, chunks = 4, (heads // 4,) * 4
    inputs = (prompt_pages, decode_owner, slot_offset, own, queries, key_absorb, value_expand)
    combined, result, peaks, totals, sent_rows, bias, picked, filled, own_copy, value_copy = pl.pallas_call(
        functools.partial(own_kernel, n_cp, count, chunks, group, slot_count),
        in_specs=[hbm] * 7,
        out_specs=[vmem] * 10,
        out_shape=[
            jax.ShapeDtypeStruct((heads * rows, ROW), jnp.bfloat16),
            jax.ShapeDtypeStruct((heads * rows, VDIM), jnp.float32),
            jax.ShapeDtypeStruct((heads * rows, LANES), jnp.float32),
            jax.ShapeDtypeStruct((heads * rows, LANES), jnp.float32),
            jax.ShapeDtypeStruct((kept + PAGE, -(-ROW // LANES) * LANES), jnp.bfloat16),
            jax.ShapeDtypeStruct((rows, count * rows), jnp.float32),
            jax.ShapeDtypeStruct((kept, (n_cp - 1) * rows), jnp.bfloat16),
            jax.ShapeDtypeStruct((8, LANES), jnp.float32),
            jax.ShapeDtypeStruct(own.shape, jnp.bfloat16),
            jax.ShapeDtypeStruct(value_expand.shape, jnp.bfloat16),
        ],
        scratch_shapes=[
            pltpu.SMEM(prompt_pages.shape, jnp.int32),
            pltpu.SMEM(decode_owner.shape, jnp.int32),
            pltpu.SMEM(slot_offset.shape, jnp.int32),
            pltpu.VMEM((rows, heads * HEAD), jnp.bfloat16),
            pltpu.VMEM((heads, NOPE, LAT), jnp.bfloat16),
            pltpu.VMEM((rows, LAT), jnp.bfloat16),
            pltpu.SemaphoreType.DMA((4 + 3 * len(chunks),)),
        ],
        cost_estimate=pl.CostEstimate(
            flops=2 * rows * heads * (2 * NOPE * LAT + rows * (ROW + VDIM)),
            bytes_accessed=2 * (queries.size + key_absorb.size + heads * rows * ROW),
            transcendentals=rows * heads * rows,
        ),
        compiler_params=params,
        name="own",
    )(*[pltpu.with_memory_space_constraint(x, pltpu.HBM) for x in inputs])
    sent_rows = lax.ppermute(sent_rows, "cp", [(c, (c + n_cp - 1) % n_cp) for c in range(n_cp)])
    blocks, picked = lax.optimization_barrier((blocks, picked))
    pieces = swap(blocks, dec_count)
    found, fetched_values = pl.pallas_call(
        functools.partial(arrived_kernel, count // 2),
        in_specs=[vmem] * (3 + len(blocks)),
        out_specs=[vmem] * 2,
        out_shape=[
            jax.ShapeDtypeStruct((kept, ROW), jnp.float32),
            jax.ShapeDtypeStruct((count // 2 * rows, heads * VDIM), jnp.bfloat16),
        ],
        cost_estimate=pl.CostEstimate(flops=2**20, bytes_accessed=2**10, transcendentals=0),
        compiler_params=params,
        name="arrived",
    )(picked, own_copy, value_copy, *blocks)

    group = 4 if count <= 4 else 2
    operands = (combined, result, peaks, totals, value_copy, bias, fetched_values, picked, found, filled, *pieces)
    attended, encoded, scales = pl.pallas_call(
        functools.partial(earlier_kernel, count, group),
        in_specs=[vmem] * len(operands),
        out_specs=[vmem] * 3,
        out_shape=[
            jax.ShapeDtypeStruct((rows, heads * VDIM), jnp.bfloat16),
            jax.ShapeDtypeStruct((kept, ROW), jnp.bfloat16),
            jax.ShapeDtypeStruct((NBLK, kept), jnp.bfloat16),
        ],
        scratch_shapes=[
            pltpu.VMEM((ROW, count * rows), jnp.bfloat16),
            pltpu.VMEM((len(blocks) * rows, LAT), jnp.bfloat16),
        ],
        cost_estimate=pl.CostEstimate(flops=2**20, bytes_accessed=2**10, transcendentals=0),
        compiler_params=params,
        name="earlier",
    )(*operands)
    sent_rows, attended = lax.optimization_barrier((sent_rows, attended))
    operands = (attended, encoded, scales, sent_rows)
    attended, page_cache, page_scales = pl.pallas_call(
        store_kernel,
        in_specs=[vmem] * len(operands),
        out_specs=[hbm] * 3,
        out_shape=[
            jax.ShapeDtypeStruct((rows, heads * VDIM), jnp.bfloat16),
            jax.ShapeDtypeStruct((slot_count, PAGE, ROW), jnp.bfloat16),
            jax.ShapeDtypeStruct((slot_count, NBLK, PAGE), jnp.bfloat16),
        ],
        scratch_shapes=[
            pltpu.VMEM((slot_count, PAGE, ROW), jnp.bfloat16),
            pltpu.VMEM((slot_count, NBLK, PAGE), jnp.bfloat16),
            pltpu.SemaphoreType.DMA((2 + 2,)),
        ],
        cost_estimate=pl.CostEstimate(flops=2**20, bytes_accessed=2**10, transcendentals=0),
        compiler_params=params,
        name="store",
    )(*operands)
    page_cache = page_cache.reshape(1, 1, slot_count, PAGE, ROW)
    page_scales = page_scales.transpose(0, 2, 1).reshape(1, 1, slot_count, PAGE, NBLK)
    return attended, page_cache, page_scales


def solution(mesh):
    return jax.shard_map(
        on_device,
        mesh=mesh,
        in_specs=(
            P(("grp", "cp"), "dec"),
            P(("grp", "cp"), None),
            P("dec", None, None),
            P("dec", None, None),
            P("grp"),
            P("grp", None),
            P("grp"),
        ),
        out_specs=(
            P(("grp", "cp"), "dec"),
            P(("grp", "cp"), "dec", None, None, None),
            P(("grp", "cp"), "dec", None, None, None),
        ),
        check_vma=False,
    )
```

```python
import functools
import math

import jax
import jax.numpy as jnp
from jax import lax
from jax.experimental import pallas as pl
from jax.experimental.pallas import tpu as pltpu
from jax.sharding import PartitionSpec as P

LAT = 512
ROPE = 64
NOPE = 128
VDIM = 128
PAGE = 16
BLOCK = 128
NBLK = LAT // BLOCK
ROW = LAT + ROPE
HEAD = NOPE + ROPE
LANES = 128
SWAP = 2

masked_fill = -1e30
amax_epsilon = 1e-06
exp2_scale = math.log2(math.e) / math.sqrt(HEAD)

NT = (((1,), (1,)), ((), ()))


def prompt_starts(prompt_pages):
    starts = [jnp.int32(0)]
    for k in range(prompt_pages.shape[0] - 1):
        starts.append(starts[-1] + prompt_pages[k])
    return starts


def visible_bias(prompt_pages, rows, steps_back):
    first = lax.axis_index("cp") * rows
    token = first + lax.broadcasted_iota(jnp.int32, (rows, 1), 0)
    begin = jnp.zeros((rows, 1), jnp.int32)
    for start in prompt_starts(prompt_pages):
        begin = jnp.maximum(begin, jnp.where(start * PAGE <= token, start * PAGE, 0))
    spot = first - steps_back * rows + lax.broadcasted_iota(jnp.int32, (1, rows), 1)
    return jnp.where((spot >= begin) & (spot <= token), 0.0, masked_fill)


def swap_pair(position, n_cp):
    odd = lax.rem(lax.axis_index("dec"), 2)
    within = lax.rem(position + 1, 2)
    swapped = position - within + lax.rem(within + odd, 2)
    paired = (position >= 1) & (position <= (n_cp - 1) // 2 * 2)
    return jnp.where(paired, swapped, position)


def slot_pages(owner, slot_count, prompt_pages, decode_owner, slot_offset):
    prompts, width = decode_owner.shape
    cycle = width * lax.axis_size("dec") * slot_count
    starts = prompt_starts(prompt_pages)
    pages, start, offset, place = jnp.int32(0), jnp.int32(0), jnp.int32(0), jnp.int32(0)
    for k in range(prompts):
        for p in range(width):
            mine = decode_owner[k, p] == owner
            pages = jnp.where(mine, prompt_pages[k], pages)
            start = jnp.where(mine, starts[k], start)
            offset = jnp.where(mine, slot_offset[k], offset)
            place = jnp.where(mine, p, place)
    result = []
    for c in range(slot_count):
        turn = width * (lax.axis_index("dec") * slot_count + c) + place
        page = lax.rem(turn - offset + 2 * cycle, cycle)
        result.append((page < pages, start + page))
    return result


def row_picker(targets, columns):
    kept = len(targets) * PAGE
    row = lax.broadcasted_iota(jnp.int32, (kept, 1), 0)
    target = jnp.full((kept, 1), -1, jnp.int32)
    for c, column in enumerate(targets):
        target = jnp.where(row // PAGE == c, column + row % PAGE, target)
    column = lax.broadcasted_iota(jnp.int32, (1, columns), 1)
    return jnp.where(column == target, 1.0, 0.0).astype(jnp.bfloat16)


def head_values(latents, value_expand, h):
    both = jnp.concatenate([value_expand[h], value_expand[h + 1]], axis=1)
    return jnp.dot(latents, both, preferred_element_type=jnp.float32).astype(jnp.bfloat16)


def own_kernel(n_cp, count, chunks, group, slot_count, *refs):
    inputs, refs = refs[:7], refs[7:]
    combined, result, peaks, totals, sent_rows, bias, picked, filled, own, value_expand = refs[:10]
    prompt_pages, decode_owner, slot_offset, queries, key_absorb, latents, sems = refs[10:]
    pages_hbm, owner_hbm, offset_hbm, own_hbm, queries_hbm, absorb_hbm, expand_hbm = inputs
    rows = own.shape[1]
    heads = key_absorb.shape[0]
    small = [
        pltpu.make_async_copy(source, target, sems.at[i])
        for i, (source, target) in enumerate(zip(inputs[:4], (prompt_pages, decode_owner, slot_offset, own)))
    ]
    large = {}
    first = 0
    for chunk in chunks:
        at = 4 + 3 * len(large)
        some = pl.ds(first, chunk)
        wide = pl.ds(first * HEAD, chunk * HEAD)
        large[first] = (
            pltpu.make_async_copy(queries_hbm.at[:, wide], queries.at[:, wide], sems.at[at]),
            pltpu.make_async_copy(absorb_hbm.at[some], key_absorb.at[some], sems.at[at + 1]),
            pltpu.make_async_copy(expand_hbm.at[some], value_expand.at[some], sems.at[at + 2]),
        )
        first += chunk
    for copy in small:
        copy.start()
    for chunk_copies in large.values():
        for copy in chunk_copies:
            copy.start()
    steps = heads // group

    def absorb(g):
        for copy in large.get(g * group, ())[:2 if g == 0 else 3]:
            copy.wait()
        for h in range(g * group, (g + 1) * group):
            at = h * HEAD
            absorbed = jnp.dot(queries[:, at:at + NOPE], key_absorb[h], preferred_element_type=jnp.float32)
            combined[h * rows:(h + 1) * rows, :LAT] = absorbed.astype(jnp.bfloat16)
            combined[h * rows:(h + 1) * rows, LAT:] = queries[:, at + NOPE:at + HEAD]

    def score(g):
        return jnp.dot(combined[g * group * rows:(g + 1) * group * rows, :], own[...], preferred_element_type=jnp.float32)

    def value(g):
        return [head_values(latents[...], value_expand, g * group + i) for i in range(0, group, 2)]

    def finish(g, scores, both):
        span = slice(g * group * rows, (g + 1) * group * rows)
        scores = (scores.reshape(group, rows, rows) + own_bias[None]).reshape(group * rows, rows)
        peak = jnp.max(scores, axis=1, keepdims=True)
        weights = jnp.exp2((scores - peak) * exp2_scale)
        total = jnp.sum(weights, axis=1, keepdims=True)
        weights = weights.astype(jnp.bfloat16)
        for i in range(group):
            mine = both[i // 2][:, i % 2 * VDIM:(i % 2 + 1) * VDIM]
            out = jnp.dot(weights[i * rows:(i + 1) * rows], mine, preferred_element_type=jnp.float32)
            result[(g * group + i) * rows:(g * group + i + 1) * rows, :] = out
        peaks[span, :] = jnp.broadcast_to(peak, (group * rows, LANES))
        totals[span, :] = jnp.broadcast_to(total, (group * rows, LANES))

    for copy in small:
        copy.wait()
    latents[...] = own[:LAT, :].T
    own_bias = visible_bias(prompt_pages, rows, 0)
    index_work(n_cp, count, slot_count, prompt_pages, decode_owner, slot_offset, own[...], sent_rows, bias, picked, filled)
    scores, both = {}, {}
    for step in range(steps + 2):
        if step == 1:
            large[0][2].wait()
        if step < steps:
            absorb(step)
        if 0 <= step - 1 < steps:
            scores[step - 1] = score(step - 1)
            both[step - 1] = value(step - 1)
        if 0 <= step - 2:
            finish(step - 2, scores.pop(step - 2), both.pop(step - 2))


def index_work(n_cp, count, slot_count, prompt_pages, decode_owner, slot_offset, block, sent_rows, bias, picked, filled):
    rows = block.shape[1]
    me = lax.axis_index("cp")
    behind = lax.rem(me + n_cp - 1, n_cp)
    targets, here = [], []
    for valid, page in slot_pages(behind, slot_count, prompt_pages, decode_owner, slot_offset):
        here.append(valid & (page * PAGE // rows == me))
        targets.append(jnp.where(here[-1], lax.rem(page * PAGE, rows), -PAGE))
    choice = row_picker(targets, rows)
    sent = lax.dot_general(choice, block, NT, preferred_element_type=jnp.float32)
    encoded, scales = encode(sent, slot_lanes(here))
    kept = choice.shape[0]
    sent_rows[...] = jnp.zeros(sent_rows.shape, jnp.bfloat16)
    sent_rows[:kept, :ROW] = encoded
    sent_rows[kept:kept + NBLK, :kept] = scales
    for b in range(count):
        bias[:, b * rows:(b + 1) * rows] = visible_bias(prompt_pages, rows, swap_pair(jnp.int32(b + 1), n_cp))
    targets, found = [], []
    for valid, page in slot_pages(me, slot_count, prompt_pages, decode_owner, slot_offset):
        steps_back = lax.rem(me - page * PAGE // rows + n_cp, n_cp)
        column = swap_pair(steps_back, n_cp) * rows + lax.rem(page * PAGE, rows)
        targets.append(jnp.where(valid, column, -PAGE))
        found.append(valid & (steps_back < n_cp - 1))
    filled[:1, :] = slot_lanes(found, filled.shape[1])
    picked[...] = row_picker(targets, (n_cp - 1) * rows)


def pick_rows(picked, index, block):
    rows = block.shape[1]
    return lax.dot_general(picked[:, index * rows:(index + 1) * rows], block, NT, preferred_element_type=jnp.float32)


def arrived_kernel(used, picked, own, value_expand, *refs):
    blocks, (found, values) = refs[:-2], refs[-2:]
    rows = own.shape[1]
    for i in range(used):
        latents = blocks[i][:LAT, :].T
        for h in range(0, value_expand.shape[0], 2):
            values[i * rows:(i + 1) * rows, h * VDIM:(h + 2) * VDIM] = head_values(latents, value_expand, h)
    total = pick_rows(picked, 0, own[...])
    for i, block in enumerate(blocks):
        total = total + pick_rows(picked, 1 + 2 * i, block[...])
    found[...] = total


def slot_lanes(flags, width=None):
    lane = lax.broadcasted_iota(jnp.int32, (1, width or len(flags) * PAGE), 1)
    lanes = jnp.zeros(lane.shape, jnp.float32)
    for c, flag in enumerate(flags):
        lanes = jnp.where(lane // PAGE == c, flag.astype(jnp.float32), lanes)
    return lanes


def encode(rows, filled):
    kept = rows.shape[0]
    which = lax.broadcasted_iota(jnp.int32, (kept, LANES), 1)
    table = jnp.zeros((kept, LANES), jnp.float32)
    encoded = []
    for b in range(NBLK):
        values = rows[:, b * BLOCK:(b + 1) * BLOCK]
        scale = jnp.max(jnp.abs(values), axis=1, keepdims=True) + amax_epsilon
        scale = scale.astype(jnp.bfloat16).astype(jnp.float32)
        encoded.append((values / scale).astype(jnp.bfloat16))
        table = jnp.where(which == b, scale, table)
    encoded.append(rows[:, LAT:].astype(jnp.bfloat16))
    scales = (table.T[:NBLK] * filled).astype(jnp.bfloat16)
    return jnp.concatenate(encoded, axis=1), scales


def earlier_kernel(count, group, *refs):
    combined, own_result, peaks, totals, value_expand, bias, fetched_values, picked, found, filled = refs[:10]
    arrived, (result, encoded, scales, keys, latents) = refs[10:-5], refs[-5:]
    rows, width = bias.shape
    heads = value_expand.shape[0]
    steps = heads // group

    def span(g):
        at = g * group * rows
        return slice(at, at + group * rows)

    def score(g):
        scores = jnp.dot(combined[span(g), :], keys[...], preferred_element_type=jnp.float32)
        return (scores.reshape(group, rows, width) + bias[...][None]).reshape(group * rows, width)

    def weigh(g, scores):
        old_peak = peaks[span(g), :]
        parts = [scores[:, b:b + LANES] for b in range(0, width, LANES)]
        peak = jnp.maximum(old_peak, jnp.max(functools.reduce(jnp.maximum, parts), axis=1, keepdims=True))
        parts = [jnp.exp2((part - peak) * exp2_scale) for part in parts]
        total = jnp.sum(functools.reduce(jnp.add, parts), axis=1, keepdims=True)
        factor = jnp.exp2((old_peak - peak) * exp2_scale)
        inverse = 1.0 / (totals[span(g), :] * factor + total)
        weights = jnp.concatenate([part.astype(jnp.bfloat16) for part in parts], axis=1)
        return weights, factor * inverse, inverse

    def value(g):
        return [
            [head_values(latents[i * rows:(i + 1) * rows, :], value_expand, h) for h in range(g * group, (g + 1) * group, 2)]
            for i in range(count // 2)
        ]

    def finish(g, weights, factor, inverse, swapped):
        for i in range(group):
            part = slice(i * rows, (i + 1) * rows)
            h = g * group + i
            values = []
            for b in range(count // 2):
                values.append(fetched_values[b * rows:(b + 1) * rows, h * VDIM:(h + 1) * VDIM])
                values.append(swapped[b][i // 2][:, i % 2 * VDIM:(i % 2 + 1) * VDIM])
            out = jnp.dot(weights[part], jnp.concatenate(values, axis=0), preferred_element_type=jnp.float32)
            out = own_result[h * rows:(h + 1) * rows, :] * factor[part] + out * inverse[part]
            result[:, h * VDIM:(h + 1) * VDIM] = out.astype(jnp.bfloat16)

    def swapped_block(i):
        return jnp.concatenate([part[...] for part in arrived[i * (1 + SWAP) + 1:(i + 1) * (1 + SWAP)]], axis=0)

    def encode_found():
        total = found[...]
        latent_rows, rotary_rows = total[:, :LAT], total[:, LAT:]
        for i in range(len(arrived) // (1 + SWAP)):
            choice = picked[:, (2 + 2 * i) * rows:(3 + 2 * i) * rows]
            latent_rows = latent_rows + jnp.dot(choice, latents[i * rows:(i + 1) * rows, :], preferred_element_type=jnp.float32)
            rotary = swapped_block(i)[LAT:]
            rotary_rows = rotary_rows + lax.dot_general(choice, rotary, NT, preferred_element_type=jnp.float32)
        every = jnp.concatenate([latent_rows, rotary_rows], axis=1)
        encoded[...], scales[...] = encode(every, filled[:1, :every.shape[0]])

    for i in range(len(arrived) // (1 + SWAP)):
        latents[i * rows:(i + 1) * rows, :] = swapped_block(i)[:LAT].T

    @pl.when(lax.axis_index("cp") == 0)
    def _():
        for h in range(heads):
            part = slice(h * rows, (h + 1) * rows)
            result[:, h * VDIM:(h + 1) * VDIM] = (own_result[part, :] / totals[part, :]).astype(jnp.bfloat16)
        encode_found()

    @pl.when(lax.axis_index("cp") > 0)
    def _():
        for i in range(count // 2):
            at = 2 * i * rows
            keys[:, at:at + rows] = arrived[i * (1 + SWAP)][...]
            keys[:, at + rows:at + 2 * rows] = swapped_block(i)
        scores, values, weights = {}, {}, {}
        for step in range(steps + 2):
            if step < steps:
                scores[step] = score(step)
            if step == 2:
                encode_found()
            if 0 <= step - 2:
                finish(step - 2, *weights.pop(step - 2), values.pop(step - 2))
            if 0 <= step - 1 < steps:
                values[step - 1] = value(step - 1)
                weights[step - 1] = weigh(step - 1, scores.pop(step - 1))


def store_kernel(result, encoded, scales, sent_rows, attended, page_cache, page_scales, cache_buf, scale_buf, sems):
    count = sems.shape[0] - 2
    wide = result.shape[1] // count
    copies = []
    for i in range(count):
        some = pl.ds(i * wide, wide)
        copies.append(pltpu.make_async_copy(result.at[:, some], attended.at[:, some], sems.at[i]))
        copies[-1].start()
    kept = encoded.shape[0]
    for c in range(page_cache.shape[0]):
        part = slice(c * PAGE, (c + 1) * PAGE)
        cache_buf[c] = encoded[part, :] + sent_rows[part, :ROW]
        scale_buf[c] = (scales[...] + sent_rows[kept:kept + NBLK, :kept])[:, part]
    for i, (source, target) in enumerate(((cache_buf, page_cache), (scale_buf, page_scales))):
        copies.append(pltpu.make_async_copy(source, target, sems.at[count + i]))
        copies[-1].start()
    for copy in copies:
        copy.wait()


def fetch(own, n_cp, n_dec):
    blocks = []
    for step in range(1, n_cp - 1, 2):
        pairs = [(c * n_dec + e, (c + step + e % 2) % n_cp * n_dec + e) for c in range(n_cp) for e in range(n_dec)]
        blocks.append(lax.ppermute(own, ("cp", "dec"), pairs))
    return blocks


def swap(blocks, n_dec):
    pieces = []
    for block in blocks:
        parts = [block[at:at + ROW // SWAP] for at in range(0, ROW, ROW // SWAP)]
        pieces += [block] + [lax.ppermute(part, "dec", [(e, e ^ 1) for e in range(n_dec)]) for part in parts]
    return pieces


def on_device(queries, latent_rows, key_absorb, value_expand, prompt_pages, decode_owner, slot_offset):
    n_cp = lax.axis_size("cp")
    dec_count = lax.axis_size("dec")
    heads = key_absorb.shape[0]
    rows = latent_rows.shape[0]
    prompts, width = decode_owner.shape
    slot_count = 3 * (rows // PAGE) // (2 * dec_count)
    kept = slot_count * PAGE
    reach = width * dec_count * slot_count * PAGE
    count = -(-reach // rows) - (1 if prompts == 2 else 0)
    count = min(n_cp - 2, count + count % 2)
    own = latent_rows.T
    blocks = fetch(own, n_cp, dec_count)

    vmem = pl.BlockSpec(memory_space=pltpu.VMEM)
    hbm = pl.BlockSpec(memory_space=pltpu.HBM)
    params = pltpu.CompilerParams(vmem_limit_bytes=32 * 2**20)
    group, chunks = 4, (heads // 2, heads // 2)
    inputs = (prompt_pages, decode_owner, slot_offset, own, queries, key_absorb, value_expand)
    combined, result, peaks, totals, sent_rows, bias, picked, filled, own_copy, value_copy = pl.pallas_call(
        functools.partial(own_kernel, n_cp, count, chunks, group, slot_count),
        in_specs=[hbm] * 7,
        out_specs=[vmem] * 10,
        out_shape=[
            jax.ShapeDtypeStruct((heads * rows, ROW), jnp.bfloat16),
            jax.ShapeDtypeStruct((heads * rows, VDIM), jnp.float32),
            jax.ShapeDtypeStruct((heads * rows, LANES), jnp.float32),
            jax.ShapeDtypeStruct((heads * rows, LANES), jnp.float32),
            jax.ShapeDtypeStruct((kept + PAGE, -(-ROW // LANES) * LANES), jnp.bfloat16),
            jax.ShapeDtypeStruct((rows, count * rows), jnp.float32),
            jax.ShapeDtypeStruct((kept, (n_cp - 1) * rows), jnp.bfloat16),
            jax.ShapeDtypeStruct((8, LANES), jnp.float32),
            jax.ShapeDtypeStruct(own.shape, jnp.bfloat16),
            jax.ShapeDtypeStruct(value_expand.shape, jnp.bfloat16),
        ],
        scratch_shapes=[
            pltpu.SMEM(prompt_pages.shape, jnp.int32),
            pltpu.SMEM(decode_owner.shape, jnp.int32),
            pltpu.SMEM(slot_offset.shape, jnp.int32),
            pltpu.VMEM((rows, heads * HEAD), jnp.bfloat16),
            pltpu.VMEM((heads, NOPE, LAT), jnp.bfloat16),
            pltpu.VMEM((rows, LAT), jnp.bfloat16),
            pltpu.SemaphoreType.DMA((4 + 3 * len(chunks),)),
        ],
        cost_estimate=pl.CostEstimate(
            flops=2 * rows * heads * (2 * NOPE * LAT + rows * (ROW + VDIM)),
            bytes_accessed=2 * (queries.size + key_absorb.size + heads * rows * ROW),
            transcendentals=rows * heads * rows,
        ),
        compiler_params=params,
        name="own",
    )(*[pltpu.with_memory_space_constraint(x, pltpu.HBM) for x in inputs])
    sent_rows = lax.ppermute(sent_rows, "cp", [(c, (c + n_cp - 1) % n_cp) for c in range(n_cp)])
    blocks, picked = lax.optimization_barrier((blocks, picked))
    pieces = swap(blocks, dec_count)
    found, fetched_values = pl.pallas_call(
        functools.partial(arrived_kernel, count // 2),
        in_specs=[vmem] * (3 + len(blocks)),
        out_specs=[vmem] * 2,
        out_shape=[
            jax.ShapeDtypeStruct((kept, ROW), jnp.float32),
            jax.ShapeDtypeStruct((count // 2 * rows, heads * VDIM), jnp.bfloat16),
        ],
        cost_estimate=pl.CostEstimate(flops=2**20, bytes_accessed=2**10, transcendentals=0),
        compiler_params=params,
        name="arrived",
    )(picked, own_copy, value_copy, *blocks)

    group = 4 if count <= 4 else 2
    operands = (combined, result, peaks, totals, value_copy, bias, fetched_values, picked, found, filled, *pieces)
    attended, encoded, scales = pl.pallas_call(
        functools.partial(earlier_kernel, count, group),
        in_specs=[vmem] * len(operands),
        out_specs=[vmem] * 3,
        out_shape=[
            jax.ShapeDtypeStruct((rows, heads * VDIM), jnp.bfloat16),
            jax.ShapeDtypeStruct((kept, ROW), jnp.bfloat16),
            jax.ShapeDtypeStruct((NBLK, kept), jnp.bfloat16),
        ],
        scratch_shapes=[
            pltpu.VMEM((ROW, count * rows), jnp.bfloat16),
            pltpu.VMEM((len(blocks) * rows, LAT), jnp.bfloat16),
        ],
        cost_estimate=pl.CostEstimate(flops=2**20, bytes_accessed=2**10, transcendentals=0),
        compiler_params=params,
        name="earlier",
    )(*operands)
    sent_rows, attended = lax.optimization_barrier((sent_rows, attended))
    operands = (attended, encoded, scales, sent_rows)
    attended, page_cache, page_scales = pl.pallas_call(
        store_kernel,
        in_specs=[vmem] * len(operands),
        out_specs=[hbm] * 3,
        out_shape=[
            jax.ShapeDtypeStruct((rows, heads * VDIM), jnp.bfloat16),
            jax.ShapeDtypeStruct((slot_count, PAGE, ROW), jnp.bfloat16),
            jax.ShapeDtypeStruct((slot_count, NBLK, PAGE), jnp.bfloat16),
        ],
        scratch_shapes=[
            pltpu.VMEM((slot_count, PAGE, ROW), jnp.bfloat16),
            pltpu.VMEM((slot_count, NBLK, PAGE), jnp.bfloat16),
            pltpu.SemaphoreType.DMA((4 + 2,)),
        ],
        cost_estimate=pl.CostEstimate(flops=2**20, bytes_accessed=2**10, transcendentals=0),
        compiler_params=params,
        name="store",
    )(*operands)
    page_cache = page_cache.reshape(1, 1, slot_count, PAGE, ROW)
    page_scales = page_scales.transpose(0, 2, 1).reshape(1, 1, slot_count, PAGE, NBLK)
    return attended, page_cache, page_scales


def solution(mesh):
    return jax.shard_map(
        on_device,
        mesh=mesh,
        in_specs=(
            P(("grp", "cp"), "dec"),
            P(("grp", "cp"), None),
            P("dec", None, None),
            P("dec", None, None),
            P("grp"),
            P("grp", None),
            P("grp"),
        ),
        out_specs=(
            P(("grp", "cp"), "dec"),
            P(("grp", "cp"), "dec", None, None, None),
            P(("grp", "cp"), "dec", None, None, None),
        ),
        check_vma=False,
    )
```

```python
import functools
import math

import jax
import jax.numpy as jnp
from jax import lax
from jax.experimental import pallas as pl
from jax.experimental.pallas import tpu as pltpu
from jax.sharding import PartitionSpec as P

LAT = 512
ROPE = 64
NOPE = 128
VDIM = 128
PAGE = 16
BLOCK = 128
NBLK = LAT // BLOCK
ROW = LAT + ROPE
HEAD = NOPE + ROPE
LANES = 128
SWAP = 2

masked_fill = -1e30
amax_epsilon = 1e-06
exp2_scale = math.log2(math.e) / math.sqrt(HEAD)

NT = (((1,), (1,)), ((), ()))


def prompt_starts(prompt_pages):
    starts = [jnp.int32(0)]
    for k in range(prompt_pages.shape[0] - 1):
        starts.append(starts[-1] + prompt_pages[k])
    return starts


def visible_bias(prompt_pages, rows, steps_back):
    first = lax.axis_index("cp") * rows
    token = first + lax.broadcasted_iota(jnp.int32, (rows, 1), 0)
    begin = jnp.zeros((rows, 1), jnp.int32)
    for start in prompt_starts(prompt_pages):
        begin = jnp.maximum(begin, jnp.where(start * PAGE <= token, start * PAGE, 0))
    spot = first - steps_back * rows + lax.broadcasted_iota(jnp.int32, (1, rows), 1)
    return jnp.where((spot >= begin) & (spot <= token), 0.0, masked_fill)


def swap_pair(position, n_cp):
    odd = lax.rem(lax.axis_index("dec"), 2)
    within = lax.rem(position + 1, 2)
    swapped = position - within + lax.rem(within + odd, 2)
    paired = (position >= 1) & (position <= (n_cp - 1) // 2 * 2)
    return jnp.where(paired, swapped, position)


def slot_pages(owner, slot_count, prompt_pages, decode_owner, slot_offset):
    prompts, width = decode_owner.shape
    cycle = width * lax.axis_size("dec") * slot_count
    starts = prompt_starts(prompt_pages)
    pages, start, offset, place = jnp.int32(0), jnp.int32(0), jnp.int32(0), jnp.int32(0)
    for k in range(prompts):
        for p in range(width):
            mine = decode_owner[k, p] == owner
            pages = jnp.where(mine, prompt_pages[k], pages)
            start = jnp.where(mine, starts[k], start)
            offset = jnp.where(mine, slot_offset[k], offset)
            place = jnp.where(mine, p, place)
    result = []
    for c in range(slot_count):
        turn = width * (lax.axis_index("dec") * slot_count + c) + place
        page = lax.rem(turn - offset + 2 * cycle, cycle)
        result.append((page < pages, start + page))
    return result


def row_picker(targets, columns):
    kept = len(targets) * PAGE
    row = lax.broadcasted_iota(jnp.int32, (kept, 1), 0)
    target = jnp.full((kept, 1), -1, jnp.int32)
    for c, column in enumerate(targets):
        target = jnp.where(row // PAGE == c, column + row % PAGE, target)
    column = lax.broadcasted_iota(jnp.int32, (1, columns), 1)
    return jnp.where(column == target, 1.0, 0.0).astype(jnp.bfloat16)


def head_values(latents, value_expand, h):
    both = jnp.concatenate([value_expand[h], value_expand[h + 1]], axis=1)
    return jnp.dot(latents, both, preferred_element_type=jnp.float32).astype(jnp.bfloat16)


def own_kernel(n_cp, count, chunks, group, slot_count, *refs):
    inputs, refs = refs[:7], refs[7:]
    combined, result, peaks, totals, sent_rows, bias, picked, filled, own, value_expand = refs[:10]
    prompt_pages, decode_owner, slot_offset, queries, key_absorb, latents, sems = refs[10:]
    pages_hbm, owner_hbm, offset_hbm, own_hbm, queries_hbm, absorb_hbm, expand_hbm = inputs
    rows = own.shape[1]
    heads = key_absorb.shape[0]
    small = [
        pltpu.make_async_copy(source, target, sems.at[i])
        for i, (source, target) in enumerate(zip(inputs[:4], (prompt_pages, decode_owner, slot_offset, own)))
    ]
    large = {}
    first = 0
    for chunk in chunks:
        at = 4 + 3 * len(large)
        some = pl.ds(first, chunk)
        wide = pl.ds(first * HEAD, chunk * HEAD)
        large[first] = (
            pltpu.make_async_copy(queries_hbm.at[:, wide], queries.at[:, wide], sems.at[at]),
            pltpu.make_async_copy(absorb_hbm.at[some], key_absorb.at[some], sems.at[at + 1]),
            pltpu.make_async_copy(expand_hbm.at[some], value_expand.at[some], sems.at[at + 2]),
        )
        first += chunk
    for copy in small:
        copy.start()
    for chunk_copies in large.values():
        for copy in chunk_copies:
            copy.start()
    steps = heads // group

    def absorb(g):
        for copy in large.get(g * group, ())[:2 if g == 0 else 3]:
            copy.wait()
        for h in range(g * group, (g + 1) * group):
            at = h * HEAD
            absorbed = jnp.dot(queries[:, at:at + NOPE], key_absorb[h], preferred_element_type=jnp.float32)
            combined[h * rows:(h + 1) * rows, :LAT] = absorbed.astype(jnp.bfloat16)
            combined[h * rows:(h + 1) * rows, LAT:] = queries[:, at + NOPE:at + HEAD]

    def score(g):
        return jnp.dot(combined[g * group * rows:(g + 1) * group * rows, :], own[...], preferred_element_type=jnp.float32)

    def value(g):
        return [head_values(latents[...], value_expand, g * group + i) for i in range(0, group, 2)]

    def finish(g, scores, both):
        span = slice(g * group * rows, (g + 1) * group * rows)
        scores = (scores.reshape(group, rows, rows) + own_bias[None]).reshape(group * rows, rows)
        peak = jnp.max(scores, axis=1, keepdims=True)
        weights = jnp.exp2((scores - peak) * exp2_scale)
        total = jnp.sum(weights, axis=1, keepdims=True)
        weights = weights.astype(jnp.bfloat16)
        for i in range(group):
            mine = both[i // 2][:, i % 2 * VDIM:(i % 2 + 1) * VDIM]
            out = jnp.dot(weights[i * rows:(i + 1) * rows], mine, preferred_element_type=jnp.float32)
            result[(g * group + i) * rows:(g * group + i + 1) * rows, :] = out
        peaks[span, :] = jnp.broadcast_to(peak, (group * rows, LANES))
        totals[span, :] = jnp.broadcast_to(total, (group * rows, LANES))

    for copy in small:
        copy.wait()
    latents[...] = own[:LAT, :].T
    own_bias = visible_bias(prompt_pages, rows, 0)
    index_work(n_cp, count, slot_count, prompt_pages, decode_owner, slot_offset, own[...], sent_rows, bias, picked, filled)
    scores, both = {}, {}
    for step in range(steps + 2):
        if step == 1:
            large[0][2].wait()
        if step < steps:
            absorb(step)
        if 0 <= step - 1 < steps:
            scores[step - 1] = score(step - 1)
            both[step - 1] = value(step - 1)
        if 0 <= step - 2:
            finish(step - 2, scores.pop(step - 2), both.pop(step - 2))


def index_work(n_cp, count, slot_count, prompt_pages, decode_owner, slot_offset, block, sent_rows, bias, picked, filled):
    rows = block.shape[1]
    me = lax.axis_index("cp")
    behind = lax.rem(me + n_cp - 1, n_cp)
    targets, here = [], []
    for valid, page in slot_pages(behind, slot_count, prompt_pages, decode_owner, slot_offset):
        here.append(valid & (page * PAGE // rows == me))
        targets.append(jnp.where(here[-1], lax.rem(page * PAGE, rows), -PAGE))
    choice = row_picker(targets, rows)
    sent = lax.dot_general(choice, block, NT, preferred_element_type=jnp.float32)
    encoded, scales = encode(sent, slot_lanes(here))
    kept = choice.shape[0]
    sent_rows[...] = jnp.zeros(sent_rows.shape, jnp.bfloat16)
    sent_rows[:kept, :ROW] = encoded
    sent_rows[kept:kept + NBLK, :kept] = scales
    for b in range(count):
        bias[:, b * rows:(b + 1) * rows] = visible_bias(prompt_pages, rows, swap_pair(jnp.int32(b + 1), n_cp))
    targets, found = [], []
    for valid, page in slot_pages(me, slot_count, prompt_pages, decode_owner, slot_offset):
        steps_back = lax.rem(me - page * PAGE // rows + n_cp, n_cp)
        column = swap_pair(steps_back, n_cp) * rows + lax.rem(page * PAGE, rows)
        targets.append(jnp.where(valid, column, -PAGE))
        found.append(valid & (steps_back < n_cp - 1))
    filled[:1, :] = slot_lanes(found, filled.shape[1])
    picked[...] = row_picker(targets, (n_cp - 1) * rows)


def pick_rows(picked, index, block):
    rows = block.shape[1]
    return lax.dot_general(picked[:, index * rows:(index + 1) * rows], block, NT, preferred_element_type=jnp.float32)


def arrived_kernel(used, picked, own, value_expand, *refs):
    blocks, (found, values) = refs[:-2], refs[-2:]
    rows = own.shape[1]
    for i in range(used):
        latents = blocks[i][:LAT, :].T
        for h in range(0, value_expand.shape[0], 2):
            values[i * rows:(i + 1) * rows, h * VDIM:(h + 2) * VDIM] = head_values(latents, value_expand, h)
    total = pick_rows(picked, 0, own[...])
    for i, block in enumerate(blocks):
        total = total + pick_rows(picked, 1 + 2 * i, block[...])
    found[...] = total


def slot_lanes(flags, width=None):
    lane = lax.broadcasted_iota(jnp.int32, (1, width or len(flags) * PAGE), 1)
    lanes = jnp.zeros(lane.shape, jnp.float32)
    for c, flag in enumerate(flags):
        lanes = jnp.where(lane // PAGE == c, flag.astype(jnp.float32), lanes)
    return lanes


def encode(rows, filled):
    kept = rows.shape[0]
    which = lax.broadcasted_iota(jnp.int32, (kept, LANES), 1)
    table = jnp.zeros((kept, LANES), jnp.float32)
    encoded = []
    for b in range(NBLK):
        values = rows[:, b * BLOCK:(b + 1) * BLOCK]
        scale = jnp.max(jnp.abs(values), axis=1, keepdims=True) + amax_epsilon
        scale = scale.astype(jnp.bfloat16).astype(jnp.float32)
        encoded.append((values / scale).astype(jnp.bfloat16))
        table = jnp.where(which == b, scale, table)
    encoded.append(rows[:, LAT:].astype(jnp.bfloat16))
    scales = (table.T[:NBLK] * filled).astype(jnp.bfloat16)
    return jnp.concatenate(encoded, axis=1), scales


def earlier_kernel(count, group, *refs):
    combined, own_result, peaks, totals, value_expand, bias, fetched_values, picked, found, filled, sent_rows = refs[:11]
    arrived = refs[11:-9]
    attended, page_cache, page_scales, keys, latents, result, cache_buf, scale_buf, sems = refs[-9:]
    rows, width = bias.shape
    heads = value_expand.shape[0]
    steps = heads // group

    def span(g):
        at = g * group * rows
        return slice(at, at + group * rows)

    def score(g):
        scores = jnp.dot(combined[span(g), :], keys[...], preferred_element_type=jnp.float32)
        return (scores.reshape(group, rows, width) + bias[...][None]).reshape(group * rows, width)

    def weigh(g, scores):
        old_peak = peaks[span(g), :]
        parts = [scores[:, b:b + LANES] for b in range(0, width, LANES)]
        peak = jnp.maximum(old_peak, jnp.max(functools.reduce(jnp.maximum, parts), axis=1, keepdims=True))
        parts = [jnp.exp2((part - peak) * exp2_scale) for part in parts]
        total = jnp.sum(functools.reduce(jnp.add, parts), axis=1, keepdims=True)
        factor = jnp.exp2((old_peak - peak) * exp2_scale)
        inverse = 1.0 / (totals[span(g), :] * factor + total)
        weights = jnp.concatenate([part.astype(jnp.bfloat16) for part in parts], axis=1)
        return weights, factor * inverse, inverse

    def value(g):
        return [
            [head_values(latents[i * rows:(i + 1) * rows, :], value_expand, h) for h in range(g * group, (g + 1) * group, 2)]
            for i in range(count // 2)
        ]

    def finish(g, weights, factor, inverse, swapped):
        for i in range(group):
            part = slice(i * rows, (i + 1) * rows)
            h = g * group + i
            values = []
            for b in range(count // 2):
                values.append(fetched_values[b * rows:(b + 1) * rows, h * VDIM:(h + 1) * VDIM])
                values.append(swapped[b][i // 2][:, i % 2 * VDIM:(i % 2 + 1) * VDIM])
            out = jnp.dot(weights[part], jnp.concatenate(values, axis=0), preferred_element_type=jnp.float32)
            out = own_result[h * rows:(h + 1) * rows, :] * factor[part] + out * inverse[part]
            result[:, h * VDIM:(h + 1) * VDIM] = out.astype(jnp.bfloat16)

    def swapped_block(i):
        return jnp.concatenate([part[...] for part in arrived[i * (1 + SWAP) + 1:(i + 1) * (1 + SWAP)]], axis=0)

    def encode_found():
        total = found[...]
        latent_rows, rotary_rows = total[:, :LAT], total[:, LAT:]
        for i in range(len(arrived) // (1 + SWAP)):
            choice = picked[:, (2 + 2 * i) * rows:(3 + 2 * i) * rows]
            latent_rows = latent_rows + jnp.dot(choice, latents[i * rows:(i + 1) * rows, :], preferred_element_type=jnp.float32)
            rotary = swapped_block(i)[LAT:]
            rotary_rows = rotary_rows + lax.dot_general(choice, rotary, NT, preferred_element_type=jnp.float32)
        every = jnp.concatenate([latent_rows, rotary_rows], axis=1)
        kept = every.shape[0]
        encoded, scales = encode(every, filled[:1, :kept])
        scales = scales + sent_rows[kept:kept + NBLK, :kept]
        for c in range(page_cache.shape[0]):
            part = slice(c * PAGE, (c + 1) * PAGE)
            cache_buf[c] = encoded[part, :] + sent_rows[part, :ROW]
            scale_buf[c] = scales[:, part]

    def send(g):
        at = pl.ds(g * group * VDIM, group * VDIM)
        return pltpu.make_async_copy(result.at[:, at], attended.at[:, at], sems.at[g])

    cache_copies = [
        pltpu.make_async_copy(cache_buf, page_cache, sems.at[steps]),
        pltpu.make_async_copy(scale_buf, page_scales, sems.at[steps + 1]),
    ]

    def send_most():
        for copy in cache_copies + [send(g) for g in range(steps - 1)]:
            copy.start()

    for i in range(len(arrived) // (1 + SWAP)):
        latents[i * rows:(i + 1) * rows, :] = swapped_block(i)[:LAT].T

    @pl.when(lax.axis_index("cp") == 0)
    def _():
        for h in range(heads):
            part = slice(h * rows, (h + 1) * rows)
            result[:, h * VDIM:(h + 1) * VDIM] = (own_result[part, :] / totals[part, :]).astype(jnp.bfloat16)
        encode_found()
        send_most()

    @pl.when(lax.axis_index("cp") > 0)
    def _():
        for i in range(count // 2):
            at = 2 * i * rows
            keys[:, at:at + rows] = arrived[i * (1 + SWAP)][...]
            keys[:, at + rows:at + 2 * rows] = swapped_block(i)
        scores, values, weights = {}, {}, {}
        for step in range(steps + 2):
            if step < steps:
                scores[step] = score(step)
            if step == 2:
                encode_found()
            if step == steps + 1:
                send_most()
            if 0 <= step - 2:
                finish(step - 2, *weights.pop(step - 2), values.pop(step - 2))
            if 0 <= step - 1 < steps:
                values[step - 1] = value(step - 1)
                weights[step - 1] = weigh(step - 1, scores.pop(step - 1))

    send(steps - 1).start()
    for copy in cache_copies + [send(g) for g in range(steps)]:
        copy.wait()


def fetch(own, n_cp, n_dec):
    blocks = []
    for step in range(1, n_cp - 1, 2):
        pairs = [(c * n_dec + e, (c + step + e % 2) % n_cp * n_dec + e) for c in range(n_cp) for e in range(n_dec)]
        blocks.append(lax.ppermute(own, ("cp", "dec"), pairs))
    return blocks


def swap(blocks, n_dec):
    pieces = []
    for block in blocks:
        parts = [block[at:at + ROW // SWAP] for at in range(0, ROW, ROW // SWAP)]
        pieces += [block] + [lax.ppermute(part, "dec", [(e, e ^ 1) for e in range(n_dec)]) for part in parts]
    return pieces


def on_device(queries, latent_rows, key_absorb, value_expand, prompt_pages, decode_owner, slot_offset):
    n_cp = lax.axis_size("cp")
    dec_count = lax.axis_size("dec")
    heads = key_absorb.shape[0]
    rows = latent_rows.shape[0]
    prompts, width = decode_owner.shape
    slot_count = 3 * (rows // PAGE) // (2 * dec_count)
    kept = slot_count * PAGE
    reach = width * dec_count * slot_count * PAGE
    count = -(-reach // rows) - (1 if prompts == 2 else 0)
    count = min(n_cp - 2, count + count % 2)
    own = latent_rows.T
    blocks = fetch(own, n_cp, dec_count)

    vmem = pl.BlockSpec(memory_space=pltpu.VMEM)
    hbm = pl.BlockSpec(memory_space=pltpu.HBM)
    params = pltpu.CompilerParams(vmem_limit_bytes=32 * 2**20)
    group, chunks = 4, (heads // 2, heads // 2)
    inputs = (prompt_pages, decode_owner, slot_offset, own, queries, key_absorb, value_expand)
    combined, result, peaks, totals, sent_rows, bias, picked, filled, own_copy, value_copy = pl.pallas_call(
        functools.partial(own_kernel, n_cp, count, chunks, group, slot_count),
        in_specs=[hbm] * 7,
        out_specs=[vmem] * 10,
        out_shape=[
            jax.ShapeDtypeStruct((heads * rows, ROW), jnp.bfloat16),
            jax.ShapeDtypeStruct((heads * rows, VDIM), jnp.float32),
            jax.ShapeDtypeStruct((heads * rows, LANES), jnp.float32),
            jax.ShapeDtypeStruct((heads * rows, LANES), jnp.float32),
            jax.ShapeDtypeStruct((kept + PAGE, -(-ROW // LANES) * LANES), jnp.bfloat16),
            jax.ShapeDtypeStruct((rows, count * rows), jnp.float32),
            jax.ShapeDtypeStruct((kept, (n_cp - 1) * rows), jnp.bfloat16),
            jax.ShapeDtypeStruct((8, LANES), jnp.float32),
            jax.ShapeDtypeStruct(own.shape, jnp.bfloat16),
            jax.ShapeDtypeStruct(value_expand.shape, jnp.bfloat16),
        ],
        scratch_shapes=[
            pltpu.SMEM(prompt_pages.shape, jnp.int32),
            pltpu.SMEM(decode_owner.shape, jnp.int32),
            pltpu.SMEM(slot_offset.shape, jnp.int32),
            pltpu.VMEM((rows, heads * HEAD), jnp.bfloat16),
            pltpu.VMEM((heads, NOPE, LAT), jnp.bfloat16),
            pltpu.VMEM((rows, LAT), jnp.bfloat16),
            pltpu.SemaphoreType.DMA((4 + 3 * len(chunks),)),
        ],
        cost_estimate=pl.CostEstimate(
            flops=2 * rows * heads * (2 * NOPE * LAT + rows * (ROW + VDIM)),
            bytes_accessed=2 * (queries.size + key_absorb.size + heads * rows * ROW),
            transcendentals=rows * heads * rows,
        ),
        compiler_params=params,
        name="own",
    )(*[pltpu.with_memory_space_constraint(x, pltpu.HBM) for x in inputs])
    sent_rows = lax.ppermute(sent_rows, "cp", [(c, (c + n_cp - 1) % n_cp) for c in range(n_cp)])
    blocks, picked = lax.optimization_barrier((blocks, picked))
    pieces = swap(blocks, dec_count)
    found, fetched_values = pl.pallas_call(
        functools.partial(arrived_kernel, count // 2),
        in_specs=[vmem] * (3 + len(blocks)),
        out_specs=[vmem] * 2,
        out_shape=[
            jax.ShapeDtypeStruct((kept, ROW), jnp.float32),
            jax.ShapeDtypeStruct((count // 2 * rows, heads * VDIM), jnp.bfloat16),
        ],
        cost_estimate=pl.CostEstimate(flops=2**20, bytes_accessed=2**10, transcendentals=0),
        compiler_params=params,
        name="arrived",
    )(picked, own_copy, value_copy, *blocks)

    group = 4 if count <= 4 else 2
    operands = (combined, result, peaks, totals, value_copy, bias, fetched_values, picked, found, filled, sent_rows, *pieces)
    attended, page_cache, page_scales = pl.pallas_call(
        functools.partial(earlier_kernel, count, group),
        in_specs=[vmem] * len(operands),
        out_specs=[hbm] * 3,
        out_shape=[
            jax.ShapeDtypeStruct((rows, heads * VDIM), jnp.bfloat16),
            jax.ShapeDtypeStruct((slot_count, PAGE, ROW), jnp.bfloat16),
            jax.ShapeDtypeStruct((slot_count, NBLK, PAGE), jnp.bfloat16),
        ],
        scratch_shapes=[
            pltpu.VMEM((ROW, count * rows), jnp.bfloat16),
            pltpu.VMEM((len(blocks) * rows, LAT), jnp.bfloat16),
            pltpu.VMEM((rows, heads * VDIM), jnp.bfloat16),
            pltpu.VMEM((slot_count, PAGE, ROW), jnp.bfloat16),
            pltpu.VMEM((slot_count, NBLK, PAGE), jnp.bfloat16),
            pltpu.SemaphoreType.DMA((heads // group + 2,)),
        ],
        cost_estimate=pl.CostEstimate(flops=2**20, bytes_accessed=2**10, transcendentals=0),
        compiler_params=params,
        name="earlier",
    )(*operands)
    page_cache = page_cache.reshape(1, 1, slot_count, PAGE, ROW)
    page_scales = page_scales.transpose(0, 2, 1).reshape(1, 1, slot_count, PAGE, NBLK)
    return attended, page_cache, page_scales


def solution(mesh):
    return jax.shard_map(
        on_device,
        mesh=mesh,
        in_specs=(
            P(("grp", "cp"), "dec"),
            P(("grp", "cp"), None),
            P("dec", None, None),
            P("dec", None, None),
            P("grp"),
            P("grp", None),
            P("grp"),
        ),
        out_specs=(
            P(("grp", "cp"), "dec"),
            P(("grp", "cp"), "dec", None, None, None),
            P(("grp", "cp"), "dec", None, None, None),
        ),
        check_vma=False,
    )
```

```python
import functools
import math

import jax
import jax.numpy as jnp
from jax import lax
from jax.experimental import pallas as pl
from jax.experimental.pallas import tpu as pltpu
from jax.sharding import PartitionSpec as P

LAT = 512
ROPE = 64
NOPE = 128
VDIM = 128
PAGE = 16
BLOCK = 128
NBLK = LAT // BLOCK
ROW = LAT + ROPE
HEAD = NOPE + ROPE
LANES = 128
SWAP = 2

masked_fill = -1e30
amax_epsilon = 1e-06
exp2_scale = math.log2(math.e) / math.sqrt(HEAD)

NT = (((1,), (1,)), ((), ()))


def prompt_starts(prompt_pages):
    starts = [jnp.int32(0)]
    for k in range(prompt_pages.shape[0] - 1):
        starts.append(starts[-1] + prompt_pages[k])
    return starts


def visible_bias(prompt_pages, rows, steps_back):
    first = lax.axis_index("cp") * rows
    token = first + lax.broadcasted_iota(jnp.int32, (rows, 1), 0)
    begin = jnp.zeros((rows, 1), jnp.int32)
    for start in prompt_starts(prompt_pages):
        begin = jnp.maximum(begin, jnp.where(start * PAGE <= token, start * PAGE, 0))
    spot = first - steps_back * rows + lax.broadcasted_iota(jnp.int32, (1, rows), 1)
    return jnp.where((spot >= begin) & (spot <= token), 0.0, masked_fill)


def swap_pair(position, n_cp):
    odd = lax.rem(lax.axis_index("dec"), 2)
    within = lax.rem(position + 1, 2)
    swapped = position - within + lax.rem(within + odd, 2)
    paired = (position >= 1) & (position <= (n_cp - 1) // 2 * 2)
    return jnp.where(paired, swapped, position)


def slot_pages(owner, slot_count, prompt_pages, decode_owner, slot_offset):
    prompts, width = decode_owner.shape
    cycle = width * lax.axis_size("dec") * slot_count
    starts = prompt_starts(prompt_pages)
    pages, start, offset, place = jnp.int32(0), jnp.int32(0), jnp.int32(0), jnp.int32(0)
    for k in range(prompts):
        for p in range(width):
            mine = decode_owner[k, p] == owner
            pages = jnp.where(mine, prompt_pages[k], pages)
            start = jnp.where(mine, starts[k], start)
            offset = jnp.where(mine, slot_offset[k], offset)
            place = jnp.where(mine, p, place)
    result = []
    for c in range(slot_count):
        turn = width * (lax.axis_index("dec") * slot_count + c) + place
        page = lax.rem(turn - offset + 2 * cycle, cycle)
        result.append((page < pages, start + page))
    return result


def row_picker(targets, columns):
    kept = len(targets) * PAGE
    row = lax.broadcasted_iota(jnp.int32, (kept, 1), 0)
    target = jnp.full((kept, 1), -1, jnp.int32)
    for c, column in enumerate(targets):
        target = jnp.where(row // PAGE == c, column + row % PAGE, target)
    column = lax.broadcasted_iota(jnp.int32, (1, columns), 1)
    return jnp.where(column == target, 1.0, 0.0).astype(jnp.bfloat16)


def head_values(latents, value_expand, h):
    both = jnp.concatenate([value_expand[h], value_expand[h + 1]], axis=1)
    return jnp.dot(latents, both, preferred_element_type=jnp.float32).astype(jnp.bfloat16)


def own_kernel(n_cp, count, chunks, group, slot_count, *refs):
    inputs, refs = refs[:7], refs[7:]
    combined, result, peaks, totals, sent_rows, bias, picked, filled, own, value_expand = refs[:10]
    prompt_pages, decode_owner, slot_offset, queries, key_absorb, latents, sems = refs[10:]
    pages_hbm, owner_hbm, offset_hbm, own_hbm, queries_hbm, absorb_hbm, expand_hbm = inputs
    rows = own.shape[1]
    heads = key_absorb.shape[0]
    small = [
        pltpu.make_async_copy(source, target, sems.at[i])
        for i, (source, target) in enumerate(zip(inputs[:4], (prompt_pages, decode_owner, slot_offset, own)))
    ]
    large = {}
    first = 0
    for chunk in chunks:
        at = 4 + 3 * len(large)
        some = pl.ds(first, chunk)
        wide = pl.ds(first * HEAD, chunk * HEAD)
        large[first] = (
            pltpu.make_async_copy(queries_hbm.at[:, wide], queries.at[:, wide], sems.at[at]),
            pltpu.make_async_copy(absorb_hbm.at[some], key_absorb.at[some], sems.at[at + 1]),
            pltpu.make_async_copy(expand_hbm.at[some], value_expand.at[some], sems.at[at + 2]),
        )
        first += chunk
    for copy in small:
        copy.start()
    for chunk_copies in large.values():
        for copy in chunk_copies:
            copy.start()
    steps = heads // group

    def absorb(g):
        for copy in large.get(g * group, ())[:2 if g == 0 else 3]:
            copy.wait()
        for h in range(g * group, (g + 1) * group):
            at = h * HEAD
            absorbed = jnp.dot(queries[:, at:at + NOPE], key_absorb[h], preferred_element_type=jnp.float32)
            combined[h * rows:(h + 1) * rows, :LAT] = absorbed.astype(jnp.bfloat16)
            combined[h * rows:(h + 1) * rows, LAT:] = queries[:, at + NOPE:at + HEAD]

    def score(g):
        return jnp.dot(combined[g * group * rows:(g + 1) * group * rows, :], own[...], preferred_element_type=jnp.float32)

    def value(g):
        return [head_values(latents[...], value_expand, g * group + i) for i in range(0, group, 2)]

    def finish(g, scores, both):
        span = slice(g * group * rows, (g + 1) * group * rows)
        scores = (scores.reshape(group, rows, rows) + own_bias[None]).reshape(group * rows, rows)
        peak = jnp.max(scores, axis=1, keepdims=True)
        weights = jnp.exp2((scores - peak) * exp2_scale)
        total = jnp.sum(weights, axis=1, keepdims=True)
        weights = weights.astype(jnp.bfloat16)
        for i in range(group):
            mine = both[i // 2][:, i % 2 * VDIM:(i % 2 + 1) * VDIM]
            out = jnp.dot(weights[i * rows:(i + 1) * rows], mine, preferred_element_type=jnp.float32)
            result[(g * group + i) * rows:(g * group + i + 1) * rows, :] = out
        peaks[span, :] = jnp.broadcast_to(peak, (group * rows, LANES))
        totals[span, :] = jnp.broadcast_to(total, (group * rows, LANES))

    for copy in small:
        copy.wait()
    latents[...] = own[:LAT, :].T
    own_bias = visible_bias(prompt_pages, rows, 0)
    index_work(n_cp, count, slot_count, prompt_pages, decode_owner, slot_offset, own[...], sent_rows, bias, picked, filled)
    scores, both = {}, {}
    for step in range(steps + 2):
        if step == 1:
            large[0][2].wait()
        if step < steps:
            absorb(step)
        if 0 <= step - 1 < steps:
            scores[step - 1] = score(step - 1)
            both[step - 1] = value(step - 1)
        if 0 <= step - 2:
            finish(step - 2, scores.pop(step - 2), both.pop(step - 2))


def index_work(n_cp, count, slot_count, prompt_pages, decode_owner, slot_offset, block, sent_rows, bias, picked, filled):
    rows = block.shape[1]
    me = lax.axis_index("cp")
    behind = lax.rem(me + n_cp - 1, n_cp)
    targets, here = [], []
    for valid, page in slot_pages(behind, slot_count, prompt_pages, decode_owner, slot_offset):
        here.append(valid & (page * PAGE // rows == me))
        targets.append(jnp.where(here[-1], lax.rem(page * PAGE, rows), -PAGE))
    choice = row_picker(targets, rows)
    sent = lax.dot_general(choice, block, NT, preferred_element_type=jnp.float32)
    encoded, scales = encode(sent, slot_lanes(here))
    kept = choice.shape[0]
    sent_rows[...] = jnp.zeros(sent_rows.shape, jnp.bfloat16)
    sent_rows[:kept, :ROW] = encoded
    sent_rows[kept:kept + NBLK, :kept] = scales
    for b in range(count):
        bias[:, b * rows:(b + 1) * rows] = visible_bias(prompt_pages, rows, swap_pair(jnp.int32(b + 1), n_cp))
    targets, found = [], []
    for valid, page in slot_pages(me, slot_count, prompt_pages, decode_owner, slot_offset):
        steps_back = lax.rem(me - page * PAGE // rows + n_cp, n_cp)
        column = swap_pair(steps_back, n_cp) * rows + lax.rem(page * PAGE, rows)
        targets.append(jnp.where(valid, column, -PAGE))
        found.append(valid & (steps_back < n_cp - 1))
    filled[:1, :] = slot_lanes(found, filled.shape[1])
    picked[...] = row_picker(targets, (n_cp - 1) * rows)


def pick_rows(picked, index, block):
    rows = block.shape[1]
    return lax.dot_general(picked[:, index * rows:(index + 1) * rows], block, NT, preferred_element_type=jnp.float32)


def arrived_kernel(used, picked, own, value_expand, *refs):
    blocks, (found, values) = refs[:-2], refs[-2:]
    rows = own.shape[1]
    for i in range(used):
        latents = blocks[i][:LAT, :].T
        for h in range(0, value_expand.shape[0], 2):
            values[i * rows:(i + 1) * rows, h * VDIM:(h + 2) * VDIM] = head_values(latents, value_expand, h)
    total = pick_rows(picked, 0, own[...])
    for i, block in enumerate(blocks):
        total = total + pick_rows(picked, 1 + 2 * i, block[...])
    found[...] = total


def slot_lanes(flags, width=None):
    lane = lax.broadcasted_iota(jnp.int32, (1, width or len(flags) * PAGE), 1)
    lanes = jnp.zeros(lane.shape, jnp.float32)
    for c, flag in enumerate(flags):
        lanes = jnp.where(lane // PAGE == c, flag.astype(jnp.float32), lanes)
    return lanes


def encode(rows, filled):
    kept = rows.shape[0]
    which = lax.broadcasted_iota(jnp.int32, (kept, LANES), 1)
    table = jnp.zeros((kept, LANES), jnp.float32)
    encoded = []
    for b in range(NBLK):
        values = rows[:, b * BLOCK:(b + 1) * BLOCK]
        scale = jnp.max(jnp.abs(values), axis=1, keepdims=True) + amax_epsilon
        scale = scale.astype(jnp.bfloat16).astype(jnp.float32)
        encoded.append((values / scale).astype(jnp.bfloat16))
        table = jnp.where(which == b, scale, table)
    encoded.append(rows[:, LAT:].astype(jnp.bfloat16))
    scales = (table.T[:NBLK] * filled).astype(jnp.bfloat16)
    return jnp.concatenate(encoded, axis=1), scales


def earlier_kernel(count, group, *refs):
    combined, own_result, peaks, totals, value_expand, bias, fetched_values, picked, found, filled = refs[:10]
    arrived, (result, encoded, scales, latents) = refs[10:-4], refs[-4:]
    rows, width = bias.shape
    heads = value_expand.shape[0]
    steps = heads // group

    def span(g):
        at = g * group * rows
        return slice(at, at + group * rows)

    def score(g):
        blocks = []
        for i in range(count // 2):
            blocks += [arrived[i * (1 + SWAP)][...], swapped_block(i)]
        scores = jnp.dot(combined[span(g), :], jnp.concatenate(blocks, axis=1), preferred_element_type=jnp.float32)
        return (scores.reshape(group, rows, width) + bias[...][None]).reshape(group * rows, width)

    def weigh(g, scores):
        old_peak = peaks[span(g), :]
        parts = [scores[:, b:b + LANES] for b in range(0, width, LANES)]
        peak = jnp.maximum(old_peak, jnp.max(functools.reduce(jnp.maximum, parts), axis=1, keepdims=True))
        parts = [jnp.exp2((part - peak) * exp2_scale) for part in parts]
        total = jnp.sum(functools.reduce(jnp.add, parts), axis=1, keepdims=True)
        factor = jnp.exp2((old_peak - peak) * exp2_scale)
        inverse = 1.0 / (totals[span(g), :] * factor + total)
        weights = jnp.concatenate([part.astype(jnp.bfloat16) for part in parts], axis=1)
        return weights, factor * inverse, inverse

    def value(g):
        return [
            [head_values(latents[i * rows:(i + 1) * rows, :], value_expand, h) for h in range(g * group, (g + 1) * group, 2)]
            for i in range(count // 2)
        ]

    def finish(g, weights, factor, inverse, swapped):
        for i in range(group):
            part = slice(i * rows, (i + 1) * rows)
            h = g * group + i
            values = []
            for b in range(count // 2):
                values.append(fetched_values[b * rows:(b + 1) * rows, h * VDIM:(h + 1) * VDIM])
                values.append(swapped[b][i // 2][:, i % 2 * VDIM:(i % 2 + 1) * VDIM])
            out = jnp.dot(weights[part], jnp.concatenate(values, axis=0), preferred_element_type=jnp.float32)
            out = own_result[h * rows:(h + 1) * rows, :] * factor[part] + out * inverse[part]
            result[:, h * VDIM:(h + 1) * VDIM] = out.astype(jnp.bfloat16)

    def swapped_block(i):
        return jnp.concatenate([part[...] for part in arrived[i * (1 + SWAP) + 1:(i + 1) * (1 + SWAP)]], axis=0)

    def encode_found():
        total = found[...]
        latent_rows, rotary_rows = total[:, :LAT], total[:, LAT:]
        for i in range(len(arrived) // (1 + SWAP)):
            choice = picked[:, (2 + 2 * i) * rows:(3 + 2 * i) * rows]
            latent_rows = latent_rows + jnp.dot(choice, latents[i * rows:(i + 1) * rows, :], preferred_element_type=jnp.float32)
            rotary = swapped_block(i)[LAT:]
            rotary_rows = rotary_rows + lax.dot_general(choice, rotary, NT, preferred_element_type=jnp.float32)
        every = jnp.concatenate([latent_rows, rotary_rows], axis=1)
        encoded[...], scales[...] = encode(every, filled[:1, :every.shape[0]])

    for i in range(len(arrived) // (1 + SWAP)):
        latents[i * rows:(i + 1) * rows, :] = swapped_block(i)[:LAT].T

    @pl.when(lax.axis_index("cp") == 0)
    def _():
        for h in range(heads):
            part = slice(h * rows, (h + 1) * rows)
            result[:, h * VDIM:(h + 1) * VDIM] = (own_result[part, :] / totals[part, :]).astype(jnp.bfloat16)
        encode_found()

    @pl.when(lax.axis_index("cp") > 0)
    def _():
        scores, values, weights = {}, {}, {}
        for step in range(steps + 2):
            if step < steps:
                scores[step] = score(step)
            if step == 2:
                encode_found()
            if 0 <= step - 2:
                finish(step - 2, *weights.pop(step - 2), values.pop(step - 2))
            if 0 <= step - 1 < steps:
                values[step - 1] = value(step - 1)
                weights[step - 1] = weigh(step - 1, scores.pop(step - 1))


def store_kernel(result, encoded, scales, sent_rows, attended, page_cache, page_scales, cache_buf, scale_buf, sems):
    count = sems.shape[0] - 2
    wide = result.shape[1] // count
    copies = []
    for i in range(count):
        some = pl.ds(i * wide, wide)
        copies.append(pltpu.make_async_copy(result.at[:, some], attended.at[:, some], sems.at[i]))
        copies[-1].start()
    kept = encoded.shape[0]
    for c in range(page_cache.shape[0]):
        part = slice(c * PAGE, (c + 1) * PAGE)
        cache_buf[c] = encoded[part, :] + sent_rows[part, :ROW]
        scale_buf[c] = (scales[...] + sent_rows[kept:kept + NBLK, :kept])[:, part]
    for i, (source, target) in enumerate(((cache_buf, page_cache), (scale_buf, page_scales))):
        copies.append(pltpu.make_async_copy(source, target, sems.at[count + i]))
        copies[-1].start()
    for copy in copies:
        copy.wait()


def fetch(own, n_cp, n_dec):
    blocks = []
    for step in range(1, n_cp - 1, 2):
        pairs = [(c * n_dec + e, (c + step + e % 2) % n_cp * n_dec + e) for c in range(n_cp) for e in range(n_dec)]
        blocks.append(lax.ppermute(own, ("cp", "dec"), pairs))
    return blocks


def swap(blocks, n_dec):
    pieces = []
    for block in blocks:
        parts = [block[at:at + ROW // SWAP] for at in range(0, ROW, ROW // SWAP)]
        pieces += [block] + [lax.ppermute(part, "dec", [(e, e ^ 1) for e in range(n_dec)]) for part in parts]
    return pieces


def on_device(queries, latent_rows, key_absorb, value_expand, prompt_pages, decode_owner, slot_offset):
    n_cp = lax.axis_size("cp")
    dec_count = lax.axis_size("dec")
    heads = key_absorb.shape[0]
    rows = latent_rows.shape[0]
    prompts, width = decode_owner.shape
    slot_count = 3 * (rows // PAGE) // (2 * dec_count)
    kept = slot_count * PAGE
    reach = width * dec_count * slot_count * PAGE
    count = -(-reach // rows) - (1 if prompts == 2 else 0)
    count = min(n_cp - 2, count + count % 2)
    own = latent_rows.T
    blocks = fetch(own, n_cp, dec_count)

    vmem = pl.BlockSpec(memory_space=pltpu.VMEM)
    hbm = pl.BlockSpec(memory_space=pltpu.HBM)
    params = pltpu.CompilerParams(vmem_limit_bytes=32 * 2**20)
    group, chunks = 4, (heads // 2, heads // 2)
    inputs = (prompt_pages, decode_owner, slot_offset, own, queries, key_absorb, value_expand)
    combined, result, peaks, totals, sent_rows, bias, picked, filled, own_copy, value_copy = pl.pallas_call(
        functools.partial(own_kernel, n_cp, count, chunks, group, slot_count),
        in_specs=[hbm] * 7,
        out_specs=[vmem] * 10,
        out_shape=[
            jax.ShapeDtypeStruct((heads * rows, ROW), jnp.bfloat16),
            jax.ShapeDtypeStruct((heads * rows, VDIM), jnp.float32),
            jax.ShapeDtypeStruct((heads * rows, LANES), jnp.float32),
            jax.ShapeDtypeStruct((heads * rows, LANES), jnp.float32),
            jax.ShapeDtypeStruct((kept + PAGE, -(-ROW // LANES) * LANES), jnp.bfloat16),
            jax.ShapeDtypeStruct((rows, count * rows), jnp.float32),
            jax.ShapeDtypeStruct((kept, (n_cp - 1) * rows), jnp.bfloat16),
            jax.ShapeDtypeStruct((8, LANES), jnp.float32),
            jax.ShapeDtypeStruct(own.shape, jnp.bfloat16),
            jax.ShapeDtypeStruct(value_expand.shape, jnp.bfloat16),
        ],
        scratch_shapes=[
            pltpu.SMEM(prompt_pages.shape, jnp.int32),
            pltpu.SMEM(decode_owner.shape, jnp.int32),
            pltpu.SMEM(slot_offset.shape, jnp.int32),
            pltpu.VMEM((rows, heads * HEAD), jnp.bfloat16),
            pltpu.VMEM((heads, NOPE, LAT), jnp.bfloat16),
            pltpu.VMEM((rows, LAT), jnp.bfloat16),
            pltpu.SemaphoreType.DMA((4 + 3 * len(chunks),)),
        ],
        cost_estimate=pl.CostEstimate(
            flops=2 * rows * heads * (2 * NOPE * LAT + rows * (ROW + VDIM)),
            bytes_accessed=2 * (queries.size + key_absorb.size + heads * rows * ROW),
            transcendentals=rows * heads * rows,
        ),
        compiler_params=params,
        name="own",
    )(*[pltpu.with_memory_space_constraint(x, pltpu.HBM) for x in inputs])
    sent_rows = lax.ppermute(sent_rows, "cp", [(c, (c + n_cp - 1) % n_cp) for c in range(n_cp)])
    blocks, picked = lax.optimization_barrier((blocks, picked))
    pieces = swap(blocks, dec_count)
    found, fetched_values = pl.pallas_call(
        functools.partial(arrived_kernel, count // 2),
        in_specs=[vmem] * (3 + len(blocks)),
        out_specs=[vmem] * 2,
        out_shape=[
            jax.ShapeDtypeStruct((kept, ROW), jnp.float32),
            jax.ShapeDtypeStruct((count // 2 * rows, heads * VDIM), jnp.bfloat16),
        ],
        cost_estimate=pl.CostEstimate(flops=2**20, bytes_accessed=2**10, transcendentals=0),
        compiler_params=params,
        name="arrived",
    )(picked, own_copy, value_copy, *blocks)

    group = 4 if count <= 4 else 2
    operands = (combined, result, peaks, totals, value_copy, bias, fetched_values, picked, found, filled, *pieces)
    attended, encoded, scales = pl.pallas_call(
        functools.partial(earlier_kernel, count, group),
        in_specs=[vmem] * len(operands),
        out_specs=[vmem] * 3,
        out_shape=[
            jax.ShapeDtypeStruct((rows, heads * VDIM), jnp.bfloat16),
            jax.ShapeDtypeStruct((kept, ROW), jnp.bfloat16),
            jax.ShapeDtypeStruct((NBLK, kept), jnp.bfloat16),
        ],
        scratch_shapes=[
            pltpu.VMEM((len(blocks) * rows, LAT), jnp.bfloat16),
        ],
        cost_estimate=pl.CostEstimate(flops=2**20, bytes_accessed=2**10, transcendentals=0),
        compiler_params=params,
        name="earlier",
    )(*operands)
    sent_rows, attended = lax.optimization_barrier((sent_rows, attended))
    operands = (attended, encoded, scales, sent_rows)
    attended, page_cache, page_scales = pl.pallas_call(
        store_kernel,
        in_specs=[vmem] * len(operands),
        out_specs=[hbm] * 3,
        out_shape=[
            jax.ShapeDtypeStruct((rows, heads * VDIM), jnp.bfloat16),
            jax.ShapeDtypeStruct((slot_count, PAGE, ROW), jnp.bfloat16),
            jax.ShapeDtypeStruct((slot_count, NBLK, PAGE), jnp.bfloat16),
        ],
        scratch_shapes=[
            pltpu.VMEM((slot_count, PAGE, ROW), jnp.bfloat16),
            pltpu.VMEM((slot_count, NBLK, PAGE), jnp.bfloat16),
            pltpu.SemaphoreType.DMA((2 + 2,)),
        ],
        cost_estimate=pl.CostEstimate(flops=2**20, bytes_accessed=2**10, transcendentals=0),
        compiler_params=params,
        name="store",
    )(*operands)
    page_cache = page_cache.reshape(1, 1, slot_count, PAGE, ROW)
    page_scales = page_scales.transpose(0, 2, 1).reshape(1, 1, slot_count, PAGE, NBLK)
    return attended, page_cache, page_scales


def solution(mesh):
    return jax.shard_map(
        on_device,
        mesh=mesh,
        in_specs=(
            P(("grp", "cp"), "dec"),
            P(("grp", "cp"), None),
            P("dec", None, None),
            P("dec", None, None),
            P("grp"),
            P("grp", None),
            P("grp"),
        ),
        out_specs=(
            P(("grp", "cp"), "dec"),
            P(("grp", "cp"), "dec", None, None, None),
            P(("grp", "cp"), "dec", None, None, None),
        ),
        check_vma=False,
    )
```
